32 devices in a mesh: dp: 4 (over z), seq: 8 (over y, x, core).
Axes of the slice: x: 2, y: 2, z: 4, core: 2. Of those that a mesh axis runs over, the one named last changes fastest.
Arguments:
- tokens: bfloat16 [8, 1024, 768], P('dp', 'seq'), may hold values from -6 to 6
- cotangent: bfloat16 [8, 1024, 768], P('dp', 'seq'), may hold values from -6 to 6
- token_docs: int32 [8, 1024], P('dp', 'seq'), may hold values from -1 to 3, as said below
- segment_docs: int32 [8, 8], P('dp'), may hold values from 0 to 3, as said below
- segment_positions: int32 [8, 8], P('dp', 'seq'), may hold values from 0 to 7, as said below
- local_mix: bfloat16 [768, 2304], P(('dp', 'seq')), may hold values from -0.21875 to 0.21875
- local_out: bfloat16 [768, 768], P(('dp', 'seq')), may hold values from -0.625 to 0.625
- local_up: bfloat16 [768, 3072], P(('dp', 'seq')), may hold values from -0.21875 to 0.21875
- local_down: bfloat16 [3072, 768], P(('dp', 'seq')), may hold values from -0.109375 to 0.109375
- local_vectors: bfloat16 [8, 768], P(None, ('dp', 'seq'))
- local_up_bias: bfloat16 [3072], P(('dp', 'seq')), may hold values from -3 to 3
- cross_mix: bfloat16 [768, 2304], P(('dp', 'seq')), may hold values from -0.21875 to 0.21875
- cross_out: bfloat16 [768, 768], P(('dp', 'seq')), may hold values from -0.4375 to 0.4375
- cross_up: bfloat16 [768, 3072], P(('dp', 'seq')), may hold values from -0.21875 to 0.21875
- cross_down: bfloat16 [3072, 768], P(('dp', 'seq')), may hold values from -0.109375 to 0.109375
- cross_vectors: bfloat16 [8, 768], P(None, ('dp', 'seq'))
- cross_up_bias: bfloat16 [3072], P(('dp', 'seq')), may hold values from -3 to 3
- position_table: bfloat16 [64, 768], P(None, ('dp', 'seq')), may hold values from -3 to 3
Outputs:
- layer_out: bfloat16 [8, 1024, 768], P('dp', 'seq')
- input_grad: float32 [8, 1024, 768], P('dp', 'seq')
- local_mix_grad: float32 [768, 2304], P(('dp', 'seq'))
- local_out_grad: float32 [768, 768], P(('dp', 'seq'))
- local_up_grad: float32 [768, 3072], P(('dp', 'seq'))
- local_down_grad: float32 [3072, 768], P(('dp', 'seq'))
- local_vectors_grad: float32 [8, 768], P(None, ('dp', 'seq'))
- local_up_bias_grad: float32 [3072], P(('dp', 'seq'))
- cross_mix_grad: float32 [768, 2304], P(('dp', 'seq'))
- cross_out_grad: float32 [768, 768], P(('dp', 'seq'))
- cross_up_grad: float32 [768, 3072], P(('dp', 'seq'))
- cross_down_grad: float32 [3072, 768], P(('dp', 'seq'))
- cross_vectors_grad: float32 [8, 768], P(None, ('dp', 'seq'))
- cross_up_bias_grad: float32 [3072], P(('dp', 'seq'))
- position_table_grad: float32 [64, 768], P(None, ('dp', 'seq'))
The draws below stay inside these ranges and needn't reach their ends.
Inputs may be any that keep to these rules, and one draw needn't show every extreme that they name: `token_docs`: each segment of 128 tokens belongs to one document: its live tokens carry that document's number and the padding at the end of a document's last segment carries -1; a document's last segment holds 72 to 128 live tokens, every other segment is full, and every segment's first token is live. `segment_docs`: the document number of each segment, equal to token_docs of its first token; in each sequence the numbers start at 0 and rise by one at each new document; every document but a sequence's last covers two segments or more. `segment_positions`: a segment's place within its document, counted from 0; a document covers at most 16 segments.
All inputs are finite; a program needn't handle non-finite values.
Results may differ from the reference program's by a relative error of at most 0.02.
Values may be sent and summed in bfloat16 or wider, within the bound.
No kernel may reach another device: no remote copies, remote signals or barrier semaphores. Data moves between devices by JAX's collectives and lax.ppermute only.
A program may use at most 320 MiB of HBM per device.

```python
from functools import partial
import jax
import jax.numpy as jnp
from jax import lax

D = 768
HEADS = 12
HEAD_DIM = 64
FF = 3072
NPOS = 64
SEG = 128
SEGS = 8
LENGTH = 1024
SEQS = 8


def layout(key):
    folded = jax.random.fold_in(key, 7)
    break_key, live_key = jax.random.split(folded)
    breaks = jax.random.randint(break_key, (SEGS, SEQS), 0, 5) == 0
    row_index = jnp.arange(SEGS, dtype=jnp.int32)[:, None]
    column_index = jnp.arange(SEQS, dtype=jnp.int32)[None, :]
    breaks = jnp.where(column_index == SEQS - 1, True, breaks)
    breaks = jnp.where((column_index == 0) & (row_index < 16), False, breaks)

    def advance(counter, chance):
        begins = (counter < 0) | (counter >= 1) & chance | (counter >= 15)
        counter = jnp.where(begins, 0, counter + 1).astype(jnp.int32)
        return (counter, (counter, begins.astype(jnp.int32)))
    initial = jnp.full((SEQS,), -1, jnp.int32)
    unused, (counters, beginnings) = lax.scan(advance, initial, breaks)
    counters = counters.T.astype(jnp.int32)
    beginnings = beginnings.T
    documents = (jnp.cumsum(beginnings, axis=1) - 1).astype(jnp.int32)
    endings = jnp.concatenate([beginnings[:, 1:], jnp.ones((SEQS, 1), jnp.int32)], axis=1)
    live_count = jax.random.randint(live_key, (SEQS, SEGS), SEG * 9 // 16, SEG + 1)
    seq_grid = jnp.arange(SEQS, dtype=jnp.int32)[:, None]
    seg_grid = jnp.arange(SEGS, dtype=jnp.int32)[None, :]
    live_count = jnp.where((seq_grid == SEQS - 1) & (seg_grid == SEGS - 1), SEG * 9 // 16, live_count)
    live_count = jnp.where(endings > 0, live_count, SEG)
    inside = jnp.arange(SEG, dtype=jnp.int32)[None, None, :] < live_count[:, :, None]
    per_token = jnp.where(inside, documents[:, :, None], -1).astype(jnp.int32)
    return (per_token.reshape(SEQS, SEGS * SEG), documents, counters)


def draw_token_docs(key, part):
    return layout(key)[0]


def draw_segment_docs(key, part):
    return layout(key)[1]


def draw_segment_positions(key, part):
    return layout(key)[2]


def vector_rows(key):
    noise_values = 0.5 * jax.random.normal(key, (8, D), jnp.float32)
    row_index = jnp.arange(8)[:, None]
    gain_rows = (row_index == 3) | (row_index == 6)
    return jnp.where(gain_rows, 1.0 + 0.6 * noise_values, noise_values).astype(jnp.bfloat16)


def draw_local_vectors(key, part):
    return vector_rows(jax.random.fold_in(key, 21))


def draw_cross_vectors(key, part):
    return vector_rows(jax.random.fold_in(key, 22))


def levels(key, extent, cuts, smallest, largest):
    level = 1.0
    for position, blocks in cuts:
        steps = jax.random.uniform(jax.random.fold_in(jax.random.fold_in(key, 6), position), (blocks,), jnp.float32, smallest / len(cuts), largest / len(cuts))
        level = level * jnp.repeat(jnp.exp(steps), extent[position] // blocks).reshape((-1,) + (1,) * (len(extent) - 1 - position))
    return level


def noise(stream_key, extent, spread, most, cuts=(), held_as=jnp.bfloat16):
    level = levels(stream_key, extent, cuts, -0.22, 0.18) if cuts else 1.0
    drawn = jax.random.normal(stream_key, extent, jnp.float32) * spread * level
    return jnp.minimum(jnp.maximum(drawn, -most), most).astype(held_as)


def setup_inputs(seed: int = 0) -> dict:
    arg_keys = jax.random.split(jax.random.key(seed), 19)
    return {
        "tokens": noise(arg_keys[0], (SEQS, LENGTH, D), 1.0, 6.0, ((0, 4), (1, 8))),
        "cotangent": noise(arg_keys[1], (SEQS, LENGTH, D), 1.0, 6.0, ((0, 4), (1, 8))),
        "token_docs": draw_token_docs(jax.random.fold_in(arg_keys[18], 71), 0),
        "segment_docs": draw_segment_docs(jax.random.fold_in(arg_keys[18], 71), 0),
        "segment_positions": draw_segment_positions(jax.random.fold_in(arg_keys[18], 71), 0),
        "local_mix": noise(arg_keys[5], (D, 3 * D), D ** -0.5, 0.21875, ((0, 32),)),
        "local_out": noise(arg_keys[6], (D, D), (D // 8) ** -0.5, 0.625, ((0, 32),)),
        "local_up": noise(arg_keys[7], (D, FF), D ** -0.5, 0.21875, ((0, 32),)),
        "local_down": noise(arg_keys[8], (FF, D), FF ** -0.5, 0.109375, ((0, 32),)),
        "local_vectors": draw_local_vectors(jax.random.fold_in(arg_keys[18], 71), 0),
        "local_up_bias": noise(arg_keys[10], (FF,), 0.5, 3.0, ((0, 32),)),
        "cross_mix": noise(arg_keys[11], (D, 3 * D), D ** -0.5, 0.21875, ((0, 32),)),
        "cross_out": noise(arg_keys[12], (D, D), (D // 4) ** -0.5, 0.4375, ((0, 32),)),
        "cross_up": noise(arg_keys[13], (D, FF), D ** -0.5, 0.21875, ((0, 32),)),
        "cross_down": noise(arg_keys[14], (FF, D), FF ** -0.5, 0.109375, ((0, 32),)),
        "cross_vectors": draw_cross_vectors(jax.random.fold_in(arg_keys[18], 71), 0),
        "cross_up_bias": noise(arg_keys[16], (FF,), 0.5, 3.0, ((0, 32),)),
        "position_table": noise(arg_keys[17], (NPOS, D), 0.5, 3.0, ((1, 32),)),
    }


@jax.custom_vjp
def low(v):
    return lax.optimization_barrier(v.astype(jnp.bfloat16)).astype(jnp.float32)

@jax.custom_vjp
def low_back(v):
    return v

def low_keep(v):
    return (low(v), None)

def low_pass(kept, grad):
    return (grad,)

def back_keep(v):
    return (v, None)

def back_low(kept, grad):
    return (low(grad),)
low.defvjp(low_keep, low_pass)
low_back.defvjp(back_keep, back_low)
epsilon = 1e-05
masked_score = -1000000000.0

def product(left_side, right_side):
    return jnp.dot(left_side, right_side, precision=lax.Precision.HIGHEST)

def layer_norm(values, gain_row, shift_row):
    centered = values - lax.optimization_barrier(jnp.mean(values, axis=-1, keepdims=True))
    variance = lax.optimization_barrier(jnp.mean(centered * centered, axis=-1, keepdims=True))
    return centered * lax.rsqrt(variance + epsilon) * gain_row + shift_row

def attention(query_rows, key_rows, value_rows, allowed, score_form, context_form):
    scores = low_back(jnp.einsum(score_form, query_rows, key_rows, precision=lax.Precision.HIGHEST) * HEAD_DIM ** (-0.5))
    scores = jnp.where(allowed, scores, masked_score)
    weights = low(jax.nn.softmax(scores, axis=-1))
    return jnp.einsum(context_form, weights, value_rows, precision=lax.Precision.HIGHEST)

def segment_attend(mixed_rows, token_docs):
    segment_count = token_docs.shape[0] // SEG
    split_heads = mixed_rows.reshape(segment_count, SEG, 3, HEADS, HEAD_DIM)
    doc_grid = token_docs.reshape(segment_count, SEG)
    allowed = doc_grid[:, None, :, None] == doc_grid[:, None, None, :]
    context = attention(split_heads[:, :, 0], split_heads[:, :, 1], split_heads[:, :, 2], allowed, 'nqhd,nkhd->nhqk', 'nhqk,nkhd->nqhd')
    return context.reshape(segment_count * SEG, D)

def cross_attend(mixed_rows, segment_docs):
    segment_count = segment_docs.shape[0]
    split_heads = mixed_rows.reshape(segment_count, 3, HEADS, HEAD_DIM)
    allowed = segment_docs[:, None] == segment_docs[None, :]
    context = attention(split_heads[:, 0], split_heads[:, 1], split_heads[:, 2], allowed[None], 'qhd,khd->hqk', 'hqk,khd->qhd')
    return context.reshape(segment_count, D)

def encoder_block(inputs, params, attend):
    mix_weight, out_weight, up_weight, down_weight, vectors, up_bias = params
    in_bias = jnp.concatenate([vectors[0], jnp.zeros_like(vectors[0]), vectors[1]])
    mixed_rows = low(low_back(product(low(inputs), mix_weight) + in_bias))
    context = low(low_back(attend(mixed_rows)))
    branch = low_back(product(context, out_weight) + vectors[2])
    first_norm = layer_norm(inputs + branch, vectors[3], vectors[4])
    hidden = low_back(product(low(first_norm), up_weight) + up_bias)
    active = low(jax.nn.gelu(hidden, approximate=False))
    second = low_back(product(active, down_weight) + vectors[5])
    return layer_norm(first_norm + second, vectors[6], vectors[7])

def sequence_layer(params, inputs, token_docs, segment_docs, segment_positions):
    local_params, cross_params, position_rows = params
    segment_count = segment_docs.shape[0]
    first_out = encoder_block(inputs, local_params, partial(segment_attend, token_docs=token_docs))
    segment_grid = first_out.reshape(segment_count, SEG, D)
    position_picks = (segment_positions[:, None] == jnp.arange(NPOS, dtype=jnp.int32)[None, :]).astype(jnp.float32)
    heads_in = segment_grid[:, 0, :] + product(position_picks, position_rows)
    heads_out = encoder_block(heads_in, cross_params, partial(cross_attend, segment_docs=segment_docs))
    joined = jnp.concatenate([heads_out[:, None, :], segment_grid[:, 1:, :]], axis=1)
    return joined.reshape(segment_count * SEG, D)

def widen(array_in):
    return array_in.astype(jnp.float32)

def reference(tokens, cotangent, token_docs, segment_docs, segment_positions, local_mix, local_out, local_up, local_down, local_vectors, local_up_bias, cross_mix, cross_out, cross_up, cross_down, cross_vectors, cross_up_bias, position_table):
    local_params = tuple((widen(array_in) for array_in in (local_mix, local_out, local_up, local_down, local_vectors, local_up_bias)))
    cross_params = tuple((widen(array_in) for array_in in (cross_mix, cross_out, cross_up, cross_down, cross_vectors, cross_up_bias)))
    all_params = (local_params, cross_params, widen(position_table))
    layer_step = jax.checkpoint(sequence_layer)

    def forward(params, inputs):

        def scan_step(carried, pieces):
            return (carried, layer_step(params, pieces[0], pieces[1], pieces[2], pieces[3]))
        unused, outputs = lax.scan(scan_step, jnp.zeros((), jnp.float32), (inputs, token_docs, segment_docs, segment_positions))
        return outputs
    outputs, pullback = jax.vjp(forward, all_params, widen(tokens))
    param_grads, input_grad = pullback(widen(cotangent))
    local_grads, cross_grads, table_grad = param_grads
    return (outputs.astype(jnp.bfloat16), input_grad, local_grads[0], local_grads[1], local_grads[2], local_grads[3], local_grads[4], local_grads[5], cross_grads[0], cross_grads[1], cross_grads[2], cross_grads[3], cross_grads[4], cross_grads[5], table_grad)
```

```python
from functools import partial
import math

import jax
import jax.numpy as jnp
from jax import lax
from jax.experimental import pallas as pl
from jax.experimental.pallas import tpu as pltpu
from jax.sharding import PartitionSpec as P

D = 768
HEADS = 12
HEAD_DIM = 64
SEG = 128
MICRO = 2


epsilon = 1e-05
masked_score = -1000000000.0
owner_dims = (0, 0, 0, 0, 1, 0, 0, 0, 0, 0, 1, 0, 1)


def layer_norm(values, gain_row, shift_row):
    centered = values - jnp.mean(values, axis=-1, keepdims=True)
    variance = jnp.mean(centered * centered, axis=-1, keepdims=True)
    return centered * lax.rsqrt(variance + epsilon) * gain_row + shift_row


def gelu_exact(hidden):
    return jax.nn.gelu(hidden, approximate=False)


def contract(left_side, right_side, left_dim, right_dim):
    return lax.dot_general(
        left_side,
        right_side,
        (((left_dim,), (right_dim,)), ((), ())),
        preferred_element_type=jnp.float32,
    )


def contract_exact(left_side, right_side, left_dim, right_dim):
    return lax.dot_general(
        left_side,
        right_side,
        (((left_dim,), (right_dim,)), ((), ())),
        precision=lax.Precision.HIGHEST,
        preferred_element_type=jnp.float32,
    )


def owner_pack(grads, devices):
    pieces = []
    for grad_value, split_dim in zip(grads, owner_dims):
        if split_dim == 0:
            pieces.append(grad_value.reshape(devices, -1))
        else:
            row_count = grad_value.shape[0]
            pieces.append(
                grad_value.reshape(row_count, devices, -1).transpose(1, 0, 2).reshape(devices, -1)
            )
    return jnp.concatenate(pieces, axis=1)


def owner_unpack(packed, shard_shapes):
    results = []
    offset = 0
    for shard_shape in shard_shapes:
        length = math.prod(shard_shape)
        results.append(packed[0, offset : offset + length].reshape(shard_shape))
        offset = offset + length
    return tuple(results)


def fetch_weights(
    local_mix,
    local_out,
    local_up,
    local_down,
    local_vectors,
    local_up_bias,
    cross_mix,
    cross_out,
    cross_up,
    cross_down,
    cross_vectors,
    cross_up_bias,
    position_table,
):
    return (
        lax.all_gather(local_mix, ("dp", "seq"), axis=0, tiled=True),
        lax.all_gather(local_out, ("dp", "seq"), axis=0, tiled=True),
        lax.all_gather(local_up, ("dp", "seq"), axis=0, tiled=True),
        lax.all_gather(local_down, ("dp", "seq"), axis=0, tiled=True),
        lax.all_gather(local_vectors, ("dp", "seq"), axis=1, tiled=True),
        lax.all_gather(local_up_bias, ("dp", "seq"), axis=0, tiled=True),
        lax.all_gather(cross_mix, ("dp", "seq"), axis=0, tiled=True),
        lax.all_gather(cross_out, ("dp", "seq"), axis=0, tiled=True),
        lax.all_gather(cross_up, ("dp", "seq"), axis=0, tiled=True),
        lax.all_gather(cross_down, ("dp", "seq"), axis=0, tiled=True),
        lax.all_gather(cross_vectors, ("dp", "seq"), axis=1, tiled=True),
        lax.all_gather(cross_up_bias, ("dp", "seq"), axis=0, tiled=True),
        lax.all_gather(position_table, ("dp", "seq"), axis=1, tiled=True),
    )


def segment_parts(mixed_rows, token_docs):
    segment_count = token_docs.shape[0]
    split_heads = mixed_rows.reshape(segment_count, SEG, 3, HEADS, HEAD_DIM)
    allowed = token_docs[:, None, :, None] == token_docs[:, None, None, :]
    scores = jnp.einsum(
        "nqhd,nkhd->nhqk",
        split_heads[:, :, 0],
        split_heads[:, :, 1],
        preferred_element_type=jnp.float32,
    ) * HEAD_DIM ** (-0.5)
    scores = jnp.where(allowed, scores, masked_score)
    return (split_heads, scores)


def segment_forward(mixed_rows, token_docs):
    split_heads, scores = segment_parts(mixed_rows, token_docs)
    log_total = jax.nn.logsumexp(scores, axis=-1)
    weights = jax.nn.softmax(scores, axis=-1).astype(jnp.bfloat16)
    context = jnp.einsum(
        "nhqk,nkhd->nqhd", weights, split_heads[:, :, 2], preferred_element_type=jnp.float32
    )
    return (context.reshape(-1, D).astype(jnp.bfloat16), log_total)


def segment_backward(context_grad, log_total, mixed_rows, token_docs):
    split_heads, scores = segment_parts(mixed_rows, token_docs)
    segment_count = token_docs.shape[0]
    probs = jnp.exp(scores - log_total[..., None])
    grad_heads = context_grad.reshape(segment_count, SEG, HEADS, HEAD_DIM)
    prob_grad = jnp.einsum(
        "nqhd,nkhd->nhqk", grad_heads, split_heads[:, :, 2], preferred_element_type=jnp.float32
    )
    value_grad = jnp.einsum(
        "nhqk,nqhd->nkhd",
        probs.astype(jnp.bfloat16),
        grad_heads,
        preferred_element_type=jnp.float32,
    )
    score_grad = probs * (prob_grad - jnp.sum(probs * prob_grad, axis=-1, keepdims=True))
    score_low = score_grad.astype(jnp.bfloat16) * HEAD_DIM ** (-0.5)
    query_grad = jnp.einsum(
        "nhqk,nkhd->nqhd", score_low, split_heads[:, :, 1], preferred_element_type=jnp.float32
    )
    key_grad = jnp.einsum(
        "nhqk,nqhd->nkhd", score_low, split_heads[:, :, 0], preferred_element_type=jnp.float32
    )
    row_total = segment_count * SEG
    return jnp.concatenate(
        [
            query_grad.reshape(row_total, D),
            key_grad.reshape(row_total, D),
            value_grad.reshape(row_total, D),
        ],
        axis=1,
    )


def cross_parts(mixed_rows, gathered, segment_docs):
    group_size = segment_docs.shape[0]
    per_device = mixed_rows.shape[0] // group_size
    query_rows = mixed_rows[:, :D].reshape(group_size, per_device, HEADS, HEAD_DIM)
    key_rows = gathered[:, :, :D].reshape(group_size, -1, HEADS, HEAD_DIM)
    value_rows = gathered[:, :, D:].reshape(group_size, -1, HEADS, HEAD_DIM)
    own_docs = lax.dynamic_slice_in_dim(
        segment_docs, lax.axis_index("seq") * per_device, per_device, 1
    )
    allowed = own_docs[:, None, :, None] == segment_docs[:, None, None, :]
    scores = jnp.einsum(
        "bqhd,bkhd->bhqk", query_rows, key_rows, preferred_element_type=jnp.float32
    ) * HEAD_DIM ** (-0.5)
    scores = jnp.where(allowed, scores, masked_score)
    return (query_rows, key_rows, value_rows, scores)


def cross_forward(mixed_rows, segment_docs):
    group_size = segment_docs.shape[0]
    per_device = mixed_rows.shape[0] // group_size
    pair_rows = mixed_rows[:, D:].reshape(group_size, per_device, 2 * D)
    gathered = lax.all_gather(pair_rows, "seq", axis=1, tiled=True)
    query_rows, key_rows, value_rows, scores = cross_parts(mixed_rows, gathered, segment_docs)
    log_total = jax.nn.logsumexp(scores, axis=-1)
    weights = jax.nn.softmax(scores, axis=-1).astype(jnp.bfloat16)
    context = jnp.einsum("bhqk,bkhd->bqhd", weights, value_rows, preferred_element_type=jnp.float32)
    return (context.reshape(-1, D).astype(jnp.bfloat16), (gathered, log_total))


def cross_backward(context_grad, cross_kept, mixed_rows, segment_docs):
    gathered, log_total = cross_kept
    group_size = segment_docs.shape[0]
    row_total = mixed_rows.shape[0]
    per_device = row_total // group_size
    query_rows, key_rows, value_rows, scores = cross_parts(mixed_rows, gathered, segment_docs)
    probs = jnp.exp(scores - log_total[..., None])
    grad_heads = context_grad.reshape(group_size, per_device, HEADS, HEAD_DIM)
    prob_grad = jnp.einsum(
        "bqhd,bkhd->bhqk", grad_heads, value_rows, preferred_element_type=jnp.float32
    )
    value_grad = jnp.einsum(
        "bhqk,bqhd->bkhd",
        probs.astype(jnp.bfloat16),
        grad_heads,
        preferred_element_type=jnp.float32,
    )
    score_grad = probs * (prob_grad - jnp.sum(probs * prob_grad, axis=-1, keepdims=True))
    score_low = score_grad.astype(jnp.bfloat16) * HEAD_DIM ** (-0.5)
    query_grad = jnp.einsum(
        "bhqk,bkhd->bqhd", score_low, key_rows, preferred_element_type=jnp.float32
    )
    key_grad = jnp.einsum(
        "bhqk,bqhd->bkhd", score_low, query_rows, preferred_element_type=jnp.float32
    )
    pair_grads = jnp.concatenate(
        [key_grad.reshape(group_size, -1, D), value_grad.reshape(group_size, -1, D)], axis=2
    )
    own_pairs = lax.psum_scatter(
        pair_grads.astype(jnp.bfloat16), "seq", scatter_dimension=1, tiled=True
    ).astype(jnp.float32)
    return jnp.concatenate(
        [query_grad.reshape(row_total, D), own_pairs.reshape(row_total, 2 * D)], axis=1
    )


def block_forward(inputs, weights, attend):
    mix_weight, out_weight, up_weight, down_weight, vectors, up_bias = weights
    vector_rows = vectors.astype(jnp.float32)
    in_bias = jnp.concatenate([vector_rows[0], jnp.zeros_like(vector_rows[0]), vector_rows[1]])
    rounded = inputs.astype(jnp.bfloat16)
    mixed_rows = (
        jnp.dot(rounded, mix_weight, preferred_element_type=jnp.float32) + in_bias
    ).astype(jnp.bfloat16)
    context, attend_kept = attend(mixed_rows)
    first_sum = (
        inputs + jnp.dot(context, out_weight, preferred_element_type=jnp.float32) + vector_rows[2]
    )
    first_norm = layer_norm(first_sum, vector_rows[3], vector_rows[4])
    first_low = first_norm.astype(jnp.bfloat16)
    hidden = jnp.dot(first_low, up_weight, preferred_element_type=jnp.float32) + up_bias.astype(
        jnp.float32
    )
    active = gelu_exact(hidden).astype(jnp.bfloat16)
    second_sum = (
        first_norm
        + jnp.dot(active, down_weight, preferred_element_type=jnp.float32)
        + vector_rows[5]
    )
    output = layer_norm(second_sum, vector_rows[6], vector_rows[7])
    return (
        output,
        (
            rounded,
            mixed_rows,
            attend_kept,
            context,
            first_sum,
            first_low,
            hidden,
            active,
            second_sum,
        ),
    )


def block_backward(output_grad, block_kept, weights, attend_back):
    mix_weight, out_weight, up_weight, down_weight, vectors, up_bias = weights
    vector_rows = vectors.astype(jnp.float32)
    rounded, mixed_rows, attend_kept, context, first_sum, first_low, hidden, active, second_sum = (
        block_kept
    )
    unused, second_pull = jax.vjp(layer_norm, second_sum, vector_rows[6], vector_rows[7])
    second_grad, gain_two, shift_two = second_pull(output_grad)
    second_low = second_grad.astype(jnp.bfloat16)
    down_grad = contract(active, second_low, 0, 0)
    down_bias = jnp.sum(second_low.astype(jnp.float32), axis=0)
    active_grad = contract(second_low, down_weight, 1, 1)
    unused, gelu_pull = jax.vjp(gelu_exact, hidden)
    hidden_grad = gelu_pull(active_grad)[0]
    hidden_low = hidden_grad.astype(jnp.bfloat16)
    up_grad = contract(first_low, hidden_low, 0, 0)
    up_bias_grad = jnp.sum(hidden_low.astype(jnp.float32), axis=0)
    first_grad = second_grad + contract(hidden_low, up_weight, 1, 1)
    unused, first_pull = jax.vjp(layer_norm, first_sum, vector_rows[3], vector_rows[4])
    sum_grad, gain_one, shift_one = first_pull(first_grad)
    branch_low = sum_grad.astype(jnp.bfloat16)
    out_grad = contract(context, branch_low, 0, 0)
    out_bias = jnp.sum(branch_low.astype(jnp.float32), axis=0)
    context_low = contract(branch_low, out_weight, 1, 1).astype(jnp.bfloat16)
    mixed_low = attend_back(context_low, attend_kept, mixed_rows).astype(jnp.bfloat16)
    mix_grad = contract(rounded, mixed_low, 0, 0)
    mixed_sums = jnp.sum(mixed_low.astype(jnp.float32), axis=0)
    input_grad = sum_grad + contract(mixed_low, mix_weight, 1, 1)
    vectors_grad = jnp.stack(
        [
            mixed_sums[:D],
            mixed_sums[2 * D :],
            out_bias,
            gain_one,
            shift_one,
            down_bias,
            gain_two,
            shift_two,
        ]
    )
    return (input_grad, (mix_grad, out_grad, up_grad, down_grad, vectors_grad, up_bias_grad))


def shards(
    tokens,
    cotangent,
    token_docs,
    segment_docs,
    segment_positions,
    local_mix,
    local_out,
    local_up,
    local_down,
    local_vectors,
    local_up_bias,
    cross_mix,
    cross_out,
    cross_up,
    cross_down,
    cross_vectors,
    cross_up_bias,
    position_table,
):
    sequence_count, span, width = tokens.shape
    group_size = sequence_count // MICRO
    segment_count = span // SEG
    devices = lax.axis_size(("dp", "seq"))
    shard_shapes = tuple(
        (
            array_in.shape
            for array_in in (
                local_mix,
                local_out,
                local_up,
                local_down,
                local_vectors,
                local_up_bias,
                cross_mix,
                cross_out,
                cross_up,
                cross_down,
                cross_vectors,
                cross_up_bias,
                position_table,
            )
        )
    )
    layer_outputs = []
    input_grads = []
    totals = ()
    for micro_step in range(MICRO):
        lower_row = micro_step * group_size
        upper_row = lower_row + group_size
        gathered = fetch_weights(
            local_mix,
            local_out,
            local_up,
            local_down,
            local_vectors,
            local_up_bias,
            cross_mix,
            cross_out,
            cross_up,
            cross_down,
            cross_vectors,
            cross_up_bias,
            position_table,
        )
        local_weights = gathered[0:6]
        cross_weights = gathered[6:12]
        position_rows = gathered[12]
        inputs = tokens[lower_row:upper_row].reshape(group_size * span, width).astype(jnp.float32)
        docs_here = token_docs[lower_row:upper_row]
        segments_here = segment_docs[lower_row:upper_row]
        first_out, first_kept = block_forward(
            inputs, local_weights, partial(segment_forward, token_docs=docs_here)
        )
        segment_grid = first_out.reshape(group_size * segment_count, SEG, width)
        places = segment_positions[lower_row:upper_row].reshape(group_size * segment_count)
        position_picks = (
            places[:, None] == jnp.arange(position_rows.shape[0], dtype=jnp.int32)[None, :]
        ).astype(jnp.bfloat16)
        heads_in = segment_grid[:, 0, :] + jnp.dot(
            position_picks, position_rows, preferred_element_type=jnp.float32
        )
        heads_out, cross_kept = block_forward(
            heads_in, cross_weights, partial(cross_forward, segment_docs=segments_here)
        )
        joined = jnp.concatenate([heads_out[:, None, :], segment_grid[:, 1:, :]], axis=1)
        layer_outputs.append(joined.astype(jnp.bfloat16))
        gathered = fetch_weights(
            local_mix,
            local_out,
            local_up,
            local_down,
            local_vectors,
            local_up_bias,
            cross_mix,
            cross_out,
            cross_up,
            cross_down,
            cross_vectors,
            cross_up_bias,
            position_table,
        )
        local_weights = gathered[0:6]
        cross_weights = gathered[6:12]
        output_grad = cotangent[lower_row:upper_row].astype(jnp.float32)
        heads_grad, cross_grads = block_backward(
            output_grad[:, 0, :],
            cross_kept,
            cross_weights,
            partial(cross_backward, segment_docs=segments_here),
        )
        table_grad = contract_exact(position_picks.astype(jnp.float32), heads_grad, 0, 0)
        first_grad = jnp.concatenate(
            [heads_grad[:, None, :], output_grad[:, 1:, :]], axis=1
        ).reshape(group_size * span, width)
        input_grad, local_grads = block_backward(
            first_grad, first_kept, local_weights, partial(segment_backward, token_docs=docs_here)
        )
        input_grads.append(input_grad.reshape(group_size, span, width))
        step_grads = local_grads + cross_grads + (table_grad,)
        if micro_step == 0:
            totals = tuple(step_grads)
        else:
            totals = tuple(
                (total_sum + step_sum for total_sum, step_sum in zip(totals, step_grads))
            )
    packed_total = lax.psum_scatter(
        owner_pack(totals, devices), ("dp", "seq"), scatter_dimension=0, tiled=True
    )
    summed = owner_unpack(packed_total, shard_shapes)
    layer_output = jnp.concatenate(layer_outputs, axis=0)
    input_gradient = jnp.concatenate(input_grads, axis=0)
    return (layer_output, input_gradient) + tuple(summed)


PLANE = 4


def swap_dp(array_in, shift):
    return lax.ppermute(array_in, "dp", [(i, (i + shift) % 4) for i in range(4)])


def swap_core(array_in):
    return lax.ppermute(array_in, "seq", [(i, i ^ 1) for i in range(8)])


def swap_chip(array_in, mask):
    return lax.ppermute(array_in, "seq", [(i, i ^ (2 * mask)) for i in range(8)])


def swap_one(array_in):
    return lax.ppermute(array_in, "seq", [(i, i ^ (2 if i % 2 == 0 else 4)) for i in range(8)])


def swap_two(array_in):
    return lax.ppermute(array_in, "seq", [(i, i ^ (4 if i % 2 == 0 else 2)) for i in range(8)])


def place_in():
    layer = lax.axis_index("dp")
    spot = lax.axis_index("seq")
    return layer, spot // 2, spot % 2


def copies(pieces, shape, spots):
    count = len(pieces)

    def kernel(*refs):
        total, held, sems = refs[count], refs[count + 1 : -1], refs[-1]
        places = spots(*place_in())
        inward = [
            pltpu.make_async_copy(refs[i], held[i], sems.at[0, i]) for i in range(count)
        ]
        outward = [
            pltpu.make_async_copy(held[i], total.at[places[i]], sems.at[1, i])
            for i in range(count)
        ]
        for copy in inward:
            copy.start()
        for before, after in zip(inward, outward):
            before.wait()
            after.start()
        for copy in outward:
            copy.wait()

    size = 2 * math.prod(shape) * pieces[0].dtype.itemsize
    return pl.pallas_call(
        kernel,
        out_shape=jax.ShapeDtypeStruct(shape, pieces[0].dtype),
        in_specs=[pl.BlockSpec(memory_space=pl.ANY)] * count,
        out_specs=pl.BlockSpec(memory_space=pl.ANY),
        scratch_shapes=[pltpu.VMEM(piece.shape, piece.dtype) for piece in pieces]
        + [pltpu.SemaphoreType.DMA((2, count))],
        compiler_params=pltpu.CompilerParams(vmem_limit_bytes=24 * 2**20),
        cost_estimate=pl.CostEstimate(flops=0, bytes_accessed=size, transcendentals=0),
    )(*pieces)


def gather_dp(shard):
    pieces = [shard] + [swap_dp(shard, shift) for shift in (1, 2, 3)]
    return copies(
        pieces,
        (4,) + shard.shape,
        lambda layer, chip, core: [lax.rem(layer + 4 - shift, 4) for shift in range(4)],
    )


def gather_core(piece, axis):
    other = swap_core(piece)
    shape = piece.shape[:axis] + (2,) + piece.shape[axis:]
    every = (slice(None),) * axis
    return copies([piece, other], shape, lambda layer, chip, core: [every + (core,), every + (1 - core,)])


def gather_all(shard):
    column = gather_dp(shard)
    first = swap_one(column)
    second = swap_two(column)
    third = swap_two(first)
    mine = [column, first, second, third]
    every = slice(None)

    def spots(layer, chip, core):
        near, far = chip ^ (1 + core), chip ^ (2 - core)
        found = [(every, spot, core) for spot in (chip, near, far, chip ^ 3)]
        return found + [(every, spot, 1 - core) for spot in (chip, far, near, chip ^ 3)]

    return copies(mine + [swap_core(piece) for piece in mine], (4, 4, 2) + shard.shape, spots)


def pick(array_in, index, axis):
    return lax.dynamic_index_in_dim(array_in, index, axis, keepdims=False)


def wide(array_in):
    return array_in.astype(jnp.float32)


def low(array_in):
    return array_in.astype(jnp.bfloat16)


def scatter_sum(parts):
    layer, chip, core = place_in()
    rows, columns = parts.shape[3:]
    spots = jnp.stack([chip ^ (1 + core), chip ^ 3, chip ^ (2 - core), chip, core, layer])

    def whole(take):
        return pl.BlockSpec((None, None, None, rows, columns), take)

    def part(take):
        return pl.BlockSpec((None, None, rows, columns), take)

    def single(take):
        return pl.BlockSpec((None, rows, columns), take)

    def run(kernel, grid, in_specs, out_specs, out_shape, *operands):
        size = sum(math.prod(a.shape) * a.dtype.itemsize for a in jax.tree.leaves(out_shape))
        return pl.pallas_call(
            kernel,
            grid_spec=pltpu.PrefetchScalarGridSpec(
                num_scalar_prefetch=1, grid=grid, in_specs=in_specs, out_specs=out_specs
            ),
            out_shape=out_shape,
            cost_estimate=pl.CostEstimate(
                flops=size, bytes_accessed=3 * size, transcendentals=0
            ),
        )(spots, *operands)

    def shaped(*lead, dtype=jnp.bfloat16):
        return jax.ShapeDtypeStruct(lead + (rows, columns), dtype)

    def take_out(parts_ref, gone_ref, held, sems):
        other = 1 - lax.rem(lax.axis_index("seq"), 2)
        inward = [
            pltpu.make_async_copy(parts_ref.at[z, :, other], held.at[z], sems.at[0, z])
            for z in range(4)
        ]
        outward = [
            pltpu.make_async_copy(held.at[z], gone_ref.at[z], sems.at[1, z]) for z in range(4)
        ]
        for copy in inward:
            copy.start()
        for before, after in zip(inward, outward):
            before.wait()
            after.start()
        for copy in outward:
            copy.wait()

    gone = pl.pallas_call(
        take_out,
        out_shape=shaped(4, 4),
        in_specs=[pl.BlockSpec(memory_space=pl.ANY)],
        out_specs=pl.BlockSpec(memory_space=pl.ANY),
        scratch_shapes=[
            pltpu.VMEM((4, 4, rows, columns), jnp.bfloat16),
            pltpu.SemaphoreType.DMA((2, 4)),
        ],
        compiler_params=pltpu.CompilerParams(vmem_limit_bytes=24 * 2**20),
        cost_estimate=pl.CostEstimate(flops=0, bytes_accessed=parts.size * 2, transcendentals=0),
    )(parts)
    got = swap_core(gone)

    def add_two(spots_ref, a_ref, b_ref, o_ref):
        o_ref[...] = low(wide(a_ref[...]) + wide(b_ref[...]))

    sent = run(
        add_two,
        (2, 4),
        [
            whole(lambda i, z, s: (z, s[i], s[4], 0, 0)),
            part(lambda i, z, s: (z, s[i], 0, 0)),
        ],
        part(lambda i, z, s: (i, z, 0, 0)),
        shaped(2, 4),
        parts,
        got,
    )
    back = swap_one(sent)

    def add_three(spots_ref, a_ref, b_ref, c_ref, o_ref):
        o_ref[...] = low(wide(a_ref[...]) + wide(b_ref[...]) + wide(c_ref[...]))

    onward = run(
        add_three,
        (4,),
        [
            whole(lambda z, s: (z, s[2], s[4], 0, 0)),
            part(lambda z, s: (z, s[2], 0, 0)),
            part(lambda z, s: (1, z, 0, 0)),
        ],
        single(lambda z, s: (z, 0, 0)),
        shaped(4),
        parts,
        got,
        back,
    )
    last = swap_two(onward)

    def add_four(spots_ref, a_ref, b_ref, c_ref, d_ref, own_ref, out_a, out_b, out_c):
        total = wide(a_ref[...]) + wide(b_ref[...]) + wide(c_ref[...]) + wide(d_ref[...])
        step = pl.program_id(0)

        @pl.when(step == 3)
        def _():
            own_ref[...] = total

        for shift, ref in ((1, out_a), (2, out_b), (3, out_c)):

            @pl.when(step == shift - 1)
            def _(ref=ref):
                ref[...] = low(total)

    flat = pl.BlockSpec((rows, columns), lambda k, s: (0, 0))

    def level(k, s):
        return lax.rem(s[5] + 1 + k, 4)

    own, *others = run(
        add_four,
        (4,),
        [
            whole(lambda k, s: (level(k, s), s[3], s[4], 0, 0)),
            part(lambda k, s: (level(k, s), s[3], 0, 0)),
            part(lambda k, s: (0, level(k, s), 0, 0)),
            single(lambda k, s: (level(k, s), 0, 0)),
        ],
        [flat] * 4,
        [shaped(dtype=jnp.float32)] + [shaped()] * 3,
        parts,
        got,
        back,
        last,
    )
    total = own
    for shift, other in zip((1, 2, 3), others):
        total = total + wide(swap_dp(other, shift))
    return total


def plane_pieces(piece):
    return [piece] + [swap_chip(piece, mask) for mask in (1, 2, 3)]


def plane_gather(piece):
    layer, chip, core = place_in()
    pieces = jnp.stack(plane_pieces(piece))
    return jnp.stack([pick(pieces, chip ^ spot, 0) for spot in range(4)])


def plane_sum(piece):
    pieces = plane_pieces(piece)
    return (pieces[0] + pieces[1]) + (pieces[2] + pieces[3])


def own_rows(pair_in):
    layer, chip, core = place_in()
    kept = pick(pair_in, core, 0)
    got = swap_core(pick(pair_in, 1 - core, 0))
    both = jnp.where(core == 0, jnp.stack([kept, got]), jnp.stack([got, kept]))
    return plane_gather(both).reshape((8,) + pair_in.shape[1:])


def give_rows(both):
    layer, chip, core = place_in()
    kept = pick(both, core, 0)
    got = swap_core(pick(both, 1 - core, 0))
    return jnp.where(core == 0, jnp.stack([kept, got]), jnp.stack([got, kept]))


def norm_parts(values):
    centered = values - jnp.mean(values, axis=-1, keepdims=True)
    variance = jnp.mean(centered * centered, axis=-1, keepdims=True)
    scale = lax.rsqrt(variance + epsilon)
    return centered * scale, scale


def norm_back(grad, normed, scale, gain):
    scaled = grad * gain
    return scale * (
        scaled
        - jnp.mean(scaled, axis=-1, keepdims=True)
        - normed * jnp.mean(scaled * normed, axis=-1, keepdims=True)
    )


def gelu_slope(hidden):
    return 0.5 * (1.0 + lax.erf(hidden * math.sqrt(0.5))) + hidden * jnp.exp(
        -0.5 * hidden * hidden
    ) * (1.0 / math.sqrt(2.0 * math.pi))


def cross_weights(cross_mix, cross_up, cross_down):
    mix_parts = cross_mix.reshape(24, 3, 4, 192).transpose(2, 0, 1, 3).reshape(4, 24, 576)
    up_parts = cross_up.reshape(24, 4, 4, 192).transpose(2, 0, 1, 3).reshape(4, 24, 768)
    parts = jnp.concatenate([mix_parts, up_parts], axis=2)
    chip = place_in()[1]
    pieces = [
        swap_chip(pick(parts, chip ^ mask, 0), mask) if mask else pick(parts, chip, 0)
        for mask in range(4)
    ]
    rows = copies(
        pieces, (4, 24, 1344), lambda layer, chip, core: [chip ^ mask for mask in range(4)]
    )
    column = gather_dp(jnp.concatenate([rows.reshape(96, 1344), cross_down], axis=1))
    mix_up = gather_core(column[:, :, :1344].reshape(4, 4, 24, 1344), 2).reshape(768, 1344)
    down = gather_core(column[:, :, 1344:], 1).reshape(768, 768)
    return mix_up[:, :576], mix_up[:, 576:], down


def plane_shards(
    tokens,
    cotangent,
    token_docs,
    segment_docs,
    segment_positions,
    local_mix,
    local_out,
    local_up,
    local_down,
    local_vectors,
    local_up_bias,
    cross_mix,
    cross_out,
    cross_up,
    cross_down,
    cross_vectors,
    cross_up_bias,
    position_table,
):
    layer, chip, core = place_in()
    rank = lax.axis_index(("dp", "seq"))
    small = jnp.concatenate(
        [
            local_vectors,
            cross_vectors,
            position_table,
            local_up_bias.reshape(4, 24),
            cross_up_bias.reshape(4, 24),
        ]
    )
    small_pad = jnp.pad(small.T, ((0, 0), (0, 40)))
    first_group = gather_all(jnp.concatenate([local_mix, local_out, small_pad], axis=1)).reshape(
        768, 3200
    )
    second_group = gather_all(jnp.concatenate([local_up, cross_out], axis=1)).reshape(768, 3840)
    down_weight = gather_all(local_down).reshape(3072, 768)
    mix_weight, out_weight = first_group[:, :2304], first_group[:, 2304:3072]
    rows = first_group[:, 3072:3160].T
    up_weight, cross_out_weight = second_group[:, :3072], second_group[:, 3072:]
    position_rows = rows[16:80]
    up_bias = rows[80:84].reshape(4, 32, 24).transpose(1, 0, 2).reshape(3072)
    cross_bias = rows[84:88].reshape(4, 4, 4, 2, 24).transpose(1, 2, 3, 0, 4).reshape(4, 4, 192)
    local_weights = (mix_weight, out_weight, up_weight, down_weight, rows[:8], up_bias)
    mix_part, up_part, down_part = cross_weights(cross_mix, cross_up, cross_down)
    cross_rows = wide(rows[8:16])

    inputs = wide(tokens).reshape(256, D)
    first_out, first_kept = block_forward(
        inputs, local_weights, partial(segment_forward, token_docs=token_docs)
    )
    segment_grid = first_out.reshape(2, SEG, D)
    places = segment_positions.reshape(2)
    position_picks = low(places[:, None] == jnp.arange(64, dtype=jnp.int32)[None, :])
    heads_in = segment_grid[:, 0, :] + jnp.dot(
        position_picks, position_rows, preferred_element_type=jnp.float32
    )

    docs = pick(segment_docs, core, 0)
    allowed = docs[:, None] == docs[None, :]
    row_in = own_rows(heads_in)
    row_low = low(row_in)
    query_bias = pick(cross_rows[0].reshape(4, 192), chip, 0)
    value_bias = pick(cross_rows[1].reshape(4, 192), chip, 0)
    part_bias = jnp.concatenate([query_bias, jnp.zeros_like(query_bias), value_bias])
    mixed = low(jnp.dot(row_low, mix_part, preferred_element_type=jnp.float32) + part_bias)
    heads = mixed.reshape(8, 3, 3, HEAD_DIM)
    query, key, value = heads[:, 0], heads[:, 1], heads[:, 2]
    scores = jnp.einsum("qhd,khd->hqk", query, key, preferred_element_type=jnp.float32) * (
        HEAD_DIM ** (-0.5)
    )
    probs = jax.nn.softmax(jnp.where(allowed[None], scores, masked_score), axis=-1)
    probs_low = low(probs)
    context_part = low(
        jnp.einsum("hqk,khd->qhd", probs_low, value, preferred_element_type=jnp.float32)
    ).reshape(8, 192)
    context = plane_gather(context_part).transpose(1, 0, 2).reshape(8, D)
    first_sum = (
        row_in
        + jnp.dot(context, cross_out_weight, preferred_element_type=jnp.float32)
        + cross_rows[2]
    )
    first_n, first_scale = norm_parts(first_sum)
    first_norm = first_n * cross_rows[3] + cross_rows[4]
    first_low = low(first_norm)
    hidden = jnp.dot(first_low, up_part, preferred_element_type=jnp.float32) + wide(
        pick(cross_bias, chip, 1)
    ).reshape(768)
    active = low(gelu_exact(hidden))
    second_sum = (
        first_norm
        + plane_sum(jnp.dot(active, down_part, preferred_element_type=jnp.float32))
        + cross_rows[5]
    )
    second_n, second_scale = norm_parts(second_sum)
    row_out = second_n * cross_rows[6] + cross_rows[7]
    heads_out = give_rows(lax.dynamic_slice_in_dim(row_out, 2 * chip, 2, 0))
    layer_output = low(jnp.concatenate([heads_out[:, None, :], segment_grid[:, 1:, :]], axis=1))

    row_grad = wide(own_rows(cotangent[:, 0, :]))
    second_grad = norm_back(row_grad, second_n, second_scale, cross_rows[6])
    second_low = low(second_grad)
    hidden_low = low(contract(second_low, down_part, 1, 1) * gelu_slope(hidden))
    first_grad = second_grad + plane_sum(contract(hidden_low, up_part, 1, 1))
    sum_grad = norm_back(first_grad, first_n, first_scale, cross_rows[3])
    branch_low = low(sum_grad)
    out_part = lax.dynamic_slice_in_dim(cross_out_weight, 192 * chip, 192, 0)
    context_low = low(contract(branch_low, out_part, 1, 1)).reshape(8, 3, HEAD_DIM)
    prob_grad = jnp.einsum("qhd,khd->hqk", context_low, value, preferred_element_type=jnp.float32)
    value_grad = jnp.einsum(
        "hqk,qhd->khd", probs_low, context_low, preferred_element_type=jnp.float32
    )
    score_low = low(probs * (prob_grad - jnp.sum(probs * prob_grad, axis=-1, keepdims=True)))
    query_grad = jnp.einsum("hqk,khd->qhd", score_low, key, preferred_element_type=jnp.float32)
    key_grad = jnp.einsum("hqk,qhd->khd", score_low, query, preferred_element_type=jnp.float32)
    scale = HEAD_DIM ** (-0.5)
    mixed_low = low(
        jnp.stack([query_grad * scale, key_grad * scale, value_grad], axis=1)
    ).reshape(8, 576)
    row_parts = contract(mixed_low, mix_part, 1, 1).reshape(4, 2, D)
    pair_grad = pick(row_parts, chip, 0) + lax.dynamic_slice_in_dim(sum_grad, 2 * chip, 2, 0)
    for mask in (1, 2, 3):
        pair_grad = pair_grad + swap_chip(pick(row_parts, chip ^ mask, 0), mask)
    heads_grad = give_rows(pair_grad)

    def pair_of(array_in):
        return lax.dynamic_slice_in_dim(array_in, 2 * chip, 2, 0)

    sums = jnp.stack(
        [
            jnp.sum(first_grad * first_n, axis=0),
            jnp.sum(first_grad, axis=0),
            jnp.sum(row_grad * second_n, axis=0),
            jnp.sum(row_grad, axis=0),
        ]
    )
    my_sum = low(pick(sums, chip, 0))[None]
    my_places = jnp.broadcast_to(low(wide(places))[:, None], (2, D))
    pairs = [pair_of(a) for a in (row_low, context, first_low, branch_low, second_low)]
    packed = jnp.concatenate(
        [hidden_low, active]
        + [mixed_low.reshape(6, D)]
        + pairs
        + [low(pair_of(sum_grad)), my_sum, my_places]
    )
    packed = jnp.pad(packed, ((0, 5), (0, 0)))
    everyone = gather_all(packed)

    def all_rows(piece):
        return piece.transpose(0, 2, 1, 3, 4).reshape(64, -1)

    hidden_all = everyone[:, :, :, 0:8]
    active_all = everyone[:, :, :, 8:16]
    mixed_all = everyone[:, :, :, 16:22].reshape(4, 4, 2, 8, 3, 192)
    mixed_all = mixed_all.transpose(0, 2, 3, 4, 1, 5).reshape(64, 3 * D)
    singles = [all_rows(everyone[:, :, :, 22 + 2 * i : 24 + 2 * i]) for i in range(6)]
    singles = [s.reshape(64, D) for s in singles]
    row_all, context_all, first_all, branch_all, second_all, sum_all = singles
    sums_all = jnp.sum(wide(everyone[:, :, :, 34]), axis=(0, 2))
    places_all = everyone[:, :, :, 35:37, 0]

    def own_columns(array_in):
        return lax.dynamic_slice_in_dim(array_in, 24 * rank, 24, 1)

    hidden_rows = (
        hidden_all.reshape(4, 4, 2, 8, 4, 2, 96)
        .transpose(0, 2, 3, 4, 1, 5, 6)
        .reshape(64, 3072)
    )
    active_own = lax.dynamic_slice(
        active_all, (0, chip, 0, 0, 192 * layer + 96 * core), (4, 1, 2, 8, 96)
    ).reshape(64, 96)
    cross_mix_grad = contract(own_columns(row_all), mixed_all, 0, 0)
    cross_out_grad = contract(own_columns(context_all), branch_all, 0, 0)
    cross_up_grad = contract(own_columns(first_all), hidden_rows, 0, 0)
    cross_down_grad = contract(active_own, second_all, 0, 0)
    mixed_sum = jnp.sum(wide(mixed_all), axis=0)
    cross_vectors_grad = own_columns(
        jnp.stack(
            [
                mixed_sum[:D],
                mixed_sum[2 * D :],
                jnp.sum(wide(branch_all), axis=0),
                sums_all[0],
                sums_all[1],
                jnp.sum(wide(second_all), axis=0),
                sums_all[2],
                sums_all[3],
            ]
        )
    )
    cross_bias_grad = lax.dynamic_slice_in_dim(
        jnp.sum(wide(hidden_rows), axis=0), 96 * rank, 96, 0
    )
    grads_all = wide(own_columns(sum_all)) + contract(mixed_all, cross_mix, 1, 1)
    places_rows = places_all.transpose(0, 3, 1, 2).reshape(64)
    picks_all = wide(
        wide(places_rows)[:, None] == jnp.arange(64, dtype=jnp.float32)[None, :]
    )
    table_grad = contract_exact(picks_all, grads_all, 0, 0)

    output_grad = wide(cotangent)
    local_grad = jnp.concatenate([heads_grad[:, None, :], output_grad[:, 1:, :]], axis=1).reshape(
        256, D
    )
    input_grad, local_grads = block_backward(
        local_grad, first_kept, local_weights, partial(segment_backward, token_docs=token_docs)
    )
    mix_grad, out_grad, up_grad, down_grad, vectors_grad, bias_grad = local_grads
    down_sum = scatter_sum(low(down_grad).reshape(4, 4, 2, 96, D))
    up_sum = scatter_sum(low(up_grad).reshape(4, 4, 2, 24, 3072))
    small_grads = jnp.concatenate(
        [
            vectors_grad.reshape(8, 32, 24).transpose(1, 2, 0),
            bias_grad.reshape(32, 4, 24).transpose(0, 2, 1),
        ],
        axis=2,
    ).reshape(D, 12)
    mix_parts = jnp.concatenate(
        [low(mix_grad), low(out_grad), low(jnp.pad(small_grads, ((0, 0), (0, 116))))], axis=1
    )
    mix_sum = scatter_sum(mix_parts.reshape(4, 4, 2, 24, 3200))
    return (
        layer_output,
        input_grad.reshape(2, SEG, D),
        mix_sum[:, :2304],
        mix_sum[:, 2304:3072],
        up_sum,
        down_sum,
        mix_sum[:, 3072:3080].T,
        mix_sum[:, 3080:3084].T.reshape(96),
        cross_mix_grad,
        cross_out_grad,
        cross_up_grad,
        cross_down_grad,
        cross_vectors_grad,
        cross_bias_grad,
        table_grad,
    )


def solution(mesh):
    flat = dict(mesh.shape) == {"dp": 4, "seq": 8}
    return jax.shard_map(
        plane_shards if flat else shards,
        mesh=mesh,
        in_specs=(
            P("dp", "seq", None),
            P("dp", "seq", None),
            P("dp", "seq"),
            P("dp", None),
            P("dp", "seq"),
            P(("dp", "seq"), None),
            P(("dp", "seq"), None),
            P(("dp", "seq"), None),
            P(("dp", "seq"), None),
            P(None, ("dp", "seq")),
            P(("dp", "seq")),
            P(("dp", "seq"), None),
            P(("dp", "seq"), None),
            P(("dp", "seq"), None),
            P(("dp", "seq"), None),
            P(None, ("dp", "seq")),
            P(("dp", "seq")),
            P(None, ("dp", "seq")),
        ),
        out_specs=(
            P("dp", "seq", None),
            P("dp", "seq", None),
            P(("dp", "seq"), None),
            P(("dp", "seq"), None),
            P(("dp", "seq"), None),
            P(("dp", "seq"), None),
            P(None, ("dp", "seq")),
            P(("dp", "seq")),
            P(("dp", "seq"), None),
            P(("dp", "seq"), None),
            P(("dp", "seq"), None),
            P(("dp", "seq"), None),
            P(None, ("dp", "seq")),
            P(("dp", "seq")),
            P(None, ("dp", "seq")),
        ),
        check_vma=False,
    )
```

```python
from functools import partial
import math

import jax
import jax.numpy as jnp
from jax import lax
from jax.experimental import pallas as pl
from jax.experimental.pallas import tpu as pltpu
from jax.sharding import PartitionSpec as P

D = 768
HEADS = 12
HEAD_DIM = 64
SEG = 128
MICRO = 2


epsilon = 1e-05
masked_score = -1000000000.0
owner_dims = (0, 0, 0, 0, 1, 0, 0, 0, 0, 0, 1, 0, 1)


def layer_norm(values, gain_row, shift_row):
    centered = values - jnp.mean(values, axis=-1, keepdims=True)
    variance = jnp.mean(centered * centered, axis=-1, keepdims=True)
    return centered * lax.rsqrt(variance + epsilon) * gain_row + shift_row


def gelu_exact(hidden):
    return jax.nn.gelu(hidden, approximate=False)


def contract(left_side, right_side, left_dim, right_dim):
    return lax.dot_general(
        left_side,
        right_side,
        (((left_dim,), (right_dim,)), ((), ())),
        preferred_element_type=jnp.float32,
    )


def contract_exact(left_side, right_side, left_dim, right_dim):
    return lax.dot_general(
        left_side,
        right_side,
        (((left_dim,), (right_dim,)), ((), ())),
        precision=lax.Precision.HIGHEST,
        preferred_element_type=jnp.float32,
    )


def owner_pack(grads, devices):
    pieces = []
    for grad_value, split_dim in zip(grads, owner_dims):
        if split_dim == 0:
            pieces.append(grad_value.reshape(devices, -1))
        else:
            row_count = grad_value.shape[0]
            pieces.append(
                grad_value.reshape(row_count, devices, -1).transpose(1, 0, 2).reshape(devices, -1)
            )
    return jnp.concatenate(pieces, axis=1)


def owner_unpack(packed, shard_shapes):
    results = []
    offset = 0
    for shard_shape in shard_shapes:
        length = math.prod(shard_shape)
        results.append(packed[0, offset : offset + length].reshape(shard_shape))
        offset = offset + length
    return tuple(results)


def fetch_weights(
    local_mix,
    local_out,
    local_up,
    local_down,
    local_vectors,
    local_up_bias,
    cross_mix,
    cross_out,
    cross_up,
    cross_down,
    cross_vectors,
    cross_up_bias,
    position_table,
):
    return (
        lax.all_gather(local_mix, ("dp", "seq"), axis=0, tiled=True),
        lax.all_gather(local_out, ("dp", "seq"), axis=0, tiled=True),
        lax.all_gather(local_up, ("dp", "seq"), axis=0, tiled=True),
        lax.all_gather(local_down, ("dp", "seq"), axis=0, tiled=True),
        lax.all_gather(local_vectors, ("dp", "seq"), axis=1, tiled=True),
        lax.all_gather(local_up_bias, ("dp", "seq"), axis=0, tiled=True),
        lax.all_gather(cross_mix, ("dp", "seq"), axis=0, tiled=True),
        lax.all_gather(cross_out, ("dp", "seq"), axis=0, tiled=True),
        lax.all_gather(cross_up, ("dp", "seq"), axis=0, tiled=True),
        lax.all_gather(cross_down, ("dp", "seq"), axis=0, tiled=True),
        lax.all_gather(cross_vectors, ("dp", "seq"), axis=1, tiled=True),
        lax.all_gather(cross_up_bias, ("dp", "seq"), axis=0, tiled=True),
        lax.all_gather(position_table, ("dp", "seq"), axis=1, tiled=True),
    )


def segment_parts(mixed_rows, token_docs):
    segment_count = token_docs.shape[0]
    split_heads = mixed_rows.reshape(segment_count, SEG, 3, HEADS, HEAD_DIM)
    allowed = token_docs[:, None, :, None] == token_docs[:, None, None, :]
    scores = jnp.einsum(
        "nqhd,nkhd->nhqk",
        split_heads[:, :, 0],
        split_heads[:, :, 1],
        preferred_element_type=jnp.float32,
    ) * HEAD_DIM ** (-0.5)
    scores = jnp.where(allowed, scores, masked_score)
    return (split_heads, scores)


def segment_forward(mixed_rows, token_docs):
    split_heads, scores = segment_parts(mixed_rows, token_docs)
    log_total = jax.nn.logsumexp(scores, axis=-1)
    weights = jax.nn.softmax(scores, axis=-1).astype(jnp.bfloat16)
    context = jnp.einsum(
        "nhqk,nkhd->nqhd", weights, split_heads[:, :, 2], preferred_element_type=jnp.float32
    )
    return (context.reshape(-1, D).astype(jnp.bfloat16), log_total)


def segment_backward(context_grad, log_total, mixed_rows, token_docs):
    split_heads, scores = segment_parts(mixed_rows, token_docs)
    segment_count = token_docs.shape[0]
    probs = jnp.exp(scores - log_total[..., None])
    grad_heads = context_grad.reshape(segment_count, SEG, HEADS, HEAD_DIM)
    prob_grad = jnp.einsum(
        "nqhd,nkhd->nhqk", grad_heads, split_heads[:, :, 2], preferred_element_type=jnp.float32
    )
    value_grad = jnp.einsum(
        "nhqk,nqhd->nkhd",
        probs.astype(jnp.bfloat16),
        grad_heads,
        preferred_element_type=jnp.float32,
    )
    score_grad = probs * (prob_grad - jnp.sum(probs * prob_grad, axis=-1, keepdims=True))
    score_low = score_grad.astype(jnp.bfloat16) * HEAD_DIM ** (-0.5)
    query_grad = jnp.einsum(
        "nhqk,nkhd->nqhd", score_low, split_heads[:, :, 1], preferred_element_type=jnp.float32
    )
    key_grad = jnp.einsum(
        "nhqk,nqhd->nkhd", score_low, split_heads[:, :, 0], preferred_element_type=jnp.float32
    )
    row_total = segment_count * SEG
    return jnp.concatenate(
        [
            query_grad.reshape(row_total, D),
            key_grad.reshape(row_total, D),
            value_grad.reshape(row_total, D),
        ],
        axis=1,
    )


def cross_parts(mixed_rows, gathered, segment_docs):
    group_size = segment_docs.shape[0]
    per_device = mixed_rows.shape[0] // group_size
    query_rows = mixed_rows[:, :D].reshape(group_size, per_device, HEADS, HEAD_DIM)
    key_rows = gathered[:, :, :D].reshape(group_size, -1, HEADS, HEAD_DIM)
    value_rows = gathered[:, :, D:].reshape(group_size, -1, HEADS, HEAD_DIM)
    own_docs = lax.dynamic_slice_in_dim(
        segment_docs, lax.axis_index("seq") * per_device, per_device, 1
    )
    allowed = own_docs[:, None, :, None] == segment_docs[:, None, None, :]
    scores = jnp.einsum(
        "bqhd,bkhd->bhqk", query_rows, key_rows, preferred_element_type=jnp.float32
    ) * HEAD_DIM ** (-0.5)
    scores = jnp.where(allowed, scores, masked_score)
    return (query_rows, key_rows, value_rows, scores)


def cross_forward(mixed_rows, segment_docs):
    group_size = segment_docs.shape[0]
    per_device = mixed_rows.shape[0] // group_size
    pair_rows = mixed_rows[:, D:].reshape(group_size, per_device, 2 * D)
    gathered = lax.all_gather(pair_rows, "seq", axis=1, tiled=True)
    query_rows, key_rows, value_rows, scores = cross_parts(mixed_rows, gathered, segment_docs)
    log_total = jax.nn.logsumexp(scores, axis=-1)
    weights = jax.nn.softmax(scores, axis=-1).astype(jnp.bfloat16)
    context = jnp.einsum("bhqk,bkhd->bqhd", weights, value_rows, preferred_element_type=jnp.float32)
    return (context.reshape(-1, D).astype(jnp.bfloat16), (gathered, log_total))


def cross_backward(context_grad, cross_kept, mixed_rows, segment_docs):
    gathered, log_total = cross_kept
    group_size = segment_docs.shape[0]
    row_total = mixed_rows.shape[0]
    per_device = row_total // group_size
    query_rows, key_rows, value_rows, scores = cross_parts(mixed_rows, gathered, segment_docs)
    probs = jnp.exp(scores - log_total[..., None])
    grad_heads = context_grad.reshape(group_size, per_device, HEADS, HEAD_DIM)
    prob_grad = jnp.einsum(
        "bqhd,bkhd->bhqk", grad_heads, value_rows, preferred_element_type=jnp.float32
    )
    value_grad = jnp.einsum(
        "bhqk,bqhd->bkhd",
        probs.astype(jnp.bfloat16),
        grad_heads,
        preferred_element_type=jnp.float32,
    )
    score_grad = probs * (prob_grad - jnp.sum(probs * prob_grad, axis=-1, keepdims=True))
    score_low = score_grad.astype(jnp.bfloat16) * HEAD_DIM ** (-0.5)
    query_grad = jnp.einsum(
        "bhqk,bkhd->bqhd", score_low, key_rows, preferred_element_type=jnp.float32
    )
    key_grad = jnp.einsum(
        "bhqk,bqhd->bkhd", score_low, query_rows, preferred_element_type=jnp.float32
    )
    pair_grads = jnp.concatenate(
        [key_grad.reshape(group_size, -1, D), value_grad.reshape(group_size, -1, D)], axis=2
    )
    own_pairs = lax.psum_scatter(
        pair_grads.astype(jnp.bfloat16), "seq", scatter_dimension=1, tiled=True
    ).astype(jnp.float32)
    return jnp.concatenate(
        [query_grad.reshape(row_total, D), own_pairs.reshape(row_total, 2 * D)], axis=1
    )


def block_forward(inputs, weights, attend):
    mix_weight, out_weight, up_weight, down_weight, vectors, up_bias = weights
    vector_rows = vectors.astype(jnp.float32)
    in_bias = jnp.concatenate([vector_rows[0], jnp.zeros_like(vector_rows[0]), vector_rows[1]])
    rounded = inputs.astype(jnp.bfloat16)
    mixed_rows = (
        jnp.dot(rounded, mix_weight, preferred_element_type=jnp.float32) + in_bias
    ).astype(jnp.bfloat16)
    context, attend_kept = attend(mixed_rows)
    first_sum = (
        inputs + jnp.dot(context, out_weight, preferred_element_type=jnp.float32) + vector_rows[2]
    )
    first_norm = layer_norm(first_sum, vector_rows[3], vector_rows[4])
    first_low = first_norm.astype(jnp.bfloat16)
    hidden = jnp.dot(first_low, up_weight, preferred_element_type=jnp.float32) + up_bias.astype(
        jnp.float32
    )
    active = gelu_exact(hidden).astype(jnp.bfloat16)
    second_sum = (
        first_norm
        + jnp.dot(active, down_weight, preferred_element_type=jnp.float32)
        + vector_rows[5]
    )
    output = layer_norm(second_sum, vector_rows[6], vector_rows[7])
    return (
        output,
        (
            rounded,
            mixed_rows,
            attend_kept,
            context,
            first_sum,
            first_low,
            hidden,
            active,
            second_sum,
        ),
    )


def block_backward(output_grad, block_kept, weights, attend_back):
    mix_weight, out_weight, up_weight, down_weight, vectors, up_bias = weights
    vector_rows = vectors.astype(jnp.float32)
    rounded, mixed_rows, attend_kept, context, first_sum, first_low, hidden, active, second_sum = (
        block_kept
    )
    unused, second_pull = jax.vjp(layer_norm, second_sum, vector_rows[6], vector_rows[7])
    second_grad, gain_two, shift_two = second_pull(output_grad)
    second_low = second_grad.astype(jnp.bfloat16)
    down_grad = contract(active, second_low, 0, 0)
    down_bias = jnp.sum(second_low.astype(jnp.float32), axis=0)
    active_grad = contract(second_low, down_weight, 1, 1)
    unused, gelu_pull = jax.vjp(gelu_exact, hidden)
    hidden_grad = gelu_pull(active_grad)[0]
    hidden_low = hidden_grad.astype(jnp.bfloat16)
    up_grad = contract(first_low, hidden_low, 0, 0)
    up_bias_grad = jnp.sum(hidden_low.astype(jnp.float32), axis=0)
    first_grad = second_grad + contract(hidden_low, up_weight, 1, 1)
    unused, first_pull = jax.vjp(layer_norm, first_sum, vector_rows[3], vector_rows[4])
    sum_grad, gain_one, shift_one = first_pull(first_grad)
    branch_low = sum_grad.astype(jnp.bfloat16)
    out_grad = contract(context, branch_low, 0, 0)
    out_bias = jnp.sum(branch_low.astype(jnp.float32), axis=0)
    context_low = contract(branch_low, out_weight, 1, 1).astype(jnp.bfloat16)
    mixed_low = attend_back(context_low, attend_kept, mixed_rows).astype(jnp.bfloat16)
    mix_grad = contract(rounded, mixed_low, 0, 0)
    mixed_sums = jnp.sum(mixed_low.astype(jnp.float32), axis=0)
    input_grad = sum_grad + contract(mixed_low, mix_weight, 1, 1)
    vectors_grad = jnp.stack(
        [
            mixed_sums[:D],
            mixed_sums[2 * D :],
            out_bias,
            gain_one,
            shift_one,
            down_bias,
            gain_two,
            shift_two,
        ]
    )
    return (input_grad, (mix_grad, out_grad, up_grad, down_grad, vectors_grad, up_bias_grad))


def shards(
    tokens,
    cotangent,
    token_docs,
    segment_docs,
    segment_positions,
    local_mix,
    local_out,
    local_up,
    local_down,
    local_vectors,
    local_up_bias,
    cross_mix,
    cross_out,
    cross_up,
    cross_down,
    cross_vectors,
    cross_up_bias,
    position_table,
):
    sequence_count, span, width = tokens.shape
    group_size = sequence_count // MICRO
    segment_count = span // SEG
    devices = lax.axis_size(("dp", "seq"))
    shard_shapes = tuple(
        (
            array_in.shape
            for array_in in (
                local_mix,
                local_out,
                local_up,
                local_down,
                local_vectors,
                local_up_bias,
                cross_mix,
                cross_out,
                cross_up,
                cross_down,
                cross_vectors,
                cross_up_bias,
                position_table,
            )
        )
    )
    layer_outputs = []
    input_grads = []
    totals = ()
    for micro_step in range(MICRO):
        lower_row = micro_step * group_size
        upper_row = lower_row + group_size
        gathered = fetch_weights(
            local_mix,
            local_out,
            local_up,
            local_down,
            local_vectors,
            local_up_bias,
            cross_mix,
            cross_out,
            cross_up,
            cross_down,
            cross_vectors,
            cross_up_bias,
            position_table,
        )
        local_weights = gathered[0:6]
        cross_weights = gathered[6:12]
        position_rows = gathered[12]
        inputs = tokens[lower_row:upper_row].reshape(group_size * span, width).astype(jnp.float32)
        docs_here = token_docs[lower_row:upper_row]
        segments_here = segment_docs[lower_row:upper_row]
        first_out, first_kept = block_forward(
            inputs, local_weights, partial(segment_forward, token_docs=docs_here)
        )
        segment_grid = first_out.reshape(group_size * segment_count, SEG, width)
        places = segment_positions[lower_row:upper_row].reshape(group_size * segment_count)
        position_picks = (
            places[:, None] == jnp.arange(position_rows.shape[0], dtype=jnp.int32)[None, :]
        ).astype(jnp.bfloat16)
        heads_in = segment_grid[:, 0, :] + jnp.dot(
            position_picks, position_rows, preferred_element_type=jnp.float32
        )
        heads_out, cross_kept = block_forward(
            heads_in, cross_weights, partial(cross_forward, segment_docs=segments_here)
        )
        joined = jnp.concatenate([heads_out[:, None, :], segment_grid[:, 1:, :]], axis=1)
        layer_outputs.append(joined.astype(jnp.bfloat16))
        gathered = fetch_weights(
            local_mix,
            local_out,
            local_up,
            local_down,
            local_vectors,
            local_up_bias,
            cross_mix,
            cross_out,
            cross_up,
            cross_down,
            cross_vectors,
            cross_up_bias,
            position_table,
        )
        local_weights = gathered[0:6]
        cross_weights = gathered[6:12]
        output_grad = cotangent[lower_row:upper_row].astype(jnp.float32)
        heads_grad, cross_grads = block_backward(
            output_grad[:, 0, :],
            cross_kept,
            cross_weights,
            partial(cross_backward, segment_docs=segments_here),
        )
        table_grad = contract_exact(position_picks.astype(jnp.float32), heads_grad, 0, 0)
        first_grad = jnp.concatenate(
            [heads_grad[:, None, :], output_grad[:, 1:, :]], axis=1
        ).reshape(group_size * span, width)
        input_grad, local_grads = block_backward(
            first_grad, first_kept, local_weights, partial(segment_backward, token_docs=docs_here)
        )
        input_grads.append(input_grad.reshape(group_size, span, width))
        step_grads = local_grads + cross_grads + (table_grad,)
        if micro_step == 0:
            totals = tuple(step_grads)
        else:
            totals = tuple(
                (total_sum + step_sum for total_sum, step_sum in zip(totals, step_grads))
            )
    packed_total = lax.psum_scatter(
        owner_pack(totals, devices), ("dp", "seq"), scatter_dimension=0, tiled=True
    )
    summed = owner_unpack(packed_total, shard_shapes)
    layer_output = jnp.concatenate(layer_outputs, axis=0)
    input_gradient = jnp.concatenate(input_grads, axis=0)
    return (layer_output, input_gradient) + tuple(summed)


def swap_dp(array_in, shift):
    return lax.ppermute(array_in, "dp", [(i, (i + shift) % 4) for i in range(4)])


def swap_core(array_in):
    return lax.ppermute(array_in, "seq", [(i, i ^ 1) for i in range(8)])


def swap_chip(array_in, mask):
    return lax.ppermute(array_in, "seq", [(i, i ^ (2 * mask)) for i in range(8)])


def swap_one(array_in):
    return lax.ppermute(array_in, "seq", [(i, i ^ (2 if i % 2 == 0 else 4)) for i in range(8)])


def swap_two(array_in):
    return lax.ppermute(array_in, "seq", [(i, i ^ (4 if i % 2 == 0 else 2)) for i in range(8)])


def place_in():
    layer = lax.axis_index("dp")
    spot = lax.axis_index("seq")
    return layer, spot // 2, lax.rem(spot, 2)


def after(array_in, *before):
    return lax.optimization_barrier((array_in,) + before)[0]


def wide(array_in):
    return array_in.astype(jnp.float32)


def low(array_in):
    return array_in.astype(jnp.bfloat16)


def copies(pieces, shapes, moves):
    count, made = len(pieces), len(shapes)
    total = len(moves(0, 0, 0))

    def kernel(*refs):
        outs, held, sems = refs[count : count + made], refs[count + made : -1], refs[-1]
        inward = [pltpu.make_async_copy(refs[i], held[i], sems.at[0, i]) for i in range(count)]
        for copy in inward:
            copy.start()
        outward = []
        for i, (piece, part, out, place) in enumerate(moves(*place_in())):
            if inward[piece] is not None:
                inward[piece].wait()
                inward[piece] = None
            copy = pltpu.make_async_copy(held[piece].at[part], outs[out].at[place], sems.at[1, i])
            copy.start()
            outward.append(copy)
        for copy in outward:
            copy.wait()

    size = 2 * sum(math.prod(shape) for shape in shapes) * 2
    return pl.pallas_call(
        kernel,
        out_shape=[jax.ShapeDtypeStruct(shape, pieces[0].dtype) for shape in shapes],
        in_specs=[pl.BlockSpec(memory_space=pl.ANY)] * count,
        out_specs=[pl.BlockSpec(memory_space=pl.ANY)] * made,
        scratch_shapes=[pltpu.VMEM(piece.shape, piece.dtype) for piece in pieces]
        + [pltpu.SemaphoreType.DMA((2, max(count, total)))],
        compiler_params=pltpu.CompilerParams(vmem_limit_bytes=24 * 2**20),
        cost_estimate=pl.CostEstimate(flops=0, bytes_accessed=size, transcendentals=0),
    )(*pieces)


every = slice(None)


def gather_dp(shard):
    pieces = [shard] + [swap_dp(shard, shift) for shift in (1, 2, 3)]
    return copies(
        pieces,
        [(4,) + shard.shape],
        lambda layer, chip, core: [(i, every, 0, lax.rem(layer + 4 - i, 4)) for i in range(4)],
    )[0]


def plane_moves(column, *before):
    ready = after(column, *before) if before else column
    first = swap_one(ready)
    second = swap_two(ready)
    return [column, first, second, swap_two(first)]


def plane_order(chip, core):
    near, far = chip ^ (1 + core), chip ^ (2 - core)
    return (chip, near, far, chip ^ 3), (chip, far, near, chip ^ 3)


def gather_plane(mine):
    def moves(layer, chip, core):
        own, other = plane_order(chip, core)
        found = [(i, every, 0, (every, own[i], core)) for i in range(4)]
        return found + [(4 + i, every, 0, (every, other[i], 1 - core)) for i in range(4)]

    shape = (4, 4, 2) + mine[0].shape[1:]
    return copies(mine + [swap_core(piece) for piece in mine], [shape], moves)[0]


def gather_down(mine):
    def moves(layer, chip, core):
        own, other = plane_order(chip, core)
        found = []
        for i in range(8):
            spot, side = (own[i], core) if i < 4 else (other[i - 4], 1 - core)
            for quarter in range(4):
                part = (every, every, slice(quarter * D, (quarter + 1) * D))
                found.append((i, part, 0, (every, spot, side, quarter)))
        return found

    return copies(mine + [swap_core(piece) for piece in mine], [(4, 4, 2, 4, 24, D)], moves)[0]


class Sum:
    def __init__(self, kept, gone):
        layer, chip, core = place_in()
        self.kept = kept
        self.shape = kept.shape[2:]
        self.spots = jnp.stack([chip ^ (1 + core), chip ^ 3, chip ^ (2 - core), chip, layer])
        self.got = swap_core(gone)

    def part(self, take):
        return pl.BlockSpec((4, None) + self.shape, take)

    def run(self, kernel, grid, in_specs, out_specs, out_shape, *operands):
        size = sum(math.prod(a.shape) * 2 for a in operands)
        return pl.pallas_call(
            kernel,
            grid_spec=pltpu.PrefetchScalarGridSpec(
                num_scalar_prefetch=1, grid=grid, in_specs=in_specs, out_specs=out_specs
            ),
            out_shape=out_shape,
            compiler_params=pltpu.CompilerParams(vmem_limit_bytes=32 * 2**20),
            cost_estimate=pl.CostEstimate(flops=size, bytes_accessed=size, transcendentals=0),
        )(self.spots, *operands)

    def first(self, *before):
        def kernel(spots_ref, a_ref, b_ref, o_ref):
            o_ref[...] = low(wide(a_ref[...]) + wide(b_ref[...]))

        near = self.part(lambda i, s: (0, s[i], 0, 0))
        out = pl.BlockSpec((None, 4) + self.shape, lambda i, s: (i, 0, 0, 0))
        got = after(self.got, *before) if before else self.got
        sent = self.run(kernel, (2,), [near, near], out, half(2, 4, *self.shape), self.kept, got)
        self.back = swap_one(sent)
        return sent

    def second(self, *before):
        def kernel(spots_ref, a_ref, b_ref, c_ref, o_ref):
            o_ref[...] = low(wide(a_ref[...]) + wide(b_ref[...]) + wide(c_ref[...]))

        pair = (2, None) + self.shape
        far = pl.BlockSpec(pair, lambda i, s: (i, s[2], 0, 0))
        moved = pl.BlockSpec((None, 2) + self.shape, lambda i, s: (1, i, 0, 0))
        out = pl.BlockSpec((2,) + self.shape, lambda i, s: (i, 0, 0))
        back = after(self.back, *before) if before else self.back
        onward = self.run(
            kernel, (2,), [far, far, moved], out, half(4, *self.shape), self.kept, self.got, back
        )
        self.last = swap_two(onward)
        return onward

    def third(self, *before):
        def kernel(spots_ref, a_ref, b_ref, c_ref, d_ref, own_ref, *outs):
            for shift in range(4):
                level = lax.rem(spots_ref[4] + shift, 4)
                total = wide(a_ref[level]) + wide(b_ref[level]) + wide(c_ref[level])
                total = total + wide(d_ref[level])
                if shift:
                    outs[shift - 1][...] = low(total)
                else:
                    own_ref[...] = total

        here = self.part(lambda i, s: (0, s[3], 0, 0))
        moved = pl.BlockSpec((None, 4) + self.shape, lambda i, s: (0, 0, 0, 0))
        full = pl.BlockSpec((4,) + self.shape, lambda i, s: (0, 0, 0))
        flat = pl.BlockSpec(self.shape, lambda i, s: (0, 0))
        last = after(self.last, *before) if before else self.last
        self.own, *others = self.run(
            kernel,
            (1,),
            [here, here, moved, full],
            [flat] * 4,
            [shape_of(*self.shape)] + [half(*self.shape)] * 3,
            self.kept,
            self.got,
            self.back,
            last,
        )
        self.others = [swap_dp(other, shift) for shift, other in zip((1, 2, 3), others)]
        return self.own

    def total(self):
        return self.own + wide(self.others[0]) + wide(self.others[1]) + wide(self.others[2])


def norm_parts(values):
    centered = values - jnp.mean(values, axis=-1, keepdims=True)
    variance = jnp.mean(centered * centered, axis=-1, keepdims=True)
    scale = lax.rsqrt(variance + epsilon)
    return centered * scale, scale


def norm_back(grad, normed, scale, gain):
    scaled = grad * gain
    return scale * (
        scaled
        - jnp.mean(scaled, axis=-1, keepdims=True)
        - normed * jnp.mean(scaled * normed, axis=-1, keepdims=True)
    )


def gelu_slope(hidden):
    return 0.5 * (1.0 + lax.erf(hidden * math.sqrt(0.5))) + hidden * jnp.exp(
        -0.5 * hidden * hidden
    ) * (1.0 / math.sqrt(2.0 * math.pi))


def shape_of(*shape, dtype=jnp.float32):
    return jax.ShapeDtypeStruct(shape, dtype)


def half(*shape):
    return jax.ShapeDtypeStruct(shape, jnp.bfloat16)


def on_core(kernel, out_shape, operands, flops, grid=(), in_specs=None, out_specs=None, scratch=()):
    arrays = jax.tree.leaves(out_shape) + list(operands)
    size = sum(math.prod(a.shape) * a.dtype.itemsize for a in arrays)
    extra = {} if in_specs is None else {"in_specs": in_specs, "out_specs": out_specs}
    return pl.pallas_call(
        kernel,
        out_shape=out_shape,
        grid=grid,
        scratch_shapes=scratch,
        compiler_params=pltpu.CompilerParams(vmem_limit_bytes=52 * 2**20),
        cost_estimate=pl.CostEstimate(flops=flops, bytes_accessed=size, transcendentals=0),
        **extra,
    )(*operands)


def column_sum(array_in):
    return jnp.sum(array_in, axis=0, keepdims=True)


def prepare(
    mix_ref,
    out_ref,
    up_ref,
    down_ref,
    vectors_ref,
    bias_ref,
    cross_mix_ref,
    cross_out_ref,
    cross_up_ref,
    cross_vectors_ref,
    cross_bias_ref,
    table_ref,
    one_ref,
    two_ref,
    part_a,
    part_b,
    part_c,
    part_d,
    small,
    parts,
):
    one_ref[:, 0 : 3 * D] = mix_ref[...]
    one_ref[:, 3 * D : 4 * D] = out_ref[...]
    small[...] = jnp.zeros_like(small)
    small[0:8, 0:24] = wide(vectors_ref[...])
    small[8:16, 0:24] = wide(cross_vectors_ref[...])
    small[16:80, 0:24] = wide(table_ref[...])
    small[80:84, 0:24] = wide(bias_ref[...])
    small[84:88, 0:24] = wide(cross_bias_ref[...])
    one_ref[:, 4 * D : 4 * D + 128] = low(small[...].T[0:24, :])
    two_ref[:, 0 : 4 * D] = up_ref[...]
    two_ref[:, 4 * D : 5 * D] = cross_out_ref[...]
    for quarter in range(4):
        two_ref[:, (5 + quarter) * D : (6 + quarter) * D] = down_ref[quarter]
    parts[...] = jnp.zeros_like(parts)
    for spot in range(4):
        for level in range(4):
            taken = cross_up_ref[:, 192 * (4 * level + spot) : 192 * (4 * level + spot + 1)]
            parts[spot, :, 192 * level : 192 * (level + 1)] = taken
        for third in range(3):
            taken = cross_mix_ref[:, third * D + 192 * spot : third * D + 192 * (spot + 1)]
            parts[spot, :, D + 192 * third : D + 192 * (third + 1)] = taken
    chip = place_in()[1]
    for mask, ref in enumerate((part_a, part_b, part_c, part_d)):
        ref[...] = parts[chip ^ mask]


def gather_cross(parts, cross_down):
    pieces = [parts[0]] + [swap_chip(parts[mask], mask) for mask in (1, 2, 3)]

    def moves(layer, chip, core):
        found = []
        for mask in range(4):
            found.append((mask, (every, slice(0, D)), 0, (chip ^ mask, every, slice(0, D))))
            taken = (every, slice(D, D + 640))
            found.append((mask, taken, 0, (chip ^ mask, every, slice(2 * D, 2 * D + 640))))
        found.append((4, every, 0, (every, every, slice(D, 2 * D))))
        return found

    row = copies(pieces + [cross_down.reshape(4, 24, D)], [(4, 24, 2 * D + 640)], moves)[0]
    return lax.all_gather(row, "dp")


def place_cross(column):
    other = swap_core(column)

    def moves(layer, chip, core):
        found = []
        for piece, side in ((0, core), (1, 1 - core)):
            lead = (every, every, side, every)
            source = (every, every, every)
            found.append((piece, source + (slice(0, D),), 0, lead + (slice(0, D),)))
            found.append(
                (piece, source + (slice(2 * D, 2 * D + 640),), 0, lead + (slice(D, D + 640),))
            )
            found.append((piece, source + (slice(D, 2 * D),), 1, (every, side)))
        return found

    up_mix, down = copies(
        [column, other], [(4, 4, 2, 24, D + 640), (4, 2, 4, 24, D)], moves
    )
    return up_mix.reshape(D, D + 640), down.reshape(D, D)


def local_attend(tokens_ref, group_ref, docs_ref, docs_column_ref, *outs):
    mixed_ref, context_ref, probs_ref, n_ref, scale_ref, low_ref, rows_ref = outs
    rows_ref[...] = wide(group_ref[:, 4 * D : 4 * D + 128]).T
    tokens = tokens_ref[...]
    for third in range(3):
        columns = slice(third * D, (third + 1) * D)
        mixed = contract(tokens, group_ref[:, columns], 1, 0)
        if third != 1:
            mixed = mixed + rows_ref[third // 2 : third // 2 + 1, :]
        mixed_ref[:, columns] = low(mixed)
    lane = lax.broadcasted_iota(jnp.int32, (SEG, 128), 1)
    for segment in range(2):
        rows = slice(segment * SEG, (segment + 1) * SEG)
        allowed = docs_column_ref[rows, :] == docs_ref[segment : segment + 1, :]
        for pair in range(HEADS // 2):
            query, key, value = (
                mixed_ref[rows, third * D + pair * 128 : third * D + (pair + 1) * 128]
                for third in range(3)
            )
            found = []
            for side in range(2):
                here = (lane < HEAD_DIM) if side == 0 else (lane >= HEAD_DIM)
                scores = contract(jnp.where(here, query, jnp.zeros_like(query)), key, 1, 1)
                scores = jnp.where(allowed, scores * HEAD_DIM ** (-0.5), masked_score)
                powers = jnp.exp(scores - jnp.max(scores, axis=-1, keepdims=True))
                probs = powers / jnp.sum(powers, axis=-1, keepdims=True)
                probs_ref[segment * HEADS + 2 * pair + side] = probs
                found.append(contract(low(probs), value, 1, 0))
            context = jnp.where(lane < HEAD_DIM, found[0], found[1])
            context_ref[rows, pair * 128 : (pair + 1) * 128] = low(context)
    total = wide(tokens) + contract(context_ref[...], group_ref[:, 3 * D : 4 * D], 1, 0)
    normed, scale = norm_parts(total + rows_ref[2:3, :])
    n_ref[...] = normed
    scale_ref[...] = scale
    low_ref[...] = low(normed * rows_ref[3:4, :] + rows_ref[4:5, :])


def local_up_part(low_ref, weight_ref, bias_ref, active_ref, slope_ref):
    hidden = contract(low_ref[...], weight_ref[...], 1, 0) + wide(bias_ref[...])
    chance = 0.5 * (1.0 + lax.erf(hidden * math.sqrt(0.5)))
    density = jnp.exp(-0.5 * hidden * hidden) * (1.0 / math.sqrt(2.0 * math.pi))
    active_ref[...] = low(hidden * chance)
    slope_ref[...] = low(chance + hidden * density)


def local_down_part(
    active_ref, weight_ref, first_ref, rows_ref, cot_a, cot_b, places_ref, *outs
):
    n_ref, scale_ref, kept_ref, given_ref, total = outs
    step = pl.program_id(0)
    part = contract(active_ref[...], weight_ref[...], 1, 0)

    @pl.when(step == 0)
    def _():
        first_norm = first_ref[...] * rows_ref[3:4, :] + rows_ref[4:5, :]
        total[...] = first_norm + rows_ref[5:6, :] + part

    @pl.when(step > 0)
    def _():
        total[...] += part

    @pl.when(step == 3)
    def _():
        normed, scale = norm_parts(total[...])
        n_ref[...] = normed
        scale_ref[...] = scale
        core = place_in()[2]
        heads, grads = [], []
        for place, cot in ((0, cot_a), (1, cot_b)):
            row = normed[place * SEG : place * SEG + 1] * rows_ref[6:7, :] + rows_ref[7:8, :]
            heads.append(row + rows_ref[pl.ds(16 + places_ref[place, 0], 1), :])
            grads.append(wide(cot[...])[0:1])
        for ref, mine in ((kept_ref, core == 0), (given_ref, core == 1)):
            ref[...] = jnp.zeros_like(ref)
            ref[0:1, :] = jnp.where(mine, heads[0], heads[1])
            ref[1:2, :] = jnp.where(mine, grads[0], grads[1])


def join_pair(kept_ref, got_ref, out_ref):
    core = place_in()[2]
    out_ref[...] = jnp.zeros_like(out_ref)
    out_ref[0:2, :] = jnp.where(core == 0, kept_ref[0:2, :], got_ref[0:2, :])
    out_ref[2:4, :] = jnp.where(core == 0, got_ref[0:2, :], kept_ref[0:2, :])


def cross_attend(
    own_ref, a_ref, b_ref, c_ref, weight_ref, rows_ref, docs_ref, docs_column_ref, *outs
):
    in_ref, grad_ref, mixed_ref, probs_ref, context_ref = outs
    layer, chip, core = place_in()
    for mask, ref in enumerate((own_ref, a_ref, b_ref, c_ref)):
        for side in range(2):
            row = 2 * (chip ^ mask) + side
            in_ref[pl.ds(row, 1), :] = ref[2 * side : 2 * side + 1, :]
            grad_ref[pl.ds(row, 1), :] = ref[2 * side + 1 : 2 * side + 2, :]
    biases = []
    for vector in (8, 9):
        row = rows_ref[vector : vector + 1, :]
        found = row[:, 0:192]
        for spot in range(1, 4):
            found = jnp.where(chip == spot, row[:, 192 * spot : 192 * (spot + 1)], found)
        biases.append(found)
    bias = jnp.concatenate([biases[0], jnp.zeros_like(biases[0]), biases[1]], axis=1)
    mixed = low(contract(low(in_ref[...]), weight_ref[:, D : D + 576], 1, 0) + bias)
    mixed_ref[...] = mixed
    row_docs = jnp.where(core == 0, docs_ref[0:1, :], docs_ref[1:2, :])
    column_docs = jnp.where(core == 0, docs_column_ref[:, 0:1], docs_column_ref[:, 1:2])
    allowed = row_docs == column_docs
    found = []
    for head in range(3):
        query, key, value = (
            mixed[:, third * 192 + head * HEAD_DIM : third * 192 + (head + 1) * HEAD_DIM]
            for third in range(3)
        )
        scores = contract(query, key, 1, 1) * HEAD_DIM ** (-0.5)
        scores = jnp.where(allowed, scores, masked_score)
        powers = jnp.exp(scores - jnp.max(scores, axis=-1, keepdims=True))
        probs = powers / jnp.sum(powers, axis=-1, keepdims=True)
        probs_ref[head] = probs
        found.append(contract(low(probs), value, 1, 0))
    context_ref[...] = low(jnp.concatenate(found, axis=1))


def cross_up_down(
    own_ref, a_ref, b_ref, c_ref, in_ref, out_weight_ref, rows_ref, up_ref, bias_ref, down_ref, *outs
):
    n_ref, scale_ref, low_ref, hidden_ref, active_ref, part_ref = outs
    chip = place_in()[1]
    total = in_ref[...] + rows_ref[10:11, :]
    for mask, ref in enumerate((own_ref, a_ref, b_ref, c_ref)):
        start = pl.multiple_of(192 * (chip ^ mask), 64)
        total = total + contract(ref[...], out_weight_ref[pl.ds(start, 192), :], 1, 0)
    normed, scale = norm_parts(total)
    n_ref[...] = normed
    scale_ref[...] = scale
    first = low(normed * rows_ref[11:12, :] + rows_ref[12:13, :])
    low_ref[...] = first
    hidden = contract(first, up_ref[...], 1, 0) + bias_ref[...]
    hidden_ref[...] = hidden
    active = low(hidden * (0.5 * (1.0 + lax.erf(hidden * math.sqrt(0.5)))))
    active_ref[...] = active
    part_ref[...] = contract(active, down_ref[...], 1, 0)


def cross_turn(
    own_ref, a_ref, b_ref, c_ref, n_ref, rows_ref, grad_ref, hidden_ref, up_ref, down_ref, *outs
):
    out_ref, second_ref, hidden_low_ref, part_ref, sums_ref = outs
    first = n_ref[...] * rows_ref[11:12, :] + rows_ref[12:13, :]
    total = (own_ref[...] + a_ref[...]) + (b_ref[...] + c_ref[...])
    normed, scale = norm_parts(first + total + rows_ref[13:14, :])
    out_ref[...] = normed * rows_ref[14:15, :] + rows_ref[15:16, :]
    grad = grad_ref[...]
    second = norm_back(grad, normed, scale, rows_ref[14:15, :])
    second_ref[...] = second
    hidden_low = low(contract(low(second), down_ref[...], 1, 1) * gelu_slope(hidden_ref[...]))
    hidden_low_ref[...] = hidden_low
    part_ref[...] = contract(hidden_low, up_ref[...], 1, 1)
    sums_ref[...] = jnp.zeros_like(sums_ref)
    sums_ref[0:1, :] = column_sum(grad * normed)
    sums_ref[1:2, :] = column_sum(grad)


def cross_attend_back(
    own_ref,
    a_ref,
    b_ref,
    c_ref,
    second_ref,
    n_ref,
    scale_ref,
    rows_ref,
    out_weight_ref,
    mixed_ref,
    probs_ref,
    weight_ref,
    hidden_low_ref,
    active_ref,
    context_ref,
    in_ref,
    low_ref,
    sums_ref,
    places_ref,
    total_ref,
    part_ref,
    pack_ref,
    pack,
    rows,
):
    chip = place_in()[1]
    grad = second_ref[...] + (own_ref[...] + a_ref[...]) + (b_ref[...] + c_ref[...])
    normed = n_ref[...]
    total = norm_back(grad, normed, scale_ref[...], rows_ref[11:12, :])
    total_ref[...] = total
    branch = low(total)
    start = pl.multiple_of(192 * chip, 64)
    context_low = low(contract(branch, out_weight_ref[pl.ds(start, 192), :], 1, 1))
    mixed = mixed_ref[...]
    found = [[], [], []]
    for head in range(3):
        query, key, value = (
            mixed[:, third * 192 + head * HEAD_DIM : third * 192 + (head + 1) * HEAD_DIM]
            for third in range(3)
        )
        part = context_low[:, head * HEAD_DIM : (head + 1) * HEAD_DIM]
        probs = probs_ref[head]
        prob_grad = contract(part, value, 1, 1)
        score = low(probs * (prob_grad - jnp.sum(probs * prob_grad, axis=-1, keepdims=True)))
        found[0].append(contract(score, key, 1, 0) * HEAD_DIM ** (-0.5))
        found[1].append(contract(score, query, 0, 0) * HEAD_DIM ** (-0.5))
        found[2].append(contract(low(probs), part, 0, 0))
    mixed_low = low(jnp.concatenate(found[0] + found[1] + found[2], axis=1))
    part_ref[...] = contract(mixed_low, weight_ref[:, D : D + 576], 1, 1)
    pack[...] = jnp.zeros_like(pack)
    pack[0:8, :] = wide(hidden_low_ref[...])
    pack[8:16, :] = wide(active_ref[...])
    pack[16:24, 0:576] = wide(mixed_low)
    pack[16:24, 576:768] = wide(context_ref[...])
    for i, value in enumerate(
        (in_ref[...], wide(low_ref[...]), total, second_ref[...], total)
    ):
        rows[...] = value
        for side in range(2):
            row = 24 + 2 * i + side
            pack[row : row + 1, :] = rows[pl.ds(2 * chip + side, 1), :]
    rows[0:1, :] = column_sum(grad * normed)
    rows[1:2, :] = column_sum(grad)
    rows[2:4, :] = sums_ref[0:2, :]
    pack[34:35, :] = rows[pl.ds(chip, 1), :]
    for place in range(2):
        pack[35 + place : 36 + place, :] = jnp.full((1, D), wide(places_ref[place, 0]))
    pack_ref[...] = low(pack[...])


def cross_finish(own_ref, a_ref, b_ref, c_ref, total_ref, out_ref, kept_ref, given_ref, rows):
    layer, chip, core = place_in()
    rows[...] = total_ref[...] + (own_ref[...] + a_ref[...]) + (b_ref[...] + c_ref[...])
    for ref, side in ((kept_ref, core), (given_ref, 1 - core)):
        ref[...] = jnp.zeros_like(ref)
        ref[0:1, :] = rows[pl.ds(2 * chip + side, 1), :]
        ref[1:2, :] = out_ref[pl.ds(2 * chip + side, 1), :]


def cross_owner(every_ref, weight_ref, *refs):
    mix_ref, out_ref, up_ref, down_ref, vectors_ref, bias_ref, table_ref = refs[:7]
    hidden, mixed, single, active, sums, places = refs[7:]
    layer, chip, core = place_in()
    rank = 8 * layer + 2 * chip + core
    sums[...] = jnp.zeros_like(sums)
    for level in range(4):
        for side in range(2):
            group = 2 * level + side
            rows = slice(8 * group, 8 * group + 8)
            for spot in range(4):
                value = wide(every_ref[8 * level + 2 * spot + side])
                hidden[spot, rows, :] = value[0:8]
                mixed[spot, rows, :] = value[16:24]
                for i in range(5):
                    start = 8 * group + 2 * spot
                    single[i, start : start + 2, :] = value[24 + 2 * i : 26 + 2 * i]
                sums[spot : spot + 1, :] += value[34:35]
                for sequence in range(2):
                    row = 16 * level + 8 * sequence + 2 * spot + side
                    places[row : row + 1, :] = value[35 + sequence : 36 + sequence, 0:128]
            active[rows, :] = wide(every_ref[8 * level + 2 * chip + side])[8:16]

    def select(count, first):
        lane = lax.broadcasted_iota(jnp.int32, (count, D), 1)
        row = lax.broadcasted_iota(jnp.int32, (count, D), 0)
        return wide(lane == first + row)

    own = select(24, 24 * rank)
    offset = 24 * (2 * chip + core)
    units = select(96, 192 * layer + 96 * core)
    own_low = low(own)

    def columns_of(array_in):
        return low(contract(own_low, low(array_in), 1, 1))

    inputs = columns_of(single[0])
    for spot in range(4):
        part = contract(inputs, low(mixed[spot][:, 0:576]), 1, 0)
        for third in range(3):
            start = third * D + 192 * spot
            mix_ref[:, start : start + 192] = part[:, 192 * third : 192 * (third + 1)]
    own_mixed = mixed[layer]
    context = low(contract(low(select(24, 576 + offset)), low(own_mixed), 1, 1))
    out_ref[...] = contract(context, low(single[2]), 1, 0)
    first = columns_of(single[1])
    for spot in range(4):
        part = contract(first, low(hidden[spot]), 1, 0)
        for level in range(4):
            start = 192 * (4 * level + spot)
            up_ref[:, start : start + 192] = part[:, 192 * level : 192 * (level + 1)]
    units_low = low(contract(low(units), low(active[...]), 1, 1))
    down_ref[...] = contract(units_low, low(single[3]), 1, 0)
    mixed_sum = column_sum(own_mixed)
    vectors_ref[0:1, :] = contract_exact(mixed_sum, select(24, offset), 1, 1)
    vectors_ref[1:2, :] = contract_exact(mixed_sum, select(24, 384 + offset), 1, 1)
    for row, value in (
        (2, column_sum(single[2])),
        (3, sums[0:1, :]),
        (4, sums[1:2, :]),
        (5, column_sum(single[3])),
        (6, sums[2:3, :]),
        (7, sums[3:4, :]),
    ):
        vectors_ref[row : row + 1, :] = contract_exact(value, own, 1, 1)
    bias_ref[...] = contract_exact(column_sum(hidden[chip]), units, 1, 1)
    grads = contract(low(single[4]), own_low, 1, 1)
    for spot in range(4):
        for third in range(3):
            start = third * D + 192 * spot
            part = low(mixed[spot][:, 192 * third : 192 * (third + 1)])
            grads = grads + contract(part, weight_ref[:, start : start + 192], 1, 1)
    lane = wide(lax.broadcasted_iota(jnp.int32, (64, 64), 1))
    table_ref[...] = contract_exact(wide(places[:, 0:64] == lane), grads, 0, 0)


def split_cores(value, kept_ref, gone_ref):
    rows = kept_ref.shape[1]
    core = lax.rem(lax.axis_index("seq"), 2)
    parts = value.reshape(-1, 2, rows, value.shape[1])
    kept_ref[...] = low(jnp.where(core == 0, parts[:, 0], parts[:, 1]))
    gone_ref[...] = low(jnp.where(core == 0, parts[:, 1], parts[:, 0]))


def local_down_back(
    cot_ref, mine_ref, other_ref, n_ref, scale_ref, rows_ref, active_ref, slope_ref, weight_ref, *outs
):
    out_ref, second_ref, kept_ref, gone_ref, hidden_ref, sums_ref, bias_ref, second_low_ref = outs
    step = pl.program_id(0)

    @pl.when(step == 0)
    def _():
        core = place_in()[2]
        row = lax.broadcasted_iota(jnp.int32, (2 * SEG, D), 0)
        grad = wide(cot_ref[...])
        normed = n_ref[...]
        out = normed * rows_ref[6:7, :] + rows_ref[7:8, :]
        for place in range(2):
            heads = jnp.where(core == place, mine_ref[...], other_ref[...])
            grad = jnp.where(row == place * SEG, heads[0:1], grad)
            out = jnp.where(row == place * SEG, heads[1:2], out)
        out_ref[...] = low(out)
        second = norm_back(grad, normed, scale_ref[...], rows_ref[6:7, :])
        second_ref[...] = second
        second_low_ref[...] = low(second)
        sums_ref[0:1, :] = column_sum(wide(low(second)))
        sums_ref[1:2, :] = column_sum(grad * normed)
        sums_ref[2:3, :] = column_sum(grad)

    second_low = second_low_ref[...]
    split_cores(contract(active_ref[...], second_low, 0, 0), kept_ref, gone_ref)
    hidden = low(contract(second_low, weight_ref[...], 1, 1) * wide(slope_ref[...]))
    hidden_ref[...] = hidden
    bias_ref[...] = column_sum(wide(hidden))


def local_up_back(low_ref, hidden_ref, weight_ref, second_ref, kept_ref, gone_ref, first_ref):
    hidden = hidden_ref[...]
    split_cores(contract(low_ref[...], hidden, 0, 0), kept_ref, gone_ref)
    part = contract(hidden, weight_ref[...], 1, 1)
    step = pl.program_id(0)

    @pl.when(step == 0)
    def _():
        first_ref[...] = second_ref[...] + part

    @pl.when(step > 0)
    def _():
        first_ref[...] += part


def local_attend_back(
    first_ref, n_ref, scale_ref, rows_ref, context_ref, mixed_ref, probs_ref, group_ref, *outs
):
    out_ref, total_ref, sums_ref, back_ref, context_low_ref = outs
    grad, normed = first_ref[...], n_ref[...]
    total = norm_back(grad, normed, scale_ref[...], rows_ref[3:4, :])
    total_ref[...] = total
    branch = low(total)
    sums_ref[2:3, :] = column_sum(wide(branch))
    sums_ref[3:4, :] = column_sum(grad * normed)
    sums_ref[4:5, :] = column_sum(grad)
    out_ref[...] = contract(context_ref[...], branch, 0, 0)
    context_low_ref[...] = low(contract(branch, group_ref[...], 1, 1))
    lane = lax.broadcasted_iota(jnp.int32, (SEG, 128), 1)
    for segment in range(2):
        rows = slice(segment * SEG, (segment + 1) * SEG)
        for pair in range(HEADS // 2):
            places = [
                slice(third * D + pair * 128, third * D + (pair + 1) * 128) for third in range(3)
            ]
            query, key, value = (mixed_ref[rows, place] for place in places)
            grad = context_low_ref[rows, places[0]]
            found = []
            for side in range(2):
                here = (lane < HEAD_DIM) if side == 0 else (lane >= HEAD_DIM)
                probs = probs_ref[segment * HEADS + 2 * pair + side]
                prob_grad = contract(jnp.where(here, grad, jnp.zeros_like(grad)), value, 1, 1)
                value_grad = contract(low(probs), grad, 0, 0)
                score = low(
                    probs * (prob_grad - jnp.sum(probs * prob_grad, axis=-1, keepdims=True))
                )
                found.append(
                    (contract(score, key, 1, 0), contract(score, query, 0, 0), value_grad)
                )
            for third in range(3):
                merged = jnp.where(lane < HEAD_DIM, found[0][third], found[1][third])
                if third < 2:
                    merged = merged * HEAD_DIM ** (-0.5)
                back_ref[rows, places[third]] = low(merged)
    for third in (0, 2):
        columns = slice(third * D, (third + 1) * D)
        sums_ref[third // 2 : third // 2 + 1, :] = column_sum(wide(back_ref[:, columns]))


def local_mix_back(
    total_ref, back_ref, tokens_ref, group_ref, out_ref, sums_ref, more_ref, bias_ref, *outs
):
    input_ref, kept_ref, gone_ref, small_ref = outs
    tokens, total = tokens_ref[...], total_ref[...]
    for third in range(3):
        columns = slice(third * D, (third + 1) * D)
        back = back_ref[:, columns]
        grad = contract(tokens, back, 0, 0)
        split_cores(grad, kept_ref.at[:, :, columns], gone_ref.at[:, :, columns])
        total = total + contract(back, group_ref[:, columns], 1, 1)
    input_ref[...] = total
    columns = slice(3 * D, 4 * D)
    split_cores(out_ref[...], kept_ref.at[:, :, columns], gone_ref.at[:, :, columns])
    small_ref[...] = jnp.zeros_like(small_ref)
    small_ref[0:5, :] = sums_ref[0:5, :]
    small_ref[5:8, :] = more_ref[0:3, :]
    small_ref[8:12, :] = bias_ref[...]
    columns = slice(4 * D, 4 * D + 128)
    split_cores(small_ref[...].T, kept_ref.at[:, :, columns], gone_ref.at[:, :, columns])


def plane_three(array_in):
    return [array_in] + [swap_chip(array_in, mask) for mask in (1, 2, 3)]


def plane_shards(
    tokens,
    cotangent,
    token_docs,
    segment_docs,
    segment_positions,
    local_mix,
    local_out,
    local_up,
    local_down,
    local_vectors,
    local_up_bias,
    cross_mix,
    cross_out,
    cross_up,
    cross_down,
    cross_vectors,
    cross_up_bias,
    position_table,
):
    chip = place_in()[1]
    flat_tokens = tokens.reshape(256, D)
    flat_cot = cotangent.reshape(256, D)
    docs_column = token_docs.reshape(256, 1)
    segment_column = segment_docs.T

    shard_one, shard_two, *cross_pieces = on_core(
        prepare,
        [half(24, 3200), half(24, 9 * D)] + [half(24, D + 640)] * 4,
        (
            local_mix,
            local_out,
            local_up,
            local_down.reshape(4, 24, D),
            local_vectors,
            local_up_bias.reshape(4, 24),
            cross_mix,
            cross_out,
            cross_up,
            cross_vectors,
            cross_up_bias.reshape(4, 24),
            position_table,
        ),
        0,
        scratch=[pltpu.VMEM((128, 128), jnp.float32), pltpu.VMEM((4, 24, D + 640), jnp.bfloat16)],
    )
    columns = lax.all_gather(shard_two, "dp")
    column_one = gather_dp(shard_one)
    moves_one = plane_moves(column_one)
    cross_column = gather_cross(after(tuple(cross_pieces), column_one), cross_down)
    first_group = gather_plane(moves_one).reshape(D, 3200)
    columns = after(columns, moves_one[1], moves_one[2])
    moves_two = plane_moves(columns[:, :, : 5 * D])
    moves_three = plane_moves(columns[:, :, 5 * D :], moves_two[1], moves_two[2])

    mixed_rows, context_rows, probs_kept, normed_one, scale_one, low_one, rows = on_core(
        local_attend,
        [
            half(256, 3 * D),
            half(256, D),
            shape_of(24, SEG, SEG),
            shape_of(256, D),
            shape_of(256, 1),
            half(256, D),
            shape_of(128, D),
        ],
        (flat_tokens, first_group, token_docs, docs_column),
        2 * 256 * D * 5 * D,
    )
    up_bias = rows[80:84].reshape(4, 32, 24).transpose(1, 0, 2).reshape(1, 4 * D)
    cross_bias = rows[84:88].reshape(4, 4, 4, 2, 24)
    cross_bias = lax.dynamic_index_in_dim(cross_bias, chip, 2, keepdims=False)
    cross_bias = cross_bias.transpose(1, 2, 0, 3).reshape(1, D)
    second_group = gather_plane(moves_two).reshape(D, 5 * D)
    whole = pl.BlockSpec((256, D), lambda j: (0, 0))
    thin = pl.BlockSpec((256, 1), lambda j: (0, 0))
    vectors = pl.BlockSpec((128, D), lambda j: (0, 0))
    eight = pl.BlockSpec((8, D), lambda j: (0, 0))
    across = pl.BlockSpec((256, D), lambda j: (0, j))
    tall = pl.BlockSpec((D, D), lambda j: (0, j))
    deep = pl.BlockSpec((D, D), lambda j: (j, 0))
    strip = pl.BlockSpec((1, D), lambda j: (0, j))
    active_rows, slope_rows = on_core(
        local_up_part,
        [half(256, 4 * D)] * 2,
        (low_one, second_group, up_bias),
        2 * 256 * D * 4 * D,
        grid=(4,),
        in_specs=[whole, tall, strip],
        out_specs=[across, across],
    )
    cross_up_mix, cross_down_part = place_cross(after(cross_column, moves_three[1], moves_three[2]))
    down_weight = gather_down(moves_three).reshape(4 * D, D)
    normed_two, scale_two, kept, given = on_core(
        local_down_part,
        [shape_of(256, D), shape_of(256, 1), shape_of(8, D), shape_of(8, D)],
        (active_rows, down_weight, normed_one, rows, flat_cot, flat_cot, segment_positions),
        2 * 256 * D * 4 * D,
        grid=(4,),
        in_specs=[
            across,
            deep,
            whole,
            vectors,
            pl.BlockSpec((16, D), lambda j: (0, 0)),
            pl.BlockSpec((16, D), lambda j: (8, 0)),
            pl.BlockSpec(memory_space=pltpu.SMEM),
        ],
        out_specs=[whole, thin, eight, eight],
        scratch=[pltpu.VMEM((256, D), jnp.float32)],
    )

    def plain(*shapes):
        return [pl.BlockSpec(shape, lambda j, n=len(shape): (0,) * n) for shape in shapes]

    row8, mix_share = (8, D), (D, D + 640)
    out_share = pl.BlockSpec((D, D), lambda j: (0, 4))
    up_share = pl.BlockSpec((D, D), lambda j: (0, 0))
    pair = on_core(join_pair, shape_of(8, D), (kept, swap_core(given)), 0)
    row_in, row_grad, mixed, probs, context = on_core(
        cross_attend,
        [shape_of(8, D), shape_of(8, D), half(8, 576), shape_of(3, 8, 8), half(8, 192)],
        (*plane_three(pair), cross_up_mix, rows, segment_docs, segment_column),
        0,
    )
    row_n, row_scale, row_low, hidden, active, part = on_core(
        cross_up_down,
        [shape_of(8, D), shape_of(8, 1), half(8, D), shape_of(8, D), half(8, D), shape_of(8, D)],
        (
            *plane_three(context),
            row_in,
            second_group,
            rows,
            cross_up_mix,
            cross_bias,
            cross_down_part,
        ),
        0,
        grid=(1,),
        in_specs=plain(*[(8, 192)] * 4, row8)
        + [out_share]
        + plain((128, D))
        + [up_share]
        + plain((1, D), (D, D)),
        out_specs=plain(row8, (8, 1), row8, row8, row8, row8),
    )
    row_out, row_second, hidden_low, part, sums = on_core(
        cross_turn,
        [shape_of(8, D), shape_of(8, D), half(8, D), shape_of(8, D), shape_of(8, D)],
        (*plane_three(part), row_n, rows, row_grad, hidden, cross_up_mix, cross_down_part),
        0,
        grid=(1,),
        in_specs=plain(*[row8] * 4, row8, (128, D), row8, row8) + [up_share] + plain((D, D)),
        out_specs=plain(*[row8] * 5),
    )
    row_total, part, packed = on_core(
        cross_attend_back,
        [shape_of(8, D), shape_of(8, D), half(48, D)],
        (
            *plane_three(part),
            row_second,
            row_n,
            row_scale,
            rows,
            second_group,
            mixed,
            probs,
            cross_up_mix,
            hidden_low,
            active,
            context,
            row_in,
            row_low,
            sums,
            segment_positions,
        ),
        0,
        grid=(1,),
        in_specs=plain(*[row8] * 4, row8, row8, (8, 1), (128, D))
        + [out_share]
        + plain((8, 576), (3, 8, 8), mix_share, row8, row8, (8, 192), row8, row8, row8)
        + [pl.BlockSpec(memory_space=pltpu.SMEM)],
        out_specs=plain(row8, row8, (48, D)),
        scratch=[pltpu.VMEM((48, D), jnp.float32), pltpu.VMEM((8, D), jnp.float32)],
    )
    everyone = lax.all_gather(packed, ("dp", "seq"))
    kept, given = on_core(
        cross_finish,
        [shape_of(8, D), shape_of(8, D)],
        (*plane_three(part), row_total, row_out),
        0,
        scratch=[pltpu.VMEM((8, D), jnp.float32)],
    )
    got = swap_core(given)

    fours = pl.BlockSpec((4, 96, D), lambda j: (j, 0, 0))
    layer_output, second_rows, down_kept, down_gone, hidden_grads, sums_two, bias_grad = on_core(
        local_down_back,
        [
            half(256, D),
            shape_of(256, D),
            half(16, 96, D),
            half(16, 96, D),
            half(256, 4 * D),
            shape_of(8, D),
            shape_of(1, 4 * D),
        ],
        (flat_cot, kept, got, normed_two, scale_two, rows, active_rows, slope_rows, down_weight),
        4 * 256 * D * 4 * D,
        grid=(4,),
        in_specs=[whole, eight, eight, whole, thin, vectors, across, across, deep],
        out_specs=[whole, whole, fours, fours, across, eight, strip],
        scratch=[pltpu.VMEM((256, D), jnp.bfloat16)],
    )
    down_total = Sum(down_kept.reshape(4, 4, 96, D), down_gone.reshape(4, 4, 96, D))
    sixteens = pl.BlockSpec((16, 24, D), lambda j: (0, 0, j))
    up_kept, up_gone, first_rows = on_core(
        local_up_back,
        [half(16, 24, 4 * D), half(16, 24, 4 * D), shape_of(256, D)],
        (low_one, hidden_grads, second_group, second_rows),
        4 * 256 * D * 4 * D,
        grid=(4,),
        in_specs=[whole, across, tall, whole],
        out_specs=[sixteens, sixteens, whole],
    )
    up_total = Sum(up_kept.reshape(4, 4, 24, 4 * D), up_gone.reshape(4, 4, 24, 4 * D))
    down_sent = down_total.first(first_rows)
    flat = pl.BlockSpec((256, 3 * D), lambda j: (0, 0))
    out_grad, sum_rows, sums_one, back_rows = on_core(
        local_attend_back,
        [shape_of(D, D), shape_of(256, D), shape_of(8, D), half(256, 3 * D)],
        (
            after(first_rows, down_sent, up_total.got),
            normed_one,
            scale_one,
            rows,
            context_rows,
            mixed_rows,
            probs_kept,
            first_group,
        ),
        4 * 256 * D * 2 * D,
        grid=(1,),
        in_specs=[
            whole,
            whole,
            thin,
            vectors,
            whole,
            flat,
            pl.BlockSpec((24, SEG, SEG), lambda j: (0, 0, 0)),
            pl.BlockSpec((D, D), lambda j: (0, 3)),
        ],
        out_specs=[pl.BlockSpec((D, D), lambda j: (0, 0)), whole, eight, flat],
        scratch=[pltpu.VMEM((256, D), jnp.bfloat16)],
    )
    up_sent = up_total.first(back_rows)
    down_onward = down_total.second(up_sent)
    bias_rows = bias_grad.reshape(32, 4, 24).transpose(1, 0, 2).reshape(4, D)
    sides = [half(16, 24, 4 * D + 128)] * 2
    input_grad, mix_kept, mix_gone = on_core(
        local_mix_back,
        [shape_of(256, D)] + sides,
        (
            sum_rows,
            after(back_rows, down_onward),
            flat_tokens,
            first_group,
            out_grad,
            sums_one,
            sums_two,
            bias_rows,
        ),
        4 * 256 * D * 3 * D,
        scratch=[pltpu.VMEM((128, D), jnp.float32)],
    )
    mix_total = Sum(mix_kept.reshape(4, 4, 24, 3200), mix_gone.reshape(4, 4, 24, 3200))
    up_onward = up_total.second(input_grad)
    down_own = down_total.third(up_onward)
    mix_sent = mix_total.first(down_own)
    up_own = up_total.third(mix_sent)
    mix_onward = mix_total.second(up_own)
    cross_grads = on_core(
        cross_owner,
        [
            shape_of(24, 3 * D),
            shape_of(24, D),
            shape_of(24, 4 * D),
            shape_of(96, D),
            shape_of(8, 24),
            shape_of(1, 96),
            shape_of(64, 24),
        ],
        (after(everyone, mix_onward), cross_mix),
        0,
        scratch=[
            pltpu.VMEM((4, 64, D), jnp.float32),
            pltpu.VMEM((4, 64, D), jnp.float32),
            pltpu.VMEM((5, 64, D), jnp.float32),
            pltpu.VMEM((64, D), jnp.float32),
            pltpu.VMEM((8, D), jnp.float32),
            pltpu.VMEM((64, 128), jnp.float32),
        ],
    )
    mix_total.third()
    down_sum, up_sum, mix_sum = down_total.total(), up_total.total(), mix_total.total()
    return (
        layer_output.reshape(2, SEG, D),
        input_grad.reshape(2, SEG, D),
        mix_sum[:, :2304],
        mix_sum[:, 2304:3072],
        up_sum,
        down_sum,
        mix_sum[:, 3072:3080].T,
        mix_sum[:, 3080:3084].T.reshape(96),
        *cross_grads[:5],
        cross_grads[5].reshape(96),
        cross_grads[6],
    )


def solution(mesh):
    flat = dict(mesh.shape) == {"dp": 4, "seq": 8}
    return jax.shard_map(
        plane_shards if flat else shards,
        mesh=mesh,
        in_specs=(
            P("dp", "seq", None),
            P("dp", "seq", None),
            P("dp", "seq"),
            P("dp", None),
            P("dp", "seq"),
            P(("dp", "seq"), None),
            P(("dp", "seq"), None),
            P(("dp", "seq"), None),
            P(("dp", "seq"), None),
            P(None, ("dp", "seq")),
            P(("dp", "seq")),
            P(("dp", "seq"), None),
            P(("dp", "seq"), None),
            P(("dp", "seq"), None),
            P(("dp", "seq"), None),
            P(None, ("dp", "seq")),
            P(("dp", "seq")),
            P(None, ("dp", "seq")),
        ),
        out_specs=(
            P("dp", "seq", None),
            P("dp", "seq", None),
            P(("dp", "seq"), None),
            P(("dp", "seq"), None),
            P(("dp", "seq"), None),
            P(("dp", "seq"), None),
            P(None, ("dp", "seq")),
            P(("dp", "seq")),
            P(("dp", "seq"), None),
            P(("dp", "seq"), None),
            P(("dp", "seq"), None),
            P(("dp", "seq"), None),
            P(None, ("dp", "seq")),
            P(("dp", "seq")),
            P(None, ("dp", "seq")),
        ),
        check_vma=False,
    )
```

```python
from functools import partial
import math

import jax
import jax.numpy as jnp
from jax import lax
from jax.experimental import pallas as pl
from jax.experimental.pallas import tpu as pltpu
from jax.sharding import PartitionSpec as P

D = 768
HEADS = 12
HEAD_DIM = 64
SEG = 128
MICRO = 2


epsilon = 1e-05
masked_score = -1000000000.0
owner_dims = (0, 0, 0, 0, 1, 0, 0, 0, 0, 0, 1, 0, 1)


def layer_norm(values, gain_row, shift_row):
    centered = values - jnp.mean(values, axis=-1, keepdims=True)
    variance = jnp.mean(centered * centered, axis=-1, keepdims=True)
    return centered * lax.rsqrt(variance + epsilon) * gain_row + shift_row


def gelu_exact(hidden):
    return jax.nn.gelu(hidden, approximate=False)


def contract(left_side, right_side, left_dim, right_dim):
    return lax.dot_general(
        left_side,
        right_side,
        (((left_dim,), (right_dim,)), ((), ())),
        preferred_element_type=jnp.float32,
    )


def contract_exact(left_side, right_side, left_dim, right_dim):
    return lax.dot_general(
        left_side,
        right_side,
        (((left_dim,), (right_dim,)), ((), ())),
        precision=lax.Precision.HIGHEST,
        preferred_element_type=jnp.float32,
    )


def owner_pack(grads, devices):
    pieces = []
    for grad_value, split_dim in zip(grads, owner_dims):
        if split_dim == 0:
            pieces.append(grad_value.reshape(devices, -1))
        else:
            row_count = grad_value.shape[0]
            pieces.append(
                grad_value.reshape(row_count, devices, -1).transpose(1, 0, 2).reshape(devices, -1)
            )
    return jnp.concatenate(pieces, axis=1)


def owner_unpack(packed, shard_shapes):
    results = []
    offset = 0
    for shard_shape in shard_shapes:
        length = math.prod(shard_shape)
        results.append(packed[0, offset : offset + length].reshape(shard_shape))
        offset = offset + length
    return tuple(results)


def fetch_weights(
    local_mix,
    local_out,
    local_up,
    local_down,
    local_vectors,
    local_up_bias,
    cross_mix,
    cross_out,
    cross_up,
    cross_down,
    cross_vectors,
    cross_up_bias,
    position_table,
):
    return (
        lax.all_gather(local_mix, ("dp", "seq"), axis=0, tiled=True),
        lax.all_gather(local_out, ("dp", "seq"), axis=0, tiled=True),
        lax.all_gather(local_up, ("dp", "seq"), axis=0, tiled=True),
        lax.all_gather(local_down, ("dp", "seq"), axis=0, tiled=True),
        lax.all_gather(local_vectors, ("dp", "seq"), axis=1, tiled=True),
        lax.all_gather(local_up_bias, ("dp", "seq"), axis=0, tiled=True),
        lax.all_gather(cross_mix, ("dp", "seq"), axis=0, tiled=True),
        lax.all_gather(cross_out, ("dp", "seq"), axis=0, tiled=True),
        lax.all_gather(cross_up, ("dp", "seq"), axis=0, tiled=True),
        lax.all_gather(cross_down, ("dp", "seq"), axis=0, tiled=True),
        lax.all_gather(cross_vectors, ("dp", "seq"), axis=1, tiled=True),
        lax.all_gather(cross_up_bias, ("dp", "seq"), axis=0, tiled=True),
        lax.all_gather(position_table, ("dp", "seq"), axis=1, tiled=True),
    )


def segment_parts(mixed_rows, token_docs):
    segment_count = token_docs.shape[0]
    split_heads = mixed_rows.reshape(segment_count, SEG, 3, HEADS, HEAD_DIM)
    allowed = token_docs[:, None, :, None] == token_docs[:, None, None, :]
    scores = jnp.einsum(
        "nqhd,nkhd->nhqk",
        split_heads[:, :, 0],
        split_heads[:, :, 1],
        preferred_element_type=jnp.float32,
    ) * HEAD_DIM ** (-0.5)
    scores = jnp.where(allowed, scores, masked_score)
    return (split_heads, scores)


def segment_forward(mixed_rows, token_docs):
    split_heads, scores = segment_parts(mixed_rows, token_docs)
    log_total = jax.nn.logsumexp(scores, axis=-1)
    weights = jax.nn.softmax(scores, axis=-1).astype(jnp.bfloat16)
    context = jnp.einsum(
        "nhqk,nkhd->nqhd", weights, split_heads[:, :, 2], preferred_element_type=jnp.float32
    )
    return (context.reshape(-1, D).astype(jnp.bfloat16), log_total)


def segment_backward(context_grad, log_total, mixed_rows, token_docs):
    split_heads, scores = segment_parts(mixed_rows, token_docs)
    segment_count = token_docs.shape[0]
    probs = jnp.exp(scores - log_total[..., None])
    grad_heads = context_grad.reshape(segment_count, SEG, HEADS, HEAD_DIM)
    prob_grad = jnp.einsum(
        "nqhd,nkhd->nhqk", grad_heads, split_heads[:, :, 2], preferred_element_type=jnp.float32
    )
    value_grad = jnp.einsum(
        "nhqk,nqhd->nkhd",
        probs.astype(jnp.bfloat16),
        grad_heads,
        preferred_element_type=jnp.float32,
    )
    score_grad = probs * (prob_grad - jnp.sum(probs * prob_grad, axis=-1, keepdims=True))
    score_low = score_grad.astype(jnp.bfloat16) * HEAD_DIM ** (-0.5)
    query_grad = jnp.einsum(
        "nhqk,nkhd->nqhd", score_low, split_heads[:, :, 1], preferred_element_type=jnp.float32
    )
    key_grad = jnp.einsum(
        "nhqk,nqhd->nkhd", score_low, split_heads[:, :, 0], preferred_element_type=jnp.float32
    )
    row_total = segment_count * SEG
    return jnp.concatenate(
        [
            query_grad.reshape(row_total, D),
            key_grad.reshape(row_total, D),
            value_grad.reshape(row_total, D),
        ],
        axis=1,
    )


def cross_parts(mixed_rows, gathered, segment_docs):
    group_size = segment_docs.shape[0]
    per_device = mixed_rows.shape[0] // group_size
    query_rows = mixed_rows[:, :D].reshape(group_size, per_device, HEADS, HEAD_DIM)
    key_rows = gathered[:, :, :D].reshape(group_size, -1, HEADS, HEAD_DIM)
    value_rows = gathered[:, :, D:].reshape(group_size, -1, HEADS, HEAD_DIM)
    own_docs = lax.dynamic_slice_in_dim(
        segment_docs, lax.axis_index("seq") * per_device, per_device, 1
    )
    allowed = own_docs[:, None, :, None] == segment_docs[:, None, None, :]
    scores = jnp.einsum(
        "bqhd,bkhd->bhqk", query_rows, key_rows, preferred_element_type=jnp.float32
    ) * HEAD_DIM ** (-0.5)
    scores = jnp.where(allowed, scores, masked_score)
    return (query_rows, key_rows, value_rows, scores)


def cross_forward(mixed_rows, segment_docs):
    group_size = segment_docs.shape[0]
    per_device = mixed_rows.shape[0] // group_size
    pair_rows = mixed_rows[:, D:].reshape(group_size, per_device, 2 * D)
    gathered = lax.all_gather(pair_rows, "seq", axis=1, tiled=True)
    query_rows, key_rows, value_rows, scores = cross_parts(mixed_rows, gathered, segment_docs)
    log_total = jax.nn.logsumexp(scores, axis=-1)
    weights = jax.nn.softmax(scores, axis=-1).astype(jnp.bfloat16)
    context = jnp.einsum("bhqk,bkhd->bqhd", weights, value_rows, preferred_element_type=jnp.float32)
    return (context.reshape(-1, D).astype(jnp.bfloat16), (gathered, log_total))


def cross_backward(context_grad, cross_kept, mixed_rows, segment_docs):
    gathered, log_total = cross_kept
    group_size = segment_docs.shape[0]
    row_total = mixed_rows.shape[0]
    per_device = row_total // group_size
    query_rows, key_rows, value_rows, scores = cross_parts(mixed_rows, gathered, segment_docs)
    probs = jnp.exp(scores - log_total[..., None])
    grad_heads = context_grad.reshape(group_size, per_device, HEADS, HEAD_DIM)
    prob_grad = jnp.einsum(
        "bqhd,bkhd->bhqk", grad_heads, value_rows, preferred_element_type=jnp.float32
    )
    value_grad = jnp.einsum(
        "bhqk,bqhd->bkhd",
        probs.astype(jnp.bfloat16),
        grad_heads,
        preferred_element_type=jnp.float32,
    )
    score_grad = probs * (prob_grad - jnp.sum(probs * prob_grad, axis=-1, keepdims=True))
    score_low = score_grad.astype(jnp.bfloat16) * HEAD_DIM ** (-0.5)
    query_grad = jnp.einsum(
        "bhqk,bkhd->bqhd", score_low, key_rows, preferred_element_type=jnp.float32
    )
    key_grad = jnp.einsum(
        "bhqk,bqhd->bkhd", score_low, query_rows, preferred_element_type=jnp.float32
    )
    pair_grads = jnp.concatenate(
        [key_grad.reshape(group_size, -1, D), value_grad.reshape(group_size, -1, D)], axis=2
    )
    own_pairs = lax.psum_scatter(
        pair_grads.astype(jnp.bfloat16), "seq", scatter_dimension=1, tiled=True
    ).astype(jnp.float32)
    return jnp.concatenate(
        [query_grad.reshape(row_total, D), own_pairs.reshape(row_total, 2 * D)], axis=1
    )


def block_forward(inputs, weights, attend):
    mix_weight, out_weight, up_weight, down_weight, vectors, up_bias = weights
    vector_rows = vectors.astype(jnp.float32)
    in_bias = jnp.concatenate([vector_rows[0], jnp.zeros_like(vector_rows[0]), vector_rows[1]])
    rounded = inputs.astype(jnp.bfloat16)
    mixed_rows = (
        jnp.dot(rounded, mix_weight, preferred_element_type=jnp.float32) + in_bias
    ).astype(jnp.bfloat16)
    context, attend_kept = attend(mixed_rows)
    first_sum = (
        inputs + jnp.dot(context, out_weight, preferred_element_type=jnp.float32) + vector_rows[2]
    )
    first_norm = layer_norm(first_sum, vector_rows[3], vector_rows[4])
    first_low = first_norm.astype(jnp.bfloat16)
    hidden = jnp.dot(first_low, up_weight, preferred_element_type=jnp.float32) + up_bias.astype(
        jnp.float32
    )
    active = gelu_exact(hidden).astype(jnp.bfloat16)
    second_sum = (
        first_norm
        + jnp.dot(active, down_weight, preferred_element_type=jnp.float32)
        + vector_rows[5]
    )
    output = layer_norm(second_sum, vector_rows[6], vector_rows[7])
    return (
        output,
        (
            rounded,
            mixed_rows,
            attend_kept,
            context,
            first_sum,
            first_low,
            hidden,
            active,
            second_sum,
        ),
    )


def block_backward(output_grad, block_kept, weights, attend_back):
    mix_weight, out_weight, up_weight, down_weight, vectors, up_bias = weights
    vector_rows = vectors.astype(jnp.float32)
    rounded, mixed_rows, attend_kept, context, first_sum, first_low, hidden, active, second_sum = (
        block_kept
    )
    unused, second_pull = jax.vjp(layer_norm, second_sum, vector_rows[6], vector_rows[7])
    second_grad, gain_two, shift_two = second_pull(output_grad)
    second_low = second_grad.astype(jnp.bfloat16)
    down_grad = contract(active, second_low, 0, 0)
    down_bias = jnp.sum(second_low.astype(jnp.float32), axis=0)
    active_grad = contract(second_low, down_weight, 1, 1)
    unused, gelu_pull = jax.vjp(gelu_exact, hidden)
    hidden_grad = gelu_pull(active_grad)[0]
    hidden_low = hidden_grad.astype(jnp.bfloat16)
    up_grad = contract(first_low, hidden_low, 0, 0)
    up_bias_grad = jnp.sum(hidden_low.astype(jnp.float32), axis=0)
    first_grad = second_grad + contract(hidden_low, up_weight, 1, 1)
    unused, first_pull = jax.vjp(layer_norm, first_sum, vector_rows[3], vector_rows[4])
    sum_grad, gain_one, shift_one = first_pull(first_grad)
    branch_low = sum_grad.astype(jnp.bfloat16)
    out_grad = contract(context, branch_low, 0, 0)
    out_bias = jnp.sum(branch_low.astype(jnp.float32), axis=0)
    context_low = contract(branch_low, out_weight, 1, 1).astype(jnp.bfloat16)
    mixed_low = attend_back(context_low, attend_kept, mixed_rows).astype(jnp.bfloat16)
    mix_grad = contract(rounded, mixed_low, 0, 0)
    mixed_sums = jnp.sum(mixed_low.astype(jnp.float32), axis=0)
    input_grad = sum_grad + contract(mixed_low, mix_weight, 1, 1)
    vectors_grad = jnp.stack(
        [
            mixed_sums[:D],
            mixed_sums[2 * D :],
            out_bias,
            gain_one,
            shift_one,
            down_bias,
            gain_two,
            shift_two,
        ]
    )
    return (input_grad, (mix_grad, out_grad, up_grad, down_grad, vectors_grad, up_bias_grad))


def shards(
    tokens,
    cotangent,
    token_docs,
    segment_docs,
    segment_positions,
    local_mix,
    local_out,
    local_up,
    local_down,
    local_vectors,
    local_up_bias,
    cross_mix,
    cross_out,
    cross_up,
    cross_down,
    cross_vectors,
    cross_up_bias,
    position_table,
):
    sequence_count, span, width = tokens.shape
    group_size = sequence_count // MICRO
    segment_count = span // SEG
    devices = lax.axis_size(("dp", "seq"))
    shard_shapes = tuple(
        (
            array_in.shape
            for array_in in (
                local_mix,
                local_out,
                local_up,
                local_down,
                local_vectors,
                local_up_bias,
                cross_mix,
                cross_out,
                cross_up,
                cross_down,
                cross_vectors,
                cross_up_bias,
                position_table,
            )
        )
    )
    layer_outputs = []
    input_grads = []
    totals = ()
    for micro_step in range(MICRO):
        lower_row = micro_step * group_size
        upper_row = lower_row + group_size
        gathered = fetch_weights(
            local_mix,
            local_out,
            local_up,
            local_down,
            local_vectors,
            local_up_bias,
            cross_mix,
            cross_out,
            cross_up,
            cross_down,
            cross_vectors,
            cross_up_bias,
            position_table,
        )
        local_weights = gathered[0:6]
        cross_weights = gathered[6:12]
        position_rows = gathered[12]
        inputs = tokens[lower_row:upper_row].reshape(group_size * span, width).astype(jnp.float32)
        docs_here = token_docs[lower_row:upper_row]
        segments_here = segment_docs[lower_row:upper_row]
        first_out, first_kept = block_forward(
            inputs, local_weights, partial(segment_forward, token_docs=docs_here)
        )
        segment_grid = first_out.reshape(group_size * segment_count, SEG, width)
        places = segment_positions[lower_row:upper_row].reshape(group_size * segment_count)
        position_picks = (
            places[:, None] == jnp.arange(position_rows.shape[0], dtype=jnp.int32)[None, :]
        ).astype(jnp.bfloat16)
        heads_in = segment_grid[:, 0, :] + jnp.dot(
            position_picks, position_rows, preferred_element_type=jnp.float32
        )
        heads_out, cross_kept = block_forward(
            heads_in, cross_weights, partial(cross_forward, segment_docs=segments_here)
        )
        joined = jnp.concatenate([heads_out[:, None, :], segment_grid[:, 1:, :]], axis=1)
        layer_outputs.append(joined.astype(jnp.bfloat16))
        gathered = fetch_weights(
            local_mix,
            local_out,
            local_up,
            local_down,
            local_vectors,
            local_up_bias,
            cross_mix,
            cross_out,
            cross_up,
            cross_down,
            cross_vectors,
            cross_up_bias,
            position_table,
        )
        local_weights = gathered[0:6]
        cross_weights = gathered[6:12]
        output_grad = cotangent[lower_row:upper_row].astype(jnp.float32)
        heads_grad, cross_grads = block_backward(
            output_grad[:, 0, :],
            cross_kept,
            cross_weights,
            partial(cross_backward, segment_docs=segments_here),
        )
        table_grad = contract_exact(position_picks.astype(jnp.float32), heads_grad, 0, 0)
        first_grad = jnp.concatenate(
            [heads_grad[:, None, :], output_grad[:, 1:, :]], axis=1
        ).reshape(group_size * span, width)
        input_grad, local_grads = block_backward(
            first_grad, first_kept, local_weights, partial(segment_backward, token_docs=docs_here)
        )
        input_grads.append(input_grad.reshape(group_size, span, width))
        step_grads = local_grads + cross_grads + (table_grad,)
        if micro_step == 0:
            totals = tuple(step_grads)
        else:
            totals = tuple(
                (total_sum + step_sum for total_sum, step_sum in zip(totals, step_grads))
            )
    packed_total = lax.psum_scatter(
        owner_pack(totals, devices), ("dp", "seq"), scatter_dimension=0, tiled=True
    )
    summed = owner_unpack(packed_total, shard_shapes)
    layer_output = jnp.concatenate(layer_outputs, axis=0)
    input_gradient = jnp.concatenate(input_grads, axis=0)
    return (layer_output, input_gradient) + tuple(summed)


def swap_dp(array_in, shift):
    return lax.ppermute(array_in, "dp", [(i, (i + shift) % 4) for i in range(4)])


def swap_core(array_in):
    return lax.ppermute(array_in, "seq", [(i, i ^ 1) for i in range(8)])


def swap_chip(array_in, mask):
    return lax.ppermute(array_in, "seq", [(i, i ^ (2 * mask)) for i in range(8)])


def swap_one(array_in):
    return lax.ppermute(array_in, "seq", [(i, i ^ (2 if i % 2 == 0 else 4)) for i in range(8)])


def swap_two(array_in):
    return lax.ppermute(array_in, "seq", [(i, i ^ (4 if i % 2 == 0 else 2)) for i in range(8)])


def place_in():
    layer = lax.axis_index("dp")
    spot = lax.axis_index("seq")
    return layer, spot // 2, lax.rem(spot, 2)


def after(array_in, *before):
    return lax.optimization_barrier((array_in,) + before)[0]


def stage(*values):
    return lax.optimization_barrier(values)


def wide(array_in):
    return array_in.astype(jnp.float32)


def low(array_in):
    return array_in.astype(jnp.bfloat16)


def copies(pieces, shapes, moves, room=64):
    count, made = len(pieces), len(shapes)
    total = len(moves(0, 0, 0))

    def kernel(*refs):
        outs, held, sems = refs[count : count + made], refs[count + made : -1], refs[-1]
        inward = [pltpu.make_async_copy(refs[i], held[i], sems.at[0, i]) for i in range(count)]
        for copy in inward:
            copy.start()
        outward = []
        for i, (piece, part, out, place) in enumerate(moves(*place_in())):
            if inward[piece] is not None:
                inward[piece].wait()
                inward[piece] = None
            copy = pltpu.make_async_copy(held[piece].at[part], outs[out].at[place], sems.at[1, i])
            copy.start()
            outward.append(copy)
        for copy in outward:
            copy.wait()

    size = 2 * sum(math.prod(shape) for shape in shapes) * 2
    return pl.pallas_call(
        kernel,
        out_shape=[jax.ShapeDtypeStruct(shape, pieces[0].dtype) for shape in shapes],
        in_specs=[pl.BlockSpec(memory_space=pltpu.HBM)] * count,
        out_specs=[pl.BlockSpec(memory_space=pltpu.HBM)] * made,
        scratch_shapes=[pltpu.VMEM(piece.shape, piece.dtype) for piece in pieces]
        + [pltpu.SemaphoreType.DMA((2, max(count, total)))],
        compiler_params=pltpu.CompilerParams(vmem_limit_bytes=room * 2**20),
        cost_estimate=pl.CostEstimate(flops=0, bytes_accessed=0, transcendentals=0),
    )(*pieces)


every = slice(None)


def reach_dp(shard):
    return [shard] + [swap_dp(shard, shift) for shift in (1, 2, 3)]


def join_dp(pieces):
    return copies(
        pieces,
        [(4,) + pieces[0].shape],
        lambda layer, chip, core: [(i, every, 0, lax.rem(layer + 4 - i, 4)) for i in range(4)],
    )[0]


def plane_order(chip, core):
    near, far = chip ^ (1 + core), chip ^ (2 - core)
    return (chip, near, far, chip ^ 3), (chip, far, near, chip ^ 3)


def gather_plane(mine, others):
    def moves(layer, chip, core):
        own, other = plane_order(chip, core)
        found = [(i, every, 0, (every, own[i], core)) for i in range(4)]
        return found + [(4 + i, every, 0, (every, other[i], 1 - core)) for i in range(4)]

    shape = (4, 4, 2) + mine[0].shape[1:]
    return copies(mine + others, [shape], moves)[0]


def gather_down(mine, others):
    def moves(layer, chip, core):
        own, other = plane_order(chip, core)
        found = []
        for i in range(8):
            spot, side = (own[i], core) if i < 4 else (other[i - 4], 1 - core)
            for quarter in range(4):
                part = (every, every, slice(quarter * D, (quarter + 1) * D))
                found.append((i, part, 0, (every, spot, side, quarter)))
        return found

    return copies(mine + others, [(4, 4, 2, 4, 24, D)], moves, room=24)[0]


class Sum:
    def __init__(self, kept):
        self.kept = kept
        self.shape = kept.shape[2:]

    def run(self, operands, out_shapes, plan):
        shape, count, made = self.shape, len(operands), len(out_shapes)
        dry = plan(0, 0, 0)
        pieces = sum(len(sources) for sources, target in dry)

        def kernel(*refs):
            given, outs = refs[:count], refs[count : count + made]
            held, built, sems = refs[count + made : -len(dry) - 1], refs[-len(dry) - 1 : -1], refs[-1]
            inward, outward, steps = [], [], []
            for sources, target in plan(*place_in()):
                step = []
                for operand, index in sources:
                    spot = len(inward)
                    source = given[operand].at[index]
                    copy = pltpu.make_async_copy(source, held[spot], sems.at[0, spot])
                    copy.start()
                    inward.append(copy)
                    step.append(spot)
                steps.append((step, target))
            for place, (step, (out, index)) in enumerate(steps):
                total = None
                for spot in step:
                    inward[spot].wait()
                    value = wide(held[spot][...])
                    total = value if total is None else total + value
                built[place][...] = total.astype(built[place].dtype)
                target = outs[out] if index is None else outs[out].at[index]
                copy = pltpu.make_async_copy(built[place], target, sems.at[1, place])
                copy.start()
                outward.append(copy)
            for copy in outward:
                copy.wait()

        far = pl.BlockSpec(memory_space=pltpu.HBM)
        return pl.pallas_call(
            kernel,
            out_shape=out_shapes,
            in_specs=[far] * count,
            out_specs=[far] * made,
            scratch_shapes=[pltpu.VMEM(shape, jnp.bfloat16)] * pieces
            + [pltpu.VMEM(shape, out_shapes[target[0]].dtype) for sources, target in dry]
            + [pltpu.SemaphoreType.DMA((2, pieces))],
            compiler_params=pltpu.CompilerParams(vmem_limit_bytes=64 * 2**20),
            cost_estimate=pl.CostEstimate(flops=0, bytes_accessed=0, transcendentals=0),
        )(*operands)

    def first(self, got):
        self.got = got

        def plan(layer, chip, core):
            return [
                ([(0, (z, spot)), (1, (z, spot))], (0, (i, z)))
                for i, spot in enumerate((chip ^ (1 + core), chip ^ 3))
                for z in range(4)
            ]

        return self.run([self.kept, got], [half(2, 4, *self.shape)], plan)[0]

    def second(self, back):
        self.back = back

        def plan(layer, chip, core):
            spot = chip ^ (2 - core)
            return [
                ([(0, (z, spot)), (1, (z, spot)), (2, (1, z))], (0, z)) for z in range(4)
            ]

        return self.run([self.kept, self.got, back], [half(4, *self.shape)], plan)[0]

    def third(self, last):
        def plan(layer, chip, core):
            found = []
            for shift in (1, 2, 3, 0):
                z = lax.rem(layer + shift, 4)
                sources = [(0, (z, chip)), (1, (z, chip)), (2, (0, z)), (3, z)]
                found.append((sources, (shift, None)))
            return found

        self.own, *others = self.run(
            [self.kept, self.got, self.back, last],
            [shape_of(*self.shape)] + [half(*self.shape)] * 3,
            plan,
        )
        return others

    def total(self, others):
        return self.own + wide(others[0]) + wide(others[1]) + wide(others[2])


def send_dp(others):
    return [swap_dp(other, shift) for shift, other in zip((1, 2, 3), others)]


def norm_parts(values):
    centered = values - jnp.mean(values, axis=-1, keepdims=True)
    variance = jnp.mean(centered * centered, axis=-1, keepdims=True)
    scale = lax.rsqrt(variance + epsilon)
    return centered * scale, scale


def norm_back(grad, normed, scale, gain):
    scaled = grad * gain
    return scale * (
        scaled
        - jnp.mean(scaled, axis=-1, keepdims=True)
        - normed * jnp.mean(scaled * normed, axis=-1, keepdims=True)
    )


def gelu_slope(hidden):
    return 0.5 * (1.0 + lax.erf(hidden * math.sqrt(0.5))) + hidden * jnp.exp(
        -0.5 * hidden * hidden
    ) * (1.0 / math.sqrt(2.0 * math.pi))


def shape_of(*shape, dtype=jnp.float32):
    return jax.ShapeDtypeStruct(shape, dtype)


def half(*shape):
    return jax.ShapeDtypeStruct(shape, jnp.bfloat16)


def on_core(kernel, out_shape, operands, flops, room=64, grid=(), in_specs=None, out_specs=None, scratch=()):
    arrays = jax.tree.leaves(out_shape) + list(operands)
    size = sum(math.prod(a.shape) * a.dtype.itemsize for a in arrays)
    extra = {} if in_specs is None else {"in_specs": in_specs, "out_specs": out_specs}
    return pl.pallas_call(
        kernel,
        out_shape=out_shape,
        grid=grid,
        scratch_shapes=scratch,
        compiler_params=pltpu.CompilerParams(vmem_limit_bytes=room * 2**20),
        cost_estimate=pl.CostEstimate(flops=0, bytes_accessed=0, transcendentals=0),
        **extra,
    )(*operands)


def column_sum(array_in):
    return jnp.sum(array_in, axis=0, keepdims=True)


def prepare(*refs):
    given, made, held, built = refs[0:12], refs[12:19], refs[19:31], refs[31:38]
    small, turned, parts, sems = refs[38:]
    inward = [pltpu.make_async_copy(given[i], held[i], sems.at[0, i]) for i in range(12)]
    outward = [pltpu.make_async_copy(built[i], made[i], sems.at[1, i]) for i in range(7)]
    for copy in inward:
        copy.start()
    for copy in inward:
        copy.wait()
    mix_ref, out_ref, up_ref, down_ref, vectors_ref, bias_ref = held[0:6]
    cross_mix_ref, cross_out_ref, cross_up_ref, cross_vectors_ref, cross_bias_ref, table_ref = held[6:]
    one_ref, two_ref, three_ref = built[0:3]
    one_ref[:, 0 : 3 * D] = mix_ref[...]
    one_ref[:, 3 * D : 4 * D] = out_ref[...]
    small[...] = jnp.zeros_like(small)
    small[0:8, 0:24] = wide(vectors_ref[...])
    small[8:16, 0:24] = wide(cross_vectors_ref[...])
    for row in range(4):
        lanes = slice(24 * row, 24 * (row + 1))
        small[80 + row : 81 + row, 0:24] = wide(bias_ref[:, lanes])
        small[84 + row : 85 + row, 0:24] = wide(cross_bias_ref[:, lanes])
    turned[...] = small[...].T
    turned[0:24, 16:80] = wide(table_ref[...])
    one_ref[:, 4 * D : 4 * D + 128] = low(turned[0:24, :])
    outward[0].start()
    two_ref[:, 0 : 4 * D] = up_ref[...]
    two_ref[:, 4 * D : 5 * D] = cross_out_ref[...]
    for quarter in range(4):
        three_ref[:, quarter * D : (quarter + 1) * D] = down_ref[quarter]
    outward[1].start()
    outward[2].start()
    parts[...] = jnp.zeros_like(parts)
    for spot in range(4):
        for level in range(4):
            taken = cross_up_ref[:, 192 * (4 * level + spot) : 192 * (4 * level + spot + 1)]
            parts[spot, :, 192 * level : 192 * (level + 1)] = taken
        for third in range(3):
            taken = cross_mix_ref[:, third * D + 192 * spot : third * D + 192 * (spot + 1)]
            parts[spot, :, D + 192 * third : D + 192 * (third + 1)] = taken
    chip = place_in()[1]
    for mask in range(4):
        built[3 + mask][...] = parts[chip ^ mask]
        outward[3 + mask].start()
    for copy in outward:
        copy.wait()


def join_cross(pieces, cross_down):
    def moves(layer, chip, core):
        found = []
        for mask in range(4):
            found.append((mask, (every, slice(0, D)), 0, (chip ^ mask, every, slice(0, D))))
            taken = (every, slice(D, D + 640))
            found.append((mask, taken, 0, (chip ^ mask, every, slice(2 * D, 2 * D + 640))))
        found.append((4, every, 0, (every, every, slice(D, 2 * D))))
        return found

    return copies(pieces + [cross_down.reshape(4, 24, D)], [(4, 24, 2 * D + 640)], moves)[0]


def place_cross(column):
    other = swap_core(column)

    def moves(layer, chip, core):
        found = []
        for piece, side in ((0, core), (1, 1 - core)):
            lead = (every, every, side, every)
            source = (every, every, every)
            found.append((piece, source + (slice(0, D),), 0, lead + (slice(0, D),)))
            found.append(
                (piece, source + (slice(2 * D, 2 * D + 640),), 0, lead + (slice(D, D + 640),))
            )
            found.append((piece, source + (slice(D, 2 * D),), 1, (every, side)))
        return found

    up_mix, down = copies(
        [column, other], [(4, 4, 2, 24, D + 640), (4, 2, 4, 24, D)], moves, room=24
    )
    return up_mix.reshape(D, D + 640), down.reshape(D, D)


def local_attend(tokens_ref, group_ref, docs_ref, docs_column_ref, *outs):
    mixed_ref, context_ref, probs_ref, n_ref, scale_ref, low_ref, rows_ref = outs
    rows_ref[...] = wide(group_ref[:, 4 * D : 4 * D + 128]).T
    tokens = tokens_ref[...]
    for third in range(3):
        columns = slice(third * D, (third + 1) * D)
        mixed = contract(tokens, group_ref[:, columns], 1, 0)
        if third != 1:
            mixed = mixed + rows_ref[third // 2 : third // 2 + 1, :]
        mixed_ref[:, columns] = low(mixed)
    lane = lax.broadcasted_iota(jnp.int32, (SEG, 128), 1)
    for segment in range(2):
        rows = slice(segment * SEG, (segment + 1) * SEG)
        allowed = docs_column_ref[rows, :] == docs_ref[segment : segment + 1, :]
        for pair in range(HEADS // 2):
            query, key, value = (
                mixed_ref[rows, third * D + pair * 128 : third * D + (pair + 1) * 128]
                for third in range(3)
            )
            found = []
            for side in range(2):
                here = (lane < HEAD_DIM) if side == 0 else (lane >= HEAD_DIM)
                scores = contract(jnp.where(here, query, jnp.zeros_like(query)), key, 1, 1)
                scores = jnp.where(allowed, scores * HEAD_DIM ** (-0.5), masked_score)
                powers = jnp.exp(scores - jnp.max(scores, axis=-1, keepdims=True))
                probs = powers / jnp.sum(powers, axis=-1, keepdims=True)
                probs_ref[segment * HEADS + 2 * pair + side] = probs
                found.append(contract(low(probs), value, 1, 0))
            context = jnp.where(lane < HEAD_DIM, found[0], found[1])
            context_ref[rows, pair * 128 : (pair + 1) * 128] = low(context)
    total = wide(tokens) + contract(context_ref[...], group_ref[:, 3 * D : 4 * D], 1, 0)
    normed, scale = norm_parts(total + rows_ref[2:3, :])
    n_ref[...] = normed
    scale_ref[...] = scale
    low_ref[...] = low(normed * rows_ref[3:4, :] + rows_ref[4:5, :])


def local_up_part(low_ref, weight_ref, bias_ref, active_ref, slope_ref):
    hidden = contract(low_ref[...], weight_ref[...], 1, 0) + wide(bias_ref[...])
    chance = 0.5 * (1.0 + lax.erf(hidden * math.sqrt(0.5)))
    density = jnp.exp(-0.5 * hidden * hidden) * (1.0 / math.sqrt(2.0 * math.pi))
    active_ref[...] = low(hidden * chance)
    slope_ref[...] = low(chance + hidden * density)


def local_down_part(
    active_ref, weight_ref, first_ref, rows_ref, cot_a, cot_b, places_ref, *outs
):
    n_ref, scale_ref, kept_ref, given_ref, total = outs
    step = pl.program_id(0)
    part = contract(active_ref[...], weight_ref[...], 1, 0)

    @pl.when(step == 0)
    def _():
        first_norm = first_ref[...] * rows_ref[3:4, :] + rows_ref[4:5, :]
        total[...] = first_norm + rows_ref[5:6, :] + part

    @pl.when(step > 0)
    def _():
        total[...] += part

    @pl.when(step == 3)
    def _():
        normed, scale = norm_parts(total[...])
        n_ref[...] = normed
        scale_ref[...] = scale
        core = place_in()[2]
        heads, grads = [], []
        for place, cot in ((0, cot_a), (1, cot_b)):
            row = normed[place * SEG : place * SEG + 1] * rows_ref[6:7, :] + rows_ref[7:8, :]
            heads.append(row + rows_ref[pl.ds(16 + places_ref[place, 0], 1), :])
            grads.append(wide(cot[...])[0:1])
        for ref, mine in ((kept_ref, core == 0), (given_ref, core == 1)):
            ref[...] = jnp.zeros_like(ref)
            ref[0:1, :] = jnp.where(mine, heads[0], heads[1])
            ref[1:2, :] = jnp.where(mine, grads[0], grads[1])


def join_pair(kept_ref, got_ref, out_ref):
    core = place_in()[2]
    out_ref[...] = jnp.zeros_like(out_ref)
    out_ref[0:2, :] = jnp.where(core == 0, kept_ref[0:2, :], got_ref[0:2, :])
    out_ref[2:4, :] = jnp.where(core == 0, got_ref[0:2, :], kept_ref[0:2, :])


def cross_attend(
    own_ref, a_ref, b_ref, c_ref, weight_ref, rows_ref, docs_ref, docs_column_ref, *outs
):
    in_ref, grad_ref, mixed_ref, probs_ref, context_ref = outs
    layer, chip, core = place_in()
    for mask, ref in enumerate((own_ref, a_ref, b_ref, c_ref)):
        for side in range(2):
            row = 2 * (chip ^ mask) + side
            in_ref[pl.ds(row, 1), :] = ref[2 * side : 2 * side + 1, :]
            grad_ref[pl.ds(row, 1), :] = ref[2 * side + 1 : 2 * side + 2, :]
    biases = []
    for vector in (8, 9):
        row = rows_ref[vector : vector + 1, :]
        found = row[:, 0:192]
        for spot in range(1, 4):
            found = jnp.where(chip == spot, row[:, 192 * spot : 192 * (spot + 1)], found)
        biases.append(found)
    bias = jnp.concatenate([biases[0], jnp.zeros_like(biases[0]), biases[1]], axis=1)
    mixed = low(contract(low(in_ref[...]), weight_ref[:, D : D + 576], 1, 0) + bias)
    mixed_ref[...] = mixed
    row_docs = jnp.where(core == 0, docs_ref[0:1, :], docs_ref[1:2, :])
    column_docs = jnp.where(core == 0, docs_column_ref[:, 0:1], docs_column_ref[:, 1:2])
    allowed = row_docs == column_docs
    found = []
    for head in range(3):
        query, key, value = (
            mixed[:, third * 192 + head * HEAD_DIM : third * 192 + (head + 1) * HEAD_DIM]
            for third in range(3)
        )
        scores = contract(query, key, 1, 1) * HEAD_DIM ** (-0.5)
        scores = jnp.where(allowed, scores, masked_score)
        powers = jnp.exp(scores - jnp.max(scores, axis=-1, keepdims=True))
        probs = powers / jnp.sum(powers, axis=-1, keepdims=True)
        probs_ref[head] = probs
        found.append(contract(low(probs), value, 1, 0))
    context_ref[...] = low(jnp.concatenate(found, axis=1))


def cross_up_down(
    own_ref, a_ref, b_ref, c_ref, in_ref, out_weight_ref, rows_ref, up_ref, bias_ref, down_ref, *outs
):
    n_ref, scale_ref, low_ref, hidden_ref, active_ref, part_ref = outs
    chip = place_in()[1]
    total = in_ref[...] + rows_ref[10:11, :]
    for mask, ref in enumerate((own_ref, a_ref, b_ref, c_ref)):
        start = pl.multiple_of(192 * (chip ^ mask), 64)
        total = total + contract(ref[...], out_weight_ref[pl.ds(start, 192), :], 1, 0)
    normed, scale = norm_parts(total)
    n_ref[...] = normed
    scale_ref[...] = scale
    first = low(normed * rows_ref[11:12, :] + rows_ref[12:13, :])
    low_ref[...] = first
    hidden = contract(first, up_ref[...], 1, 0) + bias_ref[...]
    hidden_ref[...] = hidden
    active = low(hidden * (0.5 * (1.0 + lax.erf(hidden * math.sqrt(0.5)))))
    active_ref[...] = active
    part_ref[...] = contract(active, down_ref[...], 1, 0)


def cross_turn(
    own_ref, a_ref, b_ref, c_ref, n_ref, rows_ref, grad_ref, hidden_ref, up_ref, down_ref, *outs
):
    out_ref, second_ref, hidden_low_ref, part_ref, sums_ref = outs
    first = n_ref[...] * rows_ref[11:12, :] + rows_ref[12:13, :]
    total = (own_ref[...] + a_ref[...]) + (b_ref[...] + c_ref[...])
    normed, scale = norm_parts(first + total + rows_ref[13:14, :])
    out_ref[...] = normed * rows_ref[14:15, :] + rows_ref[15:16, :]
    grad = grad_ref[...]
    second = norm_back(grad, normed, scale, rows_ref[14:15, :])
    second_ref[...] = second
    hidden_low = low(contract(low(second), down_ref[...], 1, 1) * gelu_slope(hidden_ref[...]))
    hidden_low_ref[...] = hidden_low
    part_ref[...] = contract(hidden_low, up_ref[...], 1, 1)
    sums_ref[...] = jnp.zeros_like(sums_ref)
    sums_ref[0:1, :] = column_sum(grad * normed)
    sums_ref[1:2, :] = column_sum(grad)


def cross_attend_back(
    own_ref,
    a_ref,
    b_ref,
    c_ref,
    second_ref,
    n_ref,
    scale_ref,
    rows_ref,
    out_weight_ref,
    mixed_ref,
    probs_ref,
    weight_ref,
    hidden_low_ref,
    active_ref,
    context_ref,
    in_ref,
    low_ref,
    sums_ref,
    places_ref,
    total_ref,
    part_ref,
    pack_ref,
    pack,
    rows,
):
    chip = place_in()[1]
    grad = second_ref[...] + (own_ref[...] + a_ref[...]) + (b_ref[...] + c_ref[...])
    normed = n_ref[...]
    total = norm_back(grad, normed, scale_ref[...], rows_ref[11:12, :])
    total_ref[...] = total
    branch = low(total)
    start = pl.multiple_of(192 * chip, 64)
    context_low = low(contract(branch, out_weight_ref[pl.ds(start, 192), :], 1, 1))
    mixed = mixed_ref[...]
    found = [[], [], []]
    for head in range(3):
        query, key, value = (
            mixed[:, third * 192 + head * HEAD_DIM : third * 192 + (head + 1) * HEAD_DIM]
            for third in range(3)
        )
        part = context_low[:, head * HEAD_DIM : (head + 1) * HEAD_DIM]
        probs = probs_ref[head]
        prob_grad = contract(part, value, 1, 1)
        score = low(probs * (prob_grad - jnp.sum(probs * prob_grad, axis=-1, keepdims=True)))
        found[0].append(contract(score, key, 1, 0) * HEAD_DIM ** (-0.5))
        found[1].append(contract(score, query, 0, 0) * HEAD_DIM ** (-0.5))
        found[2].append(contract(low(probs), part, 0, 0))
    mixed_low = low(jnp.concatenate(found[0] + found[1] + found[2], axis=1))
    part_ref[...] = contract(mixed_low, weight_ref[:, D : D + 576], 1, 1)
    pack[...] = jnp.zeros_like(pack)
    pack[0:8, :] = wide(hidden_low_ref[...])
    pack[8:16, :] = wide(active_ref[...])
    pack[16:24, 0:576] = wide(mixed_low)
    pack[16:24, 576:768] = wide(context_ref[...])
    for i, value in enumerate(
        (in_ref[...], wide(low_ref[...]), total, second_ref[...], total)
    ):
        rows[...] = value
        for side in range(2):
            row = 24 + 2 * i + side
            pack[row : row + 1, :] = rows[pl.ds(2 * chip + side, 1), :]
    rows[0:1, :] = column_sum(grad * normed)
    rows[1:2, :] = column_sum(grad)
    rows[2:4, :] = sums_ref[0:2, :]
    pack[34:35, :] = rows[pl.ds(chip, 1), :]
    for place in range(2):
        pack[35 + place : 36 + place, :] = jnp.full((1, D), wide(places_ref[place, 0]))
    pack_ref[...] = low(pack[...])


def cross_finish(own_ref, a_ref, b_ref, c_ref, total_ref, out_ref, kept_ref, given_ref, rows):
    layer, chip, core = place_in()
    rows[...] = total_ref[...] + (own_ref[...] + a_ref[...]) + (b_ref[...] + c_ref[...])
    for ref, side in ((kept_ref, core), (given_ref, 1 - core)):
        ref[...] = jnp.zeros_like(ref)
        ref[0:1, :] = rows[pl.ds(2 * chip + side, 1), :]
        ref[1:2, :] = out_ref[pl.ds(2 * chip + side, 1), :]


def cross_owner(every_ref, weight_ref, *refs):
    mix_ref, out_ref, up_ref, down_ref, vectors_ref, bias_ref, table_ref = refs[:7]
    hidden, mixed, single, active, sums, places = refs[7:]
    layer, chip, core = place_in()
    rank = 8 * layer + 2 * chip + core
    sums[...] = jnp.zeros_like(sums)
    for level in range(4):
        for side in range(2):
            group = 2 * level + side
            rows = slice(8 * group, 8 * group + 8)
            for spot in range(4):
                value = wide(every_ref[8 * level + 2 * spot + side])
                hidden[spot, rows, :] = value[0:8]
                mixed[spot, rows, :] = value[16:24]
                for i in range(5):
                    start = 8 * group + 2 * spot
                    single[i, start : start + 2, :] = value[24 + 2 * i : 26 + 2 * i]
                sums[spot : spot + 1, :] += value[34:35]
                for sequence in range(2):
                    row = 16 * level + 8 * sequence + 2 * spot + side
                    places[row : row + 1, :] = value[35 + sequence : 36 + sequence, 0:128]
            active[rows, :] = wide(every_ref[8 * level + 2 * chip + side])[8:16]

    def select(count, first):
        lane = lax.broadcasted_iota(jnp.int32, (count, D), 1)
        row = lax.broadcasted_iota(jnp.int32, (count, D), 0)
        return wide(lane == first + row)

    own = select(24, 24 * rank)
    offset = 24 * (2 * chip + core)
    units = select(96, 192 * layer + 96 * core)
    own_low = low(own)

    def columns_of(array_in):
        return low(contract(own_low, low(array_in), 1, 1))

    inputs = columns_of(single[0])
    for spot in range(4):
        part = contract(inputs, low(mixed[spot][:, 0:576]), 1, 0)
        for third in range(3):
            start = third * D + 192 * spot
            mix_ref[:, start : start + 192] = part[:, 192 * third : 192 * (third + 1)]
    own_mixed = mixed[layer]
    context = low(contract(low(select(24, 576 + offset)), low(own_mixed), 1, 1))
    out_ref[...] = contract(context, low(single[2]), 1, 0)
    first = columns_of(single[1])
    for spot in range(4):
        part = contract(first, low(hidden[spot]), 1, 0)
        for level in range(4):
            start = 192 * (4 * level + spot)
            up_ref[:, start : start + 192] = part[:, 192 * level : 192 * (level + 1)]
    units_low = low(contract(low(units), low(active[...]), 1, 1))
    down_ref[...] = contract(units_low, low(single[3]), 1, 0)
    mixed_sum = column_sum(own_mixed)
    vectors_ref[0:1, :] = contract_exact(mixed_sum, select(24, offset), 1, 1)
    vectors_ref[1:2, :] = contract_exact(mixed_sum, select(24, 384 + offset), 1, 1)
    for row, value in (
        (2, column_sum(single[2])),
        (3, sums[0:1, :]),
        (4, sums[1:2, :]),
        (5, column_sum(single[3])),
        (6, sums[2:3, :]),
        (7, sums[3:4, :]),
    ):
        vectors_ref[row : row + 1, :] = contract_exact(value, own, 1, 1)
    bias_ref[...] = contract_exact(column_sum(hidden[chip]), units, 1, 1)
    grads = contract(low(single[4]), own_low, 1, 1)
    for spot in range(4):
        for third in range(3):
            start = third * D + 192 * spot
            part = low(mixed[spot][:, 192 * third : 192 * (third + 1)])
            grads = grads + contract(part, weight_ref[:, start : start + 192], 1, 1)
    lane = wide(lax.broadcasted_iota(jnp.int32, (64, 64), 1))
    table_ref[...] = contract_exact(wide(places[:, 0:64] == lane), grads, 0, 0)


def split_cores(value, kept_ref, gone_ref):
    rows = kept_ref.shape[1]
    core = lax.rem(lax.axis_index("seq"), 2)
    parts = value.reshape(-1, 2, rows, value.shape[1])
    kept_ref[...] = low(jnp.where(core == 0, parts[:, 0], parts[:, 1]))
    gone_ref[...] = low(jnp.where(core == 0, parts[:, 1], parts[:, 0]))


def local_down_back(
    cot_ref, mine_ref, other_ref, n_ref, scale_ref, rows_ref, active_ref, slope_ref, weight_ref, *outs
):
    out_ref, second_ref, kept_ref, gone_ref, hidden_ref, sums_ref, bias_ref, second_low_ref = outs
    step = pl.program_id(0)

    @pl.when(step == 0)
    def _():
        core = place_in()[2]
        row = lax.broadcasted_iota(jnp.int32, (2 * SEG, D), 0)
        grad = wide(cot_ref[...])
        normed = n_ref[...]
        out = normed * rows_ref[6:7, :] + rows_ref[7:8, :]
        for place in range(2):
            heads = jnp.where(core == place, mine_ref[...], other_ref[...])
            grad = jnp.where(row == place * SEG, heads[0:1], grad)
            out = jnp.where(row == place * SEG, heads[1:2], out)
        out_ref[...] = low(out)
        second = norm_back(grad, normed, scale_ref[...], rows_ref[6:7, :])
        second_ref[...] = second
        second_low_ref[...] = low(second)
        sums_ref[0:1, :] = column_sum(wide(low(second)))
        sums_ref[1:2, :] = column_sum(grad * normed)
        sums_ref[2:3, :] = column_sum(grad)

    second_low = second_low_ref[...]
    split_cores(contract(active_ref[...], second_low, 0, 0), kept_ref, gone_ref)
    hidden = low(contract(second_low, weight_ref[...], 1, 1) * wide(slope_ref[...]))
    hidden_ref[...] = hidden
    bias_ref[...] = column_sum(wide(hidden))


def local_up_back(low_ref, hidden_ref, weight_ref, second_ref, kept_ref, gone_ref, first_ref):
    hidden = hidden_ref[...]
    split_cores(contract(low_ref[...], hidden, 0, 0), kept_ref, gone_ref)
    part = contract(hidden, weight_ref[...], 1, 1)
    step = pl.program_id(0)

    @pl.when(step == 0)
    def _():
        first_ref[...] = second_ref[...] + part

    @pl.when(step > 0)
    def _():
        first_ref[...] += part


def local_attend_back(
    first_ref, n_ref, scale_ref, rows_ref, context_ref, mixed_ref, probs_ref, group_ref, *outs
):
    out_ref, total_ref, sums_ref, back_ref, context_low_ref = outs
    grad, normed = first_ref[...], n_ref[...]
    total = norm_back(grad, normed, scale_ref[...], rows_ref[3:4, :])
    total_ref[...] = total
    branch = low(total)
    sums_ref[2:3, :] = column_sum(wide(branch))
    sums_ref[3:4, :] = column_sum(grad * normed)
    sums_ref[4:5, :] = column_sum(grad)
    out_ref[...] = contract(context_ref[...], branch, 0, 0)
    context_low_ref[...] = low(contract(branch, group_ref[...], 1, 1))
    lane = lax.broadcasted_iota(jnp.int32, (SEG, 128), 1)
    for segment in range(2):
        rows = slice(segment * SEG, (segment + 1) * SEG)
        for pair in range(HEADS // 2):
            places = [
                slice(third * D + pair * 128, third * D + (pair + 1) * 128) for third in range(3)
            ]
            query, key, value = (mixed_ref[rows, place] for place in places)
            grad = context_low_ref[rows, places[0]]
            found = []
            for side in range(2):
                here = (lane < HEAD_DIM) if side == 0 else (lane >= HEAD_DIM)
                probs = probs_ref[segment * HEADS + 2 * pair + side]
                prob_grad = contract(jnp.where(here, grad, jnp.zeros_like(grad)), value, 1, 1)
                value_grad = contract(low(probs), grad, 0, 0)
                score = low(
                    probs * (prob_grad - jnp.sum(probs * prob_grad, axis=-1, keepdims=True))
                )
                found.append(
                    (contract(score, key, 1, 0), contract(score, query, 0, 0), value_grad)
                )
            for third in range(3):
                merged = jnp.where(lane < HEAD_DIM, found[0][third], found[1][third])
                if third < 2:
                    merged = merged * HEAD_DIM ** (-0.5)
                back_ref[rows, places[third]] = low(merged)
    for third in (0, 2):
        columns = slice(third * D, (third + 1) * D)
        sums_ref[third // 2 : third // 2 + 1, :] = column_sum(wide(back_ref[:, columns]))


def local_mix_back(
    total_ref, back_ref, tokens_ref, group_ref, out_ref, sums_ref, more_ref, bias_ref, *outs
):
    input_ref, kept_ref, gone_ref, small_ref = outs
    tokens, total = tokens_ref[...], total_ref[...]
    for third in range(3):
        columns = slice(third * D, (third + 1) * D)
        back = back_ref[:, columns]
        grad = contract(tokens, back, 0, 0)
        split_cores(grad, kept_ref.at[:, :, columns], gone_ref.at[:, :, columns])
        total = total + contract(back, group_ref[:, columns], 1, 1)
    input_ref[...] = total
    columns = slice(3 * D, 4 * D)
    split_cores(out_ref[...], kept_ref.at[:, :, columns], gone_ref.at[:, :, columns])
    small_ref[...] = jnp.zeros_like(small_ref)
    small_ref[0:5, :] = sums_ref[0:5, :]
    small_ref[5:8, :] = more_ref[0:3, :]
    small_ref[8:12, :] = bias_ref[...]
    columns = slice(4 * D, 4 * D + 128)
    split_cores(small_ref[...].T, kept_ref.at[:, :, columns], gone_ref.at[:, :, columns])


def plane_three(array_in):
    return [array_in] + [swap_chip(array_in, mask) for mask in (1, 2, 3)]


def plane_shards(
    tokens,
    cotangent,
    token_docs,
    segment_docs,
    segment_positions,
    local_mix,
    local_out,
    local_up,
    local_down,
    local_vectors,
    local_up_bias,
    cross_mix,
    cross_out,
    cross_up,
    cross_down,
    cross_vectors,
    cross_up_bias,
    position_table,
):
    chip = place_in()[1]
    flat_tokens = tokens.reshape(256, D)
    flat_cot = cotangent.reshape(256, D)
    docs_column = token_docs.reshape(256, 1)
    segment_column = segment_docs.T

    shards_in = (
        local_mix,
        local_out,
        local_up,
        local_down.reshape(4, 24, D),
        local_vectors,
        local_up_bias.reshape(1, 96),
        cross_mix,
        cross_out,
        cross_up,
        cross_vectors,
        cross_up_bias.reshape(1, 96),
        position_table.T,
    )
    made = [half(24, 3200), half(24, 5 * D), half(24, 4 * D)] + [half(24, D + 640)] * 4
    far = pl.BlockSpec(memory_space=pltpu.HBM)
    shard_one, shard_two, shard_three, *cross_pieces = on_core(
        prepare,
        made,
        shards_in,
        0,
        in_specs=[far] * 12,
        out_specs=[far] * 7,
        scratch=[pltpu.VMEM(a.shape, a.dtype) for a in list(shards_in) + made]
        + [
            pltpu.VMEM((128, 128), jnp.float32),
            pltpu.VMEM((128, 128), jnp.float32),
            pltpu.VMEM((4, 24, D + 640), jnp.bfloat16),
            pltpu.SemaphoreType.DMA((2, 12)),
        ],
    )
    cross_sent = [cross_pieces[0]] + [swap_chip(cross_pieces[mask], mask) for mask in (1, 2, 3)]
    z_one = reach_dp(shard_one)
    cross_row = join_cross(cross_sent, cross_down)
    *z_one, cross_row, shard_two = stage(*z_one, cross_row, shard_two)
    column_one = join_dp(z_one)
    column_one, shard_two = stage(column_one, shard_two)

    first, second = swap_one(column_one), swap_two(column_one)
    *z_two, first, second, column_one = stage(*reach_dp(shard_two), first, second, column_one)

    third = swap_two(first)
    others = [swap_core(piece) for piece in (column_one, first, second)]
    third, *z_two = stage(third, *others, *z_two)
    others, z_two = z_two[:3], z_two[3:]
    column_two = join_dp(z_two)
    others.append(swap_core(third))
    column_two, shard_three, *others = stage(column_two, shard_three, *others)

    first_group = gather_plane([column_one, first, second, third], others).reshape(D, 3200)
    mixed_rows, context_rows, probs_kept, normed_one, scale_one, low_one, rows = on_core(
        local_attend,
        [
            half(256, 3 * D),
            half(256, D),
            shape_of(24, SEG, SEG),
            shape_of(256, D),
            shape_of(256, 1),
            half(256, D),
            shape_of(128, D),
        ],
        (flat_tokens, first_group, token_docs, docs_column),
        2 * 256 * D * 5 * D,
    )
    first_two, second_two = swap_one(column_two), swap_two(column_two)
    *z_three, low_one, first_two, second_two, column_two = stage(
        *reach_dp(shard_three), low_one, first_two, second_two, column_two
    )

    third_two = swap_two(first_two)
    others = [swap_core(piece) for piece in (column_two, first_two, second_two)]
    column_three = join_dp(z_three)
    third_two, column_three, cross_row, *others = stage(third_two, column_three, cross_row, *others)

    cross_column = lax.all_gather(cross_row, "dp")
    first_three, second_three = swap_one(column_three), swap_two(column_three)
    others.append(swap_core(third_two))
    up_bias = rows[80:84].reshape(4, 32, 24).transpose(1, 0, 2).reshape(1, 4 * D)
    cross_bias = rows[84:88].reshape(4, 4, 4, 2, 24)
    cross_bias = lax.dynamic_index_in_dim(cross_bias, chip, 2, keepdims=False)
    cross_bias = cross_bias.transpose(1, 2, 0, 3).reshape(1, D)
    second_group = gather_plane([column_two, first_two, second_two, third_two], others)
    second_group = second_group.reshape(D, 5 * D)
    whole = pl.BlockSpec((256, D), lambda j: (0, 0))
    thin = pl.BlockSpec((256, 1), lambda j: (0, 0))
    vectors = pl.BlockSpec((128, D), lambda j: (0, 0))
    eight = pl.BlockSpec((8, D), lambda j: (0, 0))
    across = pl.BlockSpec((256, D), lambda j: (0, j))
    tall = pl.BlockSpec((D, D), lambda j: (0, j))
    deep = pl.BlockSpec((D, D), lambda j: (j, 0))
    strip = pl.BlockSpec((1, D), lambda j: (0, j))
    active_rows, slope_rows = on_core(
        local_up_part,
        [half(256, 4 * D)] * 2,
        (low_one, second_group, up_bias),
        2 * 256 * D * 4 * D,
        grid=(4,),
        in_specs=[whole, tall, strip],
        out_specs=[across, across],
    )
    active_rows, first_three, second_three, column_three = stage(
        active_rows, first_three, second_three, column_three
    )

    third_three = swap_two(first_three)
    others = [swap_core(piece) for piece in (column_three, first_three, second_three)]
    third_three, *others = stage(third_three, *others)

    others.append(swap_core(third_three))
    down_weight = gather_down([column_three, first_three, second_three, third_three], others)
    down_weight = down_weight.reshape(4 * D, D)
    cross_up_mix, cross_down_part = place_cross(after(cross_column, down_weight))
    normed_two, scale_two, kept, given = on_core(
        local_down_part,
        [shape_of(256, D), shape_of(256, 1), shape_of(8, D), shape_of(8, D)],
        (active_rows, down_weight, normed_one, rows, flat_cot, flat_cot, segment_positions),
        2 * 256 * D * 4 * D,
        room=40,
        grid=(4,),
        in_specs=[
            across,
            deep,
            whole,
            vectors,
            pl.BlockSpec((16, D), lambda j: (0, 0)),
            pl.BlockSpec((16, D), lambda j: (8, 0)),
            pl.BlockSpec(memory_space=pltpu.SMEM),
        ],
        out_specs=[whole, thin, eight, eight],
        scratch=[pltpu.VMEM((256, D), jnp.float32)],
    )

    def plain(*shapes):
        return [pl.BlockSpec(shape, lambda j, n=len(shape): (0,) * n) for shape in shapes]

    row8, mix_share = (8, D), (D, D + 640)
    out_share = pl.BlockSpec((D, D), lambda j: (0, 4))
    up_share = pl.BlockSpec((D, D), lambda j: (0, 0))
    pair = on_core(join_pair, shape_of(8, D), (kept, swap_core(given)), 0, room=12)
    row_in, row_grad, mixed, probs, context = on_core(
        cross_attend,
        [shape_of(8, D), shape_of(8, D), half(8, 576), shape_of(3, 8, 8), half(8, 192)],
        (*plane_three(pair), cross_up_mix, rows, segment_docs, segment_column),
        0,
        room=12,
    )
    row_n, row_scale, row_low, hidden, active, part = on_core(
        cross_up_down,
        [shape_of(8, D), shape_of(8, 1), half(8, D), shape_of(8, D), half(8, D), shape_of(8, D)],
        (
            *plane_three(context),
            row_in,
            second_group,
            rows,
            cross_up_mix,
            cross_bias,
            cross_down_part,
        ),
        0,
        grid=(1,),
        in_specs=plain(*[(8, 192)] * 4, row8)
        + [out_share]
        + plain((128, D))
        + [up_share]
        + plain((1, D), (D, D)),
        out_specs=plain(row8, (8, 1), row8, row8, row8, row8),
        room=12,
    )
    row_out, row_second, hidden_low, part, sums = on_core(
        cross_turn,
        [shape_of(8, D), shape_of(8, D), half(8, D), shape_of(8, D), shape_of(8, D)],
        (*plane_three(part), row_n, rows, row_grad, hidden, cross_up_mix, cross_down_part),
        0,
        grid=(1,),
        in_specs=plain(*[row8] * 4, row8, (128, D), row8, row8) + [up_share] + plain((D, D)),
        out_specs=plain(*[row8] * 5),
        room=12,
    )
    row_total, part, packed = on_core(
        cross_attend_back,
        [shape_of(8, D), shape_of(8, D), half(48, D)],
        (
            *plane_three(part),
            row_second,
            row_n,
            row_scale,
            rows,
            second_group,
            mixed,
            probs,
            cross_up_mix,
            hidden_low,
            active,
            context,
            row_in,
            row_low,
            sums,
            segment_positions,
        ),
        0,
        grid=(1,),
        in_specs=plain(*[row8] * 4, row8, row8, (8, 1), (128, D))
        + [out_share]
        + plain((8, 576), (3, 8, 8), mix_share, row8, row8, (8, 192), row8, row8, row8)
        + [pl.BlockSpec(memory_space=pltpu.SMEM)],
        out_specs=plain(row8, row8, (48, D)),
        scratch=[pltpu.VMEM((48, D), jnp.float32), pltpu.VMEM((8, D), jnp.float32)],
        room=12,
    )
    everyone = lax.all_gather(packed, ("dp", "seq"))
    kept, given = on_core(
        cross_finish,
        [shape_of(8, D), shape_of(8, D)],
        (*plane_three(part), row_total, row_out),
        0,
        scratch=[pltpu.VMEM((8, D), jnp.float32)],
        room=12,
    )
    got = swap_core(given)

    fours = pl.BlockSpec((4, 96, D), lambda j: (j, 0, 0))
    layer_output, second_rows, down_kept, down_gone, hidden_grads, sums_two, bias_grad = on_core(
        local_down_back,
        [
            half(256, D),
            shape_of(256, D),
            half(16, 96, D),
            half(16, 96, D),
            half(256, 4 * D),
            shape_of(8, D),
            shape_of(1, 4 * D),
        ],
        (flat_cot, kept, got, normed_two, scale_two, rows, active_rows, slope_rows, down_weight),
        4 * 256 * D * 4 * D,
        grid=(4,),
        in_specs=[whole, eight, eight, whole, thin, vectors, across, across, deep],
        out_specs=[whole, whole, fours, fours, across, eight, strip],
        scratch=[pltpu.VMEM((256, D), jnp.bfloat16)],
    )
    down_total = Sum(down_kept.reshape(4, 4, 96, D))
    hidden_grads, down_gone = stage(hidden_grads, down_gone.reshape(4, 4, 96, D))

    down_got = swap_core(down_gone)
    sixteens = pl.BlockSpec((16, 24, D), lambda j: (0, 0, j))
    up_kept, up_gone, first_rows = on_core(
        local_up_back,
        [half(16, 24, 4 * D), half(16, 24, 4 * D), shape_of(256, D)],
        (low_one, hidden_grads, second_group, second_rows),
        4 * 256 * D * 4 * D,
        grid=(4,),
        in_specs=[whole, across, tall, whole],
        out_specs=[sixteens, sixteens, whole],
    )
    up_total = Sum(up_kept.reshape(4, 4, 24, 4 * D))
    down_got, first_rows, up_gone = stage(down_got, first_rows, up_gone.reshape(4, 4, 24, 4 * D))

    up_got = swap_core(up_gone)
    down_sent = down_total.first(down_got)
    up_got, down_sent, first_rows = stage(up_got, down_sent, first_rows)

    down_back = swap_one(down_sent)
    flat = pl.BlockSpec((256, 3 * D), lambda j: (0, 0))
    out_grad, sum_rows, sums_one, back_rows = on_core(
        local_attend_back,
        [shape_of(D, D), shape_of(256, D), shape_of(8, D), half(256, 3 * D)],
        (
            first_rows,
            normed_one,
            scale_one,
            rows,
            context_rows,
            mixed_rows,
            probs_kept,
            first_group,
        ),
        4 * 256 * D * 2 * D,
        grid=(1,),
        in_specs=[
            whole,
            whole,
            thin,
            vectors,
            whole,
            flat,
            pl.BlockSpec((24, SEG, SEG), lambda j: (0, 0, 0)),
            pl.BlockSpec((D, D), lambda j: (0, 3)),
        ],
        out_specs=[pl.BlockSpec((D, D), lambda j: (0, 0)), whole, eight, flat],
        scratch=[pltpu.VMEM((256, D), jnp.bfloat16)],
    )
    up_sent = up_total.first(up_got)
    down_back, back_rows, up_sent = stage(down_back, back_rows, up_sent)

    up_back = swap_one(up_sent)
    down_onward = down_total.second(down_back)
    bias_rows = bias_grad.reshape(32, 4, 24).transpose(1, 0, 2).reshape(4, D)
    sides = [half(16, 24, 4 * D + 128)] * 2
    input_grad, mix_kept, mix_gone = on_core(
        local_mix_back,
        [shape_of(256, D)] + sides,
        (
            sum_rows,
            back_rows,
            flat_tokens,
            first_group,
            out_grad,
            sums_one,
            sums_two,
            bias_rows,
        ),
        4 * 256 * D * 3 * D,
        scratch=[pltpu.VMEM((128, D), jnp.float32)],
    )
    mix_total = Sum(mix_kept.reshape(4, 4, 24, 3200))
    up_back, down_onward, mix_gone = stage(up_back, down_onward, mix_gone.reshape(4, 4, 24, 3200))

    mix_got, down_last = swap_core(mix_gone), swap_two(down_onward)
    up_onward = up_total.second(up_back)
    mix_got, down_last, up_onward = stage(mix_got, down_last, up_onward)

    up_last = swap_two(up_onward)
    mix_sent = mix_total.first(mix_got)
    down_others = down_total.third(down_last)
    up_last, mix_sent, *down_others = stage(up_last, mix_sent, *down_others)

    mix_back, down_others = swap_one(mix_sent), send_dp(down_others)
    up_others = up_total.third(up_last)
    mix_back, *others = stage(mix_back, *down_others, *up_others)
    down_others, up_others = others[:3], others[3:]

    up_others = send_dp(up_others)
    mix_last = swap_two(mix_total.second(mix_back))
    down_sum = down_total.total(down_others)
    mix_last, down_sum, *up_others = stage(mix_last, down_sum, *up_others)

    mix_others = send_dp(mix_total.third(mix_last))
    up_sum = up_total.total(up_others)
    cross_grads = on_core(
        cross_owner,
        [
            shape_of(24, 3 * D),
            shape_of(24, D),
            shape_of(24, 4 * D),
            shape_of(96, D),
            shape_of(8, 24),
            shape_of(1, 96),
            shape_of(64, 24),
        ],
        (after(everyone, mix_last), cross_mix),
        0,
        scratch=[
            pltpu.VMEM((4, 64, D), jnp.float32),
            pltpu.VMEM((4, 64, D), jnp.float32),
            pltpu.VMEM((5, 64, D), jnp.float32),
            pltpu.VMEM((64, D), jnp.float32),
            pltpu.VMEM((8, D), jnp.float32),
            pltpu.VMEM((64, 128), jnp.float32),
        ],
    )
    mix_sum = mix_total.total(mix_others)
    return (
        layer_output.reshape(2, SEG, D),
        input_grad.reshape(2, SEG, D),
        mix_sum[:, :2304],
        mix_sum[:, 2304:3072],
        up_sum,
        down_sum,
        mix_sum[:, 3072:3080].T,
        mix_sum[:, 3080:3084].T.reshape(96),
        *cross_grads[:5],
        cross_grads[5].reshape(96),
        cross_grads[6],
    )


def solution(mesh):
    flat = dict(mesh.shape) == {"dp": 4, "seq": 8}
    return jax.shard_map(
        plane_shards if flat else shards,
        mesh=mesh,
        in_specs=(
            P("dp", "seq", None),
            P("dp", "seq", None),
            P("dp", "seq"),
            P("dp", None),
            P("dp", "seq"),
            P(("dp", "seq"), None),
            P(("dp", "seq"), None),
            P(("dp", "seq"), None),
            P(("dp", "seq"), None),
            P(None, ("dp", "seq")),
            P(("dp", "seq")),
            P(("dp", "seq"), None),
            P(("dp", "seq"), None),
            P(("dp", "seq"), None),
            P(("dp", "seq"), None),
            P(None, ("dp", "seq")),
            P(("dp", "seq")),
            P(None, ("dp", "seq")),
        ),
        out_specs=(
            P("dp", "seq", None),
            P("dp", "seq", None),
            P(("dp", "seq"), None),
            P(("dp", "seq"), None),
            P(("dp", "seq"), None),
            P(("dp", "seq"), None),
            P(None, ("dp", "seq")),
            P(("dp", "seq")),
            P(("dp", "seq"), None),
            P(("dp", "seq"), None),
            P(("dp", "seq"), None),
            P(("dp", "seq"), None),
            P(None, ("dp", "seq")),
            P(("dp", "seq")),
            P(None, ("dp", "seq")),
        ),
        check_vma=False,
    )
```

```python
from functools import partial
import math

import jax
import jax.numpy as jnp
from jax import lax
from jax.experimental import pallas as pl
from jax.experimental.pallas import tpu as pltpu
from jax.sharding import PartitionSpec as P

D = 768
HEADS = 12
HEAD_DIM = 64
SEG = 128
MICRO = 2


epsilon = 1e-05
masked_score = -1000000000.0
owner_dims = (0, 0, 0, 0, 1, 0, 0, 0, 0, 0, 1, 0, 1)


def layer_norm(values, gain_row, shift_row):
    centered = values - jnp.mean(values, axis=-1, keepdims=True)
    variance = jnp.mean(centered * centered, axis=-1, keepdims=True)
    return centered * lax.rsqrt(variance + epsilon) * gain_row + shift_row


def gelu_exact(hidden):
    return jax.nn.gelu(hidden, approximate=False)


def contract(left_side, right_side, left_dim, right_dim):
    return lax.dot_general(
        left_side,
        right_side,
        (((left_dim,), (right_dim,)), ((), ())),
        preferred_element_type=jnp.float32,
    )


def contract_exact(left_side, right_side, left_dim, right_dim):
    return lax.dot_general(
        left_side,
        right_side,
        (((left_dim,), (right_dim,)), ((), ())),
        precision=lax.Precision.HIGHEST,
        preferred_element_type=jnp.float32,
    )


def owner_pack(grads, devices):
    pieces = []
    for grad_value, split_dim in zip(grads, owner_dims):
        if split_dim == 0:
            pieces.append(grad_value.reshape(devices, -1))
        else:
            row_count = grad_value.shape[0]
            pieces.append(
                grad_value.reshape(row_count, devices, -1).transpose(1, 0, 2).reshape(devices, -1)
            )
    return jnp.concatenate(pieces, axis=1)


def owner_unpack(packed, shard_shapes):
    results = []
    offset = 0
    for shard_shape in shard_shapes:
        length = math.prod(shard_shape)
        results.append(packed[0, offset : offset + length].reshape(shard_shape))
        offset = offset + length
    return tuple(results)


def fetch_weights(
    local_mix,
    local_out,
    local_up,
    local_down,
    local_vectors,
    local_up_bias,
    cross_mix,
    cross_out,
    cross_up,
    cross_down,
    cross_vectors,
    cross_up_bias,
    position_table,
):
    return (
        lax.all_gather(local_mix, ("dp", "seq"), axis=0, tiled=True),
        lax.all_gather(local_out, ("dp", "seq"), axis=0, tiled=True),
        lax.all_gather(local_up, ("dp", "seq"), axis=0, tiled=True),
        lax.all_gather(local_down, ("dp", "seq"), axis=0, tiled=True),
        lax.all_gather(local_vectors, ("dp", "seq"), axis=1, tiled=True),
        lax.all_gather(local_up_bias, ("dp", "seq"), axis=0, tiled=True),
        lax.all_gather(cross_mix, ("dp", "seq"), axis=0, tiled=True),
        lax.all_gather(cross_out, ("dp", "seq"), axis=0, tiled=True),
        lax.all_gather(cross_up, ("dp", "seq"), axis=0, tiled=True),
        lax.all_gather(cross_down, ("dp", "seq"), axis=0, tiled=True),
        lax.all_gather(cross_vectors, ("dp", "seq"), axis=1, tiled=True),
        lax.all_gather(cross_up_bias, ("dp", "seq"), axis=0, tiled=True),
        lax.all_gather(position_table, ("dp", "seq"), axis=1, tiled=True),
    )


def segment_parts(mixed_rows, token_docs):
    segment_count = token_docs.shape[0]
    split_heads = mixed_rows.reshape(segment_count, SEG, 3, HEADS, HEAD_DIM)
    allowed = token_docs[:, None, :, None] == token_docs[:, None, None, :]
    scores = jnp.einsum(
        "nqhd,nkhd->nhqk",
        split_heads[:, :, 0],
        split_heads[:, :, 1],
        preferred_element_type=jnp.float32,
    ) * HEAD_DIM ** (-0.5)
    scores = jnp.where(allowed, scores, masked_score)
    return (split_heads, scores)


def segment_forward(mixed_rows, token_docs):
    split_heads, scores = segment_parts(mixed_rows, token_docs)
    log_total = jax.nn.logsumexp(scores, axis=-1)
    weights = jax.nn.softmax(scores, axis=-1).astype(jnp.bfloat16)
    context = jnp.einsum(
        "nhqk,nkhd->nqhd", weights, split_heads[:, :, 2], preferred_element_type=jnp.float32
    )
    return (context.reshape(-1, D).astype(jnp.bfloat16), log_total)


def segment_backward(context_grad, log_total, mixed_rows, token_docs):
    split_heads, scores = segment_parts(mixed_rows, token_docs)
    segment_count = token_docs.shape[0]
    probs = jnp.exp(scores - log_total[..., None])
    grad_heads = context_grad.reshape(segment_count, SEG, HEADS, HEAD_DIM)
    prob_grad = jnp.einsum(
        "nqhd,nkhd->nhqk", grad_heads, split_heads[:, :, 2], preferred_element_type=jnp.float32
    )
    value_grad = jnp.einsum(
        "nhqk,nqhd->nkhd",
        probs.astype(jnp.bfloat16),
        grad_heads,
        preferred_element_type=jnp.float32,
    )
    score_grad = probs * (prob_grad - jnp.sum(probs * prob_grad, axis=-1, keepdims=True))
    score_low = score_grad.astype(jnp.bfloat16) * HEAD_DIM ** (-0.5)
    query_grad = jnp.einsum(
        "nhqk,nkhd->nqhd", score_low, split_heads[:, :, 1], preferred_element_type=jnp.float32
    )
    key_grad = jnp.einsum(
        "nhqk,nqhd->nkhd", score_low, split_heads[:, :, 0], preferred_element_type=jnp.float32
    )
    row_total = segment_count * SEG
    return jnp.concatenate(
        [
            query_grad.reshape(row_total, D),
            key_grad.reshape(row_total, D),
            value_grad.reshape(row_total, D),
        ],
        axis=1,
    )


def cross_parts(mixed_rows, gathered, segment_docs):
    group_size = segment_docs.shape[0]
    per_device = mixed_rows.shape[0] // group_size
    query_rows = mixed_rows[:, :D].reshape(group_size, per_device, HEADS, HEAD_DIM)
    key_rows = gathered[:, :, :D].reshape(group_size, -1, HEADS, HEAD_DIM)
    value_rows = gathered[:, :, D:].reshape(group_size, -1, HEADS, HEAD_DIM)
    own_docs = lax.dynamic_slice_in_dim(
        segment_docs, lax.axis_index("seq") * per_device, per_device, 1
    )
    allowed = own_docs[:, None, :, None] == segment_docs[:, None, None, :]
    scores = jnp.einsum(
        "bqhd,bkhd->bhqk", query_rows, key_rows, preferred_element_type=jnp.float32
    ) * HEAD_DIM ** (-0.5)
    scores = jnp.where(allowed, scores, masked_score)
    return (query_rows, key_rows, value_rows, scores)


def cross_forward(mixed_rows, segment_docs):
    group_size = segment_docs.shape[0]
    per_device = mixed_rows.shape[0] // group_size
    pair_rows = mixed_rows[:, D:].reshape(group_size, per_device, 2 * D)
    gathered = lax.all_gather(pair_rows, "seq", axis=1, tiled=True)
    query_rows, key_rows, value_rows, scores = cross_parts(mixed_rows, gathered, segment_docs)
    log_total = jax.nn.logsumexp(scores, axis=-1)
    weights = jax.nn.softmax(scores, axis=-1).astype(jnp.bfloat16)
    context = jnp.einsum("bhqk,bkhd->bqhd", weights, value_rows, preferred_element_type=jnp.float32)
    return (context.reshape(-1, D).astype(jnp.bfloat16), (gathered, log_total))


def cross_backward(context_grad, cross_kept, mixed_rows, segment_docs):
    gathered, log_total = cross_kept
    group_size = segment_docs.shape[0]
    row_total = mixed_rows.shape[0]
    per_device = row_total // group_size
    query_rows, key_rows, value_rows, scores = cross_parts(mixed_rows, gathered, segment_docs)
    probs = jnp.exp(scores - log_total[..., None])
    grad_heads = context_grad.reshape(group_size, per_device, HEADS, HEAD_DIM)
    prob_grad = jnp.einsum(
        "bqhd,bkhd->bhqk", grad_heads, value_rows, preferred_element_type=jnp.float32
    )
    value_grad = jnp.einsum(
        "bhqk,bqhd->bkhd",
        probs.astype(jnp.bfloat16),
        grad_heads,
        preferred_element_type=jnp.float32,
    )
    score_grad = probs * (prob_grad - jnp.sum(probs * prob_grad, axis=-1, keepdims=True))
    score_low = score_grad.astype(jnp.bfloat16) * HEAD_DIM ** (-0.5)
    query_grad = jnp.einsum(
        "bhqk,bkhd->bqhd", score_low, key_rows, preferred_element_type=jnp.float32
    )
    key_grad = jnp.einsum(
        "bhqk,bqhd->bkhd", score_low, query_rows, preferred_element_type=jnp.float32
    )
    pair_grads = jnp.concatenate(
        [key_grad.reshape(group_size, -1, D), value_grad.reshape(group_size, -1, D)], axis=2
    )
    own_pairs = lax.psum_scatter(
        pair_grads.astype(jnp.bfloat16), "seq", scatter_dimension=1, tiled=True
    ).astype(jnp.float32)
    return jnp.concatenate(
        [query_grad.reshape(row_total, D), own_pairs.reshape(row_total, 2 * D)], axis=1
    )


def block_forward(inputs, weights, attend):
    mix_weight, out_weight, up_weight, down_weight, vectors, up_bias = weights
    vector_rows = vectors.astype(jnp.float32)
    in_bias = jnp.concatenate([vector_rows[0], jnp.zeros_like(vector_rows[0]), vector_rows[1]])
    rounded = inputs.astype(jnp.bfloat16)
    mixed_rows = (
        jnp.dot(rounded, mix_weight, preferred_element_type=jnp.float32) + in_bias
    ).astype(jnp.bfloat16)
    context, attend_kept = attend(mixed_rows)
    first_sum = (
        inputs + jnp.dot(context, out_weight, preferred_element_type=jnp.float32) + vector_rows[2]
    )
    first_norm = layer_norm(first_sum, vector_rows[3], vector_rows[4])
    first_low = first_norm.astype(jnp.bfloat16)
    hidden = jnp.dot(first_low, up_weight, preferred_element_type=jnp.float32) + up_bias.astype(
        jnp.float32
    )
    active = gelu_exact(hidden).astype(jnp.bfloat16)
    second_sum = (
        first_norm
        + jnp.dot(active, down_weight, preferred_element_type=jnp.float32)
        + vector_rows[5]
    )
    output = layer_norm(second_sum, vector_rows[6], vector_rows[7])
    return (
        output,
        (
            rounded,
            mixed_rows,
            attend_kept,
            context,
            first_sum,
            first_low,
            hidden,
            active,
            second_sum,
        ),
    )


def block_backward(output_grad, block_kept, weights, attend_back):
    mix_weight, out_weight, up_weight, down_weight, vectors, up_bias = weights
    vector_rows = vectors.astype(jnp.float32)
    rounded, mixed_rows, attend_kept, context, first_sum, first_low, hidden, active, second_sum = (
        block_kept
    )
    unused, second_pull = jax.vjp(layer_norm, second_sum, vector_rows[6], vector_rows[7])
    second_grad, gain_two, shift_two = second_pull(output_grad)
    second_low = second_grad.astype(jnp.bfloat16)
    down_grad = contract(active, second_low, 0, 0)
    down_bias = jnp.sum(second_low.astype(jnp.float32), axis=0)
    active_grad = contract(second_low, down_weight, 1, 1)
    unused, gelu_pull = jax.vjp(gelu_exact, hidden)
    hidden_grad = gelu_pull(active_grad)[0]
    hidden_low = hidden_grad.astype(jnp.bfloat16)
    up_grad = contract(first_low, hidden_low, 0, 0)
    up_bias_grad = jnp.sum(hidden_low.astype(jnp.float32), axis=0)
    first_grad = second_grad + contract(hidden_low, up_weight, 1, 1)
    unused, first_pull = jax.vjp(layer_norm, first_sum, vector_rows[3], vector_rows[4])
    sum_grad, gain_one, shift_one = first_pull(first_grad)
    branch_low = sum_grad.astype(jnp.bfloat16)
    out_grad = contract(context, branch_low, 0, 0)
    out_bias = jnp.sum(branch_low.astype(jnp.float32), axis=0)
    context_low = contract(branch_low, out_weight, 1, 1).astype(jnp.bfloat16)
    mixed_low = attend_back(context_low, attend_kept, mixed_rows).astype(jnp.bfloat16)
    mix_grad = contract(rounded, mixed_low, 0, 0)
    mixed_sums = jnp.sum(mixed_low.astype(jnp.float32), axis=0)
    input_grad = sum_grad + contract(mixed_low, mix_weight, 1, 1)
    vectors_grad = jnp.stack(
        [
            mixed_sums[:D],
            mixed_sums[2 * D :],
            out_bias,
            gain_one,
            shift_one,
            down_bias,
            gain_two,
            shift_two,
        ]
    )
    return (input_grad, (mix_grad, out_grad, up_grad, down_grad, vectors_grad, up_bias_grad))


def shards(
    tokens,
    cotangent,
    token_docs,
    segment_docs,
    segment_positions,
    local_mix,
    local_out,
    local_up,
    local_down,
    local_vectors,
    local_up_bias,
    cross_mix,
    cross_out,
    cross_up,
    cross_down,
    cross_vectors,
    cross_up_bias,
    position_table,
):
    sequence_count, span, width = tokens.shape
    group_size = sequence_count // MICRO
    segment_count = span // SEG
    devices = lax.axis_size(("dp", "seq"))
    shard_shapes = tuple(
        (
            array_in.shape
            for array_in in (
                local_mix,
                local_out,
                local_up,
                local_down,
                local_vectors,
                local_up_bias,
                cross_mix,
                cross_out,
                cross_up,
                cross_down,
                cross_vectors,
                cross_up_bias,
                position_table,
            )
        )
    )
    layer_outputs = []
    input_grads = []
    totals = ()
    for micro_step in range(MICRO):
        lower_row = micro_step * group_size
        upper_row = lower_row + group_size
        gathered = fetch_weights(
            local_mix,
            local_out,
            local_up,
            local_down,
            local_vectors,
            local_up_bias,
            cross_mix,
            cross_out,
            cross_up,
            cross_down,
            cross_vectors,
            cross_up_bias,
            position_table,
        )
        local_weights = gathered[0:6]
        cross_weights = gathered[6:12]
        position_rows = gathered[12]
        inputs = tokens[lower_row:upper_row].reshape(group_size * span, width).astype(jnp.float32)
        docs_here = token_docs[lower_row:upper_row]
        segments_here = segment_docs[lower_row:upper_row]
        first_out, first_kept = block_forward(
            inputs, local_weights, partial(segment_forward, token_docs=docs_here)
        )
        segment_grid = first_out.reshape(group_size * segment_count, SEG, width)
        places = segment_positions[lower_row:upper_row].reshape(group_size * segment_count)
        position_picks = (
            places[:, None] == jnp.arange(position_rows.shape[0], dtype=jnp.int32)[None, :]
        ).astype(jnp.bfloat16)
        heads_in = segment_grid[:, 0, :] + jnp.dot(
            position_picks, position_rows, preferred_element_type=jnp.float32
        )
        heads_out, cross_kept = block_forward(
            heads_in, cross_weights, partial(cross_forward, segment_docs=segments_here)
        )
        joined = jnp.concatenate([heads_out[:, None, :], segment_grid[:, 1:, :]], axis=1)
        layer_outputs.append(joined.astype(jnp.bfloat16))
        gathered = fetch_weights(
            local_mix,
            local_out,
            local_up,
            local_down,
            local_vectors,
            local_up_bias,
            cross_mix,
            cross_out,
            cross_up,
            cross_down,
            cross_vectors,
            cross_up_bias,
            position_table,
        )
        local_weights = gathered[0:6]
        cross_weights = gathered[6:12]
        output_grad = cotangent[lower_row:upper_row].astype(jnp.float32)
        heads_grad, cross_grads = block_backward(
            output_grad[:, 0, :],
            cross_kept,
            cross_weights,
            partial(cross_backward, segment_docs=segments_here),
        )
        table_grad = contract_exact(position_picks.astype(jnp.float32), heads_grad, 0, 0)
        first_grad = jnp.concatenate(
            [heads_grad[:, None, :], output_grad[:, 1:, :]], axis=1
        ).reshape(group_size * span, width)
        input_grad, local_grads = block_backward(
            first_grad, first_kept, local_weights, partial(segment_backward, token_docs=docs_here)
        )
        input_grads.append(input_grad.reshape(group_size, span, width))
        step_grads = local_grads + cross_grads + (table_grad,)
        if micro_step == 0:
            totals = tuple(step_grads)
        else:
            totals = tuple(
                (total_sum + step_sum for total_sum, step_sum in zip(totals, step_grads))
            )
    packed_total = lax.psum_scatter(
        owner_pack(totals, devices), ("dp", "seq"), scatter_dimension=0, tiled=True
    )
    summed = owner_unpack(packed_total, shard_shapes)
    layer_output = jnp.concatenate(layer_outputs, axis=0)
    input_gradient = jnp.concatenate(input_grads, axis=0)
    return (layer_output, input_gradient) + tuple(summed)


def swap_dp(array_in, shift):
    return lax.ppermute(array_in, "dp", [(i, (i + shift) % 4) for i in range(4)])


def swap_core(array_in):
    return lax.ppermute(array_in, "seq", [(i, i ^ 1) for i in range(8)])


def swap_chip(array_in, mask):
    return lax.ppermute(array_in, "seq", [(i, i ^ (2 * mask)) for i in range(8)])


def swap_one(array_in):
    return lax.ppermute(array_in, "seq", [(i, i ^ (2 if i % 2 == 0 else 4)) for i in range(8)])


def swap_two(array_in):
    return lax.ppermute(array_in, "seq", [(i, i ^ (4 if i % 2 == 0 else 2)) for i in range(8)])


def place_in():
    layer = lax.axis_index("dp")
    spot = lax.axis_index("seq")
    return layer, spot // 2, lax.rem(spot, 2)


def after(array_in, *before):
    return lax.optimization_barrier((array_in,) + before)[0]


def stage(*values):
    return lax.optimization_barrier(values)


def wide(array_in):
    return array_in.astype(jnp.float32)


def low(array_in):
    return array_in.astype(jnp.bfloat16)


def copies(pieces, shapes, moves, room=64):
    count, made = len(pieces), len(shapes)
    total = len(moves(0, 0, 0))

    def kernel(*refs):
        outs, held, sems = refs[count : count + made], refs[count + made : -1], refs[-1]
        inward = [pltpu.make_async_copy(refs[i], held[i], sems.at[0, i]) for i in range(count)]
        for copy in inward:
            copy.start()
        outward = []
        for i, (piece, part, out, place) in enumerate(moves(*place_in())):
            if inward[piece] is not None:
                inward[piece].wait()
                inward[piece] = None
            copy = pltpu.make_async_copy(held[piece].at[part], outs[out].at[place], sems.at[1, i])
            copy.start()
            outward.append(copy)
        for copy in outward:
            copy.wait()

    size = 2 * sum(math.prod(shape) for shape in shapes) * 2
    return pl.pallas_call(
        kernel,
        out_shape=[jax.ShapeDtypeStruct(shape, pieces[0].dtype) for shape in shapes],
        in_specs=[pl.BlockSpec(memory_space=pltpu.HBM)] * count,
        out_specs=[pl.BlockSpec(memory_space=pltpu.HBM)] * made,
        scratch_shapes=[pltpu.VMEM(piece.shape, piece.dtype) for piece in pieces]
        + [pltpu.SemaphoreType.DMA((2, max(count, total)))],
        compiler_params=pltpu.CompilerParams(vmem_limit_bytes=room * 2**20),
        cost_estimate=pl.CostEstimate(flops=0, bytes_accessed=0, transcendentals=0),
    )(*pieces)


every = slice(None)


def reach_dp(shard):
    return [shard] + [swap_dp(shard, shift) for shift in (1, 2, 3)]


def join_dp(pieces):
    return copies(
        pieces,
        [(4,) + pieces[0].shape],
        lambda layer, chip, core: [(i, every, 0, lax.rem(layer + 4 - i, 4)) for i in range(4)],
    )[0]


def plane_order(chip, core):
    near, far = chip ^ (1 + core), chip ^ (2 - core)
    return (chip, near, far, chip ^ 3), (chip, far, near, chip ^ 3)


def join_chips(pieces):
    def moves(layer, chip, core):
        return [(i, every, 0, spot) for i, spot in enumerate(plane_order(chip, core)[0])]

    return copies(pieces, [(4,) + pieces[0].shape], moves)[0]


def gather_plane(mine, others):
    def moves(layer, chip, core):
        own, other = plane_order(chip, core)
        found = [(i, every, 0, (every, own[i], core)) for i in range(4)]
        return found + [(4 + i, every, 0, (every, other[i], 1 - core)) for i in range(4)]

    shape = (4, 4, 2) + mine[0].shape[1:]
    return copies(mine + others, [shape], moves)[0]


def gather_up(mine, others):
    def moves(layer, chip, core):
        own, other = plane_order(chip, core)
        found = []
        for i in range(8):
            spot, side = (own[i], core) if i < 4 else (other[i - 4], 1 - core)
            for out, lanes in enumerate((slice(0, 4 * D), slice(4 * D, 5 * D))):
                found.append((i, (every, every, lanes), out, (every, spot, side)))
        return found

    up, out = copies(mine + others, [(4, 4, 2, 24, 4 * D), (4, 4, 2, 24, D)], moves)
    return up.reshape(D, 4 * D), out.reshape(D, D)


def gather_down(mine, others):
    def moves(layer, chip, core):
        own, other = plane_order(chip, core)
        found = []
        for i in range(8):
            spot, side = (own[i], core) if i < 4 else (other[i - 4], 1 - core)
            for quarter in range(4):
                part = (every, every, slice(quarter * D, (quarter + 1) * D))
                found.append((i, part, 0, (every, spot, side, quarter)))
        return found

    return copies(mine + others, [(4, 4, 2, 4, 24, D)], moves)[0]


class Sum:
    def __init__(self, kept):
        self.kept = kept
        self.shape = kept.shape[2:]

    def run(self, operands, out_shapes, plan):
        shape, count, made = self.shape, len(operands), len(out_shapes)
        dry = plan(0, 0, 0)
        pieces = sum(len(sources) for sources, target in dry)

        def kernel(*refs):
            given, outs = refs[:count], refs[count : count + made]
            held, built, sems = refs[count + made : -len(dry) - 1], refs[-len(dry) - 1 : -1], refs[-1]
            inward, outward, steps = [], [], []
            for sources, target in plan(*place_in()):
                step = []
                for operand, index in sources:
                    spot = len(inward)
                    source = given[operand].at[index]
                    copy = pltpu.make_async_copy(source, held[spot], sems.at[0, spot])
                    copy.start()
                    inward.append(copy)
                    step.append(spot)
                steps.append((step, target))
            for place, (step, (out, index)) in enumerate(steps):
                total = None
                for spot in step:
                    inward[spot].wait()
                    value = wide(held[spot][...])
                    total = value if total is None else total + value
                built[place][...] = total.astype(built[place].dtype)
                target = outs[out] if index is None else outs[out].at[index]
                copy = pltpu.make_async_copy(built[place], target, sems.at[1, place])
                copy.start()
                outward.append(copy)
            for copy in outward:
                copy.wait()

        far = pl.BlockSpec(memory_space=pltpu.HBM)
        return pl.pallas_call(
            kernel,
            out_shape=out_shapes,
            in_specs=[far] * count,
            out_specs=[far] * made,
            scratch_shapes=[pltpu.VMEM(shape, jnp.bfloat16)] * pieces
            + [pltpu.VMEM(shape, out_shapes[target[0]].dtype) for sources, target in dry]
            + [pltpu.SemaphoreType.DMA((2, pieces))],
            compiler_params=pltpu.CompilerParams(vmem_limit_bytes=64 * 2**20),
            cost_estimate=pl.CostEstimate(flops=0, bytes_accessed=0, transcendentals=0),
        )(*operands)

    def first(self, got):
        self.got = got

        def plan(layer, chip, core):
            return [
                ([(0, (z, spot)), (1, (z, spot))], (0, (i, z)))
                for i, spot in enumerate((chip ^ (1 + core), chip ^ 3))
                for z in range(4)
            ]

        return self.run([self.kept, got], [half(2, 4, *self.shape)], plan)[0]

    def second(self, back):
        self.back = back

        def plan(layer, chip, core):
            spot = chip ^ (2 - core)
            return [
                ([(0, (z, spot)), (1, (z, spot)), (2, (1, z))], (0, z)) for z in range(4)
            ]

        return self.run([self.kept, self.got, back], [half(4, *self.shape)], plan)[0]

    def third(self, last):
        def plan(layer, chip, core):
            found = []
            for shift in (1, 2, 3, 0):
                z = lax.rem(layer + shift, 4)
                sources = [(0, (z, chip)), (1, (z, chip)), (2, (0, z)), (3, z)]
                found.append((sources, (shift, None)))
            return found

        self.own, *others = self.run(
            [self.kept, self.got, self.back, last],
            [shape_of(*self.shape)] + [half(*self.shape)] * 3,
            plan,
        )
        return others

    def total(self, others):
        return self.own + wide(others[0]) + wide(others[1]) + wide(others[2])


def send_dp(others):
    return [swap_dp(other, shift) for shift, other in zip((1, 2, 3), others)]


def norm_parts(values):
    centered = values - jnp.mean(values, axis=-1, keepdims=True)
    variance = jnp.mean(centered * centered, axis=-1, keepdims=True)
    scale = lax.rsqrt(variance + epsilon)
    return centered * scale, scale


def norm_back(grad, normed, scale, gain):
    scaled = grad * gain
    return scale * (
        scaled
        - jnp.mean(scaled, axis=-1, keepdims=True)
        - normed * jnp.mean(scaled * normed, axis=-1, keepdims=True)
    )


def gelu_slope(hidden):
    return 0.5 * (1.0 + lax.erf(hidden * math.sqrt(0.5))) + hidden * jnp.exp(
        -0.5 * hidden * hidden
    ) * (1.0 / math.sqrt(2.0 * math.pi))


def shape_of(*shape, dtype=jnp.float32):
    return jax.ShapeDtypeStruct(shape, dtype)


def half(*shape):
    return jax.ShapeDtypeStruct(shape, jnp.bfloat16)


def on_core(kernel, out_shape, operands, flops, room=64, grid=(), in_specs=None, out_specs=None, scratch=()):
    arrays = jax.tree.leaves(out_shape) + list(operands)
    size = sum(math.prod(a.shape) * a.dtype.itemsize for a in arrays)
    extra = {} if in_specs is None else {"in_specs": in_specs, "out_specs": out_specs}
    return pl.pallas_call(
        kernel,
        out_shape=out_shape,
        grid=grid,
        scratch_shapes=scratch,
        compiler_params=pltpu.CompilerParams(vmem_limit_bytes=room * 2**20),
        cost_estimate=pl.CostEstimate(flops=0, bytes_accessed=0, transcendentals=0),
        **extra,
    )(*operands)


def column_sum(array_in):
    return jnp.sum(array_in, axis=0, keepdims=True)


def prepare(*refs):
    given, made, held, built = refs[0:12], refs[12:19], refs[19:31], refs[31:38]
    small, turned, parts, sems = refs[38:]
    inward = [pltpu.make_async_copy(given[i], held[i], sems.at[0, i]) for i in range(12)]
    outward = [pltpu.make_async_copy(built[i], made[i], sems.at[1, i]) for i in range(7)]
    for copy in inward:
        copy.start()
    for copy in inward:
        copy.wait()
    mix_ref, out_ref, up_ref, down_ref, vectors_ref, bias_ref = held[0:6]
    cross_mix_ref, cross_out_ref, cross_up_ref, cross_vectors_ref, cross_bias_ref, table_ref = held[6:]
    one_ref, two_ref, three_ref = built[0:3]
    one_ref[:, 0 : 3 * D] = mix_ref[...]
    one_ref[:, 3 * D : 4 * D] = out_ref[...]
    small[...] = jnp.zeros_like(small)
    small[0:8, 0:24] = wide(vectors_ref[...])
    small[8:16, 0:24] = wide(cross_vectors_ref[...])
    for row in range(4):
        lanes = slice(24 * row, 24 * (row + 1))
        small[80 + row : 81 + row, 0:24] = wide(bias_ref[:, lanes])
        small[84 + row : 85 + row, 0:24] = wide(cross_bias_ref[:, lanes])
    turned[...] = small[...].T
    turned[0:24, 16:80] = wide(table_ref[...])
    one_ref[:, 4 * D : 4 * D + 128] = low(turned[0:24, :])
    outward[0].start()
    two_ref[:, 0 : 4 * D] = up_ref[...]
    two_ref[:, 4 * D : 5 * D] = cross_out_ref[...]
    for quarter in range(4):
        three_ref[:, quarter * D : (quarter + 1) * D] = down_ref[quarter]
    outward[1].start()
    outward[2].start()
    parts[...] = jnp.zeros_like(parts)
    for spot in range(4):
        for level in range(4):
            taken = cross_up_ref[:, 192 * (4 * level + spot) : 192 * (4 * level + spot + 1)]
            parts[spot, :, 192 * level : 192 * (level + 1)] = taken
        for third in range(3):
            taken = cross_mix_ref[:, third * D + 192 * spot : third * D + 192 * (spot + 1)]
            parts[spot, :, D + 192 * third : D + 192 * (third + 1)] = taken
    chip = place_in()[1]
    for mask in range(4):
        built[3 + mask][...] = parts[chip ^ mask]
        outward[3 + mask].start()
    for copy in outward:
        copy.wait()


def join_cross(pieces, cross_down):
    def moves(layer, chip, core):
        found = []
        for mask in range(4):
            found.append((mask, (every, slice(0, D)), 0, (chip ^ mask, every, slice(0, D))))
            taken = (every, slice(D, D + 640))
            found.append((mask, taken, 0, (chip ^ mask, every, slice(2 * D, 2 * D + 640))))
        found.append((4, every, 0, (every, every, slice(D, 2 * D))))
        return found

    return copies(pieces + [cross_down.reshape(4, 24, D)], [(4, 24, 2 * D + 640)], moves)[0]


def place_cross(column, other):
    def moves(layer, chip, core):
        found = []
        for piece, side in ((0, core), (1, 1 - core)):
            source, lead = (every, every, every), (every, every, side)
            found.append((piece, source + (slice(0, D),), 0, lead))
            found.append((piece, source + (slice(2 * D, 2 * D + 640),), 1, lead))
            found.append((piece, source + (slice(D, 2 * D),), 2, (every, side)))
        return found

    up, mix, down = copies(
        [column, other], [(4, 4, 2, 24, D), (4, 4, 2, 24, 640), (4, 2, 4, 24, D)], moves
    )
    return up.reshape(D, D), mix.reshape(D, 640), down.reshape(D, D)


def segment_heads(segment, mixed_ref, docs_ref, docs_column_ref, probs_ref, context_ref):
    lane = lax.broadcasted_iota(jnp.int32, (SEG, 128), 1)
    rows = slice(segment * SEG, (segment + 1) * SEG)
    allowed = docs_column_ref[rows, :] == docs_ref[segment : segment + 1, :]
    for pair in range(HEADS // 2):
        query, key, value = (
            mixed_ref[rows, third * D + pair * 128 : third * D + (pair + 1) * 128]
            for third in range(3)
        )
        found = []
        for side in range(2):
            here = (lane < HEAD_DIM) if side == 0 else (lane >= HEAD_DIM)
            scores = contract(key, jnp.where(here, query, jnp.zeros_like(query)), 1, 1)
            scores = jnp.where(allowed, scores * HEAD_DIM ** (-0.5), masked_score)
            powers = jnp.exp(scores - jnp.max(scores, axis=0, keepdims=True))
            probs = powers / jnp.sum(powers, axis=0, keepdims=True)
            probs_ref[2 * pair + side] = probs
            found.append(contract(low(probs), value, 0, 0))
        context = jnp.where(lane < HEAD_DIM, found[0], found[1])
        context_ref[:, pair * 128 : (pair + 1) * 128] = low(context)


def local_attend(tokens_ref, group_ref, docs_ref, docs_column_ref, places_ref, *outs):
    mixed_ref, context_ref, probs_ref, rows_ref, places_out = outs
    rows_ref[...] = wide(group_ref[:, 4 * D : 4 * D + 128]).T
    lane = lax.broadcasted_iota(jnp.int32, (2, 64), 1)
    places_out[...] = contract_exact(wide(places_ref[...] == lane), rows_ref[16:80, :], 1, 0)
    tokens = tokens_ref[...]
    for third in range(3):
        columns = slice(third * D, (third + 1) * D)
        mixed = contract(tokens, group_ref[:, columns], 1, 0)
        if third != 1:
            mixed = mixed + rows_ref[third // 2 : third // 2 + 1, :]
        mixed_ref[:, columns] = low(mixed)
    segment_heads(0, mixed_ref, docs_ref, docs_column_ref, probs_ref, context_ref)


def local_attend_more(
    tokens_ref, mixed_ref, before_ref, weight_ref, rows_ref, docs_ref, docs_column_ref, *outs
):
    context_ref, probs_ref, n_ref, scale_ref, low_ref, here = outs
    segment_heads(1, mixed_ref, docs_ref, docs_column_ref, probs_ref, here)
    context_ref[0:SEG, :] = before_ref[...]
    context_ref[SEG : 2 * SEG, :] = here[...]
    total = wide(tokens_ref[...]) + contract(context_ref[...], weight_ref[...], 1, 0)
    normed, scale = norm_parts(total + rows_ref[2:3, :])
    n_ref[...] = normed
    scale_ref[...] = scale
    low_ref[...] = low(normed * rows_ref[3:4, :] + rows_ref[4:5, :])


def local_up_part(low_ref, weight_ref, bias_ref, active_ref, slope_ref):
    hidden = contract(low_ref[...], weight_ref[...], 1, 0) + wide(bias_ref[...])
    chance = 0.5 * (1.0 + lax.erf(hidden * math.sqrt(0.5)))
    density = jnp.exp(-0.5 * hidden * hidden) * (1.0 / math.sqrt(2.0 * math.pi))
    active_ref[...] = low(hidden * chance)
    slope_ref[...] = low(chance + hidden * density)


def local_down_part(
    active_ref, weight_ref, first_ref, rows_ref, cot_a, cot_b, places_ref, *outs
):
    n_ref, scale_ref, kept_ref, given_ref, total = outs
    step = pl.program_id(0)
    part = contract(active_ref[...], weight_ref[...], 1, 0)

    @pl.when(step == 0)
    def _():
        first_norm = first_ref[...] * rows_ref[3:4, :] + rows_ref[4:5, :]
        total[...] = first_norm + rows_ref[5:6, :] + part

    @pl.when(step > 0)
    def _():
        total[...] += part

    @pl.when(step == 3)
    def _():
        normed, scale = norm_parts(total[...])
        n_ref[...] = normed
        scale_ref[...] = scale
        core = place_in()[2]
        heads, grads = [], []
        for place, cot in ((0, cot_a), (1, cot_b)):
            row = normed[place * SEG : place * SEG + 1] * rows_ref[6:7, :] + rows_ref[7:8, :]
            heads.append(row + places_ref[place : place + 1, :])
            grads.append(wide(cot[...])[0:1])
        for ref, mine in ((kept_ref, core == 0), (given_ref, core == 1)):
            ref[...] = jnp.zeros_like(ref)
            ref[0:1, :] = jnp.where(mine, heads[0], heads[1])
            ref[1:2, :] = jnp.where(mine, grads[0], grads[1])


def join_pair(kept_ref, got_ref, out_ref):
    core = place_in()[2]
    out_ref[...] = jnp.zeros_like(out_ref)
    out_ref[0:2, :] = jnp.where(core == 0, kept_ref[0:2, :], got_ref[0:2, :])
    out_ref[2:4, :] = jnp.where(core == 0, got_ref[0:2, :], kept_ref[0:2, :])


def cross_attend(
    own_ref, a_ref, b_ref, c_ref, weight_ref, rows_ref, docs_ref, docs_column_ref, *outs
):
    in_ref, grad_ref, mixed_ref, probs_ref, context_ref = outs
    layer, chip, core = place_in()
    for mask, ref in enumerate((own_ref, a_ref, b_ref, c_ref)):
        for side in range(2):
            row = 2 * (chip ^ mask) + side
            in_ref[pl.ds(row, 1), :] = ref[2 * side : 2 * side + 1, :]
            grad_ref[pl.ds(row, 1), :] = ref[2 * side + 1 : 2 * side + 2, :]
    biases = []
    for vector in (8, 9):
        row = rows_ref[vector : vector + 1, :]
        found = row[:, 0:192]
        for spot in range(1, 4):
            found = jnp.where(chip == spot, row[:, 192 * spot : 192 * (spot + 1)], found)
        biases.append(found)
    bias = jnp.concatenate([biases[0], jnp.zeros_like(biases[0]), biases[1]], axis=1)
    mixed = low(contract(low(in_ref[...]), weight_ref[:, 0:576], 1, 0) + bias)
    mixed_ref[...] = mixed
    row_docs = jnp.where(core == 0, docs_ref[0:1, :], docs_ref[1:2, :])
    column_docs = jnp.where(core == 0, docs_column_ref[:, 0:1], docs_column_ref[:, 1:2])
    allowed = row_docs == column_docs
    found = []
    for head in range(3):
        query, key, value = (
            mixed[:, third * 192 + head * HEAD_DIM : third * 192 + (head + 1) * HEAD_DIM]
            for third in range(3)
        )
        scores = contract(query, key, 1, 1) * HEAD_DIM ** (-0.5)
        scores = jnp.where(allowed, scores, masked_score)
        powers = jnp.exp(scores - jnp.max(scores, axis=-1, keepdims=True))
        probs = powers / jnp.sum(powers, axis=-1, keepdims=True)
        probs_ref[head] = probs
        found.append(contract(low(probs), value, 1, 0))
    context_ref[...] = low(jnp.concatenate(found, axis=1))


def cross_up_down(
    own_ref, a_ref, b_ref, c_ref, in_ref, out_weight_ref, rows_ref, up_ref, bias_ref, down_ref, *outs
):
    n_ref, scale_ref, low_ref, hidden_ref, active_ref, part_ref = outs
    chip = place_in()[1]
    total = in_ref[...] + rows_ref[10:11, :]
    for mask, ref in enumerate((own_ref, a_ref, b_ref, c_ref)):
        start = pl.multiple_of(192 * (chip ^ mask), 64)
        total = total + contract(ref[...], out_weight_ref[pl.ds(start, 192), :], 1, 0)
    normed, scale = norm_parts(total)
    n_ref[...] = normed
    scale_ref[...] = scale
    first = low(normed * rows_ref[11:12, :] + rows_ref[12:13, :])
    low_ref[...] = first
    hidden = contract(first, up_ref[...], 1, 0) + bias_ref[...]
    hidden_ref[...] = hidden
    active = low(hidden * (0.5 * (1.0 + lax.erf(hidden * math.sqrt(0.5)))))
    active_ref[...] = active
    part_ref[...] = contract(active, down_ref[...], 1, 0)


def cross_turn(
    own_ref, a_ref, b_ref, c_ref, n_ref, rows_ref, grad_ref, hidden_ref, up_ref, down_ref, *outs
):
    out_ref, second_ref, hidden_low_ref, part_ref, sums_ref = outs
    first = n_ref[...] * rows_ref[11:12, :] + rows_ref[12:13, :]
    total = (own_ref[...] + a_ref[...]) + (b_ref[...] + c_ref[...])
    normed, scale = norm_parts(first + total + rows_ref[13:14, :])
    out_ref[...] = normed * rows_ref[14:15, :] + rows_ref[15:16, :]
    grad = grad_ref[...]
    second = norm_back(grad, normed, scale, rows_ref[14:15, :])
    second_ref[...] = second
    hidden_low = low(contract(low(second), down_ref[...], 1, 1) * gelu_slope(hidden_ref[...]))
    hidden_low_ref[...] = hidden_low
    part_ref[...] = contract(hidden_low, up_ref[...], 1, 1)
    sums_ref[...] = jnp.zeros_like(sums_ref)
    sums_ref[0:1, :] = column_sum(grad * normed)
    sums_ref[1:2, :] = column_sum(grad)


def cross_attend_back(
    own_ref,
    a_ref,
    b_ref,
    c_ref,
    second_ref,
    n_ref,
    scale_ref,
    rows_ref,
    out_weight_ref,
    mixed_ref,
    probs_ref,
    weight_ref,
    hidden_low_ref,
    active_ref,
    context_ref,
    in_ref,
    low_ref,
    sums_ref,
    places_ref,
    total_ref,
    part_ref,
    pack_ref,
    pack,
    rows,
):
    chip = place_in()[1]
    grad = second_ref[...] + (own_ref[...] + a_ref[...]) + (b_ref[...] + c_ref[...])
    normed = n_ref[...]
    total = norm_back(grad, normed, scale_ref[...], rows_ref[11:12, :])
    total_ref[...] = total
    branch = low(total)
    start = pl.multiple_of(192 * chip, 64)
    context_low = low(contract(branch, out_weight_ref[pl.ds(start, 192), :], 1, 1))
    mixed = mixed_ref[...]
    found = [[], [], []]
    for head in range(3):
        query, key, value = (
            mixed[:, third * 192 + head * HEAD_DIM : third * 192 + (head + 1) * HEAD_DIM]
            for third in range(3)
        )
        part = context_low[:, head * HEAD_DIM : (head + 1) * HEAD_DIM]
        probs = probs_ref[head]
        prob_grad = contract(part, value, 1, 1)
        score = low(probs * (prob_grad - jnp.sum(probs * prob_grad, axis=-1, keepdims=True)))
        found[0].append(contract(score, key, 1, 0) * HEAD_DIM ** (-0.5))
        found[1].append(contract(score, query, 0, 0) * HEAD_DIM ** (-0.5))
        found[2].append(contract(low(probs), part, 0, 0))
    mixed_low = low(jnp.concatenate(found[0] + found[1] + found[2], axis=1))
    part_ref[...] = contract(mixed_low, weight_ref[:, 0:576], 1, 1)
    pack[...] = jnp.zeros_like(pack)
    pack[0:8, :] = wide(hidden_low_ref[...])
    pack[8:16, :] = wide(active_ref[...])
    pack[16:24, 0:576] = wide(mixed_low)
    pack[16:24, 576:768] = wide(context_ref[...])
    for i, value in enumerate(
        (in_ref[...], wide(low_ref[...]), total, second_ref[...], total)
    ):
        rows[...] = value
        for side in range(2):
            row = 24 + 2 * i + side
            pack[row : row + 1, :] = rows[pl.ds(2 * chip + side, 1), :]
    rows[0:1, :] = column_sum(grad * normed)
    rows[1:2, :] = column_sum(grad)
    rows[2:4, :] = sums_ref[0:2, :]
    pack[34:35, :] = rows[pl.ds(chip, 1), :]
    for place in range(2):
        spot = wide(places_ref[place : place + 1, :])
        pack[35 + place : 36 + place, :] = jnp.broadcast_to(spot, (1, D))
    pack_ref[...] = low(pack[...])


def cross_finish(own_ref, a_ref, b_ref, c_ref, total_ref, out_ref, kept_ref, given_ref, rows):
    layer, chip, core = place_in()
    rows[...] = total_ref[...] + (own_ref[...] + a_ref[...]) + (b_ref[...] + c_ref[...])
    for ref, side in ((kept_ref, core), (given_ref, 1 - core)):
        ref[...] = jnp.zeros_like(ref)
        ref[0:1, :] = rows[pl.ds(2 * chip + side, 1), :]
        ref[1:2, :] = out_ref[pl.ds(2 * chip + side, 1), :]


def cross_owner(mine_ref, other_ref, weight_ref, *refs):
    mix_ref, out_ref, up_ref, down_ref, vectors_ref, bias_ref, table_ref = refs[:7]
    hidden, mixed, single, active, sums, places = refs[7:]
    layer, chip, core = place_in()
    rank = 8 * layer + 2 * chip + core
    sums[...] = jnp.zeros_like(sums)
    for level in range(4):
        for side in range(2):
            group = 2 * level + side
            rows = slice(8 * group, 8 * group + 8)
            for spot in range(4):
                value = wide(
                    jnp.where(core == side, mine_ref[level, spot], other_ref[level, spot])
                )
                hidden[spot, rows, :] = value[0:8]
                mixed[spot, rows, :] = value[16:24]
                for i in range(5):
                    start = 8 * group + 2 * spot
                    single[i, start : start + 2, :] = value[24 + 2 * i : 26 + 2 * i]
                sums[spot : spot + 1, :] += value[34:35]
                for sequence in range(2):
                    row = 16 * level + 8 * sequence + 2 * spot + side
                    places[row : row + 1, :] = value[35 + sequence : 36 + sequence, 0:128]
            value = jnp.where(core == side, mine_ref[level, chip], other_ref[level, chip])
            active[rows, :] = wide(value)[8:16]

    def select(count, first):
        lane = lax.broadcasted_iota(jnp.int32, (count, D), 1)
        row = lax.broadcasted_iota(jnp.int32, (count, D), 0)
        return wide(lane == first + row)

    own = select(24, 24 * rank)
    offset = 24 * (2 * chip + core)
    units = select(96, 192 * layer + 96 * core)
    own_low = low(own)

    def columns_of(array_in):
        return low(contract(own_low, low(array_in), 1, 1))

    inputs = columns_of(single[0])
    for spot in range(4):
        part = contract(inputs, low(mixed[spot][:, 0:576]), 1, 0)
        for third in range(3):
            start = third * D + 192 * spot
            mix_ref[:, start : start + 192] = part[:, 192 * third : 192 * (third + 1)]
    own_mixed = mixed[layer]
    context = low(contract(low(select(24, 576 + offset)), low(own_mixed), 1, 1))
    out_ref[...] = contract(context, low(single[2]), 1, 0)
    first = columns_of(single[1])
    for spot in range(4):
        part = contract(first, low(hidden[spot]), 1, 0)
        for level in range(4):
            start = 192 * (4 * level + spot)
            up_ref[:, start : start + 192] = part[:, 192 * level : 192 * (level + 1)]
    units_low = low(contract(low(units), low(active[...]), 1, 1))
    down_ref[...] = contract(units_low, low(single[3]), 1, 0)
    mixed_sum = column_sum(own_mixed)
    vectors_ref[0:1, :] = contract_exact(mixed_sum, select(24, offset), 1, 1)
    vectors_ref[1:2, :] = contract_exact(mixed_sum, select(24, 384 + offset), 1, 1)
    for row, value in (
        (2, column_sum(single[2])),
        (3, sums[0:1, :]),
        (4, sums[1:2, :]),
        (5, column_sum(single[3])),
        (6, sums[2:3, :]),
        (7, sums[3:4, :]),
    ):
        vectors_ref[row : row + 1, :] = contract_exact(value, own, 1, 1)
    bias_ref[...] = contract_exact(column_sum(hidden[chip]), units, 1, 1)
    grads = contract(low(single[4]), own_low, 1, 1)
    for spot in range(4):
        for third in range(3):
            start = third * D + 192 * spot
            part = low(mixed[spot][:, 192 * third : 192 * (third + 1)])
            grads = grads + contract(part, weight_ref[:, start : start + 192], 1, 1)
    lane = wide(lax.broadcasted_iota(jnp.int32, (64, 64), 1))
    table_ref[...] = contract_exact(wide(places[:, 0:64] == lane), grads, 0, 0)


def split_cores(value, kept_ref, gone_ref):
    rows = kept_ref.shape[1]
    core = lax.rem(lax.axis_index("seq"), 2)
    parts = value.reshape(-1, 2, rows, value.shape[1])
    kept_ref[...] = low(jnp.where(core == 0, parts[:, 0], parts[:, 1]))
    gone_ref[...] = low(jnp.where(core == 0, parts[:, 1], parts[:, 0]))


def local_down_back(
    cot_ref, mine_ref, other_ref, n_ref, scale_ref, rows_ref, active_ref, slope_ref, weight_ref, *outs
):
    out_ref, second_ref, kept_ref, gone_ref, hidden_ref, sums_ref, bias_ref, second_low_ref = outs
    step = pl.program_id(0)

    @pl.when(step == 0)
    def _():
        core = place_in()[2]
        row = lax.broadcasted_iota(jnp.int32, (2 * SEG, D), 0)
        grad = wide(cot_ref[...])
        normed = n_ref[...]
        out = normed * rows_ref[6:7, :] + rows_ref[7:8, :]
        for place in range(2):
            heads = jnp.where(core == place, mine_ref[...], other_ref[...])
            grad = jnp.where(row == place * SEG, heads[0:1], grad)
            out = jnp.where(row == place * SEG, heads[1:2], out)
        out_ref[...] = low(out)
        second = norm_back(grad, normed, scale_ref[...], rows_ref[6:7, :])
        second_ref[...] = second
        second_low_ref[...] = low(second)
        sums_ref[0:1, :] = column_sum(wide(low(second)))
        sums_ref[1:2, :] = column_sum(grad * normed)
        sums_ref[2:3, :] = column_sum(grad)

    second_low = second_low_ref[...]
    split_cores(contract(active_ref[...], second_low, 0, 0), kept_ref, gone_ref)
    hidden = low(contract(second_low, weight_ref[...], 1, 1) * wide(slope_ref[...]))
    hidden_ref[...] = hidden
    bias_ref[...] = column_sum(wide(hidden))


def local_up_back(low_ref, hidden_ref, weight_ref, second_ref, kept_ref, gone_ref, first_ref):
    hidden = hidden_ref[...]
    split_cores(contract(low_ref[...], hidden, 0, 0), kept_ref, gone_ref)
    part = contract(hidden, weight_ref[...], 1, 1)
    step = pl.program_id(0)

    @pl.when(step == 0)
    def _():
        first_ref[...] = second_ref[...] + part

    @pl.when(step > 0)
    def _():
        first_ref[...] += part


def local_attend_back(
    first_ref, n_ref, scale_ref, rows_ref, context_ref, mixed_ref, probs_a, probs_b, group_ref, *outs
):
    out_ref, total_ref, sums_ref, back_ref, context_low_ref = outs
    grad, normed = first_ref[...], n_ref[...]
    total = norm_back(grad, normed, scale_ref[...], rows_ref[3:4, :])
    total_ref[...] = total
    branch = low(total)
    sums_ref[2:3, :] = column_sum(wide(branch))
    sums_ref[3:4, :] = column_sum(grad * normed)
    sums_ref[4:5, :] = column_sum(grad)
    out_ref[...] = contract(context_ref[...], branch, 0, 0)
    context_low_ref[...] = low(contract(branch, group_ref[...], 1, 1))
    lane = lax.broadcasted_iota(jnp.int32, (SEG, 128), 1)
    for segment in range(2):
        rows = slice(segment * SEG, (segment + 1) * SEG)
        for pair in range(HEADS // 2):
            places = [
                slice(third * D + pair * 128, third * D + (pair + 1) * 128) for third in range(3)
            ]
            query, key, value = (mixed_ref[rows, place] for place in places)
            grad = context_low_ref[rows, places[0]]
            found = []
            for side in range(2):
                here = (lane < HEAD_DIM) if side == 0 else (lane >= HEAD_DIM)
                probs = (probs_a, probs_b)[segment][2 * pair + side]
                prob_grad = contract(value, jnp.where(here, grad, jnp.zeros_like(grad)), 1, 1)
                value_grad = contract(low(probs), grad, 1, 0)
                score = low(
                    probs * (prob_grad - jnp.sum(probs * prob_grad, axis=0, keepdims=True))
                )
                found.append(
                    (contract(score, key, 0, 0), contract(score, query, 1, 0), value_grad)
                )
            for third in range(3):
                merged = jnp.where(lane < HEAD_DIM, found[0][third], found[1][third])
                if third < 2:
                    merged = merged * HEAD_DIM ** (-0.5)
                back_ref[rows, places[third]] = low(merged)
    for third in (0, 2):
        columns = slice(third * D, (third + 1) * D)
        sums_ref[third // 2 : third // 2 + 1, :] = column_sum(wide(back_ref[:, columns]))


def local_mix_back(
    total_ref, back_ref, tokens_ref, group_ref, out_ref, sums_ref, more_ref, bias_ref, *outs
):
    input_ref, kept_ref, gone_ref, small_ref = outs
    tokens, total = tokens_ref[...], total_ref[...]
    for third in range(3):
        columns = slice(third * D, (third + 1) * D)
        back = back_ref[:, columns]
        grad = contract(tokens, back, 0, 0)
        split_cores(grad, kept_ref.at[:, :, columns], gone_ref.at[:, :, columns])
        total = total + contract(back, group_ref[:, columns], 1, 1)
    input_ref[...] = total
    columns = slice(3 * D, 4 * D)
    split_cores(out_ref[...], kept_ref.at[:, :, columns], gone_ref.at[:, :, columns])
    small_ref[...] = jnp.zeros_like(small_ref)
    small_ref[0:5, :] = sums_ref[0:5, :]
    small_ref[5:8, :] = more_ref[0:3, :]
    small_ref[8:12, :] = bias_ref[...]
    columns = slice(4 * D, 4 * D + 128)
    split_cores(small_ref[...].T, kept_ref.at[:, :, columns], gone_ref.at[:, :, columns])


def finish_mix(own_ref, a_ref, b_ref, c_ref, mix_ref, out_ref, vectors_ref, bias_ref, wide_ref):
    total = own_ref[...] + wide(a_ref[...]) + wide(b_ref[...]) + wide(c_ref[...])
    mix_ref[...] = total[:, 0 : 3 * D]
    out_ref[...] = total[:, 3 * D : 4 * D]
    wide_ref[...] = jnp.zeros_like(wide_ref)
    wide_ref[0:24, :] = total[:, 4 * D : 4 * D + 128]
    turned = wide_ref[...].T
    vectors_ref[...] = turned[0:8, 0:24]
    for row in range(4):
        bias_ref[:, 24 * row : 24 * (row + 1)] = turned[8 + row : 9 + row, 0:24]


def plane_three(array_in):
    return [array_in] + [swap_chip(array_in, mask) for mask in (1, 2, 3)]


def plane_shards(
    tokens,
    cotangent,
    token_docs,
    segment_docs,
    segment_positions,
    local_mix,
    local_out,
    local_up,
    local_down,
    local_vectors,
    local_up_bias,
    cross_mix,
    cross_out,
    cross_up,
    cross_down,
    cross_vectors,
    cross_up_bias,
    position_table,
):
    chip = place_in()[1]
    flat_tokens = tokens.reshape(256, D)
    flat_cot = cotangent.reshape(256, D)
    docs_column = token_docs.reshape(256, 1)
    segment_column = segment_docs.T

    shards_in = (
        local_mix,
        local_out,
        local_up,
        local_down.reshape(4, 24, D),
        local_vectors,
        local_up_bias.reshape(1, 96),
        cross_mix,
        cross_out,
        cross_up,
        cross_vectors,
        cross_up_bias.reshape(1, 96),
        position_table.T,
    )
    made = [half(24, 3200), half(24, 5 * D), half(24, 4 * D)] + [half(24, D + 640)] * 4
    far = pl.BlockSpec(memory_space=pltpu.HBM)
    shard_one, shard_two, shard_three, *cross_pieces = on_core(
        prepare,
        made,
        shards_in,
        0,
        in_specs=[far] * 12,
        out_specs=[far] * 7,
        scratch=[pltpu.VMEM(a.shape, a.dtype) for a in list(shards_in) + made]
        + [
            pltpu.VMEM((128, 128), jnp.float32),
            pltpu.VMEM((128, 128), jnp.float32),
            pltpu.VMEM((4, 24, D + 640), jnp.bfloat16),
            pltpu.SemaphoreType.DMA((2, 12)),
        ],
    )
    cross_sent = [cross_pieces[0]] + [swap_chip(cross_pieces[mask], mask) for mask in (1, 2, 3)]
    z_one = reach_dp(shard_one)
    shard_two, docs_column, segment_column, *z_one = stage(
        shard_two, docs_column, segment_column, *z_one, *cross_sent
    )
    z_one, cross_sent = z_one[:4], z_one[4:]
    column_one = join_dp(z_one)
    column_one, shard_two = stage(column_one, shard_two)

    first, second = swap_one(column_one), swap_two(column_one)
    cross_row = join_cross(cross_sent, after(cross_down, column_one))
    *z_two, first, second, column_one, cross_row = stage(
        *reach_dp(shard_two), first, second, column_one, cross_row
    )

    third = swap_two(first)
    others = [swap_core(piece) for piece in (column_one, first, second)]
    column_two = join_dp(z_two)
    cross_moved = [cross_row, swap_dp(cross_row, 1)]
    third, column_two, cross_moved[1], *others = stage(third, column_two, cross_moved[1], *others)
    others.append(swap_core(third))
    column_two, shard_three, *others = stage(column_two, shard_three, *others)

    first_group = gather_plane([column_one, first, second, third], others).reshape(D, 3200)
    mixed_rows, context_first, probs_first, rows, place_rows = on_core(
        local_attend,
        [half(256, 3 * D), half(SEG, D), shape_of(12, SEG, SEG), shape_of(128, D), shape_of(2, D)],
        (flat_tokens, first_group, token_docs, docs_column, segment_positions),
        0,
    )
    first_two, second_two = swap_one(column_two), swap_two(column_two)
    *z_three, mixed_rows, first_two, second_two, column_two, cross_moved[1] = stage(
        *reach_dp(shard_three), mixed_rows, first_two, second_two, column_two, cross_moved[1]
    )
    cross_moved.append(swap_dp(cross_moved[1], 1))

    third_two = swap_two(first_two)
    others = [swap_core(piece) for piece in (column_two, first_two, second_two)]
    column_three = join_dp(z_three)
    def plain(*shapes):
        return [pl.BlockSpec(shape, lambda j, n=len(shape): (0,) * n) for shape in shapes]

    context_rows, probs_second, normed_one, scale_one, low_one = on_core(
        local_attend_more,
        [half(256, D), shape_of(12, SEG, SEG), shape_of(256, D), shape_of(256, 1), half(256, D)],
        (flat_tokens, mixed_rows, context_first, first_group, rows, token_docs, docs_column),
        0,
        grid=(1,),
        in_specs=plain((256, D), (256, 3 * D), (SEG, D))
        + [pl.BlockSpec((D, D), lambda j: (0, 3))]
        + plain((128, D), (2, SEG), (256, 1)),
        out_specs=plain((256, D), (12, SEG, SEG), (256, D), (256, 1), (256, D)),
        scratch=[pltpu.VMEM((SEG, D), jnp.bfloat16)],
    )
    up_bias = rows[80:84].reshape(4, 32, 24).transpose(1, 0, 2).reshape(1, 4 * D)
    cross_bias = rows[84:88].reshape(4, 4, 4, 2, 24)
    cross_bias = lax.dynamic_index_in_dim(cross_bias, chip, 2, keepdims=False)
    cross_bias = cross_bias.transpose(1, 2, 0, 3).reshape(1, D)
    cross_moved[2], third_two, column_three, low_one, up_bias, cross_bias, *others = stage(
        cross_moved[2], third_two, column_three, low_one, up_bias, cross_bias, *others
    )
    cross_moved.append(swap_dp(cross_moved[2], 1))

    first_three, second_three = swap_one(column_three), swap_two(column_three)
    others.append(swap_core(third_two))
    second_group, cross_out_weight = gather_up(
        [column_two, first_two, second_two, third_two], others
    )
    whole = pl.BlockSpec((256, D), lambda j: (0, 0))
    thin = pl.BlockSpec((256, 1), lambda j: (0, 0))
    vectors = pl.BlockSpec((128, D), lambda j: (0, 0))
    eight = pl.BlockSpec((8, D), lambda j: (0, 0))
    across = pl.BlockSpec((256, D), lambda j: (0, j))
    tall = pl.BlockSpec((D, D), lambda j: (0, j))
    deep = pl.BlockSpec((D, D), lambda j: (j, 0))
    strip = pl.BlockSpec((1, D), lambda j: (0, j))
    active_rows, slope_rows = on_core(
        local_up_part,
        [half(256, 4 * D)] * 2,
        (low_one, second_group, up_bias),
        2 * 256 * D * 4 * D,
        grid=(4,),
        in_specs=[whole, tall, strip],
        out_specs=[across, across],
    )
    active_rows, first_three, second_three, column_three, cross_moved[3] = stage(
        active_rows, first_three, second_three, column_three, cross_moved[3]
    )

    third_three = swap_two(first_three)
    others = [swap_core(piece) for piece in (column_three, first_three, second_three)]
    third_three, cross_column, *others = stage(third_three, join_dp(cross_moved), *others)

    others.append(swap_core(third_three))
    down_weight = gather_down([column_three, first_three, second_three, third_three], others)
    down_weight, cross_column = stage(down_weight.reshape(4 * D, D), cross_column)
    cross_other = swap_core(cross_column)
    normed_two, scale_two, kept, given = on_core(
        local_down_part,
        [shape_of(256, D), shape_of(256, 1), shape_of(8, D), shape_of(8, D)],
        (active_rows, down_weight, normed_one, rows, flat_cot, flat_cot, place_rows),
        2 * 256 * D * 4 * D,
        grid=(4,),
        in_specs=[
            across,
            deep,
            whole,
            vectors,
            pl.BlockSpec((16, D), lambda j: (0, 0)),
            pl.BlockSpec((16, D), lambda j: (8, 0)),
            pl.BlockSpec((2, D), lambda j: (0, 0)),
        ],
        out_specs=[whole, thin, eight, eight],
        scratch=[pltpu.VMEM((256, D), jnp.float32)],
    )

    row8, mix_share = (8, D), (D, 640)
    out_share = pl.BlockSpec((D, D), lambda j: (0, 0))
    up_share = pl.BlockSpec((D, D), lambda j: (0, 0))
    given, kept, cross_other = stage(given, kept, cross_other)
    got = swap_core(given)
    cross_up_part, cross_mix_part, cross_down_part = place_cross(cross_column, cross_other)
    kept, got, cross_mix_part = stage(kept, got, cross_mix_part)
    pair = on_core(join_pair, shape_of(8, D), (kept, got), 0, room=12)
    row_in, row_grad, mixed, probs, context = on_core(
        cross_attend,
        [shape_of(8, D), shape_of(8, D), half(8, 576), shape_of(3, 8, 8), half(8, 192)],
        (*plane_three(pair), cross_mix_part, rows, segment_docs, segment_column),
        0,
        room=12,
    )
    row_n, row_scale, row_low, hidden, active, part = on_core(
        cross_up_down,
        [shape_of(8, D), shape_of(8, 1), half(8, D), shape_of(8, D), half(8, D), shape_of(8, D)],
        (
            *plane_three(context),
            row_in,
            cross_out_weight,
            rows,
            cross_up_part,
            cross_bias,
            cross_down_part,
        ),
        0,
        grid=(1,),
        in_specs=plain(*[(8, 192)] * 4, row8)
        + [out_share]
        + plain((128, D))
        + [up_share]
        + plain((1, D), (D, D)),
        out_specs=plain(row8, (8, 1), row8, row8, row8, row8),
        room=12,
    )
    row_out, row_second, hidden_low, part, sums = on_core(
        cross_turn,
        [shape_of(8, D), shape_of(8, D), half(8, D), shape_of(8, D), shape_of(8, D)],
        (*plane_three(part), row_n, rows, row_grad, hidden, cross_up_part, cross_down_part),
        0,
        grid=(1,),
        in_specs=plain(*[row8] * 4, row8, (128, D), row8, row8) + [up_share] + plain((D, D)),
        out_specs=plain(*[row8] * 5),
        room=12,
    )
    row_total, part, packed = on_core(
        cross_attend_back,
        [shape_of(8, D), shape_of(8, D), half(48, D)],
        (
            *plane_three(part),
            row_second,
            row_n,
            row_scale,
            rows,
            cross_out_weight,
            mixed,
            probs,
            cross_mix_part,
            hidden_low,
            active,
            context,
            row_in,
            row_low,
            sums,
            segment_positions,
        ),
        0,
        grid=(1,),
        in_specs=plain(*[row8] * 4, row8, row8, (8, 1), (128, D))
        + [out_share]
        + plain((8, 576), (3, 8, 8), mix_share, row8, row8, (8, 192), row8, row8, row8, (2, 1)),
        out_specs=plain(row8, row8, (48, D)),
        scratch=[pltpu.VMEM((48, D), jnp.float32), pltpu.VMEM((8, D), jnp.float32)],
        room=12,
    )
    kept, given = on_core(
        cross_finish,
        [shape_of(8, D), shape_of(8, D)],
        (*plane_three(part), row_total, row_out),
        0,
        scratch=[pltpu.VMEM((8, D), jnp.float32)],
        room=12,
    )
    got, kept, packed = stage(swap_core(given), kept, packed)
    pack_one, pack_two = swap_one(packed), swap_two(packed)

    fours = pl.BlockSpec((4, 96, D), lambda j: (j, 0, 0))
    layer_output, second_rows, down_kept, down_gone, hidden_grads, sums_two, bias_grad = on_core(
        local_down_back,
        [
            half(256, D),
            shape_of(256, D),
            half(16, 96, D),
            half(16, 96, D),
            half(256, 4 * D),
            shape_of(8, D),
            shape_of(1, 4 * D),
        ],
        (flat_cot, kept, got, normed_two, scale_two, rows, active_rows, slope_rows, down_weight),
        4 * 256 * D * 4 * D,
        grid=(4,),
        in_specs=[whole, eight, eight, whole, thin, vectors, across, across, deep],
        out_specs=[whole, whole, fours, fours, across, eight, strip],
        scratch=[pltpu.VMEM((256, D), jnp.bfloat16)],
    )
    down_total = Sum(down_kept.reshape(4, 4, 96, D))
    hidden_grads, down_gone, pack_one, pack_two = stage(
        hidden_grads, down_gone.reshape(4, 4, 96, D), pack_one, pack_two
    )
    pack_three = swap_two(pack_one)

    down_got = swap_core(down_gone)
    sixteens = pl.BlockSpec((16, 24, D), lambda j: (0, 0, j))
    up_kept, up_gone, first_rows = on_core(
        local_up_back,
        [half(16, 24, 4 * D), half(16, 24, 4 * D), shape_of(256, D)],
        (low_one, hidden_grads, second_group, second_rows),
        4 * 256 * D * 4 * D,
        grid=(4,),
        in_specs=[whole, across, tall, whole],
        out_specs=[sixteens, sixteens, whole],
    )
    up_total = Sum(up_kept.reshape(4, 4, 24, 4 * D))
    down_got, first_rows, up_gone, pack_three = stage(
        down_got, first_rows, up_gone.reshape(4, 4, 24, 4 * D), pack_three
    )
    plane_pack = join_chips([packed, pack_one, pack_two, pack_three])
    packs = [plane_pack, swap_dp(plane_pack, 1), swap_dp(plane_pack, 3)]

    up_got = swap_core(up_gone)
    down_sent = down_total.first(down_got)
    down_back = swap_one(down_sent)
    flat = pl.BlockSpec((256, 3 * D), lambda j: (0, 0))
    out_grad, sum_rows, sums_one, back_rows = on_core(
        local_attend_back,
        [shape_of(D, D), shape_of(256, D), shape_of(8, D), half(256, 3 * D)],
        (
            first_rows,
            normed_one,
            scale_one,
            rows,
            context_rows,
            mixed_rows,
            probs_first,
            probs_second,
            first_group,
        ),
        4 * 256 * D * 2 * D,
        grid=(1,),
        in_specs=[
            whole,
            whole,
            thin,
            vectors,
            whole,
            flat,
            pl.BlockSpec((12, SEG, SEG), lambda j: (0, 0, 0)),
            pl.BlockSpec((12, SEG, SEG), lambda j: (0, 0, 0)),
            pl.BlockSpec((D, D), lambda j: (0, 3)),
        ],
        out_specs=[pl.BlockSpec((D, D), lambda j: (0, 0)), whole, eight, flat],
        scratch=[pltpu.VMEM((256, D), jnp.bfloat16)],
    )
    up_sent = up_total.first(up_got)
    down_back, back_rows, up_sent, *packs = stage(down_back, back_rows, up_sent, *packs)
    packs.insert(2, swap_dp(packs[0], 2))

    up_back = swap_one(up_sent)
    down_onward = down_total.second(down_back)
    bias_rows = bias_grad.reshape(32, 4, 24).transpose(1, 0, 2).reshape(4, D)
    sides = [half(16, 24, 4 * D + 128)] * 2
    input_grad, mix_kept, mix_gone = on_core(
        local_mix_back,
        [shape_of(256, D)] + sides,
        (
            sum_rows,
            back_rows,
            flat_tokens,
            first_group,
            out_grad,
            sums_one,
            sums_two,
            bias_rows,
        ),
        4 * 256 * D * 3 * D,
        scratch=[pltpu.VMEM((128, D), jnp.float32)],
    )
    mix_total = Sum(mix_kept.reshape(4, 4, 24, 3200))
    up_back, down_onward, mix_gone, packs[2] = stage(
        up_back, down_onward, mix_gone.reshape(4, 4, 24, 3200), packs[2]
    )

    mix_got, down_last = swap_core(mix_gone), swap_two(down_onward)
    up_onward = up_total.second(up_back)
    my_rows = join_dp(packs)
    mix_got, down_last, up_onward, my_rows = stage(mix_got, down_last, up_onward, my_rows)

    up_last = swap_two(up_onward)
    mix_sent = mix_total.first(mix_got)
    down_others = down_total.third(down_last)
    up_last, mix_sent, my_rows, *down_others = stage(up_last, mix_sent, my_rows, *down_others)
    other_rows = swap_core(my_rows)

    mix_back, down_others = swap_one(mix_sent), send_dp(down_others)
    up_others = up_total.third(up_last)
    mix_back, other_rows, *others = stage(mix_back, other_rows, *down_others, *up_others)
    down_others, up_others = others[:3], others[3:]

    mix_last = swap_two(mix_total.second(mix_back))
    up_others = send_dp(up_others)
    down_sum = down_total.total(down_others)
    mix_last, down_sum, other_rows, *up_others = stage(mix_last, down_sum, other_rows, *up_others)

    mix_others = send_dp(mix_total.third(mix_last))
    up_sum = up_total.total(up_others)
    cross_grads = on_core(
        cross_owner,
        [
            shape_of(24, 3 * D),
            shape_of(24, D),
            shape_of(24, 4 * D),
            shape_of(96, D),
            shape_of(8, 24),
            shape_of(1, 96),
            shape_of(64, 24),
        ],
        (my_rows, other_rows, cross_mix),
        0,
        scratch=[
            pltpu.VMEM((4, 64, D), jnp.float32),
            pltpu.VMEM((4, 64, D), jnp.float32),
            pltpu.VMEM((5, 64, D), jnp.float32),
            pltpu.VMEM((64, D), jnp.float32),
            pltpu.VMEM((8, D), jnp.float32),
            pltpu.VMEM((64, 128), jnp.float32),
        ],
    )
    mix_sum, out_sum, vectors_sum, bias_sum = on_core(
        finish_mix,
        [shape_of(24, 3 * D), shape_of(24, D), shape_of(8, 24), shape_of(1, 96)],
        (mix_total.own, *mix_others),
        0,
        room=12,
        scratch=[pltpu.VMEM((128, 128), jnp.float32)],
    )
    return (
        layer_output.reshape(2, SEG, D),
        input_grad.reshape(2, SEG, D),
        mix_sum,
        out_sum,
        up_sum,
        down_sum,
        vectors_sum,
        bias_sum.reshape(96),
        *cross_grads[:5],
        cross_grads[5].reshape(96),
        cross_grads[6],
    )


def solution(mesh):
    flat = dict(mesh.shape) == {"dp": 4, "seq": 8}
    return jax.shard_map(
        plane_shards if flat else shards,
        mesh=mesh,
        in_specs=(
            P("dp", "seq", None),
            P("dp", "seq", None),
            P("dp", "seq"),
            P("dp", None),
            P("dp", "seq"),
            P(("dp", "seq"), None),
            P(("dp", "seq"), None),
            P(("dp", "seq"), None),
            P(("dp", "seq"), None),
            P(None, ("dp", "seq")),
            P(("dp", "seq")),
            P(("dp", "seq"), None),
            P(("dp", "seq"), None),
            P(("dp", "seq"), None),
            P(("dp", "seq"), None),
            P(None, ("dp", "seq")),
            P(("dp", "seq")),
            P(None, ("dp", "seq")),
        ),
        out_specs=(
            P("dp", "seq", None),
            P("dp", "seq", None),
            P(("dp", "seq"), None),
            P(("dp", "seq"), None),
            P(("dp", "seq"), None),
            P(("dp", "seq"), None),
            P(None, ("dp", "seq")),
            P(("dp", "seq")),
            P(("dp", "seq"), None),
            P(("dp", "seq"), None),
            P(("dp", "seq"), None),
            P(("dp", "seq"), None),
            P(None, ("dp", "seq")),
            P(("dp", "seq")),
            P(None, ("dp", "seq")),
        ),
        check_vma=False,
    )
```

```python
from functools import partial
import math

import jax
import jax.numpy as jnp
from jax import lax
from jax.experimental import pallas as pl
from jax.experimental.pallas import tpu as pltpu
from jax.sharding import PartitionSpec as P

D = 768
HEADS = 12
HEAD_DIM = 64
SEG = 128
MICRO = 2


epsilon = 1e-05
masked_score = -1000000000.0
owner_dims = (0, 0, 0, 0, 1, 0, 0, 0, 0, 0, 1, 0, 1)


def layer_norm(values, gain_row, shift_row):
    centered = values - jnp.mean(values, axis=-1, keepdims=True)
    variance = jnp.mean(centered * centered, axis=-1, keepdims=True)
    return centered * lax.rsqrt(variance + epsilon) * gain_row + shift_row


def gelu_exact(hidden):
    return jax.nn.gelu(hidden, approximate=False)


def contract(left_side, right_side, left_dim, right_dim):
    return lax.dot_general(
        left_side,
        right_side,
        (((left_dim,), (right_dim,)), ((), ())),
        preferred_element_type=jnp.float32,
    )


def contract_exact(left_side, right_side, left_dim, right_dim):
    return lax.dot_general(
        left_side,
        right_side,
        (((left_dim,), (right_dim,)), ((), ())),
        precision=lax.Precision.HIGHEST,
        preferred_element_type=jnp.float32,
    )


def owner_pack(grads, devices):
    pieces = []
    for grad_value, split_dim in zip(grads, owner_dims):
        if split_dim == 0:
            pieces.append(grad_value.reshape(devices, -1))
        else:
            row_count = grad_value.shape[0]
            pieces.append(
                grad_value.reshape(row_count, devices, -1).transpose(1, 0, 2).reshape(devices, -1)
            )
    return jnp.concatenate(pieces, axis=1)


def owner_unpack(packed, shard_shapes):
    results = []
    offset = 0
    for shard_shape in shard_shapes:
        length = math.prod(shard_shape)
        results.append(packed[0, offset : offset + length].reshape(shard_shape))
        offset = offset + length
    return tuple(results)


def fetch_weights(
    local_mix,
    local_out,
    local_up,
    local_down,
    local_vectors,
    local_up_bias,
    cross_mix,
    cross_out,
    cross_up,
    cross_down,
    cross_vectors,
    cross_up_bias,
    position_table,
):
    return (
        lax.all_gather(local_mix, ("dp", "seq"), axis=0, tiled=True),
        lax.all_gather(local_out, ("dp", "seq"), axis=0, tiled=True),
        lax.all_gather(local_up, ("dp", "seq"), axis=0, tiled=True),
        lax.all_gather(local_down, ("dp", "seq"), axis=0, tiled=True),
        lax.all_gather(local_vectors, ("dp", "seq"), axis=1, tiled=True),
        lax.all_gather(local_up_bias, ("dp", "seq"), axis=0, tiled=True),
        lax.all_gather(cross_mix, ("dp", "seq"), axis=0, tiled=True),
        lax.all_gather(cross_out, ("dp", "seq"), axis=0, tiled=True),
        lax.all_gather(cross_up, ("dp", "seq"), axis=0, tiled=True),
        lax.all_gather(cross_down, ("dp", "seq"), axis=0, tiled=True),
        lax.all_gather(cross_vectors, ("dp", "seq"), axis=1, tiled=True),
        lax.all_gather(cross_up_bias, ("dp", "seq"), axis=0, tiled=True),
        lax.all_gather(position_table, ("dp", "seq"), axis=1, tiled=True),
    )


def segment_parts(mixed_rows, token_docs):
    segment_count = token_docs.shape[0]
    split_heads = mixed_rows.reshape(segment_count, SEG, 3, HEADS, HEAD_DIM)
    allowed = token_docs[:, None, :, None] == token_docs[:, None, None, :]
    scores = jnp.einsum(
        "nqhd,nkhd->nhqk",
        split_heads[:, :, 0],
        split_heads[:, :, 1],
        preferred_element_type=jnp.float32,
    ) * HEAD_DIM ** (-0.5)
    scores = jnp.where(allowed, scores, masked_score)
    return (split_heads, scores)


def segment_forward(mixed_rows, token_docs):
    split_heads, scores = segment_parts(mixed_rows, token_docs)
    log_total = jax.nn.logsumexp(scores, axis=-1)
    weights = jax.nn.softmax(scores, axis=-1).astype(jnp.bfloat16)
    context = jnp.einsum(
        "nhqk,nkhd->nqhd", weights, split_heads[:, :, 2], preferred_element_type=jnp.float32
    )
    return (context.reshape(-1, D).astype(jnp.bfloat16), log_total)


def segment_backward(context_grad, log_total, mixed_rows, token_docs):
    split_heads, scores = segment_parts(mixed_rows, token_docs)
    segment_count = token_docs.shape[0]
    probs = jnp.exp(scores - log_total[..., None])
    grad_heads = context_grad.reshape(segment_count, SEG, HEADS, HEAD_DIM)
    prob_grad = jnp.einsum(
        "nqhd,nkhd->nhqk", grad_heads, split_heads[:, :, 2], preferred_element_type=jnp.float32
    )
    value_grad = jnp.einsum(
        "nhqk,nqhd->nkhd",
        probs.astype(jnp.bfloat16),
        grad_heads,
        preferred_element_type=jnp.float32,
    )
    score_grad = probs * (prob_grad - jnp.sum(probs * prob_grad, axis=-1, keepdims=True))
    score_low = score_grad.astype(jnp.bfloat16) * HEAD_DIM ** (-0.5)
    query_grad = jnp.einsum(
        "nhqk,nkhd->nqhd", score_low, split_heads[:, :, 1], preferred_element_type=jnp.float32
    )
    key_grad = jnp.einsum(
        "nhqk,nqhd->nkhd", score_low, split_heads[:, :, 0], preferred_element_type=jnp.float32
    )
    row_total = segment_count * SEG
    return jnp.concatenate(
        [
            query_grad.reshape(row_total, D),
            key_grad.reshape(row_total, D),
            value_grad.reshape(row_total, D),
        ],
        axis=1,
    )


def cross_parts(mixed_rows, gathered, segment_docs):
    group_size = segment_docs.shape[0]
    per_device = mixed_rows.shape[0] // group_size
    query_rows = mixed_rows[:, :D].reshape(group_size, per_device, HEADS, HEAD_DIM)
    key_rows = gathered[:, :, :D].reshape(group_size, -1, HEADS, HEAD_DIM)
    value_rows = gathered[:, :, D:].reshape(group_size, -1, HEADS, HEAD_DIM)
    own_docs = lax.dynamic_slice_in_dim(
        segment_docs, lax.axis_index("seq") * per_device, per_device, 1
    )
    allowed = own_docs[:, None, :, None] == segment_docs[:, None, None, :]
    scores = jnp.einsum(
        "bqhd,bkhd->bhqk", query_rows, key_rows, preferred_element_type=jnp.float32
    ) * HEAD_DIM ** (-0.5)
    scores = jnp.where(allowed, scores, masked_score)
    return (query_rows, key_rows, value_rows, scores)


def cross_forward(mixed_rows, segment_docs):
    group_size = segment_docs.shape[0]
    per_device = mixed_rows.shape[0] // group_size
    pair_rows = mixed_rows[:, D:].reshape(group_size, per_device, 2 * D)
    gathered = lax.all_gather(pair_rows, "seq", axis=1, tiled=True)
    query_rows, key_rows, value_rows, scores = cross_parts(mixed_rows, gathered, segment_docs)
    log_total = jax.nn.logsumexp(scores, axis=-1)
    weights = jax.nn.softmax(scores, axis=-1).astype(jnp.bfloat16)
    context = jnp.einsum("bhqk,bkhd->bqhd", weights, value_rows, preferred_element_type=jnp.float32)
    return (context.reshape(-1, D).astype(jnp.bfloat16), (gathered, log_total))


def cross_backward(context_grad, cross_kept, mixed_rows, segment_docs):
    gathered, log_total = cross_kept
    group_size = segment_docs.shape[0]
    row_total = mixed_rows.shape[0]
    per_device = row_total // group_size
    query_rows, key_rows, value_rows, scores = cross_parts(mixed_rows, gathered, segment_docs)
    probs = jnp.exp(scores - log_total[..., None])
    grad_heads = context_grad.reshape(group_size, per_device, HEADS, HEAD_DIM)
    prob_grad = jnp.einsum(
        "bqhd,bkhd->bhqk", grad_heads, value_rows, preferred_element_type=jnp.float32
    )
    value_grad = jnp.einsum(
        "bhqk,bqhd->bkhd",
        probs.astype(jnp.bfloat16),
        grad_heads,
        preferred_element_type=jnp.float32,
    )
    score_grad = probs * (prob_grad - jnp.sum(probs * prob_grad, axis=-1, keepdims=True))
    score_low = score_grad.astype(jnp.bfloat16) * HEAD_DIM ** (-0.5)
    query_grad = jnp.einsum(
        "bhqk,bkhd->bqhd", score_low, key_rows, preferred_element_type=jnp.float32
    )
    key_grad = jnp.einsum(
        "bhqk,bqhd->bkhd", score_low, query_rows, preferred_element_type=jnp.float32
    )
    pair_grads = jnp.concatenate(
        [key_grad.reshape(group_size, -1, D), value_grad.reshape(group_size, -1, D)], axis=2
    )
    own_pairs = lax.psum_scatter(
        pair_grads.astype(jnp.bfloat16), "seq", scatter_dimension=1, tiled=True
    ).astype(jnp.float32)
    return jnp.concatenate(
        [query_grad.reshape(row_total, D), own_pairs.reshape(row_total, 2 * D)], axis=1
    )


def block_forward(inputs, weights, attend):
    mix_weight, out_weight, up_weight, down_weight, vectors, up_bias = weights
    vector_rows = vectors.astype(jnp.float32)
    in_bias = jnp.concatenate([vector_rows[0], jnp.zeros_like(vector_rows[0]), vector_rows[1]])
    rounded = inputs.astype(jnp.bfloat16)
    mixed_rows = (
        jnp.dot(rounded, mix_weight, preferred_element_type=jnp.float32) + in_bias
    ).astype(jnp.bfloat16)
    context, attend_kept = attend(mixed_rows)
    first_sum = (
        inputs + jnp.dot(context, out_weight, preferred_element_type=jnp.float32) + vector_rows[2]
    )
    first_norm = layer_norm(first_sum, vector_rows[3], vector_rows[4])
    first_low = first_norm.astype(jnp.bfloat16)
    hidden = jnp.dot(first_low, up_weight, preferred_element_type=jnp.float32) + up_bias.astype(
        jnp.float32
    )
    active = gelu_exact(hidden).astype(jnp.bfloat16)
    second_sum = (
        first_norm
        + jnp.dot(active, down_weight, preferred_element_type=jnp.float32)
        + vector_rows[5]
    )
    output = layer_norm(second_sum, vector_rows[6], vector_rows[7])
    return (
        output,
        (
            rounded,
            mixed_rows,
            attend_kept,
            context,
            first_sum,
            first_low,
            hidden,
            active,
            second_sum,
        ),
    )


def block_backward(output_grad, block_kept, weights, attend_back):
    mix_weight, out_weight, up_weight, down_weight, vectors, up_bias = weights
    vector_rows = vectors.astype(jnp.float32)
    rounded, mixed_rows, attend_kept, context, first_sum, first_low, hidden, active, second_sum = (
        block_kept
    )
    unused, second_pull = jax.vjp(layer_norm, second_sum, vector_rows[6], vector_rows[7])
    second_grad, gain_two, shift_two = second_pull(output_grad)
    second_low = second_grad.astype(jnp.bfloat16)
    down_grad = contract(active, second_low, 0, 0)
    down_bias = jnp.sum(second_low.astype(jnp.float32), axis=0)
    active_grad = contract(second_low, down_weight, 1, 1)
    unused, gelu_pull = jax.vjp(gelu_exact, hidden)
    hidden_grad = gelu_pull(active_grad)[0]
    hidden_low = hidden_grad.astype(jnp.bfloat16)
    up_grad = contract(first_low, hidden_low, 0, 0)
    up_bias_grad = jnp.sum(hidden_low.astype(jnp.float32), axis=0)
    first_grad = second_grad + contract(hidden_low, up_weight, 1, 1)
    unused, first_pull = jax.vjp(layer_norm, first_sum, vector_rows[3], vector_rows[4])
    sum_grad, gain_one, shift_one = first_pull(first_grad)
    branch_low = sum_grad.astype(jnp.bfloat16)
    out_grad = contract(context, branch_low, 0, 0)
    out_bias = jnp.sum(branch_low.astype(jnp.float32), axis=0)
    context_low = contract(branch_low, out_weight, 1, 1).astype(jnp.bfloat16)
    mixed_low = attend_back(context_low, attend_kept, mixed_rows).astype(jnp.bfloat16)
    mix_grad = contract(rounded, mixed_low, 0, 0)
    mixed_sums = jnp.sum(mixed_low.astype(jnp.float32), axis=0)
    input_grad = sum_grad + contract(mixed_low, mix_weight, 1, 1)
    vectors_grad = jnp.stack(
        [
            mixed_sums[:D],
            mixed_sums[2 * D :],
            out_bias,
            gain_one,
            shift_one,
            down_bias,
            gain_two,
            shift_two,
        ]
    )
    return (input_grad, (mix_grad, out_grad, up_grad, down_grad, vectors_grad, up_bias_grad))


def shards(
    tokens,
    cotangent,
    token_docs,
    segment_docs,
    segment_positions,
    local_mix,
    local_out,
    local_up,
    local_down,
    local_vectors,
    local_up_bias,
    cross_mix,
    cross_out,
    cross_up,
    cross_down,
    cross_vectors,
    cross_up_bias,
    position_table,
):
    sequence_count, span, width = tokens.shape
    group_size = sequence_count // MICRO
    segment_count = span // SEG
    devices = lax.axis_size(("dp", "seq"))
    shard_shapes = tuple(
        (
            array_in.shape
            for array_in in (
                local_mix,
                local_out,
                local_up,
                local_down,
                local_vectors,
                local_up_bias,
                cross_mix,
                cross_out,
                cross_up,
                cross_down,
                cross_vectors,
                cross_up_bias,
                position_table,
            )
        )
    )
    layer_outputs = []
    input_grads = []
    totals = ()
    for micro_step in range(MICRO):
        lower_row = micro_step * group_size
        upper_row = lower_row + group_size
        gathered = fetch_weights(
            local_mix,
            local_out,
            local_up,
            local_down,
            local_vectors,
            local_up_bias,
            cross_mix,
            cross_out,
            cross_up,
            cross_down,
            cross_vectors,
            cross_up_bias,
            position_table,
        )
        local_weights = gathered[0:6]
        cross_weights = gathered[6:12]
        position_rows = gathered[12]
        inputs = tokens[lower_row:upper_row].reshape(group_size * span, width).astype(jnp.float32)
        docs_here = token_docs[lower_row:upper_row]
        segments_here = segment_docs[lower_row:upper_row]
        first_out, first_kept = block_forward(
            inputs, local_weights, partial(segment_forward, token_docs=docs_here)
        )
        segment_grid = first_out.reshape(group_size * segment_count, SEG, width)
        places = segment_positions[lower_row:upper_row].reshape(group_size * segment_count)
        position_picks = (
            places[:, None] == jnp.arange(position_rows.shape[0], dtype=jnp.int32)[None, :]
        ).astype(jnp.bfloat16)
        heads_in = segment_grid[:, 0, :] + jnp.dot(
            position_picks, position_rows, preferred_element_type=jnp.float32
        )
        heads_out, cross_kept = block_forward(
            heads_in, cross_weights, partial(cross_forward, segment_docs=segments_here)
        )
        joined = jnp.concatenate([heads_out[:, None, :], segment_grid[:, 1:, :]], axis=1)
        layer_outputs.append(joined.astype(jnp.bfloat16))
        gathered = fetch_weights(
            local_mix,
            local_out,
            local_up,
            local_down,
            local_vectors,
            local_up_bias,
            cross_mix,
            cross_out,
            cross_up,
            cross_down,
            cross_vectors,
            cross_up_bias,
            position_table,
        )
        local_weights = gathered[0:6]
        cross_weights = gathered[6:12]
        output_grad = cotangent[lower_row:upper_row].astype(jnp.float32)
        heads_grad, cross_grads = block_backward(
            output_grad[:, 0, :],
            cross_kept,
            cross_weights,
            partial(cross_backward, segment_docs=segments_here),
        )
        table_grad = contract_exact(position_picks.astype(jnp.float32), heads_grad, 0, 0)
        first_grad = jnp.concatenate(
            [heads_grad[:, None, :], output_grad[:, 1:, :]], axis=1
        ).reshape(group_size * span, width)
        input_grad, local_grads = block_backward(
            first_grad, first_kept, local_weights, partial(segment_backward, token_docs=docs_here)
        )
        input_grads.append(input_grad.reshape(group_size, span, width))
        step_grads = local_grads + cross_grads + (table_grad,)
        if micro_step == 0:
            totals = tuple(step_grads)
        else:
            totals = tuple(
                (total_sum + step_sum for total_sum, step_sum in zip(totals, step_grads))
            )
    packed_total = lax.psum_scatter(
        owner_pack(totals, devices), ("dp", "seq"), scatter_dimension=0, tiled=True
    )
    summed = owner_unpack(packed_total, shard_shapes)
    layer_output = jnp.concatenate(layer_outputs, axis=0)
    input_gradient = jnp.concatenate(input_grads, axis=0)
    return (layer_output, input_gradient) + tuple(summed)


def swap_dp(array_in, shift):
    return lax.ppermute(array_in, "dp", [(i, (i + shift) % 4) for i in range(4)])


def swap_core(array_in):
    return lax.ppermute(array_in, "seq", [(i, i ^ 1) for i in range(8)])


def swap_chip(array_in, mask):
    return lax.ppermute(array_in, "seq", [(i, i ^ (2 * mask)) for i in range(8)])


def swap_one(array_in):
    return lax.ppermute(array_in, "seq", [(i, i ^ (2 if i % 2 == 0 else 4)) for i in range(8)])


def swap_two(array_in):
    return lax.ppermute(array_in, "seq", [(i, i ^ (4 if i % 2 == 0 else 2)) for i in range(8)])


def place_in():
    layer = lax.axis_index("dp")
    spot = lax.axis_index("seq")
    return layer, spot // 2, lax.rem(spot, 2)


def after(array_in, *before):
    return lax.optimization_barrier((array_in,) + before)[0]


def stage(*values):
    return lax.optimization_barrier(values)


def wide(array_in):
    return array_in.astype(jnp.float32)


def low(array_in):
    return array_in.astype(jnp.bfloat16)


def copies(pieces, shapes, moves, room=64):
    count, made = len(pieces), len(shapes)
    total = len(moves(0, 0, 0))

    def kernel(*refs):
        outs, held, sems = refs[count : count + made], refs[count + made : -1], refs[-1]
        inward = [pltpu.make_async_copy(refs[i], held[i], sems.at[0, i]) for i in range(count)]
        for copy in inward:
            copy.start()
        outward = []
        for i, (piece, part, out, place) in enumerate(moves(*place_in())):
            if inward[piece] is not None:
                inward[piece].wait()
                inward[piece] = None
            copy = pltpu.make_async_copy(held[piece].at[part], outs[out].at[place], sems.at[1, i])
            copy.start()
            outward.append(copy)
        for copy in outward:
            copy.wait()

    size = 2 * sum(math.prod(shape) for shape in shapes) * 2
    return pl.pallas_call(
        kernel,
        out_shape=[jax.ShapeDtypeStruct(shape, pieces[0].dtype) for shape in shapes],
        in_specs=[pl.BlockSpec(memory_space=pltpu.HBM)] * count,
        out_specs=[pl.BlockSpec(memory_space=pltpu.HBM)] * made,
        scratch_shapes=[pltpu.VMEM(piece.shape, piece.dtype) for piece in pieces]
        + [pltpu.SemaphoreType.DMA((2, max(count, total)))],
        compiler_params=pltpu.CompilerParams(vmem_limit_bytes=room * 2**20),
        cost_estimate=pl.CostEstimate(flops=0, bytes_accessed=0, transcendentals=0),
    )(*pieces)


every = slice(None)


def reach_dp(shard):
    return [shard] + [swap_dp(shard, shift) for shift in (1, 2, 3)]


def join_dp(pieces):
    return copies(
        pieces,
        [(4,) + pieces[0].shape],
        lambda layer, chip, core: [(i, every, 0, lax.rem(layer + 4 - i, 4)) for i in range(4)],
    )[0]


def plane_order(chip, core):
    near, far = chip ^ (1 + core), chip ^ (2 - core)
    return (chip, near, far, chip ^ 3), (chip, far, near, chip ^ 3)


def join_chips(pieces):
    def moves(layer, chip, core):
        return [(i, every, 0, spot) for i, spot in enumerate(plane_order(chip, core)[0])]

    return copies(pieces, [(4,) + pieces[0].shape], moves)[0]


def gather_plane(mine, others):
    def moves(layer, chip, core):
        own, other = plane_order(chip, core)
        found = [(i, every, 0, (every, own[i], core)) for i in range(4)]
        return found + [(4 + i, every, 0, (every, other[i], 1 - core)) for i in range(4)]

    shape = (4, 4, 2) + mine[0].shape[1:]
    return copies(mine + others, [shape], moves)[0]


def gather_up(mine, others):
    def moves(layer, chip, core):
        own, other = plane_order(chip, core)
        found = []
        for i in range(8):
            spot, side = (own[i], core) if i < 4 else (other[i - 4], 1 - core)
            for out, lanes in enumerate((slice(0, 4 * D), slice(4 * D, 5 * D))):
                found.append((i, (every, every, lanes), out, (every, spot, side)))
        return found

    up, out = copies(mine + others, [(4, 4, 2, 24, 4 * D), (4, 4, 2, 24, D)], moves)
    return up.reshape(D, 4 * D), out.reshape(D, D)


def gather_down(mine, others):
    def moves(layer, chip, core):
        own, other = plane_order(chip, core)
        found = []
        for i in range(8):
            spot, side = (own[i], core) if i < 4 else (other[i - 4], 1 - core)
            for quarter in range(4):
                part = (every, every, slice(quarter * D, (quarter + 1) * D))
                found.append((i, part, 0, (every, spot, side, quarter)))
        return found

    return copies(mine + others, [(4, 4, 2, 4, 24, D)], moves)[0]


class Sum:
    def __init__(self, kept):
        self.kept = kept
        self.shape = kept.shape[2:]

    def run(self, operands, out_shapes, plan):
        shape, count, made = self.shape, len(operands), len(out_shapes)
        dry = plan(0, 0, 0)
        pieces = sum(len(sources) for sources, target in dry)

        def kernel(*refs):
            given, outs = refs[:count], refs[count : count + made]
            held, built, sems = refs[count + made : -len(dry) - 1], refs[-len(dry) - 1 : -1], refs[-1]
            inward, outward, steps = [], [], []
            for sources, target in plan(*place_in()):
                step = []
                for operand, index in sources:
                    spot = len(inward)
                    source = given[operand].at[index]
                    copy = pltpu.make_async_copy(source, held[spot], sems.at[0, spot])
                    copy.start()
                    inward.append(copy)
                    step.append(spot)
                steps.append((step, target))
            for place, (step, (out, index)) in enumerate(steps):
                total = None
                for spot in step:
                    inward[spot].wait()
                    value = wide(held[spot][...])
                    total = value if total is None else total + value
                built[place][...] = total.astype(built[place].dtype)
                target = outs[out] if index is None else outs[out].at[index]
                copy = pltpu.make_async_copy(built[place], target, sems.at[1, place])
                copy.start()
                outward.append(copy)
            for copy in outward:
                copy.wait()

        far = pl.BlockSpec(memory_space=pltpu.HBM)
        return pl.pallas_call(
            kernel,
            out_shape=out_shapes,
            in_specs=[far] * count,
            out_specs=[far] * made,
            scratch_shapes=[pltpu.VMEM(shape, jnp.bfloat16)] * pieces
            + [pltpu.VMEM(shape, out_shapes[target[0]].dtype) for sources, target in dry]
            + [pltpu.SemaphoreType.DMA((2, pieces))],
            compiler_params=pltpu.CompilerParams(vmem_limit_bytes=64 * 2**20),
            cost_estimate=pl.CostEstimate(flops=0, bytes_accessed=0, transcendentals=0),
        )(*operands)

    def first(self, got):
        self.got = got

        def plan(layer, chip, core):
            return [
                ([(0, (z, spot)), (1, (z, spot))], (0, (i, z)))
                for i, spot in enumerate((chip ^ (1 + core), chip ^ 3))
                for z in range(4)
            ]

        return self.run([self.kept, got], [half(2, 4, *self.shape)], plan)[0]

    def second(self, back):
        self.back = back

        def plan(layer, chip, core):
            spot = chip ^ (2 - core)
            return [
                ([(0, (z, spot)), (1, (z, spot)), (2, (1, z))], (0, z)) for z in range(4)
            ]

        return self.run([self.kept, self.got, back], [half(4, *self.shape)], plan)[0]

    def third(self, last):
        def plan(layer, chip, core):
            found = []
            for shift in (1, 2, 3, 0):
                z = lax.rem(layer + shift, 4)
                sources = [(0, (z, chip)), (1, (z, chip)), (2, (0, z)), (3, z)]
                found.append((sources, (shift, None)))
            return found

        self.own, *others = self.run(
            [self.kept, self.got, self.back, last],
            [shape_of(*self.shape)] + [half(*self.shape)] * 3,
            plan,
        )
        return others

    def total(self, others):
        return self.own + wide(others[0]) + wide(others[1]) + wide(others[2])


def send_dp(others):
    return [swap_dp(other, shift) for shift, other in zip((1, 2, 3), others)]


def norm_parts(values):
    centered = values - jnp.mean(values, axis=-1, keepdims=True)
    variance = jnp.mean(centered * centered, axis=-1, keepdims=True)
    scale = lax.rsqrt(variance + epsilon)
    return centered * scale, scale


def norm_back(grad, normed, scale, gain):
    scaled = grad * gain
    return scale * (
        scaled
        - jnp.mean(scaled, axis=-1, keepdims=True)
        - normed * jnp.mean(scaled * normed, axis=-1, keepdims=True)
    )


def gelu_slope(hidden):
    return 0.5 * (1.0 + lax.erf(hidden * math.sqrt(0.5))) + hidden * jnp.exp(
        -0.5 * hidden * hidden
    ) * (1.0 / math.sqrt(2.0 * math.pi))


def shape_of(*shape, dtype=jnp.float32):
    return jax.ShapeDtypeStruct(shape, dtype)


def half(*shape):
    return jax.ShapeDtypeStruct(shape, jnp.bfloat16)


def on_core(kernel, out_shape, operands, flops, room=64, grid=(), in_specs=None, out_specs=None, scratch=()):
    arrays = jax.tree.leaves(out_shape) + list(operands)
    size = sum(math.prod(a.shape) * a.dtype.itemsize for a in arrays)
    extra = {} if in_specs is None else {"in_specs": in_specs, "out_specs": out_specs}
    return pl.pallas_call(
        kernel,
        out_shape=out_shape,
        grid=grid,
        scratch_shapes=scratch,
        compiler_params=pltpu.CompilerParams(vmem_limit_bytes=room * 2**20),
        cost_estimate=pl.CostEstimate(flops=0, bytes_accessed=0, transcendentals=0),
        **extra,
    )(*operands)


def column_sum(array_in):
    return jnp.sum(array_in, axis=0, keepdims=True)


def prepare(*refs):
    given, made, held, built = refs[0:12], refs[12:19], refs[19:31], refs[31:38]
    small, turned, parts, sems = refs[38:]
    inward = [pltpu.make_async_copy(given[i], held[i], sems.at[0, i]) for i in range(12)]
    outward = [pltpu.make_async_copy(built[i], made[i], sems.at[1, i]) for i in range(7)]
    for copy in inward:
        copy.start()
    for copy in inward:
        copy.wait()
    mix_ref, out_ref, up_ref, down_ref, vectors_ref, bias_ref = held[0:6]
    cross_mix_ref, cross_out_ref, cross_up_ref, cross_vectors_ref, cross_bias_ref, table_ref = held[6:]
    one_ref, two_ref, three_ref = built[0:3]
    one_ref[:, 0 : 3 * D] = mix_ref[...]
    one_ref[:, 3 * D : 4 * D] = out_ref[...]
    small[...] = jnp.zeros_like(small)
    small[0:8, 0:24] = wide(vectors_ref[...])
    small[8:16, 0:24] = wide(cross_vectors_ref[...])
    for row in range(4):
        lanes = slice(24 * row, 24 * (row + 1))
        small[80 + row : 81 + row, 0:24] = wide(bias_ref[:, lanes])
        small[84 + row : 85 + row, 0:24] = wide(cross_bias_ref[:, lanes])
    turned[...] = small[...].T
    turned[0:24, 16:80] = wide(table_ref[...])
    one_ref[:, 4 * D : 4 * D + 128] = low(turned[0:24, :])
    outward[0].start()
    two_ref[:, 0 : 4 * D] = up_ref[...]
    two_ref[:, 4 * D : 5 * D] = cross_out_ref[...]
    for quarter in range(4):
        three_ref[:, quarter * D : (quarter + 1) * D] = down_ref[quarter]
    outward[1].start()
    outward[2].start()
    parts[...] = jnp.zeros_like(parts)
    for spot in range(4):
        for level in range(4):
            taken = cross_up_ref[:, 192 * (4 * level + spot) : 192 * (4 * level + spot + 1)]
            parts[spot, :, 192 * level : 192 * (level + 1)] = taken
        for third in range(3):
            taken = cross_mix_ref[:, third * D + 192 * spot : third * D + 192 * (spot + 1)]
            parts[spot, :, D + 192 * third : D + 192 * (third + 1)] = taken
    chip = place_in()[1]
    for mask in range(4):
        built[3 + mask][...] = parts[chip ^ mask]
        outward[3 + mask].start()
    for copy in outward:
        copy.wait()


def join_cross(pieces, cross_down):
    def moves(layer, chip, core):
        found = []
        for mask in range(4):
            found.append((mask, (every, slice(0, D)), 0, (chip ^ mask, every, slice(0, D))))
            taken = (every, slice(D, D + 640))
            found.append((mask, taken, 0, (chip ^ mask, every, slice(2 * D, 2 * D + 640))))
        found.append((4, every, 0, (every, every, slice(D, 2 * D))))
        return found

    return copies(pieces + [cross_down.reshape(4, 24, D)], [(4, 24, 2 * D + 640)], moves)[0]


def place_cross(column, other):
    def moves(layer, chip, core):
        found = []
        for piece, side in ((0, core), (1, 1 - core)):
            source, lead = (every, every, every), (every, every, side)
            found.append((piece, source + (slice(0, D),), 0, lead))
            found.append((piece, source + (slice(2 * D, 2 * D + 640),), 1, lead))
            found.append((piece, source + (slice(D, 2 * D),), 2, (every, side)))
        return found

    up, mix, down = copies(
        [column, other], [(4, 4, 2, 24, D), (4, 4, 2, 24, 640), (4, 2, 4, 24, D)], moves
    )
    return up.reshape(D, D), mix.reshape(D, 640), down.reshape(D, D)


def segment_heads(segment, mixed_ref, docs_ref, probs_ref, context_ref):
    lane = lax.broadcasted_iota(jnp.int32, (SEG, 128), 1)
    rows = slice(segment * SEG, (segment + 1) * SEG)
    docs = jnp.broadcast_to(wide(docs_ref[segment : segment + 1, :]), (SEG, SEG))
    allowed = docs == docs.T
    for pair in range(HEADS // 2):
        query, key, value = (
            mixed_ref[rows, third * D + pair * 128 : third * D + (pair + 1) * 128]
            for third in range(3)
        )
        found = []
        for side in range(2):
            here = (lane < HEAD_DIM) if side == 0 else (lane >= HEAD_DIM)
            scores = contract(key, jnp.where(here, query, jnp.zeros_like(query)), 1, 1)
            scores = jnp.where(allowed, scores * HEAD_DIM ** (-0.5), masked_score)
            powers = jnp.exp(scores - jnp.max(scores, axis=0, keepdims=True))
            probs = powers / jnp.sum(powers, axis=0, keepdims=True)
            probs_ref[2 * pair + side] = probs
            found.append(contract(low(probs), value, 0, 0))
        context = jnp.where(lane < HEAD_DIM, found[0], found[1])
        context_ref[:, pair * 128 : (pair + 1) * 128] = low(context)


def local_attend(tokens_ref, group_ref, docs_ref, places_ref, *outs):
    mixed_ref, context_ref, probs_ref, rows_ref, places_out = outs
    rows_ref[...] = wide(group_ref[:, 4 * D : 4 * D + 128]).T
    lane = lax.broadcasted_iota(jnp.int32, (1, 64), 1)
    for place in range(2):
        picked = wide(places_ref[:, place : place + 1] == lane)
        places_out[place : place + 1, :] = contract_exact(picked, rows_ref[16:80, :], 1, 0)
    tokens = tokens_ref[...]
    for third in range(3):
        columns = slice(third * D, (third + 1) * D)
        mixed = contract(tokens, group_ref[:, columns], 1, 0)
        if third != 1:
            mixed = mixed + rows_ref[third // 2 : third // 2 + 1, :]
        mixed_ref[:, columns] = low(mixed)
    segment_heads(0, mixed_ref, docs_ref, probs_ref, context_ref)


def local_attend_more(
    tokens_ref, mixed_ref, before_ref, weight_ref, rows_ref, docs_ref, *outs
):
    context_ref, probs_ref, n_ref, scale_ref, low_ref, here = outs
    segment_heads(1, mixed_ref, docs_ref, probs_ref, here)
    context_ref[0:SEG, :] = before_ref[...]
    context_ref[SEG : 2 * SEG, :] = here[...]
    total = wide(tokens_ref[...]) + contract(context_ref[...], weight_ref[...], 1, 0)
    normed, scale = norm_parts(total + rows_ref[2:3, :])
    n_ref[...] = normed
    scale_ref[...] = scale
    low_ref[...] = low(normed * rows_ref[3:4, :] + rows_ref[4:5, :])


def local_up_part(low_ref, weight_ref, bias_ref, active_ref, slope_ref):
    hidden = contract(low_ref[...], weight_ref[...], 1, 0) + wide(bias_ref[...])
    chance = 0.5 * (1.0 + lax.erf(hidden * math.sqrt(0.5)))
    density = jnp.exp(-0.5 * hidden * hidden) * (1.0 / math.sqrt(2.0 * math.pi))
    active_ref[...] = low(hidden * chance)
    slope_ref[...] = low(chance + hidden * density)


def local_down_part(
    active_ref, weight_ref, first_ref, rows_ref, cot_a, cot_b, places_ref, *outs
):
    n_ref, scale_ref, kept_ref, given_ref, total = outs
    step = pl.program_id(0)
    part = contract(active_ref[...], weight_ref[...], 1, 0)

    @pl.when(step == 0)
    def _():
        first_norm = first_ref[...] * rows_ref[3:4, :] + rows_ref[4:5, :]
        total[...] = first_norm + rows_ref[5:6, :] + part

    @pl.when(step > 0)
    def _():
        total[...] += part

    @pl.when(step == 1)
    def _():
        normed, scale = norm_parts(total[...])
        n_ref[...] = normed
        scale_ref[...] = scale
        core = place_in()[2]
        heads, grads = [], []
        for place, cot in ((0, cot_a), (1, cot_b)):
            row = normed[place * SEG : place * SEG + 1] * rows_ref[6:7, :] + rows_ref[7:8, :]
            heads.append(row + places_ref[place : place + 1, :])
            grads.append(wide(cot[...])[0:1])
        for ref, mine in ((kept_ref, core == 0), (given_ref, core == 1)):
            ref[...] = jnp.zeros_like(ref)
            ref[0:1, :] = jnp.where(mine, heads[0], heads[1])
            ref[1:2, :] = jnp.where(mine, grads[0], grads[1])


def join_pair(kept_ref, got_ref, out_ref):
    core = place_in()[2]
    out_ref[...] = jnp.zeros_like(out_ref)
    out_ref[0:2, :] = jnp.where(core == 0, kept_ref[0:2, :], got_ref[0:2, :])
    out_ref[2:4, :] = jnp.where(core == 0, got_ref[0:2, :], kept_ref[0:2, :])


def cross_attend(
    own_ref, a_ref, b_ref, c_ref, weight_ref, rows_ref, docs_ref, *outs
):
    in_ref, grad_ref, mixed_ref, probs_ref, context_ref = outs
    layer, chip, core = place_in()
    for mask, ref in enumerate((own_ref, a_ref, b_ref, c_ref)):
        for side in range(2):
            row = 2 * (chip ^ mask) + side
            in_ref[pl.ds(row, 1), :] = ref[2 * side : 2 * side + 1, :]
            grad_ref[pl.ds(row, 1), :] = ref[2 * side + 1 : 2 * side + 2, :]
    biases = []
    for vector in (8, 9):
        row = rows_ref[vector : vector + 1, :]
        found = row[:, 0:192]
        for spot in range(1, 4):
            found = jnp.where(chip == spot, row[:, 192 * spot : 192 * (spot + 1)], found)
        biases.append(found)
    bias = jnp.concatenate([biases[0], jnp.zeros_like(biases[0]), biases[1]], axis=1)
    mixed = low(contract(low(in_ref[...]), weight_ref[:, 0:576], 1, 0) + bias)
    mixed_ref[...] = mixed
    row_docs = wide(jnp.where(core == 0, docs_ref[0:1, :], docs_ref[1:2, :]))
    count = row_docs.shape[1]
    lane = lax.broadcasted_iota(jnp.int32, (count, count), 1)
    line = lax.broadcasted_iota(jnp.int32, (count, count), 0)
    column_docs = jnp.sum(jnp.where(lane == line, row_docs, 0.0), axis=1, keepdims=True)
    allowed = row_docs == column_docs
    found = []
    for head in range(3):
        query, key, value = (
            mixed[:, third * 192 + head * HEAD_DIM : third * 192 + (head + 1) * HEAD_DIM]
            for third in range(3)
        )
        scores = contract(query, key, 1, 1) * HEAD_DIM ** (-0.5)
        scores = jnp.where(allowed, scores, masked_score)
        powers = jnp.exp(scores - jnp.max(scores, axis=-1, keepdims=True))
        probs = powers / jnp.sum(powers, axis=-1, keepdims=True)
        probs_ref[head] = probs
        found.append(contract(low(probs), value, 1, 0))
    context_ref[...] = low(jnp.concatenate(found, axis=1))


def cross_up_down(
    own_ref, a_ref, b_ref, c_ref, in_ref, out_weight_ref, rows_ref, up_ref, bias_ref, down_ref, *outs
):
    n_ref, scale_ref, low_ref, hidden_ref, active_ref, part_ref = outs
    chip = place_in()[1]
    total = in_ref[...] + rows_ref[10:11, :]
    for mask, ref in enumerate((own_ref, a_ref, b_ref, c_ref)):
        start = pl.multiple_of(192 * (chip ^ mask), 64)
        total = total + contract(ref[...], out_weight_ref[pl.ds(start, 192), :], 1, 0)
    normed, scale = norm_parts(total)
    n_ref[...] = normed
    scale_ref[...] = scale
    first = low(normed * rows_ref[11:12, :] + rows_ref[12:13, :])
    low_ref[...] = first
    hidden = contract(first, up_ref[...], 1, 0) + bias_ref[...]
    hidden_ref[...] = hidden
    active = low(hidden * (0.5 * (1.0 + lax.erf(hidden * math.sqrt(0.5)))))
    active_ref[...] = active
    part_ref[...] = contract(active, down_ref[...], 1, 0)


def cross_turn(
    own_ref, a_ref, b_ref, c_ref, n_ref, rows_ref, grad_ref, hidden_ref, up_ref, down_ref, *outs
):
    out_ref, second_ref, hidden_low_ref, part_ref, sums_ref = outs
    first = n_ref[...] * rows_ref[11:12, :] + rows_ref[12:13, :]
    total = (own_ref[...] + a_ref[...]) + (b_ref[...] + c_ref[...])
    normed, scale = norm_parts(first + total + rows_ref[13:14, :])
    out_ref[...] = normed * rows_ref[14:15, :] + rows_ref[15:16, :]
    grad = grad_ref[...]
    second = norm_back(grad, normed, scale, rows_ref[14:15, :])
    second_ref[...] = second
    hidden_low = low(contract(low(second), down_ref[...], 1, 1) * gelu_slope(hidden_ref[...]))
    hidden_low_ref[...] = hidden_low
    part_ref[...] = contract(hidden_low, up_ref[...], 1, 1)
    sums_ref[...] = jnp.zeros_like(sums_ref)
    sums_ref[0:1, :] = column_sum(grad * normed)
    sums_ref[1:2, :] = column_sum(grad)


def cross_attend_back(
    own_ref,
    a_ref,
    b_ref,
    c_ref,
    second_ref,
    n_ref,
    scale_ref,
    rows_ref,
    out_weight_ref,
    mixed_ref,
    probs_ref,
    weight_ref,
    hidden_low_ref,
    active_ref,
    context_ref,
    in_ref,
    low_ref,
    sums_ref,
    places_ref,
    total_ref,
    part_ref,
    pack_ref,
    pack,
    rows,
):
    chip = place_in()[1]
    grad = second_ref[...] + (own_ref[...] + a_ref[...]) + (b_ref[...] + c_ref[...])
    normed = n_ref[...]
    total = norm_back(grad, normed, scale_ref[...], rows_ref[11:12, :])
    total_ref[...] = total
    branch = low(total)
    start = pl.multiple_of(192 * chip, 64)
    context_low = low(contract(branch, out_weight_ref[pl.ds(start, 192), :], 1, 1))
    mixed = mixed_ref[...]
    found = [[], [], []]
    for head in range(3):
        query, key, value = (
            mixed[:, third * 192 + head * HEAD_DIM : third * 192 + (head + 1) * HEAD_DIM]
            for third in range(3)
        )
        part = context_low[:, head * HEAD_DIM : (head + 1) * HEAD_DIM]
        probs = probs_ref[head]
        prob_grad = contract(part, value, 1, 1)
        score = low(probs * (prob_grad - jnp.sum(probs * prob_grad, axis=-1, keepdims=True)))
        found[0].append(contract(score, key, 1, 0) * HEAD_DIM ** (-0.5))
        found[1].append(contract(score, query, 0, 0) * HEAD_DIM ** (-0.5))
        found[2].append(contract(low(probs), part, 0, 0))
    mixed_low = low(jnp.concatenate(found[0] + found[1] + found[2], axis=1))
    part_ref[...] = contract(mixed_low, weight_ref[:, 0:576], 1, 1)
    pack[...] = jnp.zeros_like(pack)
    pack[0:8, :] = wide(hidden_low_ref[...])
    pack[8:16, :] = wide(active_ref[...])
    pack[16:24, 0:576] = wide(mixed_low)
    pack[16:24, 576:768] = wide(context_ref[...])
    for i, value in enumerate(
        (in_ref[...], wide(low_ref[...]), total, second_ref[...], total)
    ):
        rows[...] = value
        for side in range(2):
            row = 24 + 2 * i + side
            pack[row : row + 1, :] = rows[pl.ds(2 * chip + side, 1), :]
    rows[0:1, :] = column_sum(grad * normed)
    rows[1:2, :] = column_sum(grad)
    rows[2:4, :] = sums_ref[0:2, :]
    pack[34:35, :] = rows[pl.ds(chip, 1), :]
    for place in range(2):
        spot = wide(places_ref[:, place : place + 1])
        pack[35 + place : 36 + place, :] = jnp.broadcast_to(spot, (1, D))
    pack_ref[...] = low(pack[...])


def cross_finish(own_ref, a_ref, b_ref, c_ref, total_ref, out_ref, kept_ref, given_ref, rows):
    layer, chip, core = place_in()
    rows[...] = total_ref[...] + (own_ref[...] + a_ref[...]) + (b_ref[...] + c_ref[...])
    for ref, side in ((kept_ref, core), (given_ref, 1 - core)):
        ref[...] = jnp.zeros_like(ref)
        ref[0:1, :] = rows[pl.ds(2 * chip + side, 1), :]
        ref[1:2, :] = out_ref[pl.ds(2 * chip + side, 1), :]


def cross_owner(mine_ref, other_ref, weight_ref, *refs):
    mix_ref, out_ref, up_ref, down_ref, vectors_ref, bias_ref, table_ref = refs[:7]
    hidden, mixed, single, active, sums, places = refs[7:]
    layer, chip, core = place_in()
    rank = 8 * layer + 2 * chip + core
    sums[...] = jnp.zeros_like(sums)
    for level in range(4):
        for side in range(2):
            group = 2 * level + side
            rows = slice(8 * group, 8 * group + 8)
            for spot in range(4):
                value = wide(
                    jnp.where(core == side, mine_ref[level, spot], other_ref[level, spot])
                )
                hidden[spot, rows, :] = value[0:8]
                mixed[spot, rows, :] = value[16:24]
                for i in range(5):
                    start = 8 * group + 2 * spot
                    single[i, start : start + 2, :] = value[24 + 2 * i : 26 + 2 * i]
                sums[spot : spot + 1, :] += value[34:35]
                for sequence in range(2):
                    row = 16 * level + 8 * sequence + 2 * spot + side
                    places[row : row + 1, :] = value[35 + sequence : 36 + sequence, 0:128]
            value = jnp.where(core == side, mine_ref[level, chip], other_ref[level, chip])
            active[rows, :] = wide(value)[8:16]

    def select(count, first):
        lane = lax.broadcasted_iota(jnp.int32, (count, D), 1)
        row = lax.broadcasted_iota(jnp.int32, (count, D), 0)
        return wide(lane == first + row)

    own = select(24, 24 * rank)
    offset = 24 * (2 * chip + core)
    units = select(96, 192 * layer + 96 * core)
    own_low = low(own)

    def columns_of(array_in):
        return low(contract(own_low, low(array_in), 1, 1))

    inputs = columns_of(single[0])
    for spot in range(4):
        part = contract(inputs, low(mixed[spot][:, 0:576]), 1, 0)
        for third in range(3):
            start = third * D + 192 * spot
            mix_ref[:, start : start + 192] = part[:, 192 * third : 192 * (third + 1)]
    own_mixed = mixed[layer]
    context = low(contract(low(select(24, 576 + offset)), low(own_mixed), 1, 1))
    out_ref[...] = contract(context, low(single[2]), 1, 0)
    first = columns_of(single[1])
    for spot in range(4):
        part = contract(first, low(hidden[spot]), 1, 0)
        for level in range(4):
            start = 192 * (4 * level + spot)
            up_ref[:, start : start + 192] = part[:, 192 * level : 192 * (level + 1)]
    units_low = low(contract(low(units), low(active[...]), 1, 1))
    down_ref[...] = contract(units_low, low(single[3]), 1, 0)
    mixed_sum = column_sum(own_mixed)
    vectors_ref[0:1, :] = contract_exact(mixed_sum, select(24, offset), 1, 1)
    vectors_ref[1:2, :] = contract_exact(mixed_sum, select(24, 384 + offset), 1, 1)
    for row, value in (
        (2, column_sum(single[2])),
        (3, sums[0:1, :]),
        (4, sums[1:2, :]),
        (5, column_sum(single[3])),
        (6, sums[2:3, :]),
        (7, sums[3:4, :]),
    ):
        vectors_ref[row : row + 1, :] = contract_exact(value, own, 1, 1)
    bias_ref[...] = contract_exact(column_sum(hidden[chip]), units, 1, 1)
    grads = contract(low(single[4]), own_low, 1, 1)
    for spot in range(4):
        for third in range(3):
            start = third * D + 192 * spot
            part = low(mixed[spot][:, 192 * third : 192 * (third + 1)])
            grads = grads + contract(part, weight_ref[:, start : start + 192], 1, 1)
    lane = wide(lax.broadcasted_iota(jnp.int32, (64, 64), 1))
    table_ref[...] = contract_exact(wide(places[:, 0:64] == lane), grads, 0, 0)


def split_cores(value, kept_ref, gone_ref):
    rows = kept_ref.shape[1]
    core = lax.rem(lax.axis_index("seq"), 2)
    parts = value.reshape(-1, 2, rows, value.shape[1])
    kept_ref[...] = low(jnp.where(core == 0, parts[:, 0], parts[:, 1]))
    gone_ref[...] = low(jnp.where(core == 0, parts[:, 1], parts[:, 0]))


def local_down_back(
    cot_ref, mine_ref, other_ref, n_ref, scale_ref, rows_ref, active_ref, slope_ref, weight_ref, *outs
):
    out_ref, second_ref, kept_ref, gone_ref, hidden_ref, sums_ref, bias_ref, second_low_ref = outs
    step = pl.program_id(0)

    @pl.when(step == 0)
    def _():
        core = place_in()[2]
        row = lax.broadcasted_iota(jnp.int32, (2 * SEG, D), 0)
        grad = wide(cot_ref[...])
        normed = n_ref[...]
        out = normed * rows_ref[6:7, :] + rows_ref[7:8, :]
        for place in range(2):
            heads = jnp.where(core == place, mine_ref[...], other_ref[...])
            grad = jnp.where(row == place * SEG, heads[0:1], grad)
            out = jnp.where(row == place * SEG, heads[1:2], out)
        out_ref[...] = low(out)
        second = norm_back(grad, normed, scale_ref[...], rows_ref[6:7, :])
        second_ref[...] = second
        second_low_ref[...] = low(second)
        sums_ref[0:1, :] = column_sum(wide(low(second)))
        sums_ref[1:2, :] = column_sum(grad * normed)
        sums_ref[2:3, :] = column_sum(grad)

    second_low = second_low_ref[...]
    split_cores(contract(active_ref[...], second_low, 0, 0), kept_ref, gone_ref)
    hidden = low(contract(second_low, weight_ref[...], 1, 1) * wide(slope_ref[...]))
    hidden_ref[...] = hidden
    bias_ref[...] = column_sum(wide(hidden))


def local_up_back(low_ref, hidden_ref, weight_ref, second_ref, kept_ref, gone_ref, first_ref):
    hidden = hidden_ref[...]
    split_cores(contract(low_ref[...], hidden, 0, 0), kept_ref, gone_ref)
    part = contract(hidden, weight_ref[...], 1, 1)
    step = pl.program_id(0)

    @pl.when(step == 0)
    def _():
        first_ref[...] = second_ref[...] + part

    @pl.when(step > 0)
    def _():
        first_ref[...] += part


def local_attend_back(
    first_ref, n_ref, scale_ref, rows_ref, context_ref, mixed_ref, probs_a, probs_b, group_ref, *outs
):
    out_ref, total_ref, sums_ref, back_ref, context_low_ref = outs
    grad, normed = first_ref[...], n_ref[...]
    total = norm_back(grad, normed, scale_ref[...], rows_ref[3:4, :])
    total_ref[...] = total
    branch = low(total)
    sums_ref[2:3, :] = column_sum(wide(branch))
    sums_ref[3:4, :] = column_sum(grad * normed)
    sums_ref[4:5, :] = column_sum(grad)
    out_ref[...] = low(contract(context_ref[...], branch, 0, 0))
    context_low_ref[...] = low(contract(branch, group_ref[...], 1, 1))
    lane = lax.broadcasted_iota(jnp.int32, (SEG, 128), 1)
    for segment in range(2):
        rows = slice(segment * SEG, (segment + 1) * SEG)
        for pair in range(HEADS // 2):
            places = [
                slice(third * D + pair * 128, third * D + (pair + 1) * 128) for third in range(3)
            ]
            query, key, value = (mixed_ref[rows, place] for place in places)
            grad = context_low_ref[rows, places[0]]
            found = []
            for side in range(2):
                here = (lane < HEAD_DIM) if side == 0 else (lane >= HEAD_DIM)
                probs = (probs_a, probs_b)[segment][2 * pair + side]
                prob_grad = contract(value, jnp.where(here, grad, jnp.zeros_like(grad)), 1, 1)
                value_grad = contract(low(probs), grad, 1, 0)
                score = low(
                    probs * (prob_grad - jnp.sum(probs * prob_grad, axis=0, keepdims=True))
                )
                found.append(
                    (contract(score, key, 0, 0), contract(score, query, 1, 0), value_grad)
                )
            for third in range(3):
                merged = jnp.where(lane < HEAD_DIM, found[0][third], found[1][third])
                if third < 2:
                    merged = merged * HEAD_DIM ** (-0.5)
                back_ref[rows, places[third]] = low(merged)
    for third in (0, 2):
        columns = slice(third * D, (third + 1) * D)
        sums_ref[third // 2 : third // 2 + 1, :] = column_sum(wide(back_ref[:, columns]))


def local_mix_back(
    total_ref, back_ref, tokens_ref, group_ref, out_ref, sums_ref, more_ref, bias_ref, *outs
):
    input_ref, kept_ref, gone_ref, small_ref = outs
    tokens, total = tokens_ref[...], total_ref[...]
    for third in range(3):
        columns = slice(third * D, (third + 1) * D)
        back = back_ref[:, columns]
        grad = contract(tokens, back, 0, 0)
        split_cores(grad, kept_ref.at[:, :, columns], gone_ref.at[:, :, columns])
        total = total + contract(back, group_ref[:, columns], 1, 1)
    input_ref[...] = total
    columns = slice(3 * D, 4 * D)
    split_cores(wide(out_ref[...]), kept_ref.at[:, :, columns], gone_ref.at[:, :, columns])
    small_ref[...] = jnp.zeros_like(small_ref)
    small_ref[0:5, :] = sums_ref[0:5, :]
    small_ref[5:8, :] = more_ref[0:3, :]
    for owner in range(32):
        for row in range(4):
            taken = bias_ref[:, 96 * owner + 24 * row : 96 * owner + 24 * (row + 1)]
            small_ref[8 + row : 9 + row, 24 * owner : 24 * (owner + 1)] = taken
    columns = slice(4 * D, 4 * D + 128)
    split_cores(small_ref[...].T, kept_ref.at[:, :, columns], gone_ref.at[:, :, columns])


def finish_mix(own_ref, a_ref, b_ref, c_ref, mix_ref, out_ref, vectors_ref, bias_ref, wide_ref):
    total = own_ref[...] + wide(a_ref[...]) + wide(b_ref[...]) + wide(c_ref[...])
    mix_ref[...] = total[:, 0 : 3 * D]
    out_ref[...] = total[:, 3 * D : 4 * D]
    wide_ref[...] = jnp.zeros_like(wide_ref)
    wide_ref[0:24, :] = total[:, 4 * D : 4 * D + 128]
    turned = wide_ref[...].T
    vectors_ref[...] = turned[0:8, 0:24]
    for row in range(4):
        bias_ref[:, 24 * row : 24 * (row + 1)] = turned[8 + row : 9 + row, 0:24]


def plane_three(array_in):
    return [array_in] + [swap_chip(array_in, mask) for mask in (1, 2, 3)]


def plane_shards(
    tokens,
    cotangent,
    token_docs,
    segment_docs,
    segment_positions,
    local_mix,
    local_out,
    local_up,
    local_down,
    local_vectors,
    local_up_bias,
    cross_mix,
    cross_out,
    cross_up,
    cross_down,
    cross_vectors,
    cross_up_bias,
    position_table,
):
    chip = place_in()[1]
    flat_tokens = tokens.reshape(256, D)
    flat_cot = cotangent.reshape(256, D)
    places_in = segment_positions.T

    shards_in = (
        local_mix,
        local_out,
        local_up,
        local_down.reshape(4, 24, D),
        local_vectors,
        local_up_bias.reshape(1, 96),
        cross_mix,
        cross_out,
        cross_up,
        cross_vectors,
        cross_up_bias.reshape(1, 96),
        position_table.T,
    )
    made = [half(24, 3200), half(24, 5 * D), half(24, 4 * D)] + [half(24, D + 640)] * 4
    far = pl.BlockSpec(memory_space=pltpu.HBM)
    shard_one, shard_two, shard_three, *cross_pieces = on_core(
        prepare,
        made,
        shards_in,
        0,
        in_specs=[far] * 12,
        out_specs=[far] * 7,
        scratch=[pltpu.VMEM(a.shape, a.dtype) for a in list(shards_in) + made]
        + [
            pltpu.VMEM((128, 128), jnp.float32),
            pltpu.VMEM((128, 128), jnp.float32),
            pltpu.VMEM((4, 24, D + 640), jnp.bfloat16),
            pltpu.SemaphoreType.DMA((2, 12)),
        ],
    )
    cross_sent = [cross_pieces[0]] + [swap_chip(cross_pieces[mask], mask) for mask in (1, 2, 3)]
    z_one = reach_dp(shard_one)
    shard_two, *z_one = stage(shard_two, *z_one, *cross_sent)
    z_one, cross_sent = z_one[:4], z_one[4:]
    column_one = join_dp(z_one)
    column_one, shard_two = stage(column_one, shard_two)

    first, second = swap_one(column_one), swap_two(column_one)
    cross_row = join_cross(cross_sent, after(cross_down, column_one))
    *z_two, first, second, column_one, cross_row = stage(
        *reach_dp(shard_two), first, second, column_one, cross_row
    )

    third = swap_two(first)
    others = [swap_core(piece) for piece in (column_one, first, second)]
    column_two = join_dp(z_two)
    cross_moved = [cross_row, swap_dp(cross_row, 1)]
    third, column_two, cross_moved[1], *others = stage(third, column_two, cross_moved[1], *others)
    others.append(swap_core(third))
    column_two, shard_three, *others = stage(column_two, shard_three, *others)

    first_group = gather_plane([column_one, first, second, third], others).reshape(D, 3200)
    mixed_rows, context_first, probs_first, rows, place_rows = on_core(
        local_attend,
        [half(256, 3 * D), half(SEG, D), shape_of(12, SEG, SEG), shape_of(128, D), shape_of(2, D)],
        (flat_tokens, first_group, token_docs, places_in),
        0,
    )
    first_two, second_two = swap_one(column_two), swap_two(column_two)
    *z_three, mixed_rows, first_two, second_two, column_two, cross_moved[1] = stage(
        *reach_dp(shard_three), mixed_rows, first_two, second_two, column_two, cross_moved[1]
    )
    cross_moved.append(swap_dp(cross_moved[1], 1))

    third_two = swap_two(first_two)
    others = [swap_core(piece) for piece in (column_two, first_two, second_two)]
    column_three = join_dp(z_three)
    def plain(*shapes):
        return [pl.BlockSpec(shape, lambda j, n=len(shape): (0,) * n) for shape in shapes]

    context_rows, probs_second, normed_one, scale_one, low_one = on_core(
        local_attend_more,
        [half(256, D), shape_of(12, SEG, SEG), shape_of(256, D), shape_of(256, 1), half(256, D)],
        (flat_tokens, mixed_rows, context_first, first_group, rows, token_docs),
        0,
        grid=(1,),
        in_specs=plain((256, D), (256, 3 * D), (SEG, D))
        + [pl.BlockSpec((D, D), lambda j: (0, 3))]
        + plain((128, D), (2, SEG)),
        out_specs=plain((256, D), (12, SEG, SEG), (256, D), (256, 1), (256, D)),
        scratch=[pltpu.VMEM((SEG, D), jnp.bfloat16)],
    )
    up_bias = rows[80:84].reshape(4, 32, 24).transpose(1, 0, 2).reshape(1, 4 * D)
    cross_moved[2], third_two, column_three, low_one, up_bias, rows_later, *others = stage(
        cross_moved[2], third_two, column_three, low_one, up_bias, rows[84:88], *others
    )
    cross_moved.append(swap_dp(cross_moved[2], 1))

    first_three, second_three = swap_one(column_three), swap_two(column_three)
    others.append(swap_core(third_two))
    second_group, cross_out_weight = gather_up(
        [column_two, first_two, second_two, third_two], others
    )
    whole = pl.BlockSpec((256, D), lambda j: (0, 0))
    thin = pl.BlockSpec((256, 1), lambda j: (0, 0))
    vectors = pl.BlockSpec((128, D), lambda j: (0, 0))
    eight = pl.BlockSpec((8, D), lambda j: (0, 0))
    across = pl.BlockSpec((256, D), lambda j: (0, j))
    tall = pl.BlockSpec((D, D), lambda j: (0, j))
    deep = pl.BlockSpec((D, D), lambda j: (j, 0))
    strip = pl.BlockSpec((1, D), lambda j: (0, j))
    across_half = pl.BlockSpec((256, 2 * D), lambda j: (0, j))
    tall_half = pl.BlockSpec((D, 2 * D), lambda j: (0, j))
    deep_half = pl.BlockSpec((2 * D, D), lambda j: (j, 0))
    strip_half = pl.BlockSpec((1, 2 * D), lambda j: (0, j))
    active_rows, slope_rows = on_core(
        local_up_part,
        [half(256, 4 * D)] * 2,
        (low_one, second_group, up_bias),
        2 * 256 * D * 4 * D,
        grid=(4,),
        in_specs=[whole, tall, strip],
        out_specs=[across, across],
    )
    active_rows, first_three, second_three, column_three, cross_moved[3], rows_later = stage(
        active_rows, first_three, second_three, column_three, cross_moved[3], rows_later
    )

    third_three = swap_two(first_three)
    others = [swap_core(piece) for piece in (column_three, first_three, second_three)]
    cross_bias = rows_later.reshape(4, 4, 4, 2, 24)
    cross_bias = lax.dynamic_index_in_dim(cross_bias, chip, 2, keepdims=False)
    cross_bias = cross_bias.transpose(1, 2, 0, 3).reshape(1, D)
    third_three, cross_column, cross_bias, *others = stage(
        third_three, join_dp(cross_moved), cross_bias, *others
    )

    others.append(swap_core(third_three))
    down_weight = gather_down([column_three, first_three, second_three, third_three], others)
    down_weight, cross_column = stage(down_weight.reshape(4 * D, D), cross_column)
    cross_other = swap_core(cross_column)
    normed_two, scale_two, kept, given = on_core(
        local_down_part,
        [shape_of(256, D), shape_of(256, 1), shape_of(8, D), shape_of(8, D)],
        (active_rows, down_weight, normed_one, rows, flat_cot, flat_cot, place_rows),
        2 * 256 * D * 4 * D,
        grid=(2,),
        in_specs=[
            across_half,
            deep_half,
            whole,
            vectors,
            pl.BlockSpec((16, D), lambda j: (0, 0)),
            pl.BlockSpec((16, D), lambda j: (8, 0)),
            pl.BlockSpec((2, D), lambda j: (0, 0)),
        ],
        out_specs=[whole, thin, eight, eight],
        scratch=[pltpu.VMEM((256, D), jnp.float32)],
    )

    row8, mix_share = (8, D), (D, 640)
    out_share = pl.BlockSpec((D, D), lambda j: (0, 0))
    up_share = pl.BlockSpec((D, D), lambda j: (0, 0))
    given, kept, cross_other = stage(given, kept, cross_other)
    got = swap_core(given)
    cross_up_part, cross_mix_part, cross_down_part = place_cross(cross_column, cross_other)
    kept, got, cross_mix_part = stage(kept, got, cross_mix_part)
    pair = on_core(join_pair, shape_of(8, D), (kept, got), 0, room=12)
    row_in, row_grad, mixed, probs, context = on_core(
        cross_attend,
        [shape_of(8, D), shape_of(8, D), half(8, 576), shape_of(3, 8, 8), half(8, 192)],
        (*plane_three(pair), cross_mix_part, rows, segment_docs),
        0,
        room=12,
    )
    row_n, row_scale, row_low, hidden, active, part = on_core(
        cross_up_down,
        [shape_of(8, D), shape_of(8, 1), half(8, D), shape_of(8, D), half(8, D), shape_of(8, D)],
        (
            *plane_three(context),
            row_in,
            cross_out_weight,
            rows,
            cross_up_part,
            cross_bias,
            cross_down_part,
        ),
        0,
        grid=(1,),
        in_specs=plain(*[(8, 192)] * 4, row8)
        + [out_share]
        + plain((128, D))
        + [up_share]
        + plain((1, D), (D, D)),
        out_specs=plain(row8, (8, 1), row8, row8, row8, row8),
        room=12,
    )
    row_out, row_second, hidden_low, part, sums = on_core(
        cross_turn,
        [shape_of(8, D), shape_of(8, D), half(8, D), shape_of(8, D), shape_of(8, D)],
        (*plane_three(part), row_n, rows, row_grad, hidden, cross_up_part, cross_down_part),
        0,
        grid=(1,),
        in_specs=plain(*[row8] * 4, row8, (128, D), row8, row8) + [up_share] + plain((D, D)),
        out_specs=plain(*[row8] * 5),
        room=12,
    )
    row_total, part, packed = on_core(
        cross_attend_back,
        [shape_of(8, D), shape_of(8, D), half(48, D)],
        (
            *plane_three(part),
            row_second,
            row_n,
            row_scale,
            rows,
            cross_out_weight,
            mixed,
            probs,
            cross_mix_part,
            hidden_low,
            active,
            context,
            row_in,
            row_low,
            sums,
            places_in,
        ),
        0,
        grid=(1,),
        in_specs=plain(*[row8] * 4, row8, row8, (8, 1), (128, D))
        + [out_share]
        + plain((8, 576), (3, 8, 8), mix_share, row8, row8, (8, 192), row8, row8, row8, (1, 2)),
        out_specs=plain(row8, row8, (48, D)),
        scratch=[pltpu.VMEM((48, D), jnp.float32), pltpu.VMEM((8, D), jnp.float32)],
        room=12,
    )
    kept, given = on_core(
        cross_finish,
        [shape_of(8, D), shape_of(8, D)],
        (*plane_three(part), row_total, row_out),
        0,
        scratch=[pltpu.VMEM((8, D), jnp.float32)],
        room=12,
    )
    got, kept, packed = stage(swap_core(given), kept, packed)
    pack_one, pack_two = swap_one(packed), swap_two(packed)

    twos = pl.BlockSpec((8, 96, D), lambda j: (j, 0, 0))
    layer_output, second_rows, down_kept, down_gone, hidden_grads, sums_two, bias_grad = on_core(
        local_down_back,
        [
            half(256, D),
            shape_of(256, D),
            half(16, 96, D),
            half(16, 96, D),
            half(256, 4 * D),
            shape_of(8, D),
            shape_of(1, 4 * D),
        ],
        (flat_cot, kept, got, normed_two, scale_two, rows, active_rows, slope_rows, down_weight),
        4 * 256 * D * 4 * D,
        grid=(2,),
        in_specs=[whole, eight, eight, whole, thin, vectors, across_half, across_half, deep_half],
        out_specs=[whole, whole, twos, twos, across_half, eight, strip_half],
        scratch=[pltpu.VMEM((256, D), jnp.bfloat16)],
    )
    down_total = Sum(down_kept.reshape(4, 4, 96, D))
    hidden_grads, down_gone, pack_one, pack_two = stage(
        hidden_grads, down_gone.reshape(4, 4, 96, D), pack_one, pack_two
    )
    pack_three = swap_two(pack_one)

    down_got = swap_core(down_gone)
    sixteens = pl.BlockSpec((16, 24, 2 * D), lambda j: (0, 0, j))
    up_kept, up_gone, first_rows = on_core(
        local_up_back,
        [half(16, 24, 4 * D), half(16, 24, 4 * D), shape_of(256, D)],
        (low_one, hidden_grads, second_group, second_rows),
        4 * 256 * D * 4 * D,
        grid=(2,),
        in_specs=[whole, across_half, tall_half, whole],
        out_specs=[sixteens, sixteens, whole],
    )
    up_total = Sum(up_kept.reshape(4, 4, 24, 4 * D))
    down_got, first_rows, up_gone, pack_three = stage(
        down_got, first_rows, up_gone.reshape(4, 4, 24, 4 * D), pack_three
    )
    plane_pack = join_chips([packed, pack_one, pack_two, pack_three])
    packs = [plane_pack, swap_dp(plane_pack, 1), swap_dp(plane_pack, 3)]

    up_got = swap_core(up_gone)
    down_sent = down_total.first(down_got)
    down_back = swap_one(down_sent)
    flat = pl.BlockSpec((256, 3 * D), lambda j: (0, 0))
    out_grad, sum_rows, sums_one, back_rows = on_core(
        local_attend_back,
        [half(D, D), shape_of(256, D), shape_of(8, D), half(256, 3 * D)],
        (
            first_rows,
            normed_one,
            scale_one,
            rows,
            context_rows,
            mixed_rows,
            probs_first,
            probs_second,
            first_group,
        ),
        4 * 256 * D * 2 * D,
        grid=(1,),
        in_specs=[
            whole,
            whole,
            thin,
            vectors,
            whole,
            flat,
            pl.BlockSpec((12, SEG, SEG), lambda j: (0, 0, 0)),
            pl.BlockSpec((12, SEG, SEG), lambda j: (0, 0, 0)),
            pl.BlockSpec((D, D), lambda j: (0, 3)),
        ],
        out_specs=[pl.BlockSpec((D, D), lambda j: (0, 0)), whole, eight, flat],
        scratch=[pltpu.VMEM((256, D), jnp.bfloat16)],
    )
    up_sent = up_total.first(up_got)
    down_back, back_rows, up_sent, *packs = stage(down_back, back_rows, up_sent, *packs)
    packs.insert(2, swap_dp(packs[0], 2))

    up_back = swap_one(up_sent)
    down_onward = down_total.second(down_back)
    sides = [half(16, 24, 4 * D + 128)] * 2
    input_grad, mix_kept, mix_gone = on_core(
        local_mix_back,
        [shape_of(256, D)] + sides,
        (
            sum_rows,
            back_rows,
            flat_tokens,
            first_group,
            out_grad,
            sums_one,
            sums_two,
            bias_grad,
        ),
        4 * 256 * D * 3 * D,
        scratch=[pltpu.VMEM((128, D), jnp.float32)],
    )
    mix_total = Sum(mix_kept.reshape(4, 4, 24, 3200))
    up_back, down_onward, mix_gone, packs[2] = stage(
        up_back, down_onward, mix_gone.reshape(4, 4, 24, 3200), packs[2]
    )

    mix_got, down_last = swap_core(mix_gone), swap_two(down_onward)
    up_onward = up_total.second(up_back)
    my_rows = join_dp(packs)
    mix_got, down_last, up_onward, my_rows = stage(mix_got, down_last, up_onward, my_rows)

    up_last = swap_two(up_onward)
    mix_sent = mix_total.first(mix_got)
    down_others = down_total.third(down_last)
    up_last, mix_sent, my_rows, *down_others = stage(up_last, mix_sent, my_rows, *down_others)
    other_rows = swap_core(my_rows)

    mix_back, down_others = swap_one(mix_sent), send_dp(down_others)
    up_others = up_total.third(up_last)
    mix_back, other_rows, *others = stage(mix_back, other_rows, *down_others, *up_others)
    down_others, up_others = others[:3], others[3:]

    mix_last = swap_two(mix_total.second(mix_back))
    up_others = send_dp(up_others)
    down_sum = down_total.total(down_others)
    mix_last, down_sum, other_rows, *up_others = stage(mix_last, down_sum, other_rows, *up_others)

    mix_others = send_dp(mix_total.third(mix_last))
    up_sum = up_total.total(up_others)
    cross_grads = on_core(
        cross_owner,
        [
            shape_of(24, 3 * D),
            shape_of(24, D),
            shape_of(24, 4 * D),
            shape_of(96, D),
            shape_of(8, 24),
            shape_of(1, 96),
            shape_of(64, 24),
        ],
        (my_rows, other_rows, cross_mix),
        0,
        scratch=[
            pltpu.VMEM((4, 64, D), jnp.float32),
            pltpu.VMEM((4, 64, D), jnp.float32),
            pltpu.VMEM((5, 64, D), jnp.float32),
            pltpu.VMEM((64, D), jnp.float32),
            pltpu.VMEM((8, D), jnp.float32),
            pltpu.VMEM((64, 128), jnp.float32),
        ],
    )
    mix_sum, out_sum, vectors_sum, bias_sum = on_core(
        finish_mix,
        [shape_of(24, 3 * D), shape_of(24, D), shape_of(8, 24), shape_of(1, 96)],
        (mix_total.own, *mix_others),
        0,
        grid=(1,),
        in_specs=plain(*[(24, 4 * D + 128)] * 4),
        out_specs=plain((24, 3 * D), (24, D), (8, 24), (1, 96)),
        scratch=[pltpu.VMEM((128, 128), jnp.float32)],
    )
    return (
        layer_output.reshape(2, SEG, D),
        input_grad.reshape(2, SEG, D),
        mix_sum,
        out_sum,
        up_sum,
        down_sum,
        vectors_sum,
        bias_sum.reshape(96),
        *cross_grads[:5],
        cross_grads[5].reshape(96),
        cross_grads[6],
    )


def solution(mesh):
    flat = dict(mesh.shape) == {"dp": 4, "seq": 8}
    return jax.shard_map(
        plane_shards if flat else shards,
        mesh=mesh,
        in_specs=(
            P("dp", "seq", None),
            P("dp", "seq", None),
            P("dp", "seq"),
            P("dp", None),
            P("dp", "seq"),
            P(("dp", "seq"), None),
            P(("dp", "seq"), None),
            P(("dp", "seq"), None),
            P(("dp", "seq"), None),
            P(None, ("dp", "seq")),
            P(("dp", "seq")),
            P(("dp", "seq"), None),
            P(("dp", "seq"), None),
            P(("dp", "seq"), None),
            P(("dp", "seq"), None),
            P(None, ("dp", "seq")),
            P(("dp", "seq")),
            P(None, ("dp", "seq")),
        ),
        out_specs=(
            P("dp", "seq", None),
            P("dp", "seq", None),
            P(("dp", "seq"), None),
            P(("dp", "seq"), None),
            P(("dp", "seq"), None),
            P(("dp", "seq"), None),
            P(None, ("dp", "seq")),
            P(("dp", "seq")),
            P(("dp", "seq"), None),
            P(("dp", "seq"), None),
            P(("dp", "seq"), None),
            P(("dp", "seq"), None),
            P(None, ("dp", "seq")),
            P(("dp", "seq")),
            P(None, ("dp", "seq")),
        ),
        check_vma=False,
    )
```

```python
from functools import partial
import math

import jax
import jax.numpy as jnp
from jax import lax
from jax.experimental import pallas as pl
from jax.experimental.pallas import tpu as pltpu
from jax.sharding import PartitionSpec as P

D = 768
HEADS = 12
HEAD_DIM = 64
SEG = 128
MICRO = 2


epsilon = 1e-05
masked_score = -1000000000.0
owner_dims = (0, 0, 0, 0, 1, 0, 0, 0, 0, 0, 1, 0, 1)


def layer_norm(values, gain_row, shift_row):
    centered = values - jnp.mean(values, axis=-1, keepdims=True)
    variance = jnp.mean(centered * centered, axis=-1, keepdims=True)
    return centered * lax.rsqrt(variance + epsilon) * gain_row + shift_row


def gelu_exact(hidden):
    return jax.nn.gelu(hidden, approximate=False)


def contract(left_side, right_side, left_dim, right_dim):
    return lax.dot_general(
        left_side,
        right_side,
        (((left_dim,), (right_dim,)), ((), ())),
        preferred_element_type=jnp.float32,
    )


def contract_exact(left_side, right_side, left_dim, right_dim):
    return lax.dot_general(
        left_side,
        right_side,
        (((left_dim,), (right_dim,)), ((), ())),
        precision=lax.Precision.HIGHEST,
        preferred_element_type=jnp.float32,
    )


def owner_pack(grads, devices):
    pieces = []
    for grad_value, split_dim in zip(grads, owner_dims):
        if split_dim == 0:
            pieces.append(grad_value.reshape(devices, -1))
        else:
            row_count = grad_value.shape[0]
            pieces.append(
                grad_value.reshape(row_count, devices, -1).transpose(1, 0, 2).reshape(devices, -1)
            )
    return jnp.concatenate(pieces, axis=1)


def owner_unpack(packed, shard_shapes):
    results = []
    offset = 0
    for shard_shape in shard_shapes:
        length = math.prod(shard_shape)
        results.append(packed[0, offset : offset + length].reshape(shard_shape))
        offset = offset + length
    return tuple(results)


def fetch_weights(
    local_mix,
    local_out,
    local_up,
    local_down,
    local_vectors,
    local_up_bias,
    cross_mix,
    cross_out,
    cross_up,
    cross_down,
    cross_vectors,
    cross_up_bias,
    position_table,
):
    return (
        lax.all_gather(local_mix, ("dp", "seq"), axis=0, tiled=True),
        lax.all_gather(local_out, ("dp", "seq"), axis=0, tiled=True),
        lax.all_gather(local_up, ("dp", "seq"), axis=0, tiled=True),
        lax.all_gather(local_down, ("dp", "seq"), axis=0, tiled=True),
        lax.all_gather(local_vectors, ("dp", "seq"), axis=1, tiled=True),
        lax.all_gather(local_up_bias, ("dp", "seq"), axis=0, tiled=True),
        lax.all_gather(cross_mix, ("dp", "seq"), axis=0, tiled=True),
        lax.all_gather(cross_out, ("dp", "seq"), axis=0, tiled=True),
        lax.all_gather(cross_up, ("dp", "seq"), axis=0, tiled=True),
        lax.all_gather(cross_down, ("dp", "seq"), axis=0, tiled=True),
        lax.all_gather(cross_vectors, ("dp", "seq"), axis=1, tiled=True),
        lax.all_gather(cross_up_bias, ("dp", "seq"), axis=0, tiled=True),
        lax.all_gather(position_table, ("dp", "seq"), axis=1, tiled=True),
    )


def segment_parts(mixed_rows, token_docs):
    segment_count = token_docs.shape[0]
    split_heads = mixed_rows.reshape(segment_count, SEG, 3, HEADS, HEAD_DIM)
    allowed = token_docs[:, None, :, None] == token_docs[:, None, None, :]
    scores = jnp.einsum(
        "nqhd,nkhd->nhqk",
        split_heads[:, :, 0],
        split_heads[:, :, 1],
        preferred_element_type=jnp.float32,
    ) * HEAD_DIM ** (-0.5)
    scores = jnp.where(allowed, scores, masked_score)
    return (split_heads, scores)


def segment_forward(mixed_rows, token_docs):
    split_heads, scores = segment_parts(mixed_rows, token_docs)
    log_total = jax.nn.logsumexp(scores, axis=-1)
    weights = jax.nn.softmax(scores, axis=-1).astype(jnp.bfloat16)
    context = jnp.einsum(
        "nhqk,nkhd->nqhd", weights, split_heads[:, :, 2], preferred_element_type=jnp.float32
    )
    return (context.reshape(-1, D).astype(jnp.bfloat16), log_total)


def segment_backward(context_grad, log_total, mixed_rows, token_docs):
    split_heads, scores = segment_parts(mixed_rows, token_docs)
    segment_count = token_docs.shape[0]
    probs = jnp.exp(scores - log_total[..., None])
    grad_heads = context_grad.reshape(segment_count, SEG, HEADS, HEAD_DIM)
    prob_grad = jnp.einsum(
        "nqhd,nkhd->nhqk", grad_heads, split_heads[:, :, 2], preferred_element_type=jnp.float32
    )
    value_grad = jnp.einsum(
        "nhqk,nqhd->nkhd",
        probs.astype(jnp.bfloat16),
        grad_heads,
        preferred_element_type=jnp.float32,
    )
    score_grad = probs * (prob_grad - jnp.sum(probs * prob_grad, axis=-1, keepdims=True))
    score_low = score_grad.astype(jnp.bfloat16) * HEAD_DIM ** (-0.5)
    query_grad = jnp.einsum(
        "nhqk,nkhd->nqhd", score_low, split_heads[:, :, 1], preferred_element_type=jnp.float32
    )
    key_grad = jnp.einsum(
        "nhqk,nqhd->nkhd", score_low, split_heads[:, :, 0], preferred_element_type=jnp.float32
    )
    row_total = segment_count * SEG
    return jnp.concatenate(
        [
            query_grad.reshape(row_total, D),
            key_grad.reshape(row_total, D),
            value_grad.reshape(row_total, D),
        ],
        axis=1,
    )


def cross_parts(mixed_rows, gathered, segment_docs):
    group_size = segment_docs.shape[0]
    per_device = mixed_rows.shape[0] // group_size
    query_rows = mixed_rows[:, :D].reshape(group_size, per_device, HEADS, HEAD_DIM)
    key_rows = gathered[:, :, :D].reshape(group_size, -1, HEADS, HEAD_DIM)
    value_rows = gathered[:, :, D:].reshape(group_size, -1, HEADS, HEAD_DIM)
    own_docs = lax.dynamic_slice_in_dim(
        segment_docs, lax.axis_index("seq") * per_device, per_device, 1
    )
    allowed = own_docs[:, None, :, None] == segment_docs[:, None, None, :]
    scores = jnp.einsum(
        "bqhd,bkhd->bhqk", query_rows, key_rows, preferred_element_type=jnp.float32
    ) * HEAD_DIM ** (-0.5)
    scores = jnp.where(allowed, scores, masked_score)
    return (query_rows, key_rows, value_rows, scores)


def cross_forward(mixed_rows, segment_docs):
    group_size = segment_docs.shape[0]
    per_device = mixed_rows.shape[0] // group_size
    pair_rows = mixed_rows[:, D:].reshape(group_size, per_device, 2 * D)
    gathered = lax.all_gather(pair_rows, "seq", axis=1, tiled=True)
    query_rows, key_rows, value_rows, scores = cross_parts(mixed_rows, gathered, segment_docs)
    log_total = jax.nn.logsumexp(scores, axis=-1)
    weights = jax.nn.softmax(scores, axis=-1).astype(jnp.bfloat16)
    context = jnp.einsum("bhqk,bkhd->bqhd", weights, value_rows, preferred_element_type=jnp.float32)
    return (context.reshape(-1, D).astype(jnp.bfloat16), (gathered, log_total))


def cross_backward(context_grad, cross_kept, mixed_rows, segment_docs):
    gathered, log_total = cross_kept
    group_size = segment_docs.shape[0]
    row_total = mixed_rows.shape[0]
    per_device = row_total // group_size
    query_rows, key_rows, value_rows, scores = cross_parts(mixed_rows, gathered, segment_docs)
    probs = jnp.exp(scores - log_total[..., None])
    grad_heads = context_grad.reshape(group_size, per_device, HEADS, HEAD_DIM)
    prob_grad = jnp.einsum(
        "bqhd,bkhd->bhqk", grad_heads, value_rows, preferred_element_type=jnp.float32
    )
    value_grad = jnp.einsum(
        "bhqk,bqhd->bkhd",
        probs.astype(jnp.bfloat16),
        grad_heads,
        preferred_element_type=jnp.float32,
    )
    score_grad = probs * (prob_grad - jnp.sum(probs * prob_grad, axis=-1, keepdims=True))
    score_low = score_grad.astype(jnp.bfloat16) * HEAD_DIM ** (-0.5)
    query_grad = jnp.einsum(
        "bhqk,bkhd->bqhd", score_low, key_rows, preferred_element_type=jnp.float32
    )
    key_grad = jnp.einsum(
        "bhqk,bqhd->bkhd", score_low, query_rows, preferred_element_type=jnp.float32
    )
    pair_grads = jnp.concatenate(
        [key_grad.reshape(group_size, -1, D), value_grad.reshape(group_size, -1, D)], axis=2
    )
    own_pairs = lax.psum_scatter(
        pair_grads.astype(jnp.bfloat16), "seq", scatter_dimension=1, tiled=True
    ).astype(jnp.float32)
    return jnp.concatenate(
        [query_grad.reshape(row_total, D), own_pairs.reshape(row_total, 2 * D)], axis=1
    )


def block_forward(inputs, weights, attend):
    mix_weight, out_weight, up_weight, down_weight, vectors, up_bias = weights
    vector_rows = vectors.astype(jnp.float32)
    in_bias = jnp.concatenate([vector_rows[0], jnp.zeros_like(vector_rows[0]), vector_rows[1]])
    rounded = inputs.astype(jnp.bfloat16)
    mixed_rows = (
        jnp.dot(rounded, mix_weight, preferred_element_type=jnp.float32) + in_bias
    ).astype(jnp.bfloat16)
    context, attend_kept = attend(mixed_rows)
    first_sum = (
        inputs + jnp.dot(context, out_weight, preferred_element_type=jnp.float32) + vector_rows[2]
    )
    first_norm = layer_norm(first_sum, vector_rows[3], vector_rows[4])
    first_low = first_norm.astype(jnp.bfloat16)
    hidden = jnp.dot(first_low, up_weight, preferred_element_type=jnp.float32) + up_bias.astype(
        jnp.float32
    )
    active = gelu_exact(hidden).astype(jnp.bfloat16)
    second_sum = (
        first_norm
        + jnp.dot(active, down_weight, preferred_element_type=jnp.float32)
        + vector_rows[5]
    )
    output = layer_norm(second_sum, vector_rows[6], vector_rows[7])
    return (
        output,
        (
            rounded,
            mixed_rows,
            attend_kept,
            context,
            first_sum,
            first_low,
            hidden,
            active,
            second_sum,
        ),
    )


def block_backward(output_grad, block_kept, weights, attend_back):
    mix_weight, out_weight, up_weight, down_weight, vectors, up_bias = weights
    vector_rows = vectors.astype(jnp.float32)
    rounded, mixed_rows, attend_kept, context, first_sum, first_low, hidden, active, second_sum = (
        block_kept
    )
    unused, second_pull = jax.vjp(layer_norm, second_sum, vector_rows[6], vector_rows[7])
    second_grad, gain_two, shift_two = second_pull(output_grad)
    second_low = second_grad.astype(jnp.bfloat16)
    down_grad = contract(active, second_low, 0, 0)
    down_bias = jnp.sum(second_low.astype(jnp.float32), axis=0)
    active_grad = contract(second_low, down_weight, 1, 1)
    unused, gelu_pull = jax.vjp(gelu_exact, hidden)
    hidden_grad = gelu_pull(active_grad)[0]
    hidden_low = hidden_grad.astype(jnp.bfloat16)
    up_grad = contract(first_low, hidden_low, 0, 0)
    up_bias_grad = jnp.sum(hidden_low.astype(jnp.float32), axis=0)
    first_grad = second_grad + contract(hidden_low, up_weight, 1, 1)
    unused, first_pull = jax.vjp(layer_norm, first_sum, vector_rows[3], vector_rows[4])
    sum_grad, gain_one, shift_one = first_pull(first_grad)
    branch_low = sum_grad.astype(jnp.bfloat16)
    out_grad = contract(context, branch_low, 0, 0)
    out_bias = jnp.sum(branch_low.astype(jnp.float32), axis=0)
    context_low = contract(branch_low, out_weight, 1, 1).astype(jnp.bfloat16)
    mixed_low = attend_back(context_low, attend_kept, mixed_rows).astype(jnp.bfloat16)
    mix_grad = contract(rounded, mixed_low, 0, 0)
    mixed_sums = jnp.sum(mixed_low.astype(jnp.float32), axis=0)
    input_grad = sum_grad + contract(mixed_low, mix_weight, 1, 1)
    vectors_grad = jnp.stack(
        [
            mixed_sums[:D],
            mixed_sums[2 * D :],
            out_bias,
            gain_one,
            shift_one,
            down_bias,
            gain_two,
            shift_two,
        ]
    )
    return (input_grad, (mix_grad, out_grad, up_grad, down_grad, vectors_grad, up_bias_grad))


def shards(
    tokens,
    cotangent,
    token_docs,
    segment_docs,
    segment_positions,
    local_mix,
    local_out,
    local_up,
    local_down,
    local_vectors,
    local_up_bias,
    cross_mix,
    cross_out,
    cross_up,
    cross_down,
    cross_vectors,
    cross_up_bias,
    position_table,
):
    sequence_count, span, width = tokens.shape
    group_size = sequence_count // MICRO
    segment_count = span // SEG
    devices = lax.axis_size(("dp", "seq"))
    shard_shapes = tuple(
        (
            array_in.shape
            for array_in in (
                local_mix,
                local_out,
                local_up,
                local_down,
                local_vectors,
                local_up_bias,
                cross_mix,
                cross_out,
                cross_up,
                cross_down,
                cross_vectors,
                cross_up_bias,
                position_table,
            )
        )
    )
    layer_outputs = []
    input_grads = []
    totals = ()
    for micro_step in range(MICRO):
        lower_row = micro_step * group_size
        upper_row = lower_row + group_size
        gathered = fetch_weights(
            local_mix,
            local_out,
            local_up,
            local_down,
            local_vectors,
            local_up_bias,
            cross_mix,
            cross_out,
            cross_up,
            cross_down,
            cross_vectors,
            cross_up_bias,
            position_table,
        )
        local_weights = gathered[0:6]
        cross_weights = gathered[6:12]
        position_rows = gathered[12]
        inputs = tokens[lower_row:upper_row].reshape(group_size * span, width).astype(jnp.float32)
        docs_here = token_docs[lower_row:upper_row]
        segments_here = segment_docs[lower_row:upper_row]
        first_out, first_kept = block_forward(
            inputs, local_weights, partial(segment_forward, token_docs=docs_here)
        )
        segment_grid = first_out.reshape(group_size * segment_count, SEG, width)
        places = segment_positions[lower_row:upper_row].reshape(group_size * segment_count)
        position_picks = (
            places[:, None] == jnp.arange(position_rows.shape[0], dtype=jnp.int32)[None, :]
        ).astype(jnp.bfloat16)
        heads_in = segment_grid[:, 0, :] + jnp.dot(
            position_picks, position_rows, preferred_element_type=jnp.float32
        )
        heads_out, cross_kept = block_forward(
            heads_in, cross_weights, partial(cross_forward, segment_docs=segments_here)
        )
        joined = jnp.concatenate([heads_out[:, None, :], segment_grid[:, 1:, :]], axis=1)
        layer_outputs.append(joined.astype(jnp.bfloat16))
        gathered = fetch_weights(
            local_mix,
            local_out,
            local_up,
            local_down,
            local_vectors,
            local_up_bias,
            cross_mix,
            cross_out,
            cross_up,
            cross_down,
            cross_vectors,
            cross_up_bias,
            position_table,
        )
        local_weights = gathered[0:6]
        cross_weights = gathered[6:12]
        output_grad = cotangent[lower_row:upper_row].astype(jnp.float32)
        heads_grad, cross_grads = block_backward(
            output_grad[:, 0, :],
            cross_kept,
            cross_weights,
            partial(cross_backward, segment_docs=segments_here),
        )
        table_grad = contract_exact(position_picks.astype(jnp.float32), heads_grad, 0, 0)
        first_grad = jnp.concatenate(
            [heads_grad[:, None, :], output_grad[:, 1:, :]], axis=1
        ).reshape(group_size * span, width)
        input_grad, local_grads = block_backward(
            first_grad, first_kept, local_weights, partial(segment_backward, token_docs=docs_here)
        )
        input_grads.append(input_grad.reshape(group_size, span, width))
        step_grads = local_grads + cross_grads + (table_grad,)
        if micro_step == 0:
            totals = tuple(step_grads)
        else:
            totals = tuple(
                (total_sum + step_sum for total_sum, step_sum in zip(totals, step_grads))
            )
    packed_total = lax.psum_scatter(
        owner_pack(totals, devices), ("dp", "seq"), scatter_dimension=0, tiled=True
    )
    summed = owner_unpack(packed_total, shard_shapes)
    layer_output = jnp.concatenate(layer_outputs, axis=0)
    input_gradient = jnp.concatenate(input_grads, axis=0)
    return (layer_output, input_gradient) + tuple(summed)


def swap_dp(array_in, shift):
    return lax.ppermute(array_in, "dp", [(i, (i + shift) % 4) for i in range(4)])


def swap_core(array_in):
    return lax.ppermute(array_in, "seq", [(i, i ^ 1) for i in range(8)])


def swap_chip(array_in, mask):
    return lax.ppermute(array_in, "seq", [(i, i ^ (2 * mask)) for i in range(8)])


def swap_one(array_in):
    return lax.ppermute(array_in, "seq", [(i, i ^ (2 if i % 2 == 0 else 4)) for i in range(8)])


def swap_two(array_in):
    return lax.ppermute(array_in, "seq", [(i, i ^ (4 if i % 2 == 0 else 2)) for i in range(8)])


def place_in():
    layer = lax.axis_index("dp")
    spot = lax.axis_index("seq")
    return layer, spot // 2, lax.rem(spot, 2)


def after(array_in, *before):
    return lax.optimization_barrier((array_in,) + before)[0]


def stage(*values):
    return lax.optimization_barrier(values)


def wide(array_in):
    return array_in.astype(jnp.float32)


def low(array_in):
    return array_in.astype(jnp.bfloat16)


def copies(pieces, shapes, moves, room=64):
    count, made = len(pieces), len(shapes)
    total = len(moves(0, 0, 0))

    def kernel(*refs):
        outs, held, sems = refs[count : count + made], refs[count + made : -1], refs[-1]
        inward = [pltpu.make_async_copy(refs[i], held[i], sems.at[0, i]) for i in range(count)]
        for copy in inward:
            copy.start()
        outward = []
        for i, (piece, part, out, place) in enumerate(moves(*place_in())):
            if inward[piece] is not None:
                inward[piece].wait()
                inward[piece] = None
            copy = pltpu.make_async_copy(held[piece].at[part], outs[out].at[place], sems.at[1, i])
            copy.start()
            outward.append(copy)
        for copy in outward:
            copy.wait()

    size = 2 * sum(math.prod(shape) for shape in shapes) * 2
    return pl.pallas_call(
        kernel,
        out_shape=[jax.ShapeDtypeStruct(shape, pieces[0].dtype) for shape in shapes],
        in_specs=[pl.BlockSpec(memory_space=pltpu.HBM)] * count,
        out_specs=[pl.BlockSpec(memory_space=pltpu.HBM)] * made,
        scratch_shapes=[pltpu.VMEM(piece.shape, piece.dtype) for piece in pieces]
        + [pltpu.SemaphoreType.DMA((2, max(count, total)))],
        compiler_params=pltpu.CompilerParams(vmem_limit_bytes=room * 2**20),
        cost_estimate=pl.CostEstimate(flops=0, bytes_accessed=0, transcendentals=0),
    )(*pieces)


every = slice(None)


def reach_dp(shard):
    return [shard] + [swap_dp(shard, shift) for shift in (1, 2, 3)]


def join_dp(pieces):
    return copies(
        pieces,
        [(4,) + pieces[0].shape],
        lambda layer, chip, core: [(i, every, 0, lax.rem(layer + 4 - i, 4)) for i in range(4)],
    )[0]


def plane_order(chip, core):
    near, far = chip ^ (1 + core), chip ^ (2 - core)
    return (chip, near, far, chip ^ 3), (chip, far, near, chip ^ 3)


def join_chips(pieces):
    def moves(layer, chip, core):
        return [(i, every, 0, spot) for i, spot in enumerate(plane_order(chip, core)[0])]

    return copies(pieces, [(4,) + pieces[0].shape], moves)[0]


def gather_plane(mine, others):
    def moves(layer, chip, core):
        own, other = plane_order(chip, core)
        found = [(i, every, 0, (every, own[i], core)) for i in range(4)]
        return found + [(4 + i, every, 0, (every, other[i], 1 - core)) for i in range(4)]

    shape = (4, 4, 2) + mine[0].shape[1:]
    return copies(mine + others, [shape], moves)[0]


def gather_up(mine, others):
    def moves(layer, chip, core):
        own, other = plane_order(chip, core)
        found = []
        for i in range(8):
            spot, side = (own[i], core) if i < 4 else (other[i - 4], 1 - core)
            for out, lanes in enumerate((slice(0, 4 * D), slice(4 * D, 5 * D))):
                found.append((i, (every, every, lanes), out, (every, spot, side)))
        return found

    up, out = copies(mine + others, [(4, 4, 2, 24, 4 * D), (4, 4, 2, 24, D)], moves)
    return up.reshape(D, 4 * D), out.reshape(D, D)


def gather_down(mine, others):
    def moves(layer, chip, core):
        own, other = plane_order(chip, core)
        found = []
        for i in range(8):
            spot, side = (own[i], core) if i < 4 else (other[i - 4], 1 - core)
            for quarter in range(4):
                part = (every, every, slice(quarter * D, (quarter + 1) * D))
                found.append((i, part, 0, (every, spot, side, quarter)))
        return found

    return copies(mine + others, [(4, 4, 2, 4, 24, D)], moves)[0]


class Sum:
    def __init__(self, kept):
        self.kept = kept
        self.shape = kept.shape[2:]

    def run(self, operands, out_shapes, plan):
        shape, count, made = self.shape, len(operands), len(out_shapes)
        dry = plan(0, 0, 0)
        pieces = sum(len(sources) for sources, target in dry)

        def kernel(*refs):
            given, outs = refs[:count], refs[count : count + made]
            held, built, sems = refs[count + made : -len(dry) - 1], refs[-len(dry) - 1 : -1], refs[-1]
            inward, outward, steps = [], [], []
            for sources, target in plan(*place_in()):
                step = []
                for operand, index in sources:
                    spot = len(inward)
                    source = given[operand].at[index]
                    copy = pltpu.make_async_copy(source, held[spot], sems.at[0, spot])
                    copy.start()
                    inward.append(copy)
                    step.append(spot)
                steps.append((step, target))
            for place, (step, (out, index)) in enumerate(steps):
                total = None
                for spot in step:
                    inward[spot].wait()
                    value = wide(held[spot][...])
                    total = value if total is None else total + value
                built[place][...] = total.astype(built[place].dtype)
                target = outs[out] if index is None else outs[out].at[index]
                copy = pltpu.make_async_copy(built[place], target, sems.at[1, place])
                copy.start()
                outward.append(copy)
            for copy in outward:
                copy.wait()

        far = pl.BlockSpec(memory_space=pltpu.HBM)
        return pl.pallas_call(
            kernel,
            out_shape=out_shapes,
            in_specs=[far] * count,
            out_specs=[far] * made,
            scratch_shapes=[pltpu.VMEM(shape, jnp.bfloat16)] * pieces
            + [pltpu.VMEM(shape, out_shapes[target[0]].dtype) for sources, target in dry]
            + [pltpu.SemaphoreType.DMA((2, pieces))],
            compiler_params=pltpu.CompilerParams(vmem_limit_bytes=64 * 2**20),
            cost_estimate=pl.CostEstimate(flops=0, bytes_accessed=0, transcendentals=0),
        )(*operands)

    def first(self, got):
        self.got = got

        def plan(layer, chip, core):
            return [
                ([(0, (z, spot)), (1, (z, spot))], (0, (i, z)))
                for i, spot in enumerate((chip ^ (1 + core), chip ^ 3))
                for z in range(4)
            ]

        return self.run([self.kept, got], [half(2, 4, *self.shape)], plan)[0]

    def second(self, back):
        self.back = back

        def plan(layer, chip, core):
            spot = chip ^ (2 - core)
            return [
                ([(0, (z, spot)), (1, (z, spot)), (2, (1, z))], (0, z)) for z in range(4)
            ]

        return self.run([self.kept, self.got, back], [half(4, *self.shape)], plan)[0]

    def third(self, last):
        def plan(layer, chip, core):
            found = []
            for shift in (1, 2, 3, 0):
                z = lax.rem(layer + shift, 4)
                sources = [(0, (z, chip)), (1, (z, chip)), (2, (0, z)), (3, z)]
                found.append((sources, (shift, None)))
            return found

        self.own, *others = self.run(
            [self.kept, self.got, self.back, last],
            [shape_of(*self.shape)] + [half(*self.shape)] * 3,
            plan,
        )
        return others

    def total(self, others):
        return self.own + wide(others[0]) + wide(others[1]) + wide(others[2])


def send_dp(others):
    return [swap_dp(other, shift) for shift, other in zip((1, 2, 3), others)]


def norm_parts(values):
    centered = values - jnp.mean(values, axis=-1, keepdims=True)
    variance = jnp.mean(centered * centered, axis=-1, keepdims=True)
    scale = lax.rsqrt(variance + epsilon)
    return centered * scale, scale


def norm_back(grad, normed, scale, gain):
    scaled = grad * gain
    return scale * (
        scaled
        - jnp.mean(scaled, axis=-1, keepdims=True)
        - normed * jnp.mean(scaled * normed, axis=-1, keepdims=True)
    )


def gelu_slope(hidden):
    return 0.5 * (1.0 + lax.erf(hidden * math.sqrt(0.5))) + hidden * jnp.exp(
        -0.5 * hidden * hidden
    ) * (1.0 / math.sqrt(2.0 * math.pi))


def shape_of(*shape, dtype=jnp.float32):
    return jax.ShapeDtypeStruct(shape, dtype)


def half(*shape):
    return jax.ShapeDtypeStruct(shape, jnp.bfloat16)


def on_core(kernel, out_shape, operands, flops, room=64, grid=(), in_specs=None, out_specs=None, scratch=()):
    arrays = jax.tree.leaves(out_shape) + list(operands)
    size = sum(math.prod(a.shape) * a.dtype.itemsize for a in arrays)
    extra = {} if in_specs is None else {"in_specs": in_specs, "out_specs": out_specs}
    return pl.pallas_call(
        kernel,
        out_shape=out_shape,
        grid=grid,
        scratch_shapes=scratch,
        compiler_params=pltpu.CompilerParams(vmem_limit_bytes=room * 2**20),
        cost_estimate=pl.CostEstimate(flops=0, bytes_accessed=0, transcendentals=0),
        **extra,
    )(*operands)


def column_sum(array_in):
    return jnp.sum(array_in, axis=0, keepdims=True)


def prepare(*refs):
    given, made, held, built = refs[0:12], refs[12:19], refs[19:31], refs[31:38]
    small, turned, parts, sems = refs[38:]
    inward = [pltpu.make_async_copy(given[i], held[i], sems.at[0, i]) for i in range(12)]
    outward = [pltpu.make_async_copy(built[i], made[i], sems.at[1, i]) for i in range(7)]
    for copy in inward:
        copy.start()
    for copy in inward:
        copy.wait()
    mix_ref, out_ref, up_ref, down_ref, vectors_ref, bias_ref = held[0:6]
    cross_mix_ref, cross_out_ref, cross_up_ref, cross_vectors_ref, cross_bias_ref, table_ref = held[6:]
    one_ref, two_ref, three_ref = built[0:3]
    one_ref[:, 0 : 3 * D] = mix_ref[...]
    one_ref[:, 3 * D : 4 * D] = out_ref[...]
    small[...] = jnp.zeros_like(small)
    small[0:8, 0:24] = wide(vectors_ref[...])
    small[8:16, 0:24] = wide(cross_vectors_ref[...])
    for row in range(4):
        lanes = slice(24 * row, 24 * (row + 1))
        small[80 + row : 81 + row, 0:24] = wide(bias_ref[:, lanes])
        small[84 + row : 85 + row, 0:24] = wide(cross_bias_ref[:, lanes])
    turned[...] = small[...].T
    turned[0:24, 16:80] = wide(table_ref[...])
    one_ref[:, 4 * D : 4 * D + 128] = low(turned[0:24, :])
    outward[0].start()
    two_ref[:, 0 : 4 * D] = up_ref[...]
    two_ref[:, 4 * D : 5 * D] = cross_out_ref[...]
    for quarter in range(4):
        three_ref[:, quarter * D : (quarter + 1) * D] = down_ref[quarter]
    outward[1].start()
    outward[2].start()
    parts[...] = jnp.zeros_like(parts)
    for spot in range(4):
        for level in range(4):
            taken = cross_up_ref[:, 192 * (4 * level + spot) : 192 * (4 * level + spot + 1)]
            parts[spot, :, 192 * level : 192 * (level + 1)] = taken
        for third in range(3):
            taken = cross_mix_ref[:, third * D + 192 * spot : third * D + 192 * (spot + 1)]
            parts[spot, :, D + 192 * third : D + 192 * (third + 1)] = taken
    chip = place_in()[1]
    for mask in range(4):
        built[3 + mask][...] = parts[chip ^ mask]
        outward[3 + mask].start()
    for copy in outward:
        copy.wait()


def join_cross(pieces, cross_down):
    def moves(layer, chip, core):
        found = []
        for mask in range(4):
            found.append((mask, (every, slice(0, D)), 0, (chip ^ mask, every, slice(0, D))))
            taken = (every, slice(D, D + 640))
            found.append((mask, taken, 0, (chip ^ mask, every, slice(2 * D, 2 * D + 640))))
        found.append((4, every, 0, (every, every, slice(D, 2 * D))))
        return found

    return copies(pieces + [cross_down.reshape(4, 24, D)], [(4, 24, 2 * D + 640)], moves)[0]


def place_cross(column, other):
    def moves(layer, chip, core):
        found = []
        for piece, side in ((0, core), (1, 1 - core)):
            source, lead = (every, every, every), (every, every, side)
            found.append((piece, source + (slice(0, D),), 0, lead))
            found.append((piece, source + (slice(2 * D, 2 * D + 640),), 1, lead))
            found.append((piece, source + (slice(D, 2 * D),), 2, (every, side)))
        return found

    up, mix, down = copies(
        [column, other], [(4, 4, 2, 24, D), (4, 4, 2, 24, 640), (4, 2, 4, 24, D)], moves
    )
    return up.reshape(D, D), mix.reshape(D, 640), down.reshape(D, D)


def segment_heads(segment, mixed_ref, docs_ref, probs_ref, context_ref):
    lane = lax.broadcasted_iota(jnp.int32, (SEG, 128), 1)
    rows = slice(segment * SEG, (segment + 1) * SEG)
    docs = jnp.broadcast_to(wide(docs_ref[segment : segment + 1, :]), (SEG, SEG))
    allowed = docs == docs.T
    for pair in range(HEADS // 2):
        query, key, value = (
            mixed_ref[rows, third * D + pair * 128 : third * D + (pair + 1) * 128]
            for third in range(3)
        )
        found = []
        for side in range(2):
            here = (lane < HEAD_DIM) if side == 0 else (lane >= HEAD_DIM)
            scores = contract(key, jnp.where(here, query, jnp.zeros_like(query)), 1, 1)
            scores = jnp.where(allowed, scores * HEAD_DIM ** (-0.5), masked_score)
            powers = jnp.exp(scores - jnp.max(scores, axis=0, keepdims=True))
            probs = powers / jnp.sum(powers, axis=0, keepdims=True)
            probs_ref[2 * pair + side] = probs
            found.append(contract(low(probs), value, 0, 0))
        context = jnp.where(lane < HEAD_DIM, found[0], found[1])
        context_ref[:, pair * 128 : (pair + 1) * 128] = low(context)


def local_attend(tokens_ref, group_ref, docs_ref, places_ref, *outs):
    mixed_ref, context_ref, probs_ref, rows_ref, places_out = outs
    rows_ref[...] = wide(group_ref[:, 4 * D : 4 * D + 128]).T
    lane = lax.broadcasted_iota(jnp.int32, (1, 64), 1)
    for place in range(2):
        picked = wide(places_ref[:, place : place + 1] == lane)
        places_out[place : place + 1, :] = contract_exact(picked, rows_ref[16:80, :], 1, 0)
    tokens = tokens_ref[...]
    for third in range(3):
        columns = slice(third * D, (third + 1) * D)
        mixed = contract(tokens, group_ref[:, columns], 1, 0)
        if third != 1:
            mixed = mixed + rows_ref[third // 2 : third // 2 + 1, :]
        mixed_ref[:, columns] = low(mixed)
    segment_heads(0, mixed_ref, docs_ref, probs_ref, context_ref)


def local_attend_more(
    tokens_ref, mixed_ref, before_ref, weight_ref, rows_ref, docs_ref, *outs
):
    context_ref, probs_ref, n_ref, scale_ref, low_ref, here = outs
    segment_heads(1, mixed_ref, docs_ref, probs_ref, here)
    context_ref[0:SEG, :] = before_ref[...]
    context_ref[SEG : 2 * SEG, :] = here[...]
    total = wide(tokens_ref[...]) + contract(context_ref[...], weight_ref[...], 1, 0)
    normed, scale = norm_parts(total + rows_ref[2:3, :])
    n_ref[...] = normed
    scale_ref[...] = scale
    low_ref[...] = low(normed * rows_ref[3:4, :] + rows_ref[4:5, :])


def local_up_part(low_ref, weight_ref, bias_ref, active_ref, slope_ref):
    hidden = contract(low_ref[...], weight_ref[...], 1, 0) + wide(bias_ref[...])
    chance = 0.5 * (1.0 + lax.erf(hidden * math.sqrt(0.5)))
    density = jnp.exp(-0.5 * hidden * hidden) * (1.0 / math.sqrt(2.0 * math.pi))
    active_ref[...] = low(hidden * chance)
    slope_ref[...] = low(chance + hidden * density)


def local_down_part(
    active_ref, weight_ref, first_ref, rows_ref, cot_a, cot_b, places_ref, *outs
):
    n_ref, scale_ref, kept_ref, given_ref, total = outs
    step = pl.program_id(0)
    part = contract(active_ref[...], weight_ref[...], 1, 0)

    @pl.when(step == 0)
    def _():
        first_norm = first_ref[...] * rows_ref[3:4, :] + rows_ref[4:5, :]
        total[...] = first_norm + rows_ref[5:6, :] + part

    @pl.when(step > 0)
    def _():
        total[...] += part

    @pl.when(step == 1)
    def _():
        normed, scale = norm_parts(total[...])
        n_ref[...] = normed
        scale_ref[...] = scale
        core = place_in()[2]
        heads, grads = [], []
        for place, cot in ((0, cot_a), (1, cot_b)):
            row = normed[place * SEG : place * SEG + 1] * rows_ref[6:7, :] + rows_ref[7:8, :]
            heads.append(row + places_ref[place : place + 1, :])
            grads.append(wide(cot[...])[0:1])
        for ref, mine in ((kept_ref, core == 0), (given_ref, core == 1)):
            ref[...] = jnp.zeros_like(ref)
            ref[0:1, :] = jnp.where(mine, heads[0], heads[1])
            ref[1:2, :] = jnp.where(mine, grads[0], grads[1])


def join_pair(kept_ref, got_ref, out_ref):
    core = place_in()[2]
    out_ref[...] = jnp.zeros_like(out_ref)
    out_ref[0:2, :] = jnp.where(core == 0, kept_ref[0:2, :], got_ref[0:2, :])
    out_ref[2:4, :] = jnp.where(core == 0, got_ref[0:2, :], kept_ref[0:2, :])


def cross_attend(
    own_ref, a_ref, b_ref, c_ref, weight_ref, rows_ref, docs_ref, *outs
):
    in_ref, grad_ref, mixed_ref, probs_ref, context_ref = outs
    layer, chip, core = place_in()
    for mask, ref in enumerate((own_ref, a_ref, b_ref, c_ref)):
        for side in range(2):
            row = 2 * (chip ^ mask) + side
            in_ref[pl.ds(row, 1), :] = ref[2 * side : 2 * side + 1, :]
            grad_ref[pl.ds(row, 1), :] = ref[2 * side + 1 : 2 * side + 2, :]
    biases = []
    for vector in (8, 9):
        row = rows_ref[vector : vector + 1, :]
        found = row[:, 0:192]
        for spot in range(1, 4):
            found = jnp.where(chip == spot, row[:, 192 * spot : 192 * (spot + 1)], found)
        biases.append(found)
    bias = jnp.concatenate([biases[0], jnp.zeros_like(biases[0]), biases[1]], axis=1)
    mixed = low(contract(low(in_ref[...]), weight_ref[:, 0:576], 1, 0) + bias)
    mixed_ref[...] = mixed
    row_docs = wide(jnp.where(core == 0, docs_ref[0:1, :], docs_ref[1:2, :]))
    count = row_docs.shape[1]
    lane = lax.broadcasted_iota(jnp.int32, (count, count), 1)
    line = lax.broadcasted_iota(jnp.int32, (count, count), 0)
    column_docs = jnp.sum(jnp.where(lane == line, row_docs, 0.0), axis=1, keepdims=True)
    allowed = row_docs == column_docs
    found = []
    for head in range(3):
        query, key, value = (
            mixed[:, third * 192 + head * HEAD_DIM : third * 192 + (head + 1) * HEAD_DIM]
            for third in range(3)
        )
        scores = contract(query, key, 1, 1) * HEAD_DIM ** (-0.5)
        scores = jnp.where(allowed, scores, masked_score)
        powers = jnp.exp(scores - jnp.max(scores, axis=-1, keepdims=True))
        probs = powers / jnp.sum(powers, axis=-1, keepdims=True)
        probs_ref[head] = probs
        found.append(contract(low(probs), value, 1, 0))
    context_ref[...] = low(jnp.concatenate(found, axis=1))


def cross_up_down(
    own_ref, a_ref, b_ref, c_ref, in_ref, out_weight_ref, rows_ref, up_ref, bias_ref, down_ref, *outs
):
    n_ref, scale_ref, low_ref, hidden_ref, active_ref, part_ref = outs
    chip = place_in()[1]
    total = in_ref[...] + rows_ref[10:11, :]
    for mask, ref in enumerate((own_ref, a_ref, b_ref, c_ref)):
        start = pl.multiple_of(192 * (chip ^ mask), 64)
        total = total + contract(ref[...], out_weight_ref[pl.ds(start, 192), :], 1, 0)
    normed, scale = norm_parts(total)
    n_ref[...] = normed
    scale_ref[...] = scale
    first = low(normed * rows_ref[11:12, :] + rows_ref[12:13, :])
    low_ref[...] = first
    hidden = contract(first, up_ref[...], 1, 0) + bias_ref[...]
    hidden_ref[...] = hidden
    active = low(hidden * (0.5 * (1.0 + lax.erf(hidden * math.sqrt(0.5)))))
    active_ref[...] = active
    part_ref[...] = contract(active, down_ref[...], 1, 0)


def cross_turn(
    own_ref, a_ref, b_ref, c_ref, n_ref, rows_ref, grad_ref, hidden_ref, up_ref, down_ref, *outs
):
    out_ref, second_ref, hidden_low_ref, part_ref, sums_ref = outs
    first = n_ref[...] * rows_ref[11:12, :] + rows_ref[12:13, :]
    total = (own_ref[...] + a_ref[...]) + (b_ref[...] + c_ref[...])
    normed, scale = norm_parts(first + total + rows_ref[13:14, :])
    out_ref[...] = normed * rows_ref[14:15, :] + rows_ref[15:16, :]
    grad = grad_ref[...]
    second = norm_back(grad, normed, scale, rows_ref[14:15, :])
    second_ref[...] = second
    hidden_low = low(contract(low(second), down_ref[...], 1, 1) * gelu_slope(hidden_ref[...]))
    hidden_low_ref[...] = hidden_low
    part_ref[...] = contract(hidden_low, up_ref[...], 1, 1)
    sums_ref[...] = jnp.zeros_like(sums_ref)
    sums_ref[0:1, :] = column_sum(grad * normed)
    sums_ref[1:2, :] = column_sum(grad)


def cross_attend_back(
    own_ref,
    a_ref,
    b_ref,
    c_ref,
    second_ref,
    n_ref,
    scale_ref,
    rows_ref,
    out_weight_ref,
    mixed_ref,
    probs_ref,
    weight_ref,
    hidden_low_ref,
    active_ref,
    context_ref,
    in_ref,
    low_ref,
    sums_ref,
    places_ref,
    total_ref,
    part_ref,
    pack_ref,
    pack,
    rows,
):
    chip = place_in()[1]
    grad = second_ref[...] + (own_ref[...] + a_ref[...]) + (b_ref[...] + c_ref[...])
    normed = n_ref[...]
    total = norm_back(grad, normed, scale_ref[...], rows_ref[11:12, :])
    total_ref[...] = total
    branch = low(total)
    start = pl.multiple_of(192 * chip, 64)
    context_low = low(contract(branch, out_weight_ref[pl.ds(start, 192), :], 1, 1))
    mixed = mixed_ref[...]
    found = [[], [], []]
    for head in range(3):
        query, key, value = (
            mixed[:, third * 192 + head * HEAD_DIM : third * 192 + (head + 1) * HEAD_DIM]
            for third in range(3)
        )
        part = context_low[:, head * HEAD_DIM : (head + 1) * HEAD_DIM]
        probs = probs_ref[head]
        prob_grad = contract(part, value, 1, 1)
        score = low(probs * (prob_grad - jnp.sum(probs * prob_grad, axis=-1, keepdims=True)))
        found[0].append(contract(score, key, 1, 0) * HEAD_DIM ** (-0.5))
        found[1].append(contract(score, query, 0, 0) * HEAD_DIM ** (-0.5))
        found[2].append(contract(low(probs), part, 0, 0))
    mixed_low = low(jnp.concatenate(found[0] + found[1] + found[2], axis=1))
    part_ref[...] = contract(mixed_low, weight_ref[:, 0:576], 1, 1)
    pack[...] = jnp.zeros_like(pack)
    pack[0:8, :] = wide(hidden_low_ref[...])
    pack[8:16, :] = wide(active_ref[...])
    pack[16:24, 0:576] = wide(mixed_low)
    pack[16:24, 576:768] = wide(context_ref[...])
    for i, value in enumerate(
        (in_ref[...], wide(low_ref[...]), total, second_ref[...], total)
    ):
        rows[...] = value
        for side in range(2):
            row = 24 + 2 * i + side
            pack[row : row + 1, :] = rows[pl.ds(2 * chip + side, 1), :]
    rows[0:1, :] = column_sum(grad * normed)
    rows[1:2, :] = column_sum(grad)
    rows[2:4, :] = sums_ref[0:2, :]
    pack[34:35, :] = rows[pl.ds(chip, 1), :]
    for place in range(2):
        spot = wide(places_ref[:, place : place + 1])
        pack[35 + place : 36 + place, :] = jnp.broadcast_to(spot, (1, D))
    pack_ref[...] = low(pack[...])


def cross_finish(own_ref, a_ref, b_ref, c_ref, total_ref, out_ref, kept_ref, given_ref, rows):
    layer, chip, core = place_in()
    rows[...] = total_ref[...] + (own_ref[...] + a_ref[...]) + (b_ref[...] + c_ref[...])
    for ref, side in ((kept_ref, core), (given_ref, 1 - core)):
        ref[...] = jnp.zeros_like(ref)
        ref[0:1, :] = rows[pl.ds(2 * chip + side, 1), :]
        ref[1:2, :] = out_ref[pl.ds(2 * chip + side, 1), :]


def cross_owner(mine_ref, other_ref, weight_ref, *refs):
    mix_ref, out_ref, up_ref, down_ref, vectors_ref, bias_ref, table_ref = refs[:7]
    hidden, mixed, single, active, sums, places = refs[7:]
    layer, chip, core = place_in()
    rank = 8 * layer + 2 * chip + core
    sums[...] = jnp.zeros_like(sums)
    for level in range(4):
        for side in range(2):
            group = 2 * level + side
            rows = slice(8 * group, 8 * group + 8)
            for spot in range(4):
                value = wide(
                    jnp.where(core == side, mine_ref[level, spot], other_ref[level, spot])
                )
                hidden[spot, rows, :] = value[0:8]
                mixed[spot, rows, :] = value[16:24]
                for i in range(5):
                    start = 8 * group + 2 * spot
                    single[i, start : start + 2, :] = value[24 + 2 * i : 26 + 2 * i]
                sums[spot : spot + 1, :] += value[34:35]
                for sequence in range(2):
                    row = 16 * level + 8 * sequence + 2 * spot + side
                    places[row : row + 1, :] = value[35 + sequence : 36 + sequence, 0:128]
            value = jnp.where(core == side, mine_ref[level, chip], other_ref[level, chip])
            active[rows, :] = wide(value)[8:16]

    def select(count, first):
        lane = lax.broadcasted_iota(jnp.int32, (count, D), 1)
        row = lax.broadcasted_iota(jnp.int32, (count, D), 0)
        return wide(lane == first + row)

    own = select(24, 24 * rank)
    offset = 24 * (2 * chip + core)
    units = select(96, 192 * layer + 96 * core)
    own_low = low(own)

    def columns_of(array_in):
        return low(contract(own_low, low(array_in), 1, 1))

    inputs = columns_of(single[0])
    for spot in range(4):
        part = contract(inputs, low(mixed[spot][:, 0:576]), 1, 0)
        for third in range(3):
            start = third * D + 192 * spot
            mix_ref[:, start : start + 192] = part[:, 192 * third : 192 * (third + 1)]
    own_mixed = mixed[layer]
    context = low(contract(low(select(24, 576 + offset)), low(own_mixed), 1, 1))
    out_ref[...] = contract(context, low(single[2]), 1, 0)
    first = columns_of(single[1])
    for spot in range(4):
        part = contract(first, low(hidden[spot]), 1, 0)
        for level in range(4):
            start = 192 * (4 * level + spot)
            up_ref[:, start : start + 192] = part[:, 192 * level : 192 * (level + 1)]
    units_low = low(contract(low(units), low(active[...]), 1, 1))
    down_ref[...] = contract(units_low, low(single[3]), 1, 0)
    mixed_sum = column_sum(own_mixed)
    vectors_ref[0:1, :] = contract_exact(mixed_sum, select(24, offset), 1, 1)
    vectors_ref[1:2, :] = contract_exact(mixed_sum, select(24, 384 + offset), 1, 1)
    for row, value in (
        (2, column_sum(single[2])),
        (3, sums[0:1, :]),
        (4, sums[1:2, :]),
        (5, column_sum(single[3])),
        (6, sums[2:3, :]),
        (7, sums[3:4, :]),
    ):
        vectors_ref[row : row + 1, :] = contract_exact(value, own, 1, 1)
    bias_ref[...] = contract_exact(column_sum(hidden[chip]), units, 1, 1)
    grads = contract(low(single[4]), own_low, 1, 1)
    for spot in range(4):
        for third in range(3):
            start = third * D + 192 * spot
            part = low(mixed[spot][:, 192 * third : 192 * (third + 1)])
            grads = grads + contract(part, weight_ref[:, start : start + 192], 1, 1)
    lane = wide(lax.broadcasted_iota(jnp.int32, (64, 64), 1))
    table_ref[...] = contract_exact(wide(places[:, 0:64] == lane), grads, 0, 0)


def split_cores(value, kept_ref, gone_ref):
    rows = kept_ref.shape[1]
    core = lax.rem(lax.axis_index("seq"), 2)
    parts = value.reshape(-1, 2, rows, value.shape[1])
    kept_ref[...] = low(jnp.where(core == 0, parts[:, 0], parts[:, 1]))
    gone_ref[...] = low(jnp.where(core == 0, parts[:, 1], parts[:, 0]))


def local_down_back(
    cot_ref, mine_ref, other_ref, n_ref, scale_ref, rows_ref, active_ref, slope_ref, weight_ref, *outs
):
    out_ref, second_ref, kept_ref, gone_ref, hidden_ref, sums_ref, bias_ref, second_low_ref = outs
    step = pl.program_id(0)

    @pl.when(step == 0)
    def _():
        core = place_in()[2]
        row = lax.broadcasted_iota(jnp.int32, (2 * SEG, D), 0)
        grad = wide(cot_ref[...])
        normed = n_ref[...]
        out = normed * rows_ref[6:7, :] + rows_ref[7:8, :]
        for place in range(2):
            heads = jnp.where(core == place, mine_ref[...], other_ref[...])
            grad = jnp.where(row == place * SEG, heads[0:1], grad)
            out = jnp.where(row == place * SEG, heads[1:2], out)
        out_ref[...] = low(out)
        second = norm_back(grad, normed, scale_ref[...], rows_ref[6:7, :])
        second_ref[...] = second
        second_low_ref[...] = low(second)
        sums_ref[0:1, :] = column_sum(wide(low(second)))
        sums_ref[1:2, :] = column_sum(grad * normed)
        sums_ref[2:3, :] = column_sum(grad)

    second_low = second_low_ref[...]
    split_cores(contract(active_ref[...], second_low, 0, 0), kept_ref, gone_ref)
    hidden = low(contract(second_low, weight_ref[...], 1, 1) * wide(slope_ref[...]))
    hidden_ref[...] = hidden
    bias_ref[...] = column_sum(wide(hidden))


def local_up_back(low_ref, hidden_ref, weight_ref, second_ref, kept_ref, gone_ref, first_ref):
    hidden = hidden_ref[...]
    split_cores(contract(low_ref[...], hidden, 0, 0), kept_ref, gone_ref)
    part = contract(hidden, weight_ref[...], 1, 1)
    step = pl.program_id(0)

    @pl.when(step == 0)
    def _():
        first_ref[...] = second_ref[...] + part

    @pl.when(step > 0)
    def _():
        first_ref[...] += part


def local_attend_back(
    first_ref, n_ref, scale_ref, rows_ref, context_ref, mixed_ref, probs_a, probs_b, group_ref, *outs
):
    out_ref, total_ref, sums_ref, back_ref, context_low_ref = outs
    grad, normed = first_ref[...], n_ref[...]
    total = norm_back(grad, normed, scale_ref[...], rows_ref[3:4, :])
    total_ref[...] = total
    branch = low(total)
    sums_ref[2:3, :] = column_sum(wide(branch))
    sums_ref[3:4, :] = column_sum(grad * normed)
    sums_ref[4:5, :] = column_sum(grad)
    out_ref[...] = low(contract(context_ref[...], branch, 0, 0))
    context_low_ref[...] = low(contract(branch, group_ref[...], 1, 1))
    lane = lax.broadcasted_iota(jnp.int32, (SEG, 128), 1)
    for segment in range(2):
        rows = slice(segment * SEG, (segment + 1) * SEG)
        for pair in range(HEADS // 2):
            places = [
                slice(third * D + pair * 128, third * D + (pair + 1) * 128) for third in range(3)
            ]
            query, key, value = (mixed_ref[rows, place] for place in places)
            grad = context_low_ref[rows, places[0]]
            found = []
            for side in range(2):
                here = (lane < HEAD_DIM) if side == 0 else (lane >= HEAD_DIM)
                probs = (probs_a, probs_b)[segment][2 * pair + side]
                prob_grad = contract(value, jnp.where(here, grad, jnp.zeros_like(grad)), 1, 1)
                value_grad = contract(low(probs), grad, 1, 0)
                score = low(
                    probs * (prob_grad - jnp.sum(probs * prob_grad, axis=0, keepdims=True))
                )
                found.append(
                    (contract(score, key, 0, 0), contract(score, query, 1, 0), value_grad)
                )
            for third in range(3):
                merged = jnp.where(lane < HEAD_DIM, found[0][third], found[1][third])
                if third < 2:
                    merged = merged * HEAD_DIM ** (-0.5)
                back_ref[rows, places[third]] = low(merged)
    for third in (0, 2):
        columns = slice(third * D, (third + 1) * D)
        sums_ref[third // 2 : third // 2 + 1, :] = column_sum(wide(back_ref[:, columns]))


def local_mix_back(
    total_ref, back_ref, tokens_ref, group_ref, out_ref, sums_ref, more_ref, bias_ref, *outs
):
    input_ref, kept_ref, gone_ref, small_ref = outs
    tokens, total = tokens_ref[...], total_ref[...]
    for third in range(3):
        columns = slice(third * D, (third + 1) * D)
        back = back_ref[:, columns]
        grad = contract(tokens, back, 0, 0)
        split_cores(grad, kept_ref.at[:, :, columns], gone_ref.at[:, :, columns])
        total = total + contract(back, group_ref[:, columns], 1, 1)
    input_ref[...] = total
    columns = slice(3 * D, 4 * D)
    split_cores(wide(out_ref[...]), kept_ref.at[:, :, columns], gone_ref.at[:, :, columns])
    small_ref[...] = jnp.zeros_like(small_ref)
    small_ref[0:5, :] = sums_ref[0:5, :]
    small_ref[5:8, :] = more_ref[0:3, :]
    for owner in range(32):
        for row in range(4):
            taken = bias_ref[:, 96 * owner + 24 * row : 96 * owner + 24 * (row + 1)]
            small_ref[8 + row : 9 + row, 24 * owner : 24 * (owner + 1)] = taken
    columns = slice(4 * D, 4 * D + 128)
    split_cores(small_ref[...].T, kept_ref.at[:, :, columns], gone_ref.at[:, :, columns])


def finish_mix(own_ref, a_ref, b_ref, c_ref, mix_ref, out_ref, vectors_ref, bias_ref, wide_ref):
    total = own_ref[...] + wide(a_ref[...]) + wide(b_ref[...]) + wide(c_ref[...])
    mix_ref[...] = total[:, 0 : 3 * D]
    out_ref[...] = total[:, 3 * D : 4 * D]
    wide_ref[...] = jnp.zeros_like(wide_ref)
    wide_ref[0:24, :] = total[:, 4 * D : 4 * D + 128]
    turned = wide_ref[...].T
    vectors_ref[...] = turned[0:8, 0:24]
    for row in range(4):
        bias_ref[:, 24 * row : 24 * (row + 1)] = turned[8 + row : 9 + row, 0:24]


def plane_three(array_in):
    return [array_in] + [swap_chip(array_in, mask) for mask in (1, 2, 3)]


def plane_shards(
    tokens,
    cotangent,
    token_docs,
    segment_docs,
    segment_positions,
    local_mix,
    local_out,
    local_up,
    local_down,
    local_vectors,
    local_up_bias,
    cross_mix,
    cross_out,
    cross_up,
    cross_down,
    cross_vectors,
    cross_up_bias,
    position_table,
):
    chip = place_in()[1]
    flat_tokens = tokens.reshape(256, D)
    flat_cot = cotangent.reshape(256, D)
    places_in = segment_positions.T

    shards_in = (
        local_mix,
        local_out,
        local_up,
        local_down.reshape(4, 24, D),
        local_vectors,
        local_up_bias.reshape(1, 96),
        cross_mix,
        cross_out,
        cross_up,
        cross_vectors,
        cross_up_bias.reshape(1, 96),
        position_table.T,
    )
    made = [half(24, 3200), half(24, 5 * D), half(24, 4 * D)] + [half(24, D + 640)] * 4
    far = pl.BlockSpec(memory_space=pltpu.HBM)
    shard_one, shard_two, shard_three, *cross_pieces = on_core(
        prepare,
        made,
        shards_in,
        0,
        in_specs=[far] * 12,
        out_specs=[far] * 7,
        scratch=[pltpu.VMEM(a.shape, a.dtype) for a in list(shards_in) + made]
        + [
            pltpu.VMEM((128, 128), jnp.float32),
            pltpu.VMEM((128, 128), jnp.float32),
            pltpu.VMEM((4, 24, D + 640), jnp.bfloat16),
            pltpu.SemaphoreType.DMA((2, 12)),
        ],
    )
    cross_sent = [cross_pieces[0]] + [swap_chip(cross_pieces[mask], mask) for mask in (1, 2, 3)]
    z_one = reach_dp(shard_one)
    shard_two, *z_one = stage(shard_two, *z_one, *cross_sent)
    z_one, cross_sent = z_one[:4], z_one[4:]
    column_one = join_dp(z_one)
    column_one, shard_two = stage(column_one, shard_two)

    first, second = swap_one(column_one), swap_two(column_one)
    cross_row = join_cross(cross_sent, after(cross_down, column_one))
    *z_two, first, second, column_one, cross_row = stage(
        *reach_dp(shard_two), first, second, column_one, cross_row
    )

    third = swap_two(first)
    others = [swap_core(piece) for piece in (column_one, first, second)]
    column_two = join_dp(z_two)
    cross_moved = [cross_row, swap_dp(cross_row, 1)]
    third, column_two, cross_moved[1], *others = stage(third, column_two, cross_moved[1], *others)
    others.append(swap_core(third))
    column_two, shard_three, *others = stage(column_two, shard_three, *others)

    first_group = gather_plane([column_one, first, second, third], others).reshape(D, 3200)
    mixed_rows, context_first, probs_first, rows, place_rows = on_core(
        local_attend,
        [half(256, 3 * D), half(SEG, D), shape_of(12, SEG, SEG), shape_of(128, D), shape_of(2, D)],
        (flat_tokens, first_group, token_docs, places_in),
        0,
    )
    first_two, second_two = swap_one(column_two), swap_two(column_two)
    *z_three, mixed_rows, first_two, second_two, column_two, cross_moved[1] = stage(
        *reach_dp(shard_three), mixed_rows, first_two, second_two, column_two, cross_moved[1]
    )
    cross_moved.append(swap_dp(cross_moved[1], 1))

    third_two = swap_two(first_two)
    others = [swap_core(piece) for piece in (column_two, first_two, second_two)]
    column_three = join_dp(z_three)
    def plain(*shapes):
        return [pl.BlockSpec(shape, lambda j, n=len(shape): (0,) * n) for shape in shapes]

    context_rows, probs_second, normed_one, scale_one, low_one = on_core(
        local_attend_more,
        [half(256, D), shape_of(12, SEG, SEG), shape_of(256, D), shape_of(256, 1), half(256, D)],
        (flat_tokens, mixed_rows, context_first, first_group, rows, token_docs),
        0,
        grid=(1,),
        in_specs=plain((256, D), (256, 3 * D), (SEG, D))
        + [pl.BlockSpec((D, D), lambda j: (0, 3))]
        + plain((128, D), (2, SEG)),
        out_specs=plain((256, D), (12, SEG, SEG), (256, D), (256, 1), (256, D)),
        scratch=[pltpu.VMEM((SEG, D), jnp.bfloat16)],
    )
    up_bias = rows[80:84].reshape(4, 32, 24).transpose(1, 0, 2).reshape(1, 4 * D)
    cross_moved[2], third_two, column_three, low_one, up_bias, rows_later, *others = stage(
        cross_moved[2], third_two, column_three, low_one, up_bias, rows[84:88], *others
    )
    cross_moved.append(swap_dp(cross_moved[2], 1))

    first_three, second_three = swap_one(column_three), swap_two(column_three)
    others.append(swap_core(third_two))
    second_group, cross_out_weight = gather_up(
        [column_two, first_two, second_two, third_two], others
    )
    whole = pl.BlockSpec((256, D), lambda j: (0, 0))
    thin = pl.BlockSpec((256, 1), lambda j: (0, 0))
    vectors = pl.BlockSpec((128, D), lambda j: (0, 0))
    eight = pl.BlockSpec((8, D), lambda j: (0, 0))
    across = pl.BlockSpec((256, D), lambda j: (0, j))
    tall = pl.BlockSpec((D, D), lambda j: (0, j))
    deep = pl.BlockSpec((D, D), lambda j: (j, 0))
    strip = pl.BlockSpec((1, D), lambda j: (0, j))
    across_half = pl.BlockSpec((256, 2 * D), lambda j: (0, j))
    tall_half = pl.BlockSpec((D, 2 * D), lambda j: (0, j))
    deep_half = pl.BlockSpec((2 * D, D), lambda j: (j, 0))
    strip_half = pl.BlockSpec((1, 2 * D), lambda j: (0, j))
    active_rows, slope_rows = on_core(
        local_up_part,
        [half(256, 4 * D)] * 2,
        (low_one, second_group, up_bias),
        2 * 256 * D * 4 * D,
        grid=(4,),
        in_specs=[whole, tall, strip],
        out_specs=[across, across],
    )
    active_rows, first_three, second_three, column_three, cross_moved[3], rows_later = stage(
        active_rows, first_three, second_three, column_three, cross_moved[3], rows_later
    )

    third_three = swap_two(first_three)
    others = [swap_core(piece) for piece in (column_three, first_three, second_three)]
    cross_bias = rows_later.reshape(4, 4, 4, 2, 24)
    cross_bias = lax.dynamic_index_in_dim(cross_bias, chip, 2, keepdims=False)
    cross_bias = cross_bias.transpose(1, 2, 0, 3).reshape(1, D)
    third_three, cross_column, cross_bias, *others = stage(
        third_three, join_dp(cross_moved), cross_bias, *others
    )

    others.append(swap_core(third_three))
    down_weight = gather_down([column_three, first_three, second_three, third_three], others)
    down_weight, cross_column = stage(down_weight.reshape(4 * D, D), cross_column)
    cross_other = swap_core(cross_column)
    normed_two, scale_two, kept, given = on_core(
        local_down_part,
        [shape_of(256, D), shape_of(256, 1), shape_of(8, D), shape_of(8, D)],
        (active_rows, down_weight, normed_one, rows, flat_cot, flat_cot, place_rows),
        2 * 256 * D * 4 * D,
        grid=(2,),
        in_specs=[
            across_half,
            deep_half,
            whole,
            vectors,
            pl.BlockSpec((16, D), lambda j: (0, 0)),
            pl.BlockSpec((16, D), lambda j: (8, 0)),
            pl.BlockSpec((2, D), lambda j: (0, 0)),
        ],
        out_specs=[whole, thin, eight, eight],
        scratch=[pltpu.VMEM((256, D), jnp.float32)],
    )

    row8, mix_share = (8, D), (D, 640)
    out_share = pl.BlockSpec((D, D), lambda j: (0, 0))
    up_share = pl.BlockSpec((D, D), lambda j: (0, 0))
    given, kept, cross_other = stage(given, kept, cross_other)
    got = swap_core(given)
    cross_up_part, cross_mix_part, cross_down_part = place_cross(cross_column, cross_other)
    kept, got, cross_mix_part = stage(kept, got, cross_mix_part)
    pair = on_core(join_pair, shape_of(8, D), (kept, got), 0, room=12)
    row_in, row_grad, mixed, probs, context = on_core(
        cross_attend,
        [shape_of(8, D), shape_of(8, D), half(8, 576), shape_of(3, 8, 8), half(8, 192)],
        (*plane_three(pair), cross_mix_part, rows, segment_docs),
        0,
        room=12,
    )
    row_n, row_scale, row_low, hidden, active, part = on_core(
        cross_up_down,
        [shape_of(8, D), shape_of(8, 1), half(8, D), shape_of(8, D), half(8, D), shape_of(8, D)],
        (
            *plane_three(context),
            row_in,
            cross_out_weight,
            rows,
            cross_up_part,
            cross_bias,
            cross_down_part,
        ),
        0,
        grid=(1,),
        in_specs=plain(*[(8, 192)] * 4, row8)
        + [out_share]
        + plain((128, D))
        + [up_share]
        + plain((1, D), (D, D)),
        out_specs=plain(row8, (8, 1), row8, row8, row8, row8),
        room=12,
    )
    row_out, row_second, hidden_low, part, sums = on_core(
        cross_turn,
        [shape_of(8, D), shape_of(8, D), half(8, D), shape_of(8, D), shape_of(8, D)],
        (*plane_three(part), row_n, rows, row_grad, hidden, cross_up_part, cross_down_part),
        0,
        grid=(1,),
        in_specs=plain(*[row8] * 4, row8, (128, D), row8, row8) + [up_share] + plain((D, D)),
        out_specs=plain(*[row8] * 5),
        room=12,
    )
    row_total, part, packed = on_core(
        cross_attend_back,
        [shape_of(8, D), shape_of(8, D), half(48, D)],
        (
            *plane_three(part),
            row_second,
            row_n,
            row_scale,
            rows,
            cross_out_weight,
            mixed,
            probs,
            cross_mix_part,
            hidden_low,
            active,
            context,
            row_in,
            row_low,
            sums,
            places_in,
        ),
        0,
        grid=(1,),
        in_specs=plain(*[row8] * 4, row8, row8, (8, 1), (128, D))
        + [out_share]
        + plain((8, 576), (3, 8, 8), mix_share, row8, row8, (8, 192), row8, row8, row8, (1, 2)),
        out_specs=plain(row8, row8, (48, D)),
        scratch=[pltpu.VMEM((48, D), jnp.float32), pltpu.VMEM((8, D), jnp.float32)],
        room=12,
    )
    kept, given = on_core(
        cross_finish,
        [shape_of(8, D), shape_of(8, D)],
        (*plane_three(part), row_total, row_out),
        0,
        scratch=[pltpu.VMEM((8, D), jnp.float32)],
        room=12,
    )
    got, kept, packed = stage(swap_core(given), kept, packed)
    pack_one, pack_two = swap_one(packed), swap_two(packed)

    twos = pl.BlockSpec((8, 96, D), lambda j: (j, 0, 0))
    layer_output, second_rows, down_kept, down_gone, hidden_grads, sums_two, bias_grad = on_core(
        local_down_back,
        [
            half(256, D),
            shape_of(256, D),
            half(16, 96, D),
            half(16, 96, D),
            half(256, 4 * D),
            shape_of(8, D),
            shape_of(1, 4 * D),
        ],
        (flat_cot, kept, got, normed_two, scale_two, rows, active_rows, slope_rows, down_weight),
        4 * 256 * D * 4 * D,
        grid=(2,),
        in_specs=[whole, eight, eight, whole, thin, vectors, across_half, across_half, deep_half],
        out_specs=[whole, whole, twos, twos, across_half, eight, strip_half],
        scratch=[pltpu.VMEM((256, D), jnp.bfloat16)],
    )
    down_total = Sum(down_kept.reshape(4, 4, 96, D))
    hidden_grads, down_gone, pack_one, pack_two = stage(
        hidden_grads, down_gone.reshape(4, 4, 96, D), pack_one, pack_two
    )
    pack_three = swap_two(pack_one)

    down_got = swap_core(down_gone)
    sixteens = pl.BlockSpec((16, 24, 2 * D), lambda j: (0, 0, j))
    up_kept, up_gone, first_rows = on_core(
        local_up_back,
        [half(16, 24, 4 * D), half(16, 24, 4 * D), shape_of(256, D)],
        (low_one, hidden_grads, second_group, second_rows),
        4 * 256 * D * 4 * D,
        grid=(2,),
        in_specs=[whole, across_half, tall_half, whole],
        out_specs=[sixteens, sixteens, whole],
    )
    up_total = Sum(up_kept.reshape(4, 4, 24, 4 * D))
    down_got, first_rows, up_gone, pack_three = stage(
        down_got, first_rows, up_gone.reshape(4, 4, 24, 4 * D), pack_three
    )
    plane_pack = join_chips([packed, pack_one, pack_two, pack_three])
    packs = [plane_pack, swap_dp(plane_pack, 1), swap_dp(plane_pack, 3)]

    up_got = swap_core(up_gone)
    down_sent = down_total.first(down_got)
    down_back = swap_one(down_sent)
    flat = pl.BlockSpec((256, 3 * D), lambda j: (0, 0))
    out_grad, sum_rows, sums_one, back_rows = on_core(
        local_attend_back,
        [half(D, D), shape_of(256, D), shape_of(8, D), half(256, 3 * D)],
        (
            first_rows,
            normed_one,
            scale_one,
            rows,
            context_rows,
            mixed_rows,
            probs_first,
            probs_second,
            first_group,
        ),
        4 * 256 * D * 2 * D,
        grid=(1,),
        in_specs=[
            whole,
            whole,
            thin,
            vectors,
            whole,
            flat,
            pl.BlockSpec((12, SEG, SEG), lambda j: (0, 0, 0)),
            pl.BlockSpec((12, SEG, SEG), lambda j: (0, 0, 0)),
            pl.BlockSpec((D, D), lambda j: (0, 3)),
        ],
        out_specs=[pl.BlockSpec((D, D), lambda j: (0, 0)), whole, eight, flat],
        scratch=[pltpu.VMEM((256, D), jnp.bfloat16)],
    )
    up_sent = up_total.first(up_got)
    down_back, back_rows, up_sent, *packs = stage(down_back, back_rows, up_sent, *packs)
    packs.insert(2, swap_dp(packs[0], 2))

    up_back = swap_one(up_sent)
    down_onward = down_total.second(down_back)
    sides = [half(16, 24, 4 * D + 128)] * 2
    input_grad, mix_kept, mix_gone = on_core(
        local_mix_back,
        [shape_of(256, D)] + sides,
        (
            sum_rows,
            back_rows,
            flat_tokens,
            first_group,
            out_grad,
            sums_one,
            sums_two,
            bias_grad,
        ),
        4 * 256 * D * 3 * D,
        scratch=[pltpu.VMEM((128, D), jnp.float32)],
    )
    mix_total = Sum(mix_kept.reshape(4, 4, 24, 3200))
    up_back, down_onward, mix_gone, packs[2] = stage(
        up_back, down_onward, mix_gone.reshape(4, 4, 24, 3200), packs[2]
    )

    mix_got, down_last = swap_core(mix_gone), swap_two(down_onward)
    up_onward = up_total.second(up_back)
    my_rows = join_dp(packs)
    mix_got, down_last, up_onward, my_rows = stage(mix_got, down_last, up_onward, my_rows)

    up_last = swap_two(up_onward)
    mix_sent = mix_total.first(mix_got)
    down_others = down_total.third(down_last)
    up_last, mix_sent, my_rows, *down_others = stage(up_last, mix_sent, my_rows, *down_others)
    other_rows = swap_core(my_rows)

    mix_back, down_others = swap_one(mix_sent), send_dp(down_others)
    up_others = up_total.third(up_last)
    mix_back, other_rows, *others = stage(mix_back, other_rows, *down_others, *up_others)
    down_others, up_others = others[:3], others[3:]

    mix_last = swap_two(mix_total.second(mix_back))
    up_others = send_dp(up_others)
    down_sum = down_total.total(down_others)
    mix_last, down_sum, other_rows = stage(mix_last, down_sum, other_rows)

    mix_others = send_dp(mix_total.third(mix_last))
    up_sum = up_total.total(up_others)
    cross_grads = on_core(
        cross_owner,
        [
            shape_of(24, 3 * D),
            shape_of(24, D),
            shape_of(24, 4 * D),
            shape_of(96, D),
            shape_of(8, 24),
            shape_of(1, 96),
            shape_of(64, 24),
        ],
        (my_rows, other_rows, cross_mix),
        0,
        scratch=[
            pltpu.VMEM((4, 64, D), jnp.float32),
            pltpu.VMEM((4, 64, D), jnp.float32),
            pltpu.VMEM((5, 64, D), jnp.float32),
            pltpu.VMEM((64, D), jnp.float32),
            pltpu.VMEM((8, D), jnp.float32),
            pltpu.VMEM((64, 128), jnp.float32),
        ],
    )
    mix_sum, out_sum, vectors_sum, bias_sum = on_core(
        finish_mix,
        [shape_of(24, 3 * D), shape_of(24, D), shape_of(8, 24), shape_of(1, 96)],
        (mix_total.own, *mix_others),
        0,
        grid=(1,),
        in_specs=plain(*[(24, 4 * D + 128)] * 4),
        out_specs=plain((24, 3 * D), (24, D), (8, 24), (1, 96)),
        scratch=[pltpu.VMEM((128, 128), jnp.float32)],
    )
    return (
        layer_output.reshape(2, SEG, D),
        input_grad.reshape(2, SEG, D),
        mix_sum,
        out_sum,
        up_sum,
        down_sum,
        vectors_sum,
        bias_sum.reshape(96),
        *cross_grads[:5],
        cross_grads[5].reshape(96),
        cross_grads[6],
    )


def solution(mesh):
    flat = dict(mesh.shape) == {"dp": 4, "seq": 8}
    return jax.shard_map(
        plane_shards if flat else shards,
        mesh=mesh,
        in_specs=(
            P("dp", "seq", None),
            P("dp", "seq", None),
            P("dp", "seq"),
            P("dp", None),
            P("dp", "seq"),
            P(("dp", "seq"), None),
            P(("dp", "seq"), None),
            P(("dp", "seq"), None),
            P(("dp", "seq"), None),
            P(None, ("dp", "seq")),
            P(("dp", "seq")),
            P(("dp", "seq"), None),
            P(("dp", "seq"), None),
            P(("dp", "seq"), None),
            P(("dp", "seq"), None),
            P(None, ("dp", "seq")),
            P(("dp", "seq")),
            P(None, ("dp", "seq")),
        ),
        out_specs=(
            P("dp", "seq", None),
            P("dp", "seq", None),
            P(("dp", "seq"), None),
            P(("dp", "seq"), None),
            P(("dp", "seq"), None),
            P(("dp", "seq"), None),
            P(None, ("dp", "seq")),
            P(("dp", "seq")),
            P(("dp", "seq"), None),
            P(("dp", "seq"), None),
            P(("dp", "seq"), None),
            P(("dp", "seq"), None),
            P(None, ("dp", "seq")),
            P(("dp", "seq")),
            P(None, ("dp", "seq")),
        ),
        check_vma=False,
    )
```

```python
from functools import partial
import math

import jax
import jax.numpy as jnp
from jax import lax
from jax.experimental import pallas as pl
from jax.experimental.pallas import tpu as pltpu
from jax.sharding import PartitionSpec as P

D = 768
HEADS = 12
HEAD_DIM = 64
SEG = 128
MICRO = 2


epsilon = 1e-05
masked_score = -1000000000.0
owner_dims = (0, 0, 0, 0, 1, 0, 0, 0, 0, 0, 1, 0, 1)


def layer_norm(values, gain_row, shift_row):
    centered = values - jnp.mean(values, axis=-1, keepdims=True)
    variance = jnp.mean(centered * centered, axis=-1, keepdims=True)
    return centered * lax.rsqrt(variance + epsilon) * gain_row + shift_row


def gelu_exact(hidden):
    return jax.nn.gelu(hidden, approximate=False)


def contract(left_side, right_side, left_dim, right_dim):
    return lax.dot_general(
        left_side,
        right_side,
        (((left_dim,), (right_dim,)), ((), ())),
        preferred_element_type=jnp.float32,
    )


def contract_exact(left_side, right_side, left_dim, right_dim):
    return lax.dot_general(
        left_side,
        right_side,
        (((left_dim,), (right_dim,)), ((), ())),
        precision=lax.Precision.HIGHEST,
        preferred_element_type=jnp.float32,
    )


def owner_pack(grads, devices):
    pieces = []
    for grad_value, split_dim in zip(grads, owner_dims):
        if split_dim == 0:
            pieces.append(grad_value.reshape(devices, -1))
        else:
            row_count = grad_value.shape[0]
            pieces.append(
                grad_value.reshape(row_count, devices, -1).transpose(1, 0, 2).reshape(devices, -1)
            )
    return jnp.concatenate(pieces, axis=1)


def owner_unpack(packed, shard_shapes):
    results = []
    offset = 0
    for shard_shape in shard_shapes:
        length = math.prod(shard_shape)
        results.append(packed[0, offset : offset + length].reshape(shard_shape))
        offset = offset + length
    return tuple(results)


def fetch_weights(
    local_mix,
    local_out,
    local_up,
    local_down,
    local_vectors,
    local_up_bias,
    cross_mix,
    cross_out,
    cross_up,
    cross_down,
    cross_vectors,
    cross_up_bias,
    position_table,
):
    return (
        lax.all_gather(local_mix, ("dp", "seq"), axis=0, tiled=True),
        lax.all_gather(local_out, ("dp", "seq"), axis=0, tiled=True),
        lax.all_gather(local_up, ("dp", "seq"), axis=0, tiled=True),
        lax.all_gather(local_down, ("dp", "seq"), axis=0, tiled=True),
        lax.all_gather(local_vectors, ("dp", "seq"), axis=1, tiled=True),
        lax.all_gather(local_up_bias, ("dp", "seq"), axis=0, tiled=True),
        lax.all_gather(cross_mix, ("dp", "seq"), axis=0, tiled=True),
        lax.all_gather(cross_out, ("dp", "seq"), axis=0, tiled=True),
        lax.all_gather(cross_up, ("dp", "seq"), axis=0, tiled=True),
        lax.all_gather(cross_down, ("dp", "seq"), axis=0, tiled=True),
        lax.all_gather(cross_vectors, ("dp", "seq"), axis=1, tiled=True),
        lax.all_gather(cross_up_bias, ("dp", "seq"), axis=0, tiled=True),
        lax.all_gather(position_table, ("dp", "seq"), axis=1, tiled=True),
    )


def segment_parts(mixed_rows, token_docs):
    segment_count = token_docs.shape[0]
    split_heads = mixed_rows.reshape(segment_count, SEG, 3, HEADS, HEAD_DIM)
    allowed = token_docs[:, None, :, None] == token_docs[:, None, None, :]
    scores = jnp.einsum(
        "nqhd,nkhd->nhqk",
        split_heads[:, :, 0],
        split_heads[:, :, 1],
        preferred_element_type=jnp.float32,
    ) * HEAD_DIM ** (-0.5)
    scores = jnp.where(allowed, scores, masked_score)
    return (split_heads, scores)


def segment_forward(mixed_rows, token_docs):
    split_heads, scores = segment_parts(mixed_rows, token_docs)
    log_total = jax.nn.logsumexp(scores, axis=-1)
    weights = jax.nn.softmax(scores, axis=-1).astype(jnp.bfloat16)
    context = jnp.einsum(
        "nhqk,nkhd->nqhd", weights, split_heads[:, :, 2], preferred_element_type=jnp.float32
    )
    return (context.reshape(-1, D).astype(jnp.bfloat16), log_total)


def segment_backward(context_grad, log_total, mixed_rows, token_docs):
    split_heads, scores = segment_parts(mixed_rows, token_docs)
    segment_count = token_docs.shape[0]
    probs = jnp.exp(scores - log_total[..., None])
    grad_heads = context_grad.reshape(segment_count, SEG, HEADS, HEAD_DIM)
    prob_grad = jnp.einsum(
        "nqhd,nkhd->nhqk", grad_heads, split_heads[:, :, 2], preferred_element_type=jnp.float32
    )
    value_grad = jnp.einsum(
        "nhqk,nqhd->nkhd",
        probs.astype(jnp.bfloat16),
        grad_heads,
        preferred_element_type=jnp.float32,
    )
    score_grad = probs * (prob_grad - jnp.sum(probs * prob_grad, axis=-1, keepdims=True))
    score_low = score_grad.astype(jnp.bfloat16) * HEAD_DIM ** (-0.5)
    query_grad = jnp.einsum(
        "nhqk,nkhd->nqhd", score_low, split_heads[:, :, 1], preferred_element_type=jnp.float32
    )
    key_grad = jnp.einsum(
        "nhqk,nqhd->nkhd", score_low, split_heads[:, :, 0], preferred_element_type=jnp.float32
    )
    row_total = segment_count * SEG
    return jnp.concatenate(
        [
            query_grad.reshape(row_total, D),
            key_grad.reshape(row_total, D),
            value_grad.reshape(row_total, D),
        ],
        axis=1,
    )


def cross_parts(mixed_rows, gathered, segment_docs):
    group_size = segment_docs.shape[0]
    per_device = mixed_rows.shape[0] // group_size
    query_rows = mixed_rows[:, :D].reshape(group_size, per_device, HEADS, HEAD_DIM)
    key_rows = gathered[:, :, :D].reshape(group_size, -1, HEADS, HEAD_DIM)
    value_rows = gathered[:, :, D:].reshape(group_size, -1, HEADS, HEAD_DIM)
    own_docs = lax.dynamic_slice_in_dim(
        segment_docs, lax.axis_index("seq") * per_device, per_device, 1
    )
    allowed = own_docs[:, None, :, None] == segment_docs[:, None, None, :]
    scores = jnp.einsum(
        "bqhd,bkhd->bhqk", query_rows, key_rows, preferred_element_type=jnp.float32
    ) * HEAD_DIM ** (-0.5)
    scores = jnp.where(allowed, scores, masked_score)
    return (query_rows, key_rows, value_rows, scores)


def cross_forward(mixed_rows, segment_docs):
    group_size = segment_docs.shape[0]
    per_device = mixed_rows.shape[0] // group_size
    pair_rows = mixed_rows[:, D:].reshape(group_size, per_device, 2 * D)
    gathered = lax.all_gather(pair_rows, "seq", axis=1, tiled=True)
    query_rows, key_rows, value_rows, scores = cross_parts(mixed_rows, gathered, segment_docs)
    log_total = jax.nn.logsumexp(scores, axis=-1)
    weights = jax.nn.softmax(scores, axis=-1).astype(jnp.bfloat16)
    context = jnp.einsum("bhqk,bkhd->bqhd", weights, value_rows, preferred_element_type=jnp.float32)
    return (context.reshape(-1, D).astype(jnp.bfloat16), (gathered, log_total))


def cross_backward(context_grad, cross_kept, mixed_rows, segment_docs):
    gathered, log_total = cross_kept
    group_size = segment_docs.shape[0]
    row_total = mixed_rows.shape[0]
    per_device = row_total // group_size
    query_rows, key_rows, value_rows, scores = cross_parts(mixed_rows, gathered, segment_docs)
    probs = jnp.exp(scores - log_total[..., None])
    grad_heads = context_grad.reshape(group_size, per_device, HEADS, HEAD_DIM)
    prob_grad = jnp.einsum(
        "bqhd,bkhd->bhqk", grad_heads, value_rows, preferred_element_type=jnp.float32
    )
    value_grad = jnp.einsum(
        "bhqk,bqhd->bkhd",
        probs.astype(jnp.bfloat16),
        grad_heads,
        preferred_element_type=jnp.float32,
    )
    score_grad = probs * (prob_grad - jnp.sum(probs * prob_grad, axis=-1, keepdims=True))
    score_low = score_grad.astype(jnp.bfloat16) * HEAD_DIM ** (-0.5)
    query_grad = jnp.einsum(
        "bhqk,bkhd->bqhd", score_low, key_rows, preferred_element_type=jnp.float32
    )
    key_grad = jnp.einsum(
        "bhqk,bqhd->bkhd", score_low, query_rows, preferred_element_type=jnp.float32
    )
    pair_grads = jnp.concatenate(
        [key_grad.reshape(group_size, -1, D), value_grad.reshape(group_size, -1, D)], axis=2
    )
    own_pairs = lax.psum_scatter(
        pair_grads.astype(jnp.bfloat16), "seq", scatter_dimension=1, tiled=True
    ).astype(jnp.float32)
    return jnp.concatenate(
        [query_grad.reshape(row_total, D), own_pairs.reshape(row_total, 2 * D)], axis=1
    )


def block_forward(inputs, weights, attend):
    mix_weight, out_weight, up_weight, down_weight, vectors, up_bias = weights
    vector_rows = vectors.astype(jnp.float32)
    in_bias = jnp.concatenate([vector_rows[0], jnp.zeros_like(vector_rows[0]), vector_rows[1]])
    rounded = inputs.astype(jnp.bfloat16)
    mixed_rows = (
        jnp.dot(rounded, mix_weight, preferred_element_type=jnp.float32) + in_bias
    ).astype(jnp.bfloat16)
    context, attend_kept = attend(mixed_rows)
    first_sum = (
        inputs + jnp.dot(context, out_weight, preferred_element_type=jnp.float32) + vector_rows[2]
    )
    first_norm = layer_norm(first_sum, vector_rows[3], vector_rows[4])
    first_low = first_norm.astype(jnp.bfloat16)
    hidden = jnp.dot(first_low, up_weight, preferred_element_type=jnp.float32) + up_bias.astype(
        jnp.float32
    )
    active = gelu_exact(hidden).astype(jnp.bfloat16)
    second_sum = (
        first_norm
        + jnp.dot(active, down_weight, preferred_element_type=jnp.float32)
        + vector_rows[5]
    )
    output = layer_norm(second_sum, vector_rows[6], vector_rows[7])
    return (
        output,
        (
            rounded,
            mixed_rows,
            attend_kept,
            context,
            first_sum,
            first_low,
            hidden,
            active,
            second_sum,
        ),
    )


def block_backward(output_grad, block_kept, weights, attend_back):
    mix_weight, out_weight, up_weight, down_weight, vectors, up_bias = weights
    vector_rows = vectors.astype(jnp.float32)
    rounded, mixed_rows, attend_kept, context, first_sum, first_low, hidden, active, second_sum = (
        block_kept
    )
    unused, second_pull = jax.vjp(layer_norm, second_sum, vector_rows[6], vector_rows[7])
    second_grad, gain_two, shift_two = second_pull(output_grad)
    second_low = second_grad.astype(jnp.bfloat16)
    down_grad = contract(active, second_low, 0, 0)
    down_bias = jnp.sum(second_low.astype(jnp.float32), axis=0)
    active_grad = contract(second_low, down_weight, 1, 1)
    unused, gelu_pull = jax.vjp(gelu_exact, hidden)
    hidden_grad = gelu_pull(active_grad)[0]
    hidden_low = hidden_grad.astype(jnp.bfloat16)
    up_grad = contract(first_low, hidden_low, 0, 0)
    up_bias_grad = jnp.sum(hidden_low.astype(jnp.float32), axis=0)
    first_grad = second_grad + contract(hidden_low, up_weight, 1, 1)
    unused, first_pull = jax.vjp(layer_norm, first_sum, vector_rows[3], vector_rows[4])
    sum_grad, gain_one, shift_one = first_pull(first_grad)
    branch_low = sum_grad.astype(jnp.bfloat16)
    out_grad = contract(context, branch_low, 0, 0)
    out_bias = jnp.sum(branch_low.astype(jnp.float32), axis=0)
    context_low = contract(branch_low, out_weight, 1, 1).astype(jnp.bfloat16)
    mixed_low = attend_back(context_low, attend_kept, mixed_rows).astype(jnp.bfloat16)
    mix_grad = contract(rounded, mixed_low, 0, 0)
    mixed_sums = jnp.sum(mixed_low.astype(jnp.float32), axis=0)
    input_grad = sum_grad + contract(mixed_low, mix_weight, 1, 1)
    vectors_grad = jnp.stack(
        [
            mixed_sums[:D],
            mixed_sums[2 * D :],
            out_bias,
            gain_one,
            shift_one,
            down_bias,
            gain_two,
            shift_two,
        ]
    )
    return (input_grad, (mix_grad, out_grad, up_grad, down_grad, vectors_grad, up_bias_grad))


def shards(
    tokens,
    cotangent,
    token_docs,
    segment_docs,
    segment_positions,
    local_mix,
    local_out,
    local_up,
    local_down,
    local_vectors,
    local_up_bias,
    cross_mix,
    cross_out,
    cross_up,
    cross_down,
    cross_vectors,
    cross_up_bias,
    position_table,
):
    sequence_count, span, width = tokens.shape
    group_size = sequence_count // MICRO
    segment_count = span // SEG
    devices = lax.axis_size(("dp", "seq"))
    shard_shapes = tuple(
        (
            array_in.shape
            for array_in in (
                local_mix,
                local_out,
                local_up,
                local_down,
                local_vectors,
                local_up_bias,
                cross_mix,
                cross_out,
                cross_up,
                cross_down,
                cross_vectors,
                cross_up_bias,
                position_table,
            )
        )
    )
    layer_outputs = []
    input_grads = []
    totals = ()
    for micro_step in range(MICRO):
        lower_row = micro_step * group_size
        upper_row = lower_row + group_size
        gathered = fetch_weights(
            local_mix,
            local_out,
            local_up,
            local_down,
            local_vectors,
            local_up_bias,
            cross_mix,
            cross_out,
            cross_up,
            cross_down,
            cross_vectors,
            cross_up_bias,
            position_table,
        )
        local_weights = gathered[0:6]
        cross_weights = gathered[6:12]
        position_rows = gathered[12]
        inputs = tokens[lower_row:upper_row].reshape(group_size * span, width).astype(jnp.float32)
        docs_here = token_docs[lower_row:upper_row]
        segments_here = segment_docs[lower_row:upper_row]
        first_out, first_kept = block_forward(
            inputs, local_weights, partial(segment_forward, token_docs=docs_here)
        )
        segment_grid = first_out.reshape(group_size * segment_count, SEG, width)
        places = segment_positions[lower_row:upper_row].reshape(group_size * segment_count)
        position_picks = (
            places[:, None] == jnp.arange(position_rows.shape[0], dtype=jnp.int32)[None, :]
        ).astype(jnp.bfloat16)
        heads_in = segment_grid[:, 0, :] + jnp.dot(
            position_picks, position_rows, preferred_element_type=jnp.float32
        )
        heads_out, cross_kept = block_forward(
            heads_in, cross_weights, partial(cross_forward, segment_docs=segments_here)
        )
        joined = jnp.concatenate([heads_out[:, None, :], segment_grid[:, 1:, :]], axis=1)
        layer_outputs.append(joined.astype(jnp.bfloat16))
        gathered = fetch_weights(
            local_mix,
            local_out,
            local_up,
            local_down,
            local_vectors,
            local_up_bias,
            cross_mix,
            cross_out,
            cross_up,
            cross_down,
            cross_vectors,
            cross_up_bias,
            position_table,
        )
        local_weights = gathered[0:6]
        cross_weights = gathered[6:12]
        output_grad = cotangent[lower_row:upper_row].astype(jnp.float32)
        heads_grad, cross_grads = block_backward(
            output_grad[:, 0, :],
            cross_kept,
            cross_weights,
            partial(cross_backward, segment_docs=segments_here),
        )
        table_grad = contract_exact(position_picks.astype(jnp.float32), heads_grad, 0, 0)
        first_grad = jnp.concatenate(
            [heads_grad[:, None, :], output_grad[:, 1:, :]], axis=1
        ).reshape(group_size * span, width)
        input_grad, local_grads = block_backward(
            first_grad, first_kept, local_weights, partial(segment_backward, token_docs=docs_here)
        )
        input_grads.append(input_grad.reshape(group_size, span, width))
        step_grads = local_grads + cross_grads + (table_grad,)
        if micro_step == 0:
            totals = tuple(step_grads)
        else:
            totals = tuple(
                (total_sum + step_sum for total_sum, step_sum in zip(totals, step_grads))
            )
    packed_total = lax.psum_scatter(
        owner_pack(totals, devices), ("dp", "seq"), scatter_dimension=0, tiled=True
    )
    summed = owner_unpack(packed_total, shard_shapes)
    layer_output = jnp.concatenate(layer_outputs, axis=0)
    input_gradient = jnp.concatenate(input_grads, axis=0)
    return (layer_output, input_gradient) + tuple(summed)


def swap_dp(array_in, shift):
    return lax.ppermute(array_in, "dp", [(i, (i + shift) % 4) for i in range(4)])


def swap_core(array_in):
    return lax.ppermute(array_in, "seq", [(i, i ^ 1) for i in range(8)])


def swap_chip(array_in, mask):
    return lax.ppermute(array_in, "seq", [(i, i ^ (2 * mask)) for i in range(8)])


def swap_one(array_in):
    return lax.ppermute(array_in, "seq", [(i, i ^ (2 if i % 2 == 0 else 4)) for i in range(8)])


def swap_two(array_in):
    return lax.ppermute(array_in, "seq", [(i, i ^ (4 if i % 2 == 0 else 2)) for i in range(8)])


def place_in():
    layer = lax.axis_index("dp")
    spot = lax.axis_index("seq")
    return layer, spot // 2, lax.rem(spot, 2)


def after(array_in, *before):
    return lax.optimization_barrier((array_in,) + before)[0]


def stage(*values):
    return lax.optimization_barrier(values)


def wide(array_in):
    return array_in.astype(jnp.float32)


def low(array_in):
    return array_in.astype(jnp.bfloat16)


def copies(pieces, shapes, moves, room=64):
    count, made = len(pieces), len(shapes)
    total = len(moves(0, 0, 0))

    def kernel(*refs):
        outs, held, sems = refs[count : count + made], refs[count + made : -1], refs[-1]
        inward = [pltpu.make_async_copy(refs[i], held[i], sems.at[0, i]) for i in range(count)]
        for copy in inward:
            copy.start()
        outward = []
        for i, (piece, part, out, place) in enumerate(moves(*place_in())):
            if inward[piece] is not None:
                inward[piece].wait()
                inward[piece] = None
            copy = pltpu.make_async_copy(held[piece].at[part], outs[out].at[place], sems.at[1, i])
            copy.start()
            outward.append(copy)
        for copy in outward:
            copy.wait()

    size = 2 * sum(math.prod(shape) for shape in shapes) * 2
    return pl.pallas_call(
        kernel,
        out_shape=[jax.ShapeDtypeStruct(shape, pieces[0].dtype) for shape in shapes],
        in_specs=[pl.BlockSpec(memory_space=pltpu.HBM)] * count,
        out_specs=[pl.BlockSpec(memory_space=pltpu.HBM)] * made,
        scratch_shapes=[pltpu.VMEM(piece.shape, piece.dtype) for piece in pieces]
        + [pltpu.SemaphoreType.DMA((2, max(count, total)))],
        compiler_params=pltpu.CompilerParams(vmem_limit_bytes=room * 2**20),
        cost_estimate=pl.CostEstimate(flops=0, bytes_accessed=0, transcendentals=0),
    )(*pieces)


every = slice(None)


def reach_dp(shard):
    return [shard] + [swap_dp(shard, shift) for shift in (1, 2, 3)]


def join_dp(pieces):
    return copies(
        pieces,
        [(4,) + pieces[0].shape],
        lambda layer, chip, core: [(i, every, 0, lax.rem(layer + 4 - i, 4)) for i in range(4)],
    )[0]


def plane_order(chip, core):
    near, far = chip ^ (1 + core), chip ^ (2 - core)
    return (chip, near, far, chip ^ 3), (chip, far, near, chip ^ 3)


def join_chips(pieces):
    def moves(layer, chip, core):
        return [(i, every, 0, spot) for i, spot in enumerate(plane_order(chip, core)[0])]

    return copies(pieces, [(4,) + pieces[0].shape], moves)[0]


def gather_plane(mine, others):
    def moves(layer, chip, core):
        own, other = plane_order(chip, core)
        found = [(i, every, 0, (every, own[i], core)) for i in range(4)]
        return found + [(4 + i, every, 0, (every, other[i], 1 - core)) for i in range(4)]

    shape = (4, 4, 2) + mine[0].shape[1:]
    return copies(mine + others, [shape], moves)[0]


def gather_up(mine, others):
    def moves(layer, chip, core):
        own, other = plane_order(chip, core)
        found = []
        for i in range(8):
            spot, side = (own[i], core) if i < 4 else (other[i - 4], 1 - core)
            for out, lanes in enumerate((slice(0, 4 * D), slice(4 * D, 5 * D))):
                found.append((i, (every, every, lanes), out, (every, spot, side)))
        return found

    up, out = copies(mine + others, [(4, 4, 2, 24, 4 * D), (4, 4, 2, 24, D)], moves)
    return up.reshape(D, 4 * D), out.reshape(D, D)


def gather_down(mine, others):
    def moves(layer, chip, core):
        own, other = plane_order(chip, core)
        found = []
        for i in range(8):
            spot, side = (own[i], core) if i < 4 else (other[i - 4], 1 - core)
            for quarter in range(4):
                part = (every, every, slice(quarter * D, (quarter + 1) * D))
                found.append((i, part, 0, (every, spot, side, quarter)))
        return found

    return copies(mine + others, [(4, 4, 2, 4, 24, D)], moves)[0]


class Sum:
    def __init__(self, kept):
        self.kept = kept
        self.shape = kept.shape[2:]

    def run(self, operands, out_shapes, plan):
        shape, count, made = self.shape, len(operands), len(out_shapes)
        dry = plan(0, 0, 0)
        pieces = sum(len(sources) for sources, target in dry)

        def kernel(*refs):
            given, outs = refs[:count], refs[count : count + made]
            held, built, sems = refs[count + made : -len(dry) - 1], refs[-len(dry) - 1 : -1], refs[-1]
            inward, outward, steps = [], [], []
            for sources, target in plan(*place_in()):
                step = []
                for operand, index in sources:
                    spot = len(inward)
                    source = given[operand].at[index]
                    copy = pltpu.make_async_copy(source, held[spot], sems.at[0, spot])
                    copy.start()
                    inward.append(copy)
                    step.append(spot)
                steps.append((step, target))
            for place, (step, (out, index)) in enumerate(steps):
                total = None
                for spot in step:
                    inward[spot].wait()
                    value = wide(held[spot][...])
                    total = value if total is None else total + value
                built[place][...] = total.astype(built[place].dtype)
                target = outs[out] if index is None else outs[out].at[index]
                copy = pltpu.make_async_copy(built[place], target, sems.at[1, place])
                copy.start()
                outward.append(copy)
            for copy in outward:
                copy.wait()

        far = pl.BlockSpec(memory_space=pltpu.HBM)
        return pl.pallas_call(
            kernel,
            out_shape=out_shapes,
            in_specs=[far] * count,
            out_specs=[far] * made,
            scratch_shapes=[pltpu.VMEM(shape, jnp.bfloat16)] * pieces
            + [pltpu.VMEM(shape, out_shapes[target[0]].dtype) for sources, target in dry]
            + [pltpu.SemaphoreType.DMA((2, pieces))],
            compiler_params=pltpu.CompilerParams(vmem_limit_bytes=64 * 2**20),
            cost_estimate=pl.CostEstimate(flops=0, bytes_accessed=0, transcendentals=0),
        )(*operands)

    def first(self, got):
        self.got = got

        def plan(layer, chip, core):
            return [
                ([(0, (z, spot)), (1, (z, spot))], (0, (i, z)))
                for i, spot in enumerate((chip ^ (1 + core), chip ^ 3))
                for z in range(4)
            ]

        return self.run([self.kept, got], [half(2, 4, *self.shape)], plan)[0]

    def second(self, back):
        self.back = back

        def plan(layer, chip, core):
            spot = chip ^ (2 - core)
            return [
                ([(0, (z, spot)), (1, (z, spot)), (2, (1, z))], (0, z)) for z in range(4)
            ]

        return self.run([self.kept, self.got, back], [half(4, *self.shape)], plan)[0]

    def third(self, last):
        def plan(layer, chip, core):
            found = []
            for shift in (1, 2, 3, 0):
                z = lax.rem(layer + shift, 4)
                sources = [(0, (z, chip)), (1, (z, chip)), (2, (0, z)), (3, z)]
                found.append((sources, (shift, None)))
            return found

        self.own, *others = self.run(
            [self.kept, self.got, self.back, last],
            [shape_of(*self.shape)] + [half(*self.shape)] * 3,
            plan,
        )
        return others

    def total(self, others):
        return self.own + wide(others[0]) + wide(others[1]) + wide(others[2])


def send_dp(others):
    return [swap_dp(other, shift) for shift, other in zip((1, 2, 3), others)]


def norm_parts(values):
    centered = values - jnp.mean(values, axis=-1, keepdims=True)
    variance = jnp.mean(centered * centered, axis=-1, keepdims=True)
    scale = lax.rsqrt(variance + epsilon)
    return centered * scale, scale


def norm_back(grad, normed, scale, gain):
    scaled = grad * gain
    return scale * (
        scaled
        - jnp.mean(scaled, axis=-1, keepdims=True)
        - normed * jnp.mean(scaled * normed, axis=-1, keepdims=True)
    )


def gelu_slope(hidden):
    return 0.5 * (1.0 + lax.erf(hidden * math.sqrt(0.5))) + hidden * jnp.exp(
        -0.5 * hidden * hidden
    ) * (1.0 / math.sqrt(2.0 * math.pi))


def shape_of(*shape, dtype=jnp.float32):
    return jax.ShapeDtypeStruct(shape, dtype)


def half(*shape):
    return jax.ShapeDtypeStruct(shape, jnp.bfloat16)


def on_core(kernel, out_shape, operands, flops, room=64, grid=(), in_specs=None, out_specs=None, scratch=()):
    arrays = jax.tree.leaves(out_shape) + list(operands)
    size = sum(math.prod(a.shape) * a.dtype.itemsize for a in arrays)
    extra = {} if in_specs is None else {"in_specs": in_specs, "out_specs": out_specs}
    return pl.pallas_call(
        kernel,
        out_shape=out_shape,
        grid=grid,
        scratch_shapes=scratch,
        compiler_params=pltpu.CompilerParams(vmem_limit_bytes=room * 2**20),
        cost_estimate=pl.CostEstimate(flops=0, bytes_accessed=0, transcendentals=0),
        **extra,
    )(*operands)


def column_sum(array_in):
    return jnp.sum(array_in, axis=0, keepdims=True)


def prepare(*refs):
    given, made, held, built = refs[0:12], refs[12:19], refs[19:31], refs[31:38]
    small, turned, parts, sems = refs[38:]
    inward = [pltpu.make_async_copy(given[i], held[i], sems.at[0, i]) for i in range(12)]
    outward = [pltpu.make_async_copy(built[i], made[i], sems.at[1, i]) for i in range(7)]
    for copy in inward:
        copy.start()
    for copy in inward:
        copy.wait()
    mix_ref, out_ref, up_ref, down_ref, vectors_ref, bias_ref = held[0:6]
    cross_mix_ref, cross_out_ref, cross_up_ref, cross_vectors_ref, cross_bias_ref, table_ref = held[6:]
    one_ref, two_ref, three_ref = built[0:3]
    one_ref[:, 0 : 3 * D] = mix_ref[...]
    one_ref[:, 3 * D : 4 * D] = out_ref[...]
    small[...] = jnp.zeros_like(small)
    small[0:8, 0:24] = wide(vectors_ref[...])
    small[8:16, 0:24] = wide(cross_vectors_ref[...])
    for row in range(4):
        lanes = slice(24 * row, 24 * (row + 1))
        small[80 + row : 81 + row, 0:24] = wide(bias_ref[:, lanes])
        small[84 + row : 85 + row, 0:24] = wide(cross_bias_ref[:, lanes])
    turned[...] = small[...].T
    turned[0:24, 16:80] = wide(table_ref[...])
    one_ref[:, 4 * D : 4 * D + 128] = low(turned[0:24, :])
    outward[0].start()
    two_ref[:, 0 : 4 * D] = up_ref[...]
    two_ref[:, 4 * D : 5 * D] = cross_out_ref[...]
    for quarter in range(4):
        three_ref[:, quarter * D : (quarter + 1) * D] = down_ref[quarter]
    outward[1].start()
    outward[2].start()
    parts[...] = jnp.zeros_like(parts)
    for spot in range(4):
        for level in range(4):
            taken = cross_up_ref[:, 192 * (4 * level + spot) : 192 * (4 * level + spot + 1)]
            parts[spot, :, 192 * level : 192 * (level + 1)] = taken
        for third in range(3):
            taken = cross_mix_ref[:, third * D + 192 * spot : third * D + 192 * (spot + 1)]
            parts[spot, :, D + 192 * third : D + 192 * (third + 1)] = taken
    chip = place_in()[1]
    for mask in range(4):
        built[3 + mask][...] = parts[chip ^ mask]
        outward[3 + mask].start()
    for copy in outward:
        copy.wait()


def join_cross(pieces, cross_down):
    def moves(layer, chip, core):
        found = []
        for mask in range(4):
            found.append((mask, (every, slice(0, D)), 0, (chip ^ mask, every, slice(0, D))))
            taken = (every, slice(D, D + 640))
            found.append((mask, taken, 0, (chip ^ mask, every, slice(2 * D, 2 * D + 640))))
        found.append((4, every, 0, (every, every, slice(D, 2 * D))))
        return found

    return copies(pieces + [cross_down.reshape(4, 24, D)], [(4, 24, 2 * D + 640)], moves)[0]


def place_cross(column, other):
    def moves(layer, chip, core):
        found = []
        for piece, side in ((0, core), (1, 1 - core)):
            source, lead = (every, every, every), (every, every, side)
            found.append((piece, source + (slice(0, D),), 0, lead))
            found.append((piece, source + (slice(2 * D, 2 * D + 640),), 1, lead))
            found.append((piece, source + (slice(D, 2 * D),), 2, (every, side)))
        return found

    up, mix, down = copies(
        [column, other], [(4, 4, 2, 24, D), (4, 4, 2, 24, 640), (4, 2, 4, 24, D)], moves
    )
    return up.reshape(D, D), mix.reshape(D, 640), down.reshape(D, D)


def segment_heads(segment, mixed_ref, docs_ref, probs_ref, context_ref):
    lane = lax.broadcasted_iota(jnp.int32, (SEG, 128), 1)
    rows = slice(segment * SEG, (segment + 1) * SEG)
    docs = jnp.broadcast_to(wide(docs_ref[segment : segment + 1, :]), (SEG, SEG))
    allowed = docs == docs.T
    for pair in range(HEADS // 2):
        query, key, value = (
            mixed_ref[rows, third * D + pair * 128 : third * D + (pair + 1) * 128]
            for third in range(3)
        )
        found = []
        for side in range(2):
            here = (lane < HEAD_DIM) if side == 0 else (lane >= HEAD_DIM)
            scores = contract(key, jnp.where(here, query, jnp.zeros_like(query)), 1, 1)
            scores = jnp.where(allowed, scores * HEAD_DIM ** (-0.5), masked_score)
            powers = jnp.exp(scores - jnp.max(scores, axis=0, keepdims=True))
            probs = powers / jnp.sum(powers, axis=0, keepdims=True)
            probs_ref[2 * pair + side] = probs
            found.append(contract(low(probs), value, 0, 0))
        context = jnp.where(lane < HEAD_DIM, found[0], found[1])
        context_ref[:, pair * 128 : (pair + 1) * 128] = low(context)


def local_attend(tokens_ref, group_ref, docs_ref, places_ref, *outs):
    mixed_ref, context_ref, probs_ref, rows_ref, places_out = outs
    rows_ref[...] = wide(group_ref[:, 4 * D : 4 * D + 128]).T
    lane = lax.broadcasted_iota(jnp.int32, (1, 64), 1)
    for place in range(2):
        picked = wide(places_ref[:, place : place + 1] == lane)
        places_out[place : place + 1, :] = contract_exact(picked, rows_ref[16:80, :], 1, 0)
    tokens = tokens_ref[...]
    for third in range(3):
        columns = slice(third * D, (third + 1) * D)
        mixed = contract(tokens, group_ref[:, columns], 1, 0)
        if third != 1:
            mixed = mixed + rows_ref[third // 2 : third // 2 + 1, :]
        mixed_ref[:, columns] = low(mixed)
    segment_heads(0, mixed_ref, docs_ref, probs_ref, context_ref)


def local_attend_more(
    tokens_ref, mixed_ref, before_ref, weight_ref, rows_ref, docs_ref, *outs
):
    context_ref, probs_ref, n_ref, scale_ref, low_ref, here = outs
    segment_heads(1, mixed_ref, docs_ref, probs_ref, here)
    context_ref[0:SEG, :] = before_ref[...]
    context_ref[SEG : 2 * SEG, :] = here[...]
    total = wide(tokens_ref[...]) + contract(context_ref[...], weight_ref[...], 1, 0)
    normed, scale = norm_parts(total + rows_ref[2:3, :])
    n_ref[...] = normed
    scale_ref[...] = scale
    low_ref[...] = low(normed * rows_ref[3:4, :] + rows_ref[4:5, :])


def local_up_part(low_ref, weight_ref, bias_ref, active_ref, slope_ref):
    hidden = contract(low_ref[...], weight_ref[...], 1, 0) + wide(bias_ref[...])
    chance = 0.5 * (1.0 + lax.erf(hidden * math.sqrt(0.5)))
    density = jnp.exp(-0.5 * hidden * hidden) * (1.0 / math.sqrt(2.0 * math.pi))
    active_ref[...] = low(hidden * chance)
    slope_ref[...] = low(chance + hidden * density)


def local_down_part(
    active_ref, weight_ref, first_ref, rows_ref, cot_a, cot_b, places_ref, *outs
):
    n_ref, scale_ref, kept_ref, given_ref, total = outs
    step = pl.program_id(0)
    part = contract(active_ref[...], weight_ref[...], 1, 0)

    @pl.when(step == 0)
    def _():
        first_norm = first_ref[...] * rows_ref[3:4, :] + rows_ref[4:5, :]
        total[...] = first_norm + rows_ref[5:6, :] + part

    @pl.when(step > 0)
    def _():
        total[...] += part

    @pl.when(step == 1)
    def _():
        normed, scale = norm_parts(total[...])
        n_ref[...] = normed
        scale_ref[...] = scale
        core = place_in()[2]
        heads, grads = [], []
        for place, cot in ((0, cot_a), (1, cot_b)):
            row = normed[place * SEG : place * SEG + 1] * rows_ref[6:7, :] + rows_ref[7:8, :]
            heads.append(row + places_ref[place : place + 1, :])
            grads.append(wide(cot[...])[0:1])
        for ref, mine in ((kept_ref, core == 0), (given_ref, core == 1)):
            ref[...] = jnp.zeros_like(ref)
            ref[0:1, :] = jnp.where(mine, heads[0], heads[1])
            ref[1:2, :] = jnp.where(mine, grads[0], grads[1])


def join_pair(kept_ref, got_ref, out_ref):
    core = place_in()[2]
    out_ref[...] = jnp.zeros_like(out_ref)
    out_ref[0:2, :] = jnp.where(core == 0, kept_ref[0:2, :], got_ref[0:2, :])
    out_ref[2:4, :] = jnp.where(core == 0, got_ref[0:2, :], kept_ref[0:2, :])


def cross_attend(
    own_ref, a_ref, b_ref, c_ref, weight_ref, rows_ref, docs_ref, *outs
):
    in_ref, grad_ref, mixed_ref, probs_ref, context_ref = outs
    layer, chip, core = place_in()
    for mask, ref in enumerate((own_ref, a_ref, b_ref, c_ref)):
        for side in range(2):
            row = 2 * (chip ^ mask) + side
            in_ref[pl.ds(row, 1), :] = ref[2 * side : 2 * side + 1, :]
            grad_ref[pl.ds(row, 1), :] = ref[2 * side + 1 : 2 * side + 2, :]
    biases = []
    for vector in (8, 9):
        row = rows_ref[vector : vector + 1, :]
        found = row[:, 0:192]
        for spot in range(1, 4):
            found = jnp.where(chip == spot, row[:, 192 * spot : 192 * (spot + 1)], found)
        biases.append(found)
    bias = jnp.concatenate([biases[0], jnp.zeros_like(biases[0]), biases[1]], axis=1)
    mixed = low(contract(low(in_ref[...]), weight_ref[:, 0:576], 1, 0) + bias)
    mixed_ref[...] = mixed
    row_docs = wide(jnp.where(core == 0, docs_ref[0:1, :], docs_ref[1:2, :]))
    count = row_docs.shape[1]
    lane = lax.broadcasted_iota(jnp.int32, (count, count), 1)
    line = lax.broadcasted_iota(jnp.int32, (count, count), 0)
    column_docs = jnp.sum(jnp.where(lane == line, row_docs, 0.0), axis=1, keepdims=True)
    allowed = row_docs == column_docs
    found = []
    for head in range(3):
        query, key, value = (
            mixed[:, third * 192 + head * HEAD_DIM : third * 192 + (head + 1) * HEAD_DIM]
            for third in range(3)
        )
        scores = contract(query, key, 1, 1) * HEAD_DIM ** (-0.5)
        scores = jnp.where(allowed, scores, masked_score)
        powers = jnp.exp(scores - jnp.max(scores, axis=-1, keepdims=True))
        probs = powers / jnp.sum(powers, axis=-1, keepdims=True)
        probs_ref[head] = probs
        found.append(contract(low(probs), value, 1, 0))
    context_ref[...] = low(jnp.concatenate(found, axis=1))


def cross_up_down(
    own_ref, a_ref, b_ref, c_ref, in_ref, out_weight_ref, rows_ref, up_ref, bias_ref, down_ref, *outs
):
    n_ref, scale_ref, low_ref, hidden_ref, active_ref, part_ref = outs
    chip = place_in()[1]
    total = in_ref[...] + rows_ref[10:11, :]
    for mask, ref in enumerate((own_ref, a_ref, b_ref, c_ref)):
        start = pl.multiple_of(192 * (chip ^ mask), 64)
        total = total + contract(ref[...], out_weight_ref[pl.ds(start, 192), :], 1, 0)
    normed, scale = norm_parts(total)
    n_ref[...] = normed
    scale_ref[...] = scale
    first = low(normed * rows_ref[11:12, :] + rows_ref[12:13, :])
    low_ref[...] = first
    hidden = contract(first, up_ref[...], 1, 0) + bias_ref[...]
    hidden_ref[...] = hidden
    active = low(hidden * (0.5 * (1.0 + lax.erf(hidden * math.sqrt(0.5)))))
    active_ref[...] = active
    part_ref[...] = contract(active, down_ref[...], 1, 0)


def cross_turn(
    own_ref, a_ref, b_ref, c_ref, n_ref, rows_ref, grad_ref, hidden_ref, up_ref, down_ref, *outs
):
    out_ref, second_ref, hidden_low_ref, part_ref, sums_ref = outs
    first = n_ref[...] * rows_ref[11:12, :] + rows_ref[12:13, :]
    total = (own_ref[...] + a_ref[...]) + (b_ref[...] + c_ref[...])
    normed, scale = norm_parts(first + total + rows_ref[13:14, :])
    out_ref[...] = normed * rows_ref[14:15, :] + rows_ref[15:16, :]
    grad = grad_ref[...]
    second = norm_back(grad, normed, scale, rows_ref[14:15, :])
    second_ref[...] = second
    hidden_low = low(contract(low(second), down_ref[...], 1, 1) * gelu_slope(hidden_ref[...]))
    hidden_low_ref[...] = hidden_low
    part_ref[...] = contract(hidden_low, up_ref[...], 1, 1)
    sums_ref[...] = jnp.zeros_like(sums_ref)
    sums_ref[0:1, :] = column_sum(grad * normed)
    sums_ref[1:2, :] = column_sum(grad)


def cross_attend_back(
    own_ref,
    a_ref,
    b_ref,
    c_ref,
    second_ref,
    n_ref,
    scale_ref,
    rows_ref,
    out_weight_ref,
    mixed_ref,
    probs_ref,
    weight_ref,
    hidden_low_ref,
    active_ref,
    context_ref,
    in_ref,
    low_ref,
    sums_ref,
    places_ref,
    total_ref,
    part_ref,
    pack_ref,
    pack,
    rows,
):
    chip = place_in()[1]
    grad = second_ref[...] + (own_ref[...] + a_ref[...]) + (b_ref[...] + c_ref[...])
    normed = n_ref[...]
    total = norm_back(grad, normed, scale_ref[...], rows_ref[11:12, :])
    total_ref[...] = total
    branch = low(total)
    start = pl.multiple_of(192 * chip, 64)
    context_low = low(contract(branch, out_weight_ref[pl.ds(start, 192), :], 1, 1))
    mixed = mixed_ref[...]
    found = [[], [], []]
    for head in range(3):
        query, key, value = (
            mixed[:, third * 192 + head * HEAD_DIM : third * 192 + (head + 1) * HEAD_DIM]
            for third in range(3)
        )
        part = context_low[:, head * HEAD_DIM : (head + 1) * HEAD_DIM]
        probs = probs_ref[head]
        prob_grad = contract(part, value, 1, 1)
        score = low(probs * (prob_grad - jnp.sum(probs * prob_grad, axis=-1, keepdims=True)))
        found[0].append(contract(score, key, 1, 0) * HEAD_DIM ** (-0.5))
        found[1].append(contract(score, query, 0, 0) * HEAD_DIM ** (-0.5))
        found[2].append(contract(low(probs), part, 0, 0))
    mixed_low = low(jnp.concatenate(found[0] + found[1] + found[2], axis=1))
    part_ref[...] = contract(mixed_low, weight_ref[:, 0:576], 1, 1)
    pack[...] = jnp.zeros_like(pack)
    pack[0:8, :] = wide(hidden_low_ref[...])
    pack[8:16, :] = wide(active_ref[...])
    pack[16:24, 0:576] = wide(mixed_low)
    pack[16:24, 576:768] = wide(context_ref[...])
    for i, value in enumerate(
        (in_ref[...], wide(low_ref[...]), total, second_ref[...], total)
    ):
        rows[...] = value
        for side in range(2):
            row = 24 + 2 * i + side
            pack[row : row + 1, :] = rows[pl.ds(2 * chip + side, 1), :]
    rows[0:1, :] = column_sum(grad * normed)
    rows[1:2, :] = column_sum(grad)
    rows[2:4, :] = sums_ref[0:2, :]
    pack[34:35, :] = rows[pl.ds(chip, 1), :]
    for place in range(2):
        spot = wide(places_ref[:, place : place + 1])
        pack[35 + place : 36 + place, :] = jnp.broadcast_to(spot, (1, D))
    pack_ref[...] = low(pack[...])


def cross_finish(own_ref, a_ref, b_ref, c_ref, total_ref, out_ref, kept_ref, given_ref, rows):
    layer, chip, core = place_in()
    rows[...] = total_ref[...] + (own_ref[...] + a_ref[...]) + (b_ref[...] + c_ref[...])
    for ref, side in ((kept_ref, core), (given_ref, 1 - core)):
        ref[...] = jnp.zeros_like(ref)
        ref[0:1, :] = rows[pl.ds(2 * chip + side, 1), :]
        ref[1:2, :] = out_ref[pl.ds(2 * chip + side, 1), :]


def cross_owner(mine_ref, other_ref, weight_ref, *refs):
    mix_ref, out_ref, up_ref, down_ref, vectors_ref, bias_ref, table_ref = refs[:7]
    hidden, mixed, single, active, sums, places = refs[7:]
    layer, chip, core = place_in()
    rank = 8 * layer + 2 * chip + core
    sums[...] = jnp.zeros_like(sums)
    for level in range(4):
        for side in range(2):
            group = 2 * level + side
            rows = slice(8 * group, 8 * group + 8)
            for spot in range(4):
                value = wide(
                    jnp.where(core == side, mine_ref[level, spot], other_ref[level, spot])
                )
                hidden[spot, rows, :] = value[0:8]
                mixed[spot, rows, :] = value[16:24]
                for i in range(5):
                    start = 8 * group + 2 * spot
                    single[i, start : start + 2, :] = value[24 + 2 * i : 26 + 2 * i]
                sums[spot : spot + 1, :] += value[34:35]
                for sequence in range(2):
                    row = 16 * level + 8 * sequence + 2 * spot + side
                    places[row : row + 1, :] = value[35 + sequence : 36 + sequence, 0:128]
            value = jnp.where(core == side, mine_ref[level, chip], other_ref[level, chip])
            active[rows, :] = wide(value)[8:16]

    def select(count, first):
        lane = lax.broadcasted_iota(jnp.int32, (count, D), 1)
        row = lax.broadcasted_iota(jnp.int32, (count, D), 0)
        return wide(lane == first + row)

    own = select(24, 24 * rank)
    offset = 24 * (2 * chip + core)
    units = select(96, 192 * layer + 96 * core)
    own_low = low(own)

    def columns_of(array_in):
        return low(contract(own_low, low(array_in), 1, 1))

    inputs = columns_of(single[0])
    for spot in range(4):
        part = contract(inputs, low(mixed[spot][:, 0:576]), 1, 0)
        for third in range(3):
            start = third * D + 192 * spot
            mix_ref[:, start : start + 192] = part[:, 192 * third : 192 * (third + 1)]
    own_mixed = mixed[layer]
    context = low(contract(low(select(24, 576 + offset)), low(own_mixed), 1, 1))
    out_ref[...] = contract(context, low(single[2]), 1, 0)
    first = columns_of(single[1])
    for spot in range(4):
        part = contract(first, low(hidden[spot]), 1, 0)
        for level in range(4):
            start = 192 * (4 * level + spot)
            up_ref[:, start : start + 192] = part[:, 192 * level : 192 * (level + 1)]
    units_low = low(contract(low(units), low(active[...]), 1, 1))
    down_ref[...] = contract(units_low, low(single[3]), 1, 0)
    mixed_sum = column_sum(own_mixed)
    vectors_ref[0:1, :] = contract_exact(mixed_sum, select(24, offset), 1, 1)
    vectors_ref[1:2, :] = contract_exact(mixed_sum, select(24, 384 + offset), 1, 1)
    for row, value in (
        (2, column_sum(single[2])),
        (3, sums[0:1, :]),
        (4, sums[1:2, :]),
        (5, column_sum(single[3])),
        (6, sums[2:3, :]),
        (7, sums[3:4, :]),
    ):
        vectors_ref[row : row + 1, :] = contract_exact(value, own, 1, 1)
    bias_ref[...] = contract_exact(column_sum(hidden[chip]), units, 1, 1)
    grads = contract(low(single[4]), own_low, 1, 1)
    for spot in range(4):
        for third in range(3):
            start = third * D + 192 * spot
            part = low(mixed[spot][:, 192 * third : 192 * (third + 1)])
            grads = grads + contract(part, weight_ref[:, start : start + 192], 1, 1)
    lane = wide(lax.broadcasted_iota(jnp.int32, (64, 64), 1))
    table_ref[...] = contract_exact(wide(places[:, 0:64] == lane), grads, 0, 0)


def split_cores(value, kept_ref, gone_ref):
    rows = kept_ref.shape[1]
    core = lax.rem(lax.axis_index("seq"), 2)
    parts = value.reshape(-1, 2, rows, value.shape[1])
    kept_ref[...] = low(jnp.where(core == 0, parts[:, 0], parts[:, 1]))
    gone_ref[...] = low(jnp.where(core == 0, parts[:, 1], parts[:, 0]))


def local_down_back(
    cot_ref, mine_ref, other_ref, n_ref, scale_ref, rows_ref, active_ref, slope_ref, weight_ref, *outs
):
    out_ref, second_ref, kept_ref, gone_ref, hidden_ref, sums_ref, bias_ref, second_low_ref = outs
    step = pl.program_id(0)

    @pl.when(step == 0)
    def _():
        core = place_in()[2]
        row = lax.broadcasted_iota(jnp.int32, (2 * SEG, D), 0)
        grad = wide(cot_ref[...])
        normed = n_ref[...]
        out = normed * rows_ref[6:7, :] + rows_ref[7:8, :]
        for place in range(2):
            heads = jnp.where(core == place, mine_ref[...], other_ref[...])
            grad = jnp.where(row == place * SEG, heads[0:1], grad)
            out = jnp.where(row == place * SEG, heads[1:2], out)
        out_ref[...] = low(out)
        second = norm_back(grad, normed, scale_ref[...], rows_ref[6:7, :])
        second_ref[...] = second
        second_low_ref[...] = low(second)
        sums_ref[0:1, :] = column_sum(wide(low(second)))
        sums_ref[1:2, :] = column_sum(grad * normed)
        sums_ref[2:3, :] = column_sum(grad)

    second_low = second_low_ref[...]
    split_cores(contract(active_ref[...], second_low, 0, 0), kept_ref, gone_ref)
    hidden = low(contract(second_low, weight_ref[...], 1, 1) * wide(slope_ref[...]))
    hidden_ref[...] = hidden
    bias_ref[...] = column_sum(wide(hidden))


def local_up_back(low_ref, hidden_ref, weight_ref, second_ref, kept_ref, gone_ref, first_ref):
    hidden = hidden_ref[...]
    split_cores(contract(low_ref[...], hidden, 0, 0), kept_ref, gone_ref)
    part = contract(hidden, weight_ref[...], 1, 1)
    step = pl.program_id(0)

    @pl.when(step == 0)
    def _():
        first_ref[...] = second_ref[...] + part

    @pl.when(step > 0)
    def _():
        first_ref[...] += part


def local_attend_back(
    first_ref, n_ref, scale_ref, rows_ref, context_ref, mixed_ref, probs_a, probs_b, group_ref, *outs
):
    out_ref, total_ref, sums_ref, back_ref, context_low_ref = outs
    grad, normed = first_ref[...], n_ref[...]
    total = norm_back(grad, normed, scale_ref[...], rows_ref[3:4, :])
    total_ref[...] = total
    branch = low(total)
    sums_ref[2:3, :] = column_sum(wide(branch))
    sums_ref[3:4, :] = column_sum(grad * normed)
    sums_ref[4:5, :] = column_sum(grad)
    out_ref[...] = low(contract(context_ref[...], branch, 0, 0))
    context_low_ref[...] = low(contract(branch, group_ref[...], 1, 1))
    lane = lax.broadcasted_iota(jnp.int32, (SEG, 128), 1)
    for segment in range(2):
        rows = slice(segment * SEG, (segment + 1) * SEG)
        for pair in range(HEADS // 2):
            places = [
                slice(third * D + pair * 128, third * D + (pair + 1) * 128) for third in range(3)
            ]
            query, key, value = (mixed_ref[rows, place] for place in places)
            grad = context_low_ref[rows, places[0]]
            found = []
            for side in range(2):
                here = (lane < HEAD_DIM) if side == 0 else (lane >= HEAD_DIM)
                probs = (probs_a, probs_b)[segment][2 * pair + side]
                prob_grad = contract(value, jnp.where(here, grad, jnp.zeros_like(grad)), 1, 1)
                value_grad = contract(low(probs), grad, 1, 0)
                score = low(
                    probs * (prob_grad - jnp.sum(probs * prob_grad, axis=0, keepdims=True))
                )
                found.append(
                    (contract(score, key, 0, 0), contract(score, query, 1, 0), value_grad)
                )
            for third in range(3):
                merged = jnp.where(lane < HEAD_DIM, found[0][third], found[1][third])
                if third < 2:
                    merged = merged * HEAD_DIM ** (-0.5)
                back_ref[rows, places[third]] = low(merged)
    for third in (0, 2):
        columns = slice(third * D, (third + 1) * D)
        sums_ref[third // 2 : third // 2 + 1, :] = column_sum(wide(back_ref[:, columns]))


def local_mix_back(
    total_ref, back_ref, tokens_ref, group_ref, out_ref, sums_ref, more_ref, bias_ref, *outs
):
    input_ref, kept_ref, gone_ref, small_ref = outs
    tokens, total = tokens_ref[...], total_ref[...]
    for third in range(3):
        columns = slice(third * D, (third + 1) * D)
        back = back_ref[:, columns]
        grad = contract(tokens, back, 0, 0)
        split_cores(grad, kept_ref.at[:, :, columns], gone_ref.at[:, :, columns])
        total = total + contract(back, group_ref[:, columns], 1, 1)
    input_ref[...] = total
    columns = slice(3 * D, 4 * D)
    split_cores(wide(out_ref[...]), kept_ref.at[:, :, columns], gone_ref.at[:, :, columns])
    small_ref[...] = jnp.zeros_like(small_ref)
    small_ref[0:5, :] = sums_ref[0:5, :]
    small_ref[5:8, :] = more_ref[0:3, :]
    for owner in range(32):
        for row in range(4):
            taken = bias_ref[:, 96 * owner + 24 * row : 96 * owner + 24 * (row + 1)]
            small_ref[8 + row : 9 + row, 24 * owner : 24 * (owner + 1)] = taken
    columns = slice(4 * D, 4 * D + 128)
    split_cores(small_ref[...].T, kept_ref.at[:, :, columns], gone_ref.at[:, :, columns])


def finish_mix(own_ref, a_ref, b_ref, c_ref, mix_ref, out_ref, vectors_ref, bias_ref, wide_ref):
    total = own_ref[...] + wide(a_ref[...]) + wide(b_ref[...]) + wide(c_ref[...])
    mix_ref[...] = total[:, 0 : 3 * D]
    out_ref[...] = total[:, 3 * D : 4 * D]
    wide_ref[...] = jnp.zeros_like(wide_ref)
    wide_ref[0:24, :] = total[:, 4 * D : 4 * D + 128]
    turned = wide_ref[...].T
    vectors_ref[...] = turned[0:8, 0:24]
    for row in range(4):
        bias_ref[:, 24 * row : 24 * (row + 1)] = turned[8 + row : 9 + row, 0:24]


def plane_three(array_in):
    return [array_in] + [swap_chip(array_in, mask) for mask in (1, 2, 3)]


def plane_shards(
    tokens,
    cotangent,
    token_docs,
    segment_docs,
    segment_positions,
    local_mix,
    local_out,
    local_up,
    local_down,
    local_vectors,
    local_up_bias,
    cross_mix,
    cross_out,
    cross_up,
    cross_down,
    cross_vectors,
    cross_up_bias,
    position_table,
):
    chip = place_in()[1]
    flat_tokens = tokens.reshape(256, D)
    flat_cot = cotangent.reshape(256, D)
    places_in = segment_positions.T

    shards_in = (
        local_mix,
        local_out,
        local_up,
        local_down.reshape(4, 24, D),
        local_vectors,
        local_up_bias.reshape(1, 96),
        cross_mix,
        cross_out,
        cross_up,
        cross_vectors,
        cross_up_bias.reshape(1, 96),
        position_table.T,
    )
    made = [half(24, 3200), half(24, 5 * D), half(24, 4 * D)] + [half(24, D + 640)] * 4
    far = pl.BlockSpec(memory_space=pltpu.HBM)
    shard_one, shard_two, shard_three, *cross_pieces = on_core(
        prepare,
        made,
        shards_in,
        0,
        in_specs=[far] * 12,
        out_specs=[far] * 7,
        scratch=[pltpu.VMEM(a.shape, a.dtype) for a in list(shards_in) + made]
        + [
            pltpu.VMEM((128, 128), jnp.float32),
            pltpu.VMEM((128, 128), jnp.float32),
            pltpu.VMEM((4, 24, D + 640), jnp.bfloat16),
            pltpu.SemaphoreType.DMA((2, 12)),
        ],
    )
    cross_sent = [cross_pieces[0]] + [swap_chip(cross_pieces[mask], mask) for mask in (1, 2, 3)]
    z_one = reach_dp(shard_one)
    shard_two, *z_one = stage(shard_two, *z_one, *cross_sent)
    z_one, cross_sent = z_one[:4], z_one[4:]
    column_one = join_dp(z_one)
    column_one, shard_two = stage(column_one, shard_two)

    first, second = swap_one(column_one), swap_two(column_one)
    cross_row = join_cross(cross_sent, after(cross_down, column_one))
    *z_two, first, second, column_one, cross_row = stage(
        *reach_dp(shard_two), first, second, column_one, cross_row
    )

    third = swap_two(first)
    others = [swap_core(piece) for piece in (column_one, first, second)]
    column_two = join_dp(z_two)
    cross_moved = [cross_row, swap_dp(cross_row, 1)]
    third, column_two, cross_moved[1], *others = stage(third, column_two, cross_moved[1], *others)
    others.append(swap_core(third))

    first_group = gather_plane([column_one, first, second, third], others).reshape(D, 3200)
    mixed_rows, context_first, probs_first, rows, place_rows = on_core(
        local_attend,
        [half(256, 3 * D), half(SEG, D), shape_of(12, SEG, SEG), shape_of(128, D), shape_of(2, D)],
        (flat_tokens, first_group, token_docs, places_in),
        0,
    )
    first_two, second_two = swap_one(column_two), swap_two(column_two)
    *z_three, mixed_rows, first_two, second_two, column_two, cross_moved[1] = stage(
        *reach_dp(shard_three), mixed_rows, first_two, second_two, column_two, cross_moved[1]
    )
    cross_moved.append(swap_dp(cross_moved[1], 1))

    third_two = swap_two(first_two)
    others = [swap_core(piece) for piece in (column_two, first_two, second_two)]
    column_three = join_dp(z_three)
    def plain(*shapes):
        return [pl.BlockSpec(shape, lambda j, n=len(shape): (0,) * n) for shape in shapes]

    context_rows, probs_second, normed_one, scale_one, low_one = on_core(
        local_attend_more,
        [half(256, D), shape_of(12, SEG, SEG), shape_of(256, D), shape_of(256, 1), half(256, D)],
        (flat_tokens, mixed_rows, context_first, first_group, rows, token_docs),
        0,
        grid=(1,),
        in_specs=plain((256, D), (256, 3 * D), (SEG, D))
        + [pl.BlockSpec((D, D), lambda j: (0, 3))]
        + plain((128, D), (2, SEG)),
        out_specs=plain((256, D), (12, SEG, SEG), (256, D), (256, 1), (256, D)),
        scratch=[pltpu.VMEM((SEG, D), jnp.bfloat16)],
    )
    up_bias = rows[80:84].reshape(4, 32, 24).transpose(1, 0, 2).reshape(1, 4 * D)
    cross_moved[2], third_two, column_three, low_one, up_bias, rows_later, *others = stage(
        cross_moved[2], third_two, column_three, low_one, up_bias, rows[84:88], *others
    )
    cross_moved.append(swap_dp(cross_moved[2], 1))

    first_three, second_three = swap_one(column_three), swap_two(column_three)
    others.append(swap_core(third_two))
    second_group, cross_out_weight = gather_up(
        [column_two, first_two, second_two, third_two], others
    )
    whole = pl.BlockSpec((256, D), lambda j: (0, 0))
    thin = pl.BlockSpec((256, 1), lambda j: (0, 0))
    vectors = pl.BlockSpec((128, D), lambda j: (0, 0))
    eight = pl.BlockSpec((8, D), lambda j: (0, 0))
    across = pl.BlockSpec((256, D), lambda j: (0, j))
    tall = pl.BlockSpec((D, D), lambda j: (0, j))
    deep = pl.BlockSpec((D, D), lambda j: (j, 0))
    strip = pl.BlockSpec((1, D), lambda j: (0, j))
    across_half = pl.BlockSpec((256, 2 * D), lambda j: (0, j))
    tall_half = pl.BlockSpec((D, 2 * D), lambda j: (0, j))
    deep_half = pl.BlockSpec((2 * D, D), lambda j: (j, 0))
    strip_half = pl.BlockSpec((1, 2 * D), lambda j: (0, j))
    active_rows, slope_rows = on_core(
        local_up_part,
        [half(256, 4 * D)] * 2,
        (low_one, second_group, up_bias),
        2 * 256 * D * 4 * D,
        grid=(4,),
        in_specs=[whole, tall, strip],
        out_specs=[across, across],
    )
    active_rows, first_three, second_three, column_three, cross_moved[3], rows_later = stage(
        active_rows, first_three, second_three, column_three, cross_moved[3], rows_later
    )

    third_three = swap_two(first_three)
    others = [swap_core(piece) for piece in (column_three, first_three, second_three)]
    cross_bias = rows_later.reshape(4, 4, 4, 2, 24)
    cross_bias = lax.dynamic_index_in_dim(cross_bias, chip, 2, keepdims=False)
    cross_bias = cross_bias.transpose(1, 2, 0, 3).reshape(1, D)
    third_three, cross_column, cross_bias, *others = stage(
        third_three, join_dp(cross_moved), cross_bias, *others
    )

    others.append(swap_core(third_three))
    down_weight = gather_down([column_three, first_three, second_three, third_three], others)
    down_weight, cross_column = stage(down_weight.reshape(4 * D, D), cross_column)
    cross_other = swap_core(cross_column)
    normed_two, scale_two, kept, given = on_core(
        local_down_part,
        [shape_of(256, D), shape_of(256, 1), shape_of(8, D), shape_of(8, D)],
        (active_rows, down_weight, normed_one, rows, flat_cot, flat_cot, place_rows),
        2 * 256 * D * 4 * D,
        grid=(2,),
        in_specs=[
            across_half,
            deep_half,
            whole,
            vectors,
            pl.BlockSpec((16, D), lambda j: (0, 0)),
            pl.BlockSpec((16, D), lambda j: (8, 0)),
            pl.BlockSpec((2, D), lambda j: (0, 0)),
        ],
        out_specs=[whole, thin, eight, eight],
        scratch=[pltpu.VMEM((256, D), jnp.float32)],
    )

    row8, mix_share = (8, D), (D, 640)
    out_share = pl.BlockSpec((D, D), lambda j: (0, 0))
    up_share = pl.BlockSpec((D, D), lambda j: (0, 0))
    given, kept, cross_other = stage(given, kept, cross_other)
    got = swap_core(given)
    cross_up_part, cross_mix_part, cross_down_part = place_cross(cross_column, cross_other)
    kept, got, cross_mix_part = stage(kept, got, cross_mix_part)
    pair = on_core(join_pair, shape_of(8, D), (kept, got), 0, room=12)
    row_in, row_grad, mixed, probs, context = on_core(
        cross_attend,
        [shape_of(8, D), shape_of(8, D), half(8, 576), shape_of(3, 8, 8), half(8, 192)],
        (*plane_three(pair), cross_mix_part, rows, segment_docs),
        0,
        room=12,
    )
    row_n, row_scale, row_low, hidden, active, part = on_core(
        cross_up_down,
        [shape_of(8, D), shape_of(8, 1), half(8, D), shape_of(8, D), half(8, D), shape_of(8, D)],
        (
            *plane_three(context),
            row_in,
            cross_out_weight,
            rows,
            cross_up_part,
            cross_bias,
            cross_down_part,
        ),
        0,
        grid=(1,),
        in_specs=plain(*[(8, 192)] * 4, row8)
        + [out_share]
        + plain((128, D))
        + [up_share]
        + plain((1, D), (D, D)),
        out_specs=plain(row8, (8, 1), row8, row8, row8, row8),
        room=12,
    )
    row_out, row_second, hidden_low, part, sums = on_core(
        cross_turn,
        [shape_of(8, D), shape_of(8, D), half(8, D), shape_of(8, D), shape_of(8, D)],
        (*plane_three(part), row_n, rows, row_grad, hidden, cross_up_part, cross_down_part),
        0,
        grid=(1,),
        in_specs=plain(*[row8] * 4, row8, (128, D), row8, row8) + [up_share] + plain((D, D)),
        out_specs=plain(*[row8] * 5),
        room=12,
    )
    row_total, part, packed = on_core(
        cross_attend_back,
        [shape_of(8, D), shape_of(8, D), half(48, D)],
        (
            *plane_three(part),
            row_second,
            row_n,
            row_scale,
            rows,
            cross_out_weight,
            mixed,
            probs,
            cross_mix_part,
            hidden_low,
            active,
            context,
            row_in,
            row_low,
            sums,
            places_in,
        ),
        0,
        grid=(1,),
        in_specs=plain(*[row8] * 4, row8, row8, (8, 1), (128, D))
        + [out_share]
        + plain((8, 576), (3, 8, 8), mix_share, row8, row8, (8, 192), row8, row8, row8, (1, 2)),
        out_specs=plain(row8, row8, (48, D)),
        scratch=[pltpu.VMEM((48, D), jnp.float32), pltpu.VMEM((8, D), jnp.float32)],
        room=12,
    )
    kept, given = on_core(
        cross_finish,
        [shape_of(8, D), shape_of(8, D)],
        (*plane_three(part), row_total, row_out),
        0,
        scratch=[pltpu.VMEM((8, D), jnp.float32)],
        room=12,
    )
    got, kept, packed = stage(swap_core(given), kept, packed)
    pack_one, pack_two = swap_one(packed), swap_two(packed)

    twos = pl.BlockSpec((8, 96, D), lambda j: (j, 0, 0))
    layer_output, second_rows, down_kept, down_gone, hidden_grads, sums_two, bias_grad = on_core(
        local_down_back,
        [
            half(256, D),
            shape_of(256, D),
            half(16, 96, D),
            half(16, 96, D),
            half(256, 4 * D),
            shape_of(8, D),
            shape_of(1, 4 * D),
        ],
        (flat_cot, kept, got, normed_two, scale_two, rows, active_rows, slope_rows, down_weight),
        4 * 256 * D * 4 * D,
        grid=(2,),
        in_specs=[whole, eight, eight, whole, thin, vectors, across_half, across_half, deep_half],
        out_specs=[whole, whole, twos, twos, across_half, eight, strip_half],
        scratch=[pltpu.VMEM((256, D), jnp.bfloat16)],
    )
    down_total = Sum(down_kept.reshape(4, 4, 96, D))
    hidden_grads, down_gone, pack_one, pack_two = stage(
        hidden_grads, down_gone.reshape(4, 4, 96, D), pack_one, pack_two
    )
    pack_three = swap_two(pack_one)

    down_got = swap_core(down_gone)
    sixteens = pl.BlockSpec((16, 24, 2 * D), lambda j: (0, 0, j))
    up_kept, up_gone, first_rows = on_core(
        local_up_back,
        [half(16, 24, 4 * D), half(16, 24, 4 * D), shape_of(256, D)],
        (low_one, hidden_grads, second_group, second_rows),
        4 * 256 * D * 4 * D,
        grid=(2,),
        in_specs=[whole, across_half, tall_half, whole],
        out_specs=[sixteens, sixteens, whole],
    )
    up_total = Sum(up_kept.reshape(4, 4, 24, 4 * D))
    down_got, first_rows, up_gone, pack_three = stage(
        down_got, first_rows, up_gone.reshape(4, 4, 24, 4 * D), pack_three
    )
    plane_pack = join_chips([packed, pack_one, pack_two, pack_three])
    packs = [plane_pack, swap_dp(plane_pack, 1), swap_dp(plane_pack, 3)]

    up_got = swap_core(up_gone)
    down_sent = down_total.first(down_got)
    down_back = swap_one(down_sent)
    flat = pl.BlockSpec((256, 3 * D), lambda j: (0, 0))
    out_grad, sum_rows, sums_one, back_rows = on_core(
        local_attend_back,
        [half(D, D), shape_of(256, D), shape_of(8, D), half(256, 3 * D)],
        (
            first_rows,
            normed_one,
            scale_one,
            rows,
            context_rows,
            mixed_rows,
            probs_first,
            probs_second,
            first_group,
        ),
        4 * 256 * D * 2 * D,
        grid=(1,),
        in_specs=[
            whole,
            whole,
            thin,
            vectors,
            whole,
            flat,
            pl.BlockSpec((12, SEG, SEG), lambda j: (0, 0, 0)),
            pl.BlockSpec((12, SEG, SEG), lambda j: (0, 0, 0)),
            pl.BlockSpec((D, D), lambda j: (0, 3)),
        ],
        out_specs=[pl.BlockSpec((D, D), lambda j: (0, 0)), whole, eight, flat],
        scratch=[pltpu.VMEM((256, D), jnp.bfloat16)],
    )
    up_sent = up_total.first(up_got)
    down_back, back_rows, up_sent, *packs = stage(down_back, back_rows, up_sent, *packs)
    packs.insert(2, swap_dp(packs[0], 2))

    up_back = swap_one(up_sent)
    down_onward = down_total.second(down_back)
    sides = [half(16, 24, 4 * D + 128)] * 2
    input_grad, mix_kept, mix_gone = on_core(
        local_mix_back,
        [shape_of(256, D)] + sides,
        (
            sum_rows,
            back_rows,
            flat_tokens,
            first_group,
            out_grad,
            sums_one,
            sums_two,
            bias_grad,
        ),
        4 * 256 * D * 3 * D,
        scratch=[pltpu.VMEM((128, D), jnp.float32)],
    )
    mix_total = Sum(mix_kept.reshape(4, 4, 24, 3200))
    up_back, down_onward, mix_gone, packs[2] = stage(
        up_back, down_onward, mix_gone.reshape(4, 4, 24, 3200), packs[2]
    )

    mix_got, down_last = swap_core(mix_gone), swap_two(down_onward)
    up_onward = up_total.second(up_back)
    my_rows = join_dp(packs)

    up_last = swap_two(up_onward)
    mix_sent = mix_total.first(mix_got)
    down_others = down_total.third(down_last)
    up_last, mix_sent, my_rows, *down_others = stage(up_last, mix_sent, my_rows, *down_others)
    other_rows = swap_core(my_rows)

    mix_back, down_others = swap_one(mix_sent), send_dp(down_others)
    up_others = up_total.third(up_last)
    mix_back, other_rows, *others = stage(mix_back, other_rows, *down_others, *up_others)
    down_others, up_others = others[:3], others[3:]

    mix_last = swap_two(mix_total.second(mix_back))
    up_others = send_dp(up_others)
    down_sum = down_total.total(down_others)
    mix_last, down_sum, other_rows = stage(mix_last, down_sum, other_rows)

    mix_others = send_dp(mix_total.third(mix_last))
    up_sum = up_total.total(up_others)
    cross_grads = on_core(
        cross_owner,
        [
            shape_of(24, 3 * D),
            shape_of(24, D),
            shape_of(24, 4 * D),
            shape_of(96, D),
            shape_of(8, 24),
            shape_of(1, 96),
            shape_of(64, 24),
        ],
        (my_rows, other_rows, cross_mix),
        0,
        scratch=[
            pltpu.VMEM((4, 64, D), jnp.float32),
            pltpu.VMEM((4, 64, D), jnp.float32),
            pltpu.VMEM((5, 64, D), jnp.float32),
            pltpu.VMEM((64, D), jnp.float32),
            pltpu.VMEM((8, D), jnp.float32),
            pltpu.VMEM((64, 128), jnp.float32),
        ],
    )
    mix_sum, out_sum, vectors_sum, bias_sum = on_core(
        finish_mix,
        [shape_of(24, 3 * D), shape_of(24, D), shape_of(8, 24), shape_of(1, 96)],
        (mix_total.own, *mix_others),
        0,
        grid=(1,),
        in_specs=plain(*[(24, 4 * D + 128)] * 4),
        out_specs=plain((24, 3 * D), (24, D), (8, 24), (1, 96)),
        scratch=[pltpu.VMEM((128, 128), jnp.float32)],
    )
    return (
        layer_output.reshape(2, SEG, D),
        input_grad.reshape(2, SEG, D),
        mix_sum,
        out_sum,
        up_sum,
        down_sum,
        vectors_sum,
        bias_sum.reshape(96),
        *cross_grads[:5],
        cross_grads[5].reshape(96),
        cross_grads[6],
    )


def solution(mesh):
    flat = dict(mesh.shape) == {"dp": 4, "seq": 8}
    return jax.shard_map(
        plane_shards if flat else shards,
        mesh=mesh,
        in_specs=(
            P("dp", "seq", None),
            P("dp", "seq", None),
            P("dp", "seq"),
            P("dp", None),
            P("dp", "seq"),
            P(("dp", "seq"), None),
            P(("dp", "seq"), None),
            P(("dp", "seq"), None),
            P(("dp", "seq"), None),
            P(None, ("dp", "seq")),
            P(("dp", "seq")),
            P(("dp", "seq"), None),
            P(("dp", "seq"), None),
            P(("dp", "seq"), None),
            P(("dp", "seq"), None),
            P(None, ("dp", "seq")),
            P(("dp", "seq")),
            P(None, ("dp", "seq")),
        ),
        out_specs=(
            P("dp", "seq", None),
            P("dp", "seq", None),
            P(("dp", "seq"), None),
            P(("dp", "seq"), None),
            P(("dp", "seq"), None),
            P(("dp", "seq"), None),
            P(None, ("dp", "seq")),
            P(("dp", "seq")),
            P(("dp", "seq"), None),
            P(("dp", "seq"), None),
            P(("dp", "seq"), None),
            P(("dp", "seq"), None),
            P(None, ("dp", "seq")),
            P(("dp", "seq")),
            P(None, ("dp", "seq")),
        ),
        check_vma=False,
    )
```

```python
from functools import partial
import math

import jax
import jax.numpy as jnp
from jax import lax
from jax.experimental import pallas as pl
from jax.experimental.pallas import tpu as pltpu
from jax.sharding import PartitionSpec as P

D = 768
HEADS = 12
HEAD_DIM = 64
SEG = 128
MICRO = 2


epsilon = 1e-05
masked_score = -1000000000.0
owner_dims = (0, 0, 0, 0, 1, 0, 0, 0, 0, 0, 1, 0, 1)


def layer_norm(values, gain_row, shift_row):
    centered = values - jnp.mean(values, axis=-1, keepdims=True)
    variance = jnp.mean(centered * centered, axis=-1, keepdims=True)
    return centered * lax.rsqrt(variance + epsilon) * gain_row + shift_row


def gelu_exact(hidden):
    return jax.nn.gelu(hidden, approximate=False)


def contract(left_side, right_side, left_dim, right_dim):
    return lax.dot_general(
        left_side,
        right_side,
        (((left_dim,), (right_dim,)), ((), ())),
        preferred_element_type=jnp.float32,
    )


def contract_exact(left_side, right_side, left_dim, right_dim):
    return lax.dot_general(
        left_side,
        right_side,
        (((left_dim,), (right_dim,)), ((), ())),
        precision=lax.Precision.HIGHEST,
        preferred_element_type=jnp.float32,
    )


def owner_pack(grads, devices):
    pieces = []
    for grad_value, split_dim in zip(grads, owner_dims):
        if split_dim == 0:
            pieces.append(grad_value.reshape(devices, -1))
        else:
            row_count = grad_value.shape[0]
            pieces.append(
                grad_value.reshape(row_count, devices, -1).transpose(1, 0, 2).reshape(devices, -1)
            )
    return jnp.concatenate(pieces, axis=1)


def owner_unpack(packed, shard_shapes):
    results = []
    offset = 0
    for shard_shape in shard_shapes:
        length = math.prod(shard_shape)
        results.append(packed[0, offset : offset + length].reshape(shard_shape))
        offset = offset + length
    return tuple(results)


def fetch_weights(
    local_mix,
    local_out,
    local_up,
    local_down,
    local_vectors,
    local_up_bias,
    cross_mix,
    cross_out,
    cross_up,
    cross_down,
    cross_vectors,
    cross_up_bias,
    position_table,
):
    return (
        lax.all_gather(local_mix, ("dp", "seq"), axis=0, tiled=True),
        lax.all_gather(local_out, ("dp", "seq"), axis=0, tiled=True),
        lax.all_gather(local_up, ("dp", "seq"), axis=0, tiled=True),
        lax.all_gather(local_down, ("dp", "seq"), axis=0, tiled=True),
        lax.all_gather(local_vectors, ("dp", "seq"), axis=1, tiled=True),
        lax.all_gather(local_up_bias, ("dp", "seq"), axis=0, tiled=True),
        lax.all_gather(cross_mix, ("dp", "seq"), axis=0, tiled=True),
        lax.all_gather(cross_out, ("dp", "seq"), axis=0, tiled=True),
        lax.all_gather(cross_up, ("dp", "seq"), axis=0, tiled=True),
        lax.all_gather(cross_down, ("dp", "seq"), axis=0, tiled=True),
        lax.all_gather(cross_vectors, ("dp", "seq"), axis=1, tiled=True),
        lax.all_gather(cross_up_bias, ("dp", "seq"), axis=0, tiled=True),
        lax.all_gather(position_table, ("dp", "seq"), axis=1, tiled=True),
    )


def segment_parts(mixed_rows, token_docs):
    segment_count = token_docs.shape[0]
    split_heads = mixed_rows.reshape(segment_count, SEG, 3, HEADS, HEAD_DIM)
    allowed = token_docs[:, None, :, None] == token_docs[:, None, None, :]
    scores = jnp.einsum(
        "nqhd,nkhd->nhqk",
        split_heads[:, :, 0],
        split_heads[:, :, 1],
        preferred_element_type=jnp.float32,
    ) * HEAD_DIM ** (-0.5)
    scores = jnp.where(allowed, scores, masked_score)
    return (split_heads, scores)


def segment_forward(mixed_rows, token_docs):
    split_heads, scores = segment_parts(mixed_rows, token_docs)
    log_total = jax.nn.logsumexp(scores, axis=-1)
    weights = jax.nn.softmax(scores, axis=-1).astype(jnp.bfloat16)
    context = jnp.einsum(
        "nhqk,nkhd->nqhd", weights, split_heads[:, :, 2], preferred_element_type=jnp.float32
    )
    return (context.reshape(-1, D).astype(jnp.bfloat16), log_total)


def segment_backward(context_grad, log_total, mixed_rows, token_docs):
    split_heads, scores = segment_parts(mixed_rows, token_docs)
    segment_count = token_docs.shape[0]
    probs = jnp.exp(scores - log_total[..., None])
    grad_heads = context_grad.reshape(segment_count, SEG, HEADS, HEAD_DIM)
    prob_grad = jnp.einsum(
        "nqhd,nkhd->nhqk", grad_heads, split_heads[:, :, 2], preferred_element_type=jnp.float32
    )
    value_grad = jnp.einsum(
        "nhqk,nqhd->nkhd",
        probs.astype(jnp.bfloat16),
        grad_heads,
        preferred_element_type=jnp.float32,
    )
    score_grad = probs * (prob_grad - jnp.sum(probs * prob_grad, axis=-1, keepdims=True))
    score_low = score_grad.astype(jnp.bfloat16) * HEAD_DIM ** (-0.5)
    query_grad = jnp.einsum(
        "nhqk,nkhd->nqhd", score_low, split_heads[:, :, 1], preferred_element_type=jnp.float32
    )
    key_grad = jnp.einsum(
        "nhqk,nqhd->nkhd", score_low, split_heads[:, :, 0], preferred_element_type=jnp.float32
    )
    row_total = segment_count * SEG
    return jnp.concatenate(
        [
            query_grad.reshape(row_total, D),
            key_grad.reshape(row_total, D),
            value_grad.reshape(row_total, D),
        ],
        axis=1,
    )


def cross_parts(mixed_rows, gathered, segment_docs):
    group_size = segment_docs.shape[0]
    per_device = mixed_rows.shape[0] // group_size
    query_rows = mixed_rows[:, :D].reshape(group_size, per_device, HEADS, HEAD_DIM)
    key_rows = gathered[:, :, :D].reshape(group_size, -1, HEADS, HEAD_DIM)
    value_rows = gathered[:, :, D:].reshape(group_size, -1, HEADS, HEAD_DIM)
    own_docs = lax.dynamic_slice_in_dim(
        segment_docs, lax.axis_index("seq") * per_device, per_device, 1
    )
    allowed = own_docs[:, None, :, None] == segment_docs[:, None, None, :]
    scores = jnp.einsum(
        "bqhd,bkhd->bhqk", query_rows, key_rows, preferred_element_type=jnp.float32
    ) * HEAD_DIM ** (-0.5)
    scores = jnp.where(allowed, scores, masked_score)
    return (query_rows, key_rows, value_rows, scores)


def cross_forward(mixed_rows, segment_docs):
    group_size = segment_docs.shape[0]
    per_device = mixed_rows.shape[0] // group_size
    pair_rows = mixed_rows[:, D:].reshape(group_size, per_device, 2 * D)
    gathered = lax.all_gather(pair_rows, "seq", axis=1, tiled=True)
    query_rows, key_rows, value_rows, scores = cross_parts(mixed_rows, gathered, segment_docs)
    log_total = jax.nn.logsumexp(scores, axis=-1)
    weights = jax.nn.softmax(scores, axis=-1).astype(jnp.bfloat16)
    context = jnp.einsum("bhqk,bkhd->bqhd", weights, value_rows, preferred_element_type=jnp.float32)
    return (context.reshape(-1, D).astype(jnp.bfloat16), (gathered, log_total))


def cross_backward(context_grad, cross_kept, mixed_rows, segment_docs):
    gathered, log_total = cross_kept
    group_size = segment_docs.shape[0]
    row_total = mixed_rows.shape[0]
    per_device = row_total // group_size
    query_rows, key_rows, value_rows, scores = cross_parts(mixed_rows, gathered, segment_docs)
    probs = jnp.exp(scores - log_total[..., None])
    grad_heads = context_grad.reshape(group_size, per_device, HEADS, HEAD_DIM)
    prob_grad = jnp.einsum(
        "bqhd,bkhd->bhqk", grad_heads, value_rows, preferred_element_type=jnp.float32
    )
    value_grad = jnp.einsum(
        "bhqk,bqhd->bkhd",
        probs.astype(jnp.bfloat16),
        grad_heads,
        preferred_element_type=jnp.float32,
    )
    score_grad = probs * (prob_grad - jnp.sum(probs * prob_grad, axis=-1, keepdims=True))
    score_low = score_grad.astype(jnp.bfloat16) * HEAD_DIM ** (-0.5)
    query_grad = jnp.einsum(
        "bhqk,bkhd->bqhd", score_low, key_rows, preferred_element_type=jnp.float32
    )
    key_grad = jnp.einsum(
        "bhqk,bqhd->bkhd", score_low, query_rows, preferred_element_type=jnp.float32
    )
    pair_grads = jnp.concatenate(
        [key_grad.reshape(group_size, -1, D), value_grad.reshape(group_size, -1, D)], axis=2
    )
    own_pairs = lax.psum_scatter(
        pair_grads.astype(jnp.bfloat16), "seq", scatter_dimension=1, tiled=True
    ).astype(jnp.float32)
    return jnp.concatenate(
        [query_grad.reshape(row_total, D), own_pairs.reshape(row_total, 2 * D)], axis=1
    )


def block_forward(inputs, weights, attend):
    mix_weight, out_weight, up_weight, down_weight, vectors, up_bias = weights
    vector_rows = vectors.astype(jnp.float32)
    in_bias = jnp.concatenate([vector_rows[0], jnp.zeros_like(vector_rows[0]), vector_rows[1]])
    rounded = inputs.astype(jnp.bfloat16)
    mixed_rows = (
        jnp.dot(rounded, mix_weight, preferred_element_type=jnp.float32) + in_bias
    ).astype(jnp.bfloat16)
    context, attend_kept = attend(mixed_rows)
    first_sum = (
        inputs + jnp.dot(context, out_weight, preferred_element_type=jnp.float32) + vector_rows[2]
    )
    first_norm = layer_norm(first_sum, vector_rows[3], vector_rows[4])
    first_low = first_norm.astype(jnp.bfloat16)
    hidden = jnp.dot(first_low, up_weight, preferred_element_type=jnp.float32) + up_bias.astype(
        jnp.float32
    )
    active = gelu_exact(hidden).astype(jnp.bfloat16)
    second_sum = (
        first_norm
        + jnp.dot(active, down_weight, preferred_element_type=jnp.float32)
        + vector_rows[5]
    )
    output = layer_norm(second_sum, vector_rows[6], vector_rows[7])
    return (
        output,
        (
            rounded,
            mixed_rows,
            attend_kept,
            context,
            first_sum,
            first_low,
            hidden,
            active,
            second_sum,
        ),
    )


def block_backward(output_grad, block_kept, weights, attend_back):
    mix_weight, out_weight, up_weight, down_weight, vectors, up_bias = weights
    vector_rows = vectors.astype(jnp.float32)
    rounded, mixed_rows, attend_kept, context, first_sum, first_low, hidden, active, second_sum = (
        block_kept
    )
    unused, second_pull = jax.vjp(layer_norm, second_sum, vector_rows[6], vector_rows[7])
    second_grad, gain_two, shift_two = second_pull(output_grad)
    second_low = second_grad.astype(jnp.bfloat16)
    down_grad = contract(active, second_low, 0, 0)
    down_bias = jnp.sum(second_low.astype(jnp.float32), axis=0)
    active_grad = contract(second_low, down_weight, 1, 1)
    unused, gelu_pull = jax.vjp(gelu_exact, hidden)
    hidden_grad = gelu_pull(active_grad)[0]
    hidden_low = hidden_grad.astype(jnp.bfloat16)
    up_grad = contract(first_low, hidden_low, 0, 0)
    up_bias_grad = jnp.sum(hidden_low.astype(jnp.float32), axis=0)
    first_grad = second_grad + contract(hidden_low, up_weight, 1, 1)
    unused, first_pull = jax.vjp(layer_norm, first_sum, vector_rows[3], vector_rows[4])
    sum_grad, gain_one, shift_one = first_pull(first_grad)
    branch_low = sum_grad.astype(jnp.bfloat16)
    out_grad = contract(context, branch_low, 0, 0)
    out_bias = jnp.sum(branch_low.astype(jnp.float32), axis=0)
    context_low = contract(branch_low, out_weight, 1, 1).astype(jnp.bfloat16)
    mixed_low = attend_back(context_low, attend_kept, mixed_rows).astype(jnp.bfloat16)
    mix_grad = contract(rounded, mixed_low, 0, 0)
    mixed_sums = jnp.sum(mixed_low.astype(jnp.float32), axis=0)
    input_grad = sum_grad + contract(mixed_low, mix_weight, 1, 1)
    vectors_grad = jnp.stack(
        [
            mixed_sums[:D],
            mixed_sums[2 * D :],
            out_bias,
            gain_one,
            shift_one,
            down_bias,
            gain_two,
            shift_two,
        ]
    )
    return (input_grad, (mix_grad, out_grad, up_grad, down_grad, vectors_grad, up_bias_grad))


def shards(
    tokens,
    cotangent,
    token_docs,
    segment_docs,
    segment_positions,
    local_mix,
    local_out,
    local_up,
    local_down,
    local_vectors,
    local_up_bias,
    cross_mix,
    cross_out,
    cross_up,
    cross_down,
    cross_vectors,
    cross_up_bias,
    position_table,
):
    sequence_count, span, width = tokens.shape
    group_size = sequence_count // MICRO
    segment_count = span // SEG
    devices = lax.axis_size(("dp", "seq"))
    shard_shapes = tuple(
        (
            array_in.shape
            for array_in in (
                local_mix,
                local_out,
                local_up,
                local_down,
                local_vectors,
                local_up_bias,
                cross_mix,
                cross_out,
                cross_up,
                cross_down,
                cross_vectors,
                cross_up_bias,
                position_table,
            )
        )
    )
    layer_outputs = []
    input_grads = []
    totals = ()
    for micro_step in range(MICRO):
        lower_row = micro_step * group_size
        upper_row = lower_row + group_size
        gathered = fetch_weights(
            local_mix,
            local_out,
            local_up,
            local_down,
            local_vectors,
            local_up_bias,
            cross_mix,
            cross_out,
            cross_up,
            cross_down,
            cross_vectors,
            cross_up_bias,
            position_table,
        )
        local_weights = gathered[0:6]
        cross_weights = gathered[6:12]
        position_rows = gathered[12]
        inputs = tokens[lower_row:upper_row].reshape(group_size * span, width).astype(jnp.float32)
        docs_here = token_docs[lower_row:upper_row]
        segments_here = segment_docs[lower_row:upper_row]
        first_out, first_kept = block_forward(
            inputs, local_weights, partial(segment_forward, token_docs=docs_here)
        )
        segment_grid = first_out.reshape(group_size * segment_count, SEG, width)
        places = segment_positions[lower_row:upper_row].reshape(group_size * segment_count)
        position_picks = (
            places[:, None] == jnp.arange(position_rows.shape[0], dtype=jnp.int32)[None, :]
        ).astype(jnp.bfloat16)
        heads_in = segment_grid[:, 0, :] + jnp.dot(
            position_picks, position_rows, preferred_element_type=jnp.float32
        )
        heads_out, cross_kept = block_forward(
            heads_in, cross_weights, partial(cross_forward, segment_docs=segments_here)
        )
        joined = jnp.concatenate([heads_out[:, None, :], segment_grid[:, 1:, :]], axis=1)
        layer_outputs.append(joined.astype(jnp.bfloat16))
        gathered = fetch_weights(
            local_mix,
            local_out,
            local_up,
            local_down,
            local_vectors,
            local_up_bias,
            cross_mix,
            cross_out,
            cross_up,
            cross_down,
            cross_vectors,
            cross_up_bias,
            position_table,
        )
        local_weights = gathered[0:6]
        cross_weights = gathered[6:12]
        output_grad = cotangent[lower_row:upper_row].astype(jnp.float32)
        heads_grad, cross_grads = block_backward(
            output_grad[:, 0, :],
            cross_kept,
            cross_weights,
            partial(cross_backward, segment_docs=segments_here),
        )
        table_grad = contract_exact(position_picks.astype(jnp.float32), heads_grad, 0, 0)
        first_grad = jnp.concatenate(
            [heads_grad[:, None, :], output_grad[:, 1:, :]], axis=1
        ).reshape(group_size * span, width)
        input_grad, local_grads = block_backward(
            first_grad, first_kept, local_weights, partial(segment_backward, token_docs=docs_here)
        )
        input_grads.append(input_grad.reshape(group_size, span, width))
        step_grads = local_grads + cross_grads + (table_grad,)
        if micro_step == 0:
            totals = tuple(step_grads)
        else:
            totals = tuple(
                (total_sum + step_sum for total_sum, step_sum in zip(totals, step_grads))
            )
    packed_total = lax.psum_scatter(
        owner_pack(totals, devices), ("dp", "seq"), scatter_dimension=0, tiled=True
    )
    summed = owner_unpack(packed_total, shard_shapes)
    layer_output = jnp.concatenate(layer_outputs, axis=0)
    input_gradient = jnp.concatenate(input_grads, axis=0)
    return (layer_output, input_gradient) + tuple(summed)


def swap_dp(array_in, shift):
    return lax.ppermute(array_in, "dp", [(i, (i + shift) % 4) for i in range(4)])


def swap_core(array_in):
    return lax.ppermute(array_in, "seq", [(i, i ^ 1) for i in range(8)])


def swap_chip(array_in, mask):
    return lax.ppermute(array_in, "seq", [(i, i ^ (2 * mask)) for i in range(8)])


def swap_one(array_in):
    return lax.ppermute(array_in, "seq", [(i, i ^ (2 if i % 2 == 0 else 4)) for i in range(8)])


def swap_two(array_in):
    return lax.ppermute(array_in, "seq", [(i, i ^ (4 if i % 2 == 0 else 2)) for i in range(8)])


def place_in():
    layer = lax.axis_index("dp")
    spot = lax.axis_index("seq")
    return layer, spot // 2, lax.rem(spot, 2)


def after(array_in, *before):
    return lax.optimization_barrier((array_in,) + before)[0]


def stage(*values):
    return lax.optimization_barrier(values)


def wide(array_in):
    return array_in.astype(jnp.float32)


def low(array_in):
    return array_in.astype(jnp.bfloat16)


def copies(pieces, shapes, moves, room=64):
    count, made = len(pieces), len(shapes)
    total = len(moves(0, 0, 0))

    def kernel(*refs):
        outs, held, sems = refs[count : count + made], refs[count + made : -1], refs[-1]
        inward = [pltpu.make_async_copy(refs[i], held[i], sems.at[0, i]) for i in range(count)]
        for copy in inward:
            copy.start()
        outward = []
        for i, (piece, part, out, place) in enumerate(moves(*place_in())):
            if inward[piece] is not None:
                inward[piece].wait()
                inward[piece] = None
            copy = pltpu.make_async_copy(held[piece].at[part], outs[out].at[place], sems.at[1, i])
            copy.start()
            outward.append(copy)
        for copy in outward:
            copy.wait()

    size = 2 * sum(math.prod(shape) for shape in shapes) * 2
    return pl.pallas_call(
        kernel,
        out_shape=[jax.ShapeDtypeStruct(shape, pieces[0].dtype) for shape in shapes],
        in_specs=[pl.BlockSpec(memory_space=pltpu.HBM)] * count,
        out_specs=[pl.BlockSpec(memory_space=pltpu.HBM)] * made,
        scratch_shapes=[pltpu.VMEM(piece.shape, piece.dtype) for piece in pieces]
        + [pltpu.SemaphoreType.DMA((2, max(count, total)))],
        compiler_params=pltpu.CompilerParams(vmem_limit_bytes=room * 2**20),
        cost_estimate=pl.CostEstimate(flops=0, bytes_accessed=0, transcendentals=0),
    )(*pieces)


every = slice(None)


def reach_dp(shard):
    return [shard] + [swap_dp(shard, shift) for shift in (1, 2, 3)]


def join_dp(pieces):
    return copies(
        pieces,
        [(4,) + pieces[0].shape],
        lambda layer, chip, core: [(i, every, 0, lax.rem(layer + 4 - i, 4)) for i in range(4)],
    )[0]


def plane_order(chip, core):
    near, far = chip ^ (1 + core), chip ^ (2 - core)
    return (chip, near, far, chip ^ 3), (chip, far, near, chip ^ 3)


def join_chips(pieces):
    def moves(layer, chip, core):
        return [(i, every, 0, spot) for i, spot in enumerate(plane_order(chip, core)[0])]

    return copies(pieces, [(4,) + pieces[0].shape], moves)[0]


def gather_plane(mine, others):
    def moves(layer, chip, core):
        own, other = plane_order(chip, core)
        found = [(i, every, 0, (every, own[i], core)) for i in range(4)]
        return found + [(4 + i, every, 0, (every, other[i], 1 - core)) for i in range(4)]

    shape = (4, 4, 2) + mine[0].shape[1:]
    return copies(mine + others, [shape], moves)[0]


def gather_up(mine, others):
    def moves(layer, chip, core):
        own, other = plane_order(chip, core)
        found = []
        for i in range(8):
            spot, side = (own[i], core) if i < 4 else (other[i - 4], 1 - core)
            for out, lanes in enumerate((slice(0, 4 * D), slice(4 * D, 5 * D))):
                found.append((i, (every, every, lanes), out, (every, spot, side)))
        return found

    up, out = copies(mine + others, [(4, 4, 2, 24, 4 * D), (4, 4, 2, 24, D)], moves)
    return up.reshape(D, 4 * D), out.reshape(D, D)


def gather_down(mine, others):
    def moves(layer, chip, core):
        own, other = plane_order(chip, core)
        found = []
        for i in range(8):
            spot, side = (own[i], core) if i < 4 else (other[i - 4], 1 - core)
            for quarter in range(4):
                part = (every, every, slice(quarter * D, (quarter + 1) * D))
                found.append((i, part, 0, (every, spot, side, quarter)))
        return found

    return copies(mine + others, [(4, 4, 2, 4, 24, D)], moves)[0]


class Sum:
    def __init__(self, kept):
        self.kept = kept
        self.shape = kept.shape[2:]

    def run(self, operands, out_shapes, plan):
        shape, count, made = self.shape, len(operands), len(out_shapes)
        dry = plan(0, 0, 0)
        pieces = sum(len(sources) for sources, target in dry)

        def kernel(*refs):
            given, outs = refs[:count], refs[count : count + made]
            held, built, sems = refs[count + made : -len(dry) - 1], refs[-len(dry) - 1 : -1], refs[-1]
            inward, outward, steps = [], [], []
            for sources, target in plan(*place_in()):
                step = []
                for operand, index in sources:
                    spot = len(inward)
                    source = given[operand].at[index]
                    copy = pltpu.make_async_copy(source, held[spot], sems.at[0, spot])
                    copy.start()
                    inward.append(copy)
                    step.append(spot)
                steps.append((step, target))
            for place, (step, (out, index)) in enumerate(steps):
                total = None
                for spot in step:
                    inward[spot].wait()
                    value = wide(held[spot][...])
                    total = value if total is None else total + value
                built[place][...] = total.astype(built[place].dtype)
                target = outs[out] if index is None else outs[out].at[index]
                copy = pltpu.make_async_copy(built[place], target, sems.at[1, place])
                copy.start()
                outward.append(copy)
            for copy in outward:
                copy.wait()

        far = pl.BlockSpec(memory_space=pltpu.HBM)
        return pl.pallas_call(
            kernel,
            out_shape=out_shapes,
            in_specs=[far] * count,
            out_specs=[far] * made,
            scratch_shapes=[pltpu.VMEM(shape, jnp.bfloat16)] * pieces
            + [pltpu.VMEM(shape, out_shapes[target[0]].dtype) for sources, target in dry]
            + [pltpu.SemaphoreType.DMA((2, pieces))],
            compiler_params=pltpu.CompilerParams(vmem_limit_bytes=64 * 2**20),
            cost_estimate=pl.CostEstimate(flops=0, bytes_accessed=0, transcendentals=0),
        )(*operands)

    def first(self, got):
        self.got = got

        def plan(layer, chip, core):
            return [
                ([(0, (z, spot)), (1, (z, spot))], (0, (i, z)))
                for i, spot in enumerate((chip ^ (1 + core), chip ^ 3))
                for z in range(4)
            ]

        return self.run([self.kept, got], [half(2, 4, *self.shape)], plan)[0]

    def second(self, back):
        self.back = back

        def plan(layer, chip, core):
            spot = chip ^ (2 - core)
            return [
                ([(0, (z, spot)), (1, (z, spot)), (2, (1, z))], (0, z)) for z in range(4)
            ]

        return self.run([self.kept, self.got, back], [half(4, *self.shape)], plan)[0]

    def third(self, last):
        def plan(layer, chip, core):
            found = []
            for shift in (1, 2, 3, 0):
                z = lax.rem(layer + shift, 4)
                sources = [(0, (z, chip)), (1, (z, chip)), (2, (0, z)), (3, z)]
                found.append((sources, (shift, None)))
            return found

        self.own, *others = self.run(
            [self.kept, self.got, self.back, last],
            [shape_of(*self.shape)] + [half(*self.shape)] * 3,
            plan,
        )
        return others

    def total(self, others):
        return self.own + wide(others[0]) + wide(others[1]) + wide(others[2])


def send_dp(others):
    return [swap_dp(other, shift) for shift, other in zip((1, 2, 3), others)]


def norm_parts(values):
    centered = values - jnp.mean(values, axis=-1, keepdims=True)
    variance = jnp.mean(centered * centered, axis=-1, keepdims=True)
    scale = lax.rsqrt(variance + epsilon)
    return centered * scale, scale


def norm_back(grad, normed, scale, gain):
    scaled = grad * gain
    return scale * (
        scaled
        - jnp.mean(scaled, axis=-1, keepdims=True)
        - normed * jnp.mean(scaled * normed, axis=-1, keepdims=True)
    )


def gelu_slope(hidden):
    return 0.5 * (1.0 + lax.erf(hidden * math.sqrt(0.5))) + hidden * jnp.exp(
        -0.5 * hidden * hidden
    ) * (1.0 / math.sqrt(2.0 * math.pi))


def shape_of(*shape, dtype=jnp.float32):
    return jax.ShapeDtypeStruct(shape, dtype)


def half(*shape):
    return jax.ShapeDtypeStruct(shape, jnp.bfloat16)


def on_core(kernel, out_shape, operands, flops, room=64, grid=(), in_specs=None, out_specs=None, scratch=()):
    arrays = jax.tree.leaves(out_shape) + list(operands)
    size = sum(math.prod(a.shape) * a.dtype.itemsize for a in arrays)
    extra = {} if in_specs is None else {"in_specs": in_specs, "out_specs": out_specs}
    return pl.pallas_call(
        kernel,
        out_shape=out_shape,
        grid=grid,
        scratch_shapes=scratch,
        compiler_params=pltpu.CompilerParams(vmem_limit_bytes=room * 2**20),
        cost_estimate=pl.CostEstimate(flops=0, bytes_accessed=0, transcendentals=0),
        **extra,
    )(*operands)


def column_sum(array_in):
    return jnp.sum(array_in, axis=0, keepdims=True)


def prepare(*refs):
    given, made, held, built = refs[0:12], refs[12:19], refs[19:31], refs[31:38]
    small, turned, parts, sems = refs[38:]
    inward = [pltpu.make_async_copy(given[i], held[i], sems.at[0, i]) for i in range(12)]
    outward = [pltpu.make_async_copy(built[i], made[i], sems.at[1, i]) for i in range(7)]
    for copy in inward:
        copy.start()
    for copy in inward:
        copy.wait()
    mix_ref, out_ref, up_ref, down_ref, vectors_ref, bias_ref = held[0:6]
    cross_mix_ref, cross_out_ref, cross_up_ref, cross_vectors_ref, cross_bias_ref, table_ref = held[6:]
    one_ref, two_ref, three_ref = built[0:3]
    one_ref[:, 0 : 3 * D] = mix_ref[...]
    one_ref[:, 3 * D : 4 * D] = out_ref[...]
    small[...] = jnp.zeros_like(small)
    small[0:8, 0:24] = wide(vectors_ref[...])
    small[8:16, 0:24] = wide(cross_vectors_ref[...])
    for row in range(4):
        lanes = slice(24 * row, 24 * (row + 1))
        small[80 + row : 81 + row, 0:24] = wide(bias_ref[:, lanes])
        small[84 + row : 85 + row, 0:24] = wide(cross_bias_ref[:, lanes])
    turned[...] = small[...].T
    turned[0:24, 16:80] = wide(table_ref[...])
    one_ref[:, 4 * D : 4 * D + 128] = low(turned[0:24, :])
    outward[0].start()
    two_ref[:, 0 : 4 * D] = up_ref[...]
    two_ref[:, 4 * D : 5 * D] = cross_out_ref[...]
    for quarter in range(4):
        three_ref[:, quarter * D : (quarter + 1) * D] = down_ref[quarter]
    outward[1].start()
    outward[2].start()
    parts[...] = jnp.zeros_like(parts)
    for spot in range(4):
        for level in range(4):
            taken = cross_up_ref[:, 192 * (4 * level + spot) : 192 * (4 * level + spot + 1)]
            parts[spot, :, 192 * level : 192 * (level + 1)] = taken
        for third in range(3):
            taken = cross_mix_ref[:, third * D + 192 * spot : third * D + 192 * (spot + 1)]
            parts[spot, :, D + 192 * third : D + 192 * (third + 1)] = taken
    chip = place_in()[1]
    for mask in range(4):
        built[3 + mask][...] = parts[chip ^ mask]
        outward[3 + mask].start()
    for copy in outward:
        copy.wait()


def join_cross(pieces, cross_down):
    def moves(layer, chip, core):
        found = []
        for mask in range(4):
            found.append((mask, (every, slice(0, D)), 0, (chip ^ mask, every, slice(0, D))))
            taken = (every, slice(D, D + 640))
            found.append((mask, taken, 0, (chip ^ mask, every, slice(2 * D, 2 * D + 640))))
        found.append((4, every, 0, (every, every, slice(D, 2 * D))))
        return found

    return copies(pieces + [cross_down.reshape(4, 24, D)], [(4, 24, 2 * D + 640)], moves)[0]


def place_cross(column, other):
    def moves(layer, chip, core):
        found = []
        for piece, side in ((0, core), (1, 1 - core)):
            source, lead = (every, every, every), (every, every, side)
            found.append((piece, source + (slice(0, D),), 0, lead))
            found.append((piece, source + (slice(2 * D, 2 * D + 640),), 1, lead))
            found.append((piece, source + (slice(D, 2 * D),), 2, (every, side)))
        return found

    up, mix, down = copies(
        [column, other], [(4, 4, 2, 24, D), (4, 4, 2, 24, 640), (4, 2, 4, 24, D)], moves
    )
    return up.reshape(D, D), mix.reshape(D, 640), down.reshape(D, D)


def segment_heads(segment, mixed_ref, docs_ref, probs_ref, context_ref):
    lane = lax.broadcasted_iota(jnp.int32, (SEG, 128), 1)
    rows = slice(segment * SEG, (segment + 1) * SEG)
    docs = jnp.broadcast_to(wide(docs_ref[segment : segment + 1, :]), (SEG, SEG))
    allowed = docs == docs.T
    for pair in range(HEADS // 2):
        query, key, value = (
            mixed_ref[rows, third * D + pair * 128 : third * D + (pair + 1) * 128]
            for third in range(3)
        )
        found = []
        for side in range(2):
            here = (lane < HEAD_DIM) if side == 0 else (lane >= HEAD_DIM)
            scores = contract(key, jnp.where(here, query, jnp.zeros_like(query)), 1, 1)
            scores = jnp.where(allowed, scores * HEAD_DIM ** (-0.5), masked_score)
            powers = jnp.exp(scores - jnp.max(scores, axis=0, keepdims=True))
            probs = powers / jnp.sum(powers, axis=0, keepdims=True)
            probs_ref[2 * pair + side] = probs
            found.append(contract(low(probs), value, 0, 0))
        context = jnp.where(lane < HEAD_DIM, found[0], found[1])
        context_ref[:, pair * 128 : (pair + 1) * 128] = low(context)


def local_attend(tokens_ref, group_ref, docs_ref, places_ref, *outs):
    mixed_ref, context_ref, probs_ref, rows_ref, places_out = outs
    rows_ref[...] = wide(group_ref[:, 4 * D : 4 * D + 128]).T
    lane = lax.broadcasted_iota(jnp.int32, (1, 64), 1)
    for place in range(2):
        picked = wide(places_ref[:, place : place + 1] == lane)
        places_out[place : place + 1, :] = contract_exact(picked, rows_ref[16:80, :], 1, 0)
    tokens = tokens_ref[...]
    for third in range(3):
        columns = slice(third * D, (third + 1) * D)
        mixed = contract(tokens, group_ref[:, columns], 1, 0)
        if third != 1:
            mixed = mixed + rows_ref[third // 2 : third // 2 + 1, :]
        mixed_ref[:, columns] = low(mixed)
    segment_heads(0, mixed_ref, docs_ref, probs_ref, context_ref)


def local_attend_more(
    tokens_ref, mixed_ref, before_ref, weight_ref, rows_ref, docs_ref, *outs
):
    context_ref, probs_ref, n_ref, scale_ref, low_ref, here = outs
    segment_heads(1, mixed_ref, docs_ref, probs_ref, here)
    context_ref[0:SEG, :] = before_ref[...]
    context_ref[SEG : 2 * SEG, :] = here[...]
    total = wide(tokens_ref[...]) + contract(context_ref[...], weight_ref[...], 1, 0)
    normed, scale = norm_parts(total + rows_ref[2:3, :])
    n_ref[...] = normed
    scale_ref[...] = scale
    low_ref[...] = low(normed * rows_ref[3:4, :] + rows_ref[4:5, :])


def local_up_part(low_ref, weight_ref, bias_ref, active_ref, slope_ref):
    hidden = contract(low_ref[...], weight_ref[...], 1, 0) + wide(bias_ref[...])
    chance = 0.5 * (1.0 + lax.erf(hidden * math.sqrt(0.5)))
    density = jnp.exp(-0.5 * hidden * hidden) * (1.0 / math.sqrt(2.0 * math.pi))
    active_ref[...] = low(hidden * chance)
    slope_ref[...] = low(chance + hidden * density)


def local_down_part(
    active_ref, weight_ref, first_ref, rows_ref, cot_a, cot_b, places_ref, *outs
):
    n_ref, scale_ref, kept_ref, given_ref, total = outs
    step = pl.program_id(0)
    part = contract(active_ref[...], weight_ref[...], 1, 0)

    @pl.when(step == 0)
    def _():
        first_norm = first_ref[...] * rows_ref[3:4, :] + rows_ref[4:5, :]
        total[...] = first_norm + rows_ref[5:6, :] + part

    @pl.when(step > 0)
    def _():
        total[...] += part

    @pl.when(step == 1)
    def _():
        normed, scale = norm_parts(total[...])
        n_ref[...] = normed
        scale_ref[...] = scale
        core = place_in()[2]
        heads, grads = [], []
        for place, cot in ((0, cot_a), (1, cot_b)):
            row = normed[place * SEG : place * SEG + 1] * rows_ref[6:7, :] + rows_ref[7:8, :]
            heads.append(row + places_ref[place : place + 1, :])
            grads.append(wide(cot[...])[0:1])
        for ref, mine in ((kept_ref, core == 0), (given_ref, core == 1)):
            ref[...] = jnp.zeros_like(ref)
            ref[0:1, :] = jnp.where(mine, heads[0], heads[1])
            ref[1:2, :] = jnp.where(mine, grads[0], grads[1])


def join_pair(kept_ref, got_ref, out_ref):
    core = place_in()[2]
    out_ref[...] = jnp.zeros_like(out_ref)
    out_ref[0:2, :] = jnp.where(core == 0, kept_ref[0:2, :], got_ref[0:2, :])
    out_ref[2:4, :] = jnp.where(core == 0, got_ref[0:2, :], kept_ref[0:2, :])


def cross_attend(
    own_ref, a_ref, b_ref, c_ref, weight_ref, rows_ref, docs_ref, *outs
):
    in_ref, grad_ref, mixed_ref, probs_ref, context_ref = outs
    layer, chip, core = place_in()
    for mask, ref in enumerate((own_ref, a_ref, b_ref, c_ref)):
        for side in range(2):
            row = 2 * (chip ^ mask) + side
            in_ref[pl.ds(row, 1), :] = ref[2 * side : 2 * side + 1, :]
            grad_ref[pl.ds(row, 1), :] = ref[2 * side + 1 : 2 * side + 2, :]
    biases = []
    for vector in (8, 9):
        row = rows_ref[vector : vector + 1, :]
        found = row[:, 0:192]
        for spot in range(1, 4):
            found = jnp.where(chip == spot, row[:, 192 * spot : 192 * (spot + 1)], found)
        biases.append(found)
    bias = jnp.concatenate([biases[0], jnp.zeros_like(biases[0]), biases[1]], axis=1)
    mixed = low(contract(low(in_ref[...]), weight_ref[:, 0:576], 1, 0) + bias)
    mixed_ref[...] = mixed
    row_docs = wide(jnp.where(core == 0, docs_ref[0:1, :], docs_ref[1:2, :]))
    count = row_docs.shape[1]
    lane = lax.broadcasted_iota(jnp.int32, (count, count), 1)
    line = lax.broadcasted_iota(jnp.int32, (count, count), 0)
    column_docs = jnp.sum(jnp.where(lane == line, row_docs, 0.0), axis=1, keepdims=True)
    allowed = row_docs == column_docs
    found = []
    for head in range(3):
        query, key, value = (
            mixed[:, third * 192 + head * HEAD_DIM : third * 192 + (head + 1) * HEAD_DIM]
            for third in range(3)
        )
        scores = contract(query, key, 1, 1) * HEAD_DIM ** (-0.5)
        scores = jnp.where(allowed, scores, masked_score)
        powers = jnp.exp(scores - jnp.max(scores, axis=-1, keepdims=True))
        probs = powers / jnp.sum(powers, axis=-1, keepdims=True)
        probs_ref[head] = probs
        found.append(contract(low(probs), value, 1, 0))
    context_ref[...] = low(jnp.concatenate(found, axis=1))


def cross_up_down(
    own_ref, a_ref, b_ref, c_ref, in_ref, out_weight_ref, rows_ref, up_ref, bias_ref, down_ref, *outs
):
    n_ref, scale_ref, low_ref, hidden_ref, active_ref, part_ref = outs
    chip = place_in()[1]
    total = in_ref[...] + rows_ref[10:11, :]
    for mask, ref in enumerate((own_ref, a_ref, b_ref, c_ref)):
        start = pl.multiple_of(192 * (chip ^ mask), 64)
        total = total + contract(ref[...], out_weight_ref[pl.ds(start, 192), :], 1, 0)
    normed, scale = norm_parts(total)
    n_ref[...] = normed
    scale_ref[...] = scale
    first = low(normed * rows_ref[11:12, :] + rows_ref[12:13, :])
    low_ref[...] = first
    hidden = contract(first, up_ref[...], 1, 0) + bias_ref[...]
    hidden_ref[...] = hidden
    active = low(hidden * (0.5 * (1.0 + lax.erf(hidden * math.sqrt(0.5)))))
    active_ref[...] = active
    part_ref[...] = contract(active, down_ref[...], 1, 0)


def cross_turn(
    own_ref, a_ref, b_ref, c_ref, n_ref, rows_ref, grad_ref, hidden_ref, up_ref, down_ref, *outs
):
    out_ref, second_ref, hidden_low_ref, part_ref, sums_ref = outs
    first = n_ref[...] * rows_ref[11:12, :] + rows_ref[12:13, :]
    total = (own_ref[...] + a_ref[...]) + (b_ref[...] + c_ref[...])
    normed, scale = norm_parts(first + total + rows_ref[13:14, :])
    out_ref[...] = normed * rows_ref[14:15, :] + rows_ref[15:16, :]
    grad = grad_ref[...]
    second = norm_back(grad, normed, scale, rows_ref[14:15, :])
    second_ref[...] = second
    hidden_low = low(contract(low(second), down_ref[...], 1, 1) * gelu_slope(hidden_ref[...]))
    hidden_low_ref[...] = hidden_low
    part_ref[...] = contract(hidden_low, up_ref[...], 1, 1)
    sums_ref[...] = jnp.zeros_like(sums_ref)
    sums_ref[0:1, :] = column_sum(grad * normed)
    sums_ref[1:2, :] = column_sum(grad)


def cross_attend_back(
    own_ref,
    a_ref,
    b_ref,
    c_ref,
    second_ref,
    n_ref,
    scale_ref,
    rows_ref,
    out_weight_ref,
    mixed_ref,
    probs_ref,
    weight_ref,
    hidden_low_ref,
    active_ref,
    context_ref,
    in_ref,
    low_ref,
    sums_ref,
    places_ref,
    total_ref,
    part_ref,
    pack_ref,
    pack,
    rows,
):
    chip = place_in()[1]
    grad = second_ref[...] + (own_ref[...] + a_ref[...]) + (b_ref[...] + c_ref[...])
    normed = n_ref[...]
    total = norm_back(grad, normed, scale_ref[...], rows_ref[11:12, :])
    total_ref[...] = total
    branch = low(total)
    start = pl.multiple_of(192 * chip, 64)
    context_low = low(contract(branch, out_weight_ref[pl.ds(start, 192), :], 1, 1))
    mixed = mixed_ref[...]
    found = [[], [], []]
    for head in range(3):
        query, key, value = (
            mixed[:, third * 192 + head * HEAD_DIM : third * 192 + (head + 1) * HEAD_DIM]
            for third in range(3)
        )
        part = context_low[:, head * HEAD_DIM : (head + 1) * HEAD_DIM]
        probs = probs_ref[head]
        prob_grad = contract(part, value, 1, 1)
        score = low(probs * (prob_grad - jnp.sum(probs * prob_grad, axis=-1, keepdims=True)))
        found[0].append(contract(score, key, 1, 0) * HEAD_DIM ** (-0.5))
        found[1].append(contract(score, query, 0, 0) * HEAD_DIM ** (-0.5))
        found[2].append(contract(low(probs), part, 0, 0))
    mixed_low = low(jnp.concatenate(found[0] + found[1] + found[2], axis=1))
    part_ref[...] = contract(mixed_low, weight_ref[:, 0:576], 1, 1)
    pack[...] = jnp.zeros_like(pack)
    pack[0:8, :] = wide(hidden_low_ref[...])
    pack[8:16, :] = wide(active_ref[...])
    pack[16:24, 0:576] = wide(mixed_low)
    pack[16:24, 576:768] = wide(context_ref[...])
    for i, value in enumerate(
        (in_ref[...], wide(low_ref[...]), total, second_ref[...], total)
    ):
        rows[...] = value
        for side in range(2):
            row = 24 + 2 * i + side
            pack[row : row + 1, :] = rows[pl.ds(2 * chip + side, 1), :]
    rows[0:1, :] = column_sum(grad * normed)
    rows[1:2, :] = column_sum(grad)
    rows[2:4, :] = sums_ref[0:2, :]
    pack[34:35, :] = rows[pl.ds(chip, 1), :]
    for place in range(2):
        spot = wide(places_ref[:, place : place + 1])
        pack[35 + place : 36 + place, :] = jnp.broadcast_to(spot, (1, D))
    pack_ref[...] = low(pack[...])


def cross_finish(own_ref, a_ref, b_ref, c_ref, total_ref, out_ref, kept_ref, given_ref, rows):
    layer, chip, core = place_in()
    rows[...] = total_ref[...] + (own_ref[...] + a_ref[...]) + (b_ref[...] + c_ref[...])
    for ref, side in ((kept_ref, core), (given_ref, 1 - core)):
        ref[...] = jnp.zeros_like(ref)
        ref[0:1, :] = rows[pl.ds(2 * chip + side, 1), :]
        ref[1:2, :] = out_ref[pl.ds(2 * chip + side, 1), :]


def cross_owner(mine_ref, other_ref, weight_ref, *refs):
    mix_ref, out_ref, up_ref, down_ref, vectors_ref, bias_ref, table_ref = refs[:7]
    hidden, mixed, single, active, sums, places = refs[7:]
    layer, chip, core = place_in()
    rank = 8 * layer + 2 * chip + core
    sums[...] = jnp.zeros_like(sums)
    for level in range(4):
        for side in range(2):
            group = 2 * level + side
            rows = slice(8 * group, 8 * group + 8)
            for spot in range(4):
                value = wide(
                    jnp.where(core == side, mine_ref[level, spot], other_ref[level, spot])
                )
                hidden[spot, rows, :] = value[0:8]
                mixed[spot, rows, :] = value[16:24]
                for i in range(5):
                    start = 8 * group + 2 * spot
                    single[i, start : start + 2, :] = value[24 + 2 * i : 26 + 2 * i]
                sums[spot : spot + 1, :] += value[34:35]
                for sequence in range(2):
                    row = 16 * level + 8 * sequence + 2 * spot + side
                    places[row : row + 1, :] = value[35 + sequence : 36 + sequence, 0:128]
            value = jnp.where(core == side, mine_ref[level, chip], other_ref[level, chip])
            active[rows, :] = wide(value)[8:16]

    def select(count, first):
        lane = lax.broadcasted_iota(jnp.int32, (count, D), 1)
        row = lax.broadcasted_iota(jnp.int32, (count, D), 0)
        return wide(lane == first + row)

    own = select(24, 24 * rank)
    offset = 24 * (2 * chip + core)
    units = select(96, 192 * layer + 96 * core)
    own_low = low(own)

    def columns_of(array_in):
        return low(contract(own_low, low(array_in), 1, 1))

    inputs = columns_of(single[0])
    for spot in range(4):
        part = contract(inputs, low(mixed[spot][:, 0:576]), 1, 0)
        for third in range(3):
            start = third * D + 192 * spot
            mix_ref[:, start : start + 192] = part[:, 192 * third : 192 * (third + 1)]
    own_mixed = mixed[layer]
    context = low(contract(low(select(24, 576 + offset)), low(own_mixed), 1, 1))
    out_ref[...] = contract(context, low(single[2]), 1, 0)
    first = columns_of(single[1])
    for spot in range(4):
        part = contract(first, low(hidden[spot]), 1, 0)
        for level in range(4):
            start = 192 * (4 * level + spot)
            up_ref[:, start : start + 192] = part[:, 192 * level : 192 * (level + 1)]
    units_low = low(contract(low(units), low(active[...]), 1, 1))
    down_ref[...] = contract(units_low, low(single[3]), 1, 0)
    mixed_sum = column_sum(own_mixed)
    vectors_ref[0:1, :] = contract_exact(mixed_sum, select(24, offset), 1, 1)
    vectors_ref[1:2, :] = contract_exact(mixed_sum, select(24, 384 + offset), 1, 1)
    for row, value in (
        (2, column_sum(single[2])),
        (3, sums[0:1, :]),
        (4, sums[1:2, :]),
        (5, column_sum(single[3])),
        (6, sums[2:3, :]),
        (7, sums[3:4, :]),
    ):
        vectors_ref[row : row + 1, :] = contract_exact(value, own, 1, 1)
    bias_ref[...] = contract_exact(column_sum(hidden[chip]), units, 1, 1)
    grads = contract(low(single[4]), own_low, 1, 1)
    for spot in range(4):
        for third in range(3):
            start = third * D + 192 * spot
            part = low(mixed[spot][:, 192 * third : 192 * (third + 1)])
            grads = grads + contract(part, weight_ref[:, start : start + 192], 1, 1)
    lane = wide(lax.broadcasted_iota(jnp.int32, (64, 64), 1))
    table_ref[...] = contract_exact(wide(places[:, 0:64] == lane), grads, 0, 0)


def split_cores(value, kept_ref, gone_ref):
    rows = kept_ref.shape[1]
    core = lax.rem(lax.axis_index("seq"), 2)
    parts = value.reshape(-1, 2, rows, value.shape[1])
    kept_ref[...] = low(jnp.where(core == 0, parts[:, 0], parts[:, 1]))
    gone_ref[...] = low(jnp.where(core == 0, parts[:, 1], parts[:, 0]))


def local_down_back(
    cot_ref, mine_ref, other_ref, n_ref, scale_ref, rows_ref, active_ref, slope_ref, weight_ref, *outs
):
    out_ref, second_ref, kept_ref, gone_ref, hidden_ref, sums_ref, bias_ref, second_low_ref = outs
    step = pl.program_id(0)

    @pl.when(step == 0)
    def _():
        core = place_in()[2]
        row = lax.broadcasted_iota(jnp.int32, (2 * SEG, D), 0)
        grad = wide(cot_ref[...])
        normed = n_ref[...]
        out = normed * rows_ref[6:7, :] + rows_ref[7:8, :]
        for place in range(2):
            heads = jnp.where(core == place, mine_ref[...], other_ref[...])
            grad = jnp.where(row == place * SEG, heads[0:1], grad)
            out = jnp.where(row == place * SEG, heads[1:2], out)
        out_ref[...] = low(out)
        second = norm_back(grad, normed, scale_ref[...], rows_ref[6:7, :])
        second_ref[...] = second
        second_low_ref[...] = low(second)
        sums_ref[0:1, :] = column_sum(wide(low(second)))
        sums_ref[1:2, :] = column_sum(grad * normed)
        sums_ref[2:3, :] = column_sum(grad)

    second_low = second_low_ref[...]
    split_cores(contract(active_ref[...], second_low, 0, 0), kept_ref, gone_ref)
    hidden = low(contract(second_low, weight_ref[...], 1, 1) * wide(slope_ref[...]))
    hidden_ref[...] = hidden
    bias_ref[...] = column_sum(wide(hidden))


def local_up_back(low_ref, hidden_ref, weight_ref, second_ref, kept_ref, gone_ref, first_ref):
    hidden = hidden_ref[...]
    split_cores(contract(low_ref[...], hidden, 0, 0), kept_ref, gone_ref)
    part = contract(hidden, weight_ref[...], 1, 1)
    step = pl.program_id(0)

    @pl.when(step == 0)
    def _():
        first_ref[...] = second_ref[...] + part

    @pl.when(step > 0)
    def _():
        first_ref[...] += part


def local_attend_back(
    first_ref, n_ref, scale_ref, rows_ref, context_ref, mixed_ref, probs_a, probs_b, group_ref, *outs
):
    out_ref, total_ref, sums_ref, back_ref, context_low_ref = outs
    grad, normed = first_ref[...], n_ref[...]
    total = norm_back(grad, normed, scale_ref[...], rows_ref[3:4, :])
    total_ref[...] = total
    branch = low(total)
    sums_ref[2:3, :] = column_sum(wide(branch))
    sums_ref[3:4, :] = column_sum(grad * normed)
    sums_ref[4:5, :] = column_sum(grad)
    out_ref[...] = low(contract(context_ref[...], branch, 0, 0))
    context_low_ref[...] = low(contract(branch, group_ref[...], 1, 1))
    lane = lax.broadcasted_iota(jnp.int32, (SEG, 128), 1)
    for segment in range(2):
        rows = slice(segment * SEG, (segment + 1) * SEG)
        for pair in range(HEADS // 2):
            places = [
                slice(third * D + pair * 128, third * D + (pair + 1) * 128) for third in range(3)
            ]
            query, key, value = (mixed_ref[rows, place] for place in places)
            grad = context_low_ref[rows, places[0]]
            found = []
            for side in range(2):
                here = (lane < HEAD_DIM) if side == 0 else (lane >= HEAD_DIM)
                probs = (probs_a, probs_b)[segment][2 * pair + side]
                prob_grad = contract(value, jnp.where(here, grad, jnp.zeros_like(grad)), 1, 1)
                value_grad = contract(low(probs), grad, 1, 0)
                score = low(
                    probs * (prob_grad - jnp.sum(probs * prob_grad, axis=0, keepdims=True))
                )
                found.append(
                    (contract(score, key, 0, 0), contract(score, query, 1, 0), value_grad)
                )
            for third in range(3):
                merged = jnp.where(lane < HEAD_DIM, found[0][third], found[1][third])
                if third < 2:
                    merged = merged * HEAD_DIM ** (-0.5)
                back_ref[rows, places[third]] = low(merged)
    for third in (0, 2):
        columns = slice(third * D, (third + 1) * D)
        sums_ref[third // 2 : third // 2 + 1, :] = column_sum(wide(back_ref[:, columns]))


def local_mix_back(
    total_ref, back_ref, tokens_ref, group_ref, out_ref, sums_ref, more_ref, bias_ref, *outs
):
    input_ref, kept_ref, gone_ref, small_ref = outs
    tokens, total = tokens_ref[...], total_ref[...]
    for third in range(3):
        columns = slice(third * D, (third + 1) * D)
        back = back_ref[:, columns]
        grad = contract(tokens, back, 0, 0)
        split_cores(grad, kept_ref.at[:, :, columns], gone_ref.at[:, :, columns])
        total = total + contract(back, group_ref[:, columns], 1, 1)
    input_ref[...] = total
    columns = slice(3 * D, 4 * D)
    split_cores(wide(out_ref[...]), kept_ref.at[:, :, columns], gone_ref.at[:, :, columns])
    small_ref[...] = jnp.zeros_like(small_ref)
    small_ref[0:5, :] = sums_ref[0:5, :]
    small_ref[5:8, :] = more_ref[0:3, :]
    for owner in range(32):
        for row in range(4):
            taken = bias_ref[:, 96 * owner + 24 * row : 96 * owner + 24 * (row + 1)]
            small_ref[8 + row : 9 + row, 24 * owner : 24 * (owner + 1)] = taken
    columns = slice(4 * D, 4 * D + 128)
    split_cores(small_ref[...].T, kept_ref.at[:, :, columns], gone_ref.at[:, :, columns])


def finish_mix(own_ref, a_ref, b_ref, c_ref, mix_ref, out_ref, vectors_ref, bias_ref, wide_ref):
    total = own_ref[...] + wide(a_ref[...]) + wide(b_ref[...]) + wide(c_ref[...])
    mix_ref[...] = total[:, 0 : 3 * D]
    out_ref[...] = total[:, 3 * D : 4 * D]
    wide_ref[...] = jnp.zeros_like(wide_ref)
    wide_ref[0:24, :] = total[:, 4 * D : 4 * D + 128]
    turned = wide_ref[...].T
    vectors_ref[...] = turned[0:8, 0:24]
    for row in range(4):
        bias_ref[:, 24 * row : 24 * (row + 1)] = turned[8 + row : 9 + row, 0:24]


def plane_three(array_in):
    return [array_in] + [swap_chip(array_in, mask) for mask in (1, 2, 3)]


def plane_shards(
    tokens,
    cotangent,
    token_docs,
    segment_docs,
    segment_positions,
    local_mix,
    local_out,
    local_up,
    local_down,
    local_vectors,
    local_up_bias,
    cross_mix,
    cross_out,
    cross_up,
    cross_down,
    cross_vectors,
    cross_up_bias,
    position_table,
):
    chip = place_in()[1]
    flat_tokens = tokens.reshape(256, D)
    flat_cot = cotangent.reshape(256, D)
    places_in = segment_positions.T

    shards_in = (
        local_mix,
        local_out,
        local_up,
        local_down.reshape(4, 24, D),
        local_vectors,
        local_up_bias.reshape(1, 96),
        cross_mix,
        cross_out,
        cross_up,
        cross_vectors,
        cross_up_bias.reshape(1, 96),
        position_table.T,
    )
    made = [half(24, 3200), half(24, 5 * D), half(24, 4 * D)] + [half(24, D + 640)] * 4
    far = pl.BlockSpec(memory_space=pltpu.HBM)
    shard_one, shard_two, shard_three, *cross_pieces = on_core(
        prepare,
        made,
        shards_in,
        0,
        in_specs=[far] * 12,
        out_specs=[far] * 7,
        scratch=[pltpu.VMEM(a.shape, a.dtype) for a in list(shards_in) + made]
        + [
            pltpu.VMEM((128, 128), jnp.float32),
            pltpu.VMEM((128, 128), jnp.float32),
            pltpu.VMEM((4, 24, D + 640), jnp.bfloat16),
            pltpu.SemaphoreType.DMA((2, 12)),
        ],
    )
    cross_sent = [cross_pieces[0]] + [swap_chip(cross_pieces[mask], mask) for mask in (1, 2, 3)]
    z_one = reach_dp(shard_one)
    shard_two, *z_one = stage(shard_two, *z_one, *cross_sent)
    z_one, cross_sent = z_one[:4], z_one[4:]
    column_one = join_dp(z_one)
    column_one, shard_two = stage(column_one, shard_two)

    first, second = swap_one(column_one), swap_two(column_one)
    cross_row = join_cross(cross_sent, after(cross_down, column_one))
    *z_two, first, second, column_one, cross_row = stage(
        *reach_dp(shard_two), first, second, column_one, cross_row
    )

    third = swap_two(first)
    others = [swap_core(piece) for piece in (column_one, first, second)]
    column_two = join_dp(z_two)
    cross_moved = [cross_row, swap_dp(cross_row, 1)]
    third, column_two, cross_moved[1], *others = stage(third, column_two, cross_moved[1], *others)
    others.append(swap_core(third))

    first_group = gather_plane([column_one, first, second, third], others).reshape(D, 3200)
    mixed_rows, context_first, probs_first, rows, place_rows = on_core(
        local_attend,
        [half(256, 3 * D), half(SEG, D), shape_of(12, SEG, SEG), shape_of(128, D), shape_of(2, D)],
        (flat_tokens, first_group, token_docs, places_in),
        0,
    )
    first_two, second_two = swap_one(column_two), swap_two(column_two)
    *z_three, mixed_rows, first_two, second_two, column_two, cross_moved[1] = stage(
        *reach_dp(shard_three), mixed_rows, first_two, second_two, column_two, cross_moved[1]
    )
    cross_moved.append(swap_dp(cross_moved[1], 1))

    third_two = swap_two(first_two)
    others = [swap_core(piece) for piece in (column_two, first_two, second_two)]
    column_three = join_dp(z_three)
    def plain(*shapes):
        return [pl.BlockSpec(shape, lambda j, n=len(shape): (0,) * n) for shape in shapes]

    context_rows, probs_second, normed_one, scale_one, low_one = on_core(
        local_attend_more,
        [half(256, D), shape_of(12, SEG, SEG), shape_of(256, D), shape_of(256, 1), half(256, D)],
        (flat_tokens, mixed_rows, context_first, first_group, rows, token_docs),
        0,
        grid=(1,),
        in_specs=plain((256, D), (256, 3 * D), (SEG, D))
        + [pl.BlockSpec((D, D), lambda j: (0, 3))]
        + plain((128, D), (2, SEG)),
        out_specs=plain((256, D), (12, SEG, SEG), (256, D), (256, 1), (256, D)),
        scratch=[pltpu.VMEM((SEG, D), jnp.bfloat16)],
    )
    up_bias = rows[80:84].reshape(4, 32, 24).transpose(1, 0, 2).reshape(1, 4 * D)
    cross_moved[2], third_two, column_three, low_one, up_bias, rows_later, *others = stage(
        cross_moved[2], third_two, column_three, low_one, up_bias, rows[84:88], *others
    )
    cross_moved.append(swap_dp(cross_moved[2], 1))

    first_three, second_three = swap_one(column_three), swap_two(column_three)
    others.append(swap_core(third_two))
    second_group, cross_out_weight = gather_up(
        [column_two, first_two, second_two, third_two], others
    )
    whole = pl.BlockSpec((256, D), lambda j: (0, 0))
    thin = pl.BlockSpec((256, 1), lambda j: (0, 0))
    vectors = pl.BlockSpec((128, D), lambda j: (0, 0))
    eight = pl.BlockSpec((8, D), lambda j: (0, 0))
    across = pl.BlockSpec((256, D), lambda j: (0, j))
    tall = pl.BlockSpec((D, D), lambda j: (0, j))
    deep = pl.BlockSpec((D, D), lambda j: (j, 0))
    strip = pl.BlockSpec((1, D), lambda j: (0, j))
    across_half = pl.BlockSpec((256, 2 * D), lambda j: (0, j))
    tall_half = pl.BlockSpec((D, 2 * D), lambda j: (0, j))
    deep_half = pl.BlockSpec((2 * D, D), lambda j: (j, 0))
    strip_half = pl.BlockSpec((1, 2 * D), lambda j: (0, j))
    active_rows, slope_rows = on_core(
        local_up_part,
        [half(256, 4 * D)] * 2,
        (low_one, second_group, up_bias),
        2 * 256 * D * 4 * D,
        grid=(4,),
        in_specs=[whole, tall, strip],
        out_specs=[across, across],
    )
    active_rows, first_three, second_three, column_three, cross_moved[3], rows_later = stage(
        active_rows, first_three, second_three, column_three, cross_moved[3], rows_later
    )

    third_three = swap_two(first_three)
    others = [swap_core(piece) for piece in (column_three, first_three, second_three)]
    cross_bias = rows_later.reshape(4, 4, 4, 2, 24)
    cross_bias = lax.dynamic_index_in_dim(cross_bias, chip, 2, keepdims=False)
    cross_bias = cross_bias.transpose(1, 2, 0, 3).reshape(1, D)
    cross_column = join_dp(cross_moved)

    others.append(swap_core(third_three))
    down_weight = gather_down([column_three, first_three, second_three, third_three], others)
    down_weight, cross_column = stage(down_weight.reshape(4 * D, D), cross_column)
    cross_other = swap_core(cross_column)
    normed_two, scale_two, kept, given = on_core(
        local_down_part,
        [shape_of(256, D), shape_of(256, 1), shape_of(8, D), shape_of(8, D)],
        (active_rows, down_weight, normed_one, rows, flat_cot, flat_cot, place_rows),
        2 * 256 * D * 4 * D,
        grid=(2,),
        in_specs=[
            across_half,
            deep_half,
            whole,
            vectors,
            pl.BlockSpec((16, D), lambda j: (0, 0)),
            pl.BlockSpec((16, D), lambda j: (8, 0)),
            pl.BlockSpec((2, D), lambda j: (0, 0)),
        ],
        out_specs=[whole, thin, eight, eight],
        scratch=[pltpu.VMEM((256, D), jnp.float32)],
    )

    row8, mix_share = (8, D), (D, 640)
    out_share = pl.BlockSpec((D, D), lambda j: (0, 0))
    up_share = pl.BlockSpec((D, D), lambda j: (0, 0))
    given, kept, cross_other = stage(given, kept, cross_other)
    got = swap_core(given)
    cross_up_part, cross_mix_part, cross_down_part = place_cross(cross_column, cross_other)
    kept, got, cross_mix_part = stage(kept, got, cross_mix_part)
    pair = on_core(join_pair, shape_of(8, D), (kept, got), 0, room=12)
    row_in, row_grad, mixed, probs, context = on_core(
        cross_attend,
        [shape_of(8, D), shape_of(8, D), half(8, 576), shape_of(3, 8, 8), half(8, 192)],
        (*plane_three(pair), cross_mix_part, rows, segment_docs),
        0,
        room=12,
    )
    row_n, row_scale, row_low, hidden, active, part = on_core(
        cross_up_down,
        [shape_of(8, D), shape_of(8, 1), half(8, D), shape_of(8, D), half(8, D), shape_of(8, D)],
        (
            *plane_three(context),
            row_in,
            cross_out_weight,
            rows,
            cross_up_part,
            cross_bias,
            cross_down_part,
        ),
        0,
        grid=(1,),
        in_specs=plain(*[(8, 192)] * 4, row8)
        + [out_share]
        + plain((128, D))
        + [up_share]
        + plain((1, D), (D, D)),
        out_specs=plain(row8, (8, 1), row8, row8, row8, row8),
        room=12,
    )
    row_out, row_second, hidden_low, part, sums = on_core(
        cross_turn,
        [shape_of(8, D), shape_of(8, D), half(8, D), shape_of(8, D), shape_of(8, D)],
        (*plane_three(part), row_n, rows, row_grad, hidden, cross_up_part, cross_down_part),
        0,
        grid=(1,),
        in_specs=plain(*[row8] * 4, row8, (128, D), row8, row8) + [up_share] + plain((D, D)),
        out_specs=plain(*[row8] * 5),
        room=12,
    )
    row_total, part, packed = on_core(
        cross_attend_back,
        [shape_of(8, D), shape_of(8, D), half(48, D)],
        (
            *plane_three(part),
            row_second,
            row_n,
            row_scale,
            rows,
            cross_out_weight,
            mixed,
            probs,
            cross_mix_part,
            hidden_low,
            active,
            context,
            row_in,
            row_low,
            sums,
            places_in,
        ),
        0,
        grid=(1,),
        in_specs=plain(*[row8] * 4, row8, row8, (8, 1), (128, D))
        + [out_share]
        + plain((8, 576), (3, 8, 8), mix_share, row8, row8, (8, 192), row8, row8, row8, (1, 2)),
        out_specs=plain(row8, row8, (48, D)),
        scratch=[pltpu.VMEM((48, D), jnp.float32), pltpu.VMEM((8, D), jnp.float32)],
        room=12,
    )
    kept, given = on_core(
        cross_finish,
        [shape_of(8, D), shape_of(8, D)],
        (*plane_three(part), row_total, row_out),
        0,
        scratch=[pltpu.VMEM((8, D), jnp.float32)],
        room=12,
    )
    got, kept, packed = stage(swap_core(given), kept, packed)
    pack_one, pack_two = swap_one(packed), swap_two(packed)

    twos = pl.BlockSpec((8, 96, D), lambda j: (j, 0, 0))
    layer_output, second_rows, down_kept, down_gone, hidden_grads, sums_two, bias_grad = on_core(
        local_down_back,
        [
            half(256, D),
            shape_of(256, D),
            half(16, 96, D),
            half(16, 96, D),
            half(256, 4 * D),
            shape_of(8, D),
            shape_of(1, 4 * D),
        ],
        (flat_cot, kept, got, normed_two, scale_two, rows, active_rows, slope_rows, down_weight),
        4 * 256 * D * 4 * D,
        grid=(2,),
        in_specs=[whole, eight, eight, whole, thin, vectors, across_half, across_half, deep_half],
        out_specs=[whole, whole, twos, twos, across_half, eight, strip_half],
        scratch=[pltpu.VMEM((256, D), jnp.bfloat16)],
    )
    down_total = Sum(down_kept.reshape(4, 4, 96, D))
    hidden_grads, down_gone, pack_one, pack_two = stage(
        hidden_grads, down_gone.reshape(4, 4, 96, D), pack_one, pack_two
    )
    pack_three = swap_two(pack_one)

    down_got = swap_core(down_gone)
    sixteens = pl.BlockSpec((16, 24, 2 * D), lambda j: (0, 0, j))
    up_kept, up_gone, first_rows = on_core(
        local_up_back,
        [half(16, 24, 4 * D), half(16, 24, 4 * D), shape_of(256, D)],
        (low_one, hidden_grads, second_group, second_rows),
        4 * 256 * D * 4 * D,
        grid=(2,),
        in_specs=[whole, across_half, tall_half, whole],
        out_specs=[sixteens, sixteens, whole],
    )
    up_total = Sum(up_kept.reshape(4, 4, 24, 4 * D))
    down_got, first_rows, up_gone, pack_three = stage(
        down_got, first_rows, up_gone.reshape(4, 4, 24, 4 * D), pack_three
    )
    plane_pack = join_chips([packed, pack_one, pack_two, pack_three])
    packs = [plane_pack, swap_dp(plane_pack, 1), swap_dp(plane_pack, 3)]

    up_got = swap_core(up_gone)
    down_sent = down_total.first(down_got)
    down_back = swap_one(down_sent)
    flat = pl.BlockSpec((256, 3 * D), lambda j: (0, 0))
    out_grad, sum_rows, sums_one, back_rows = on_core(
        local_attend_back,
        [half(D, D), shape_of(256, D), shape_of(8, D), half(256, 3 * D)],
        (
            first_rows,
            normed_one,
            scale_one,
            rows,
            context_rows,
            mixed_rows,
            probs_first,
            probs_second,
            first_group,
        ),
        4 * 256 * D * 2 * D,
        grid=(1,),
        in_specs=[
            whole,
            whole,
            thin,
            vectors,
            whole,
            flat,
            pl.BlockSpec((12, SEG, SEG), lambda j: (0, 0, 0)),
            pl.BlockSpec((12, SEG, SEG), lambda j: (0, 0, 0)),
            pl.BlockSpec((D, D), lambda j: (0, 3)),
        ],
        out_specs=[pl.BlockSpec((D, D), lambda j: (0, 0)), whole, eight, flat],
        scratch=[pltpu.VMEM((256, D), jnp.bfloat16)],
    )
    up_sent = up_total.first(up_got)
    down_back, back_rows, up_sent, *packs = stage(down_back, back_rows, up_sent, *packs)
    packs.insert(2, swap_dp(packs[0], 2))

    up_back = swap_one(up_sent)
    down_onward = down_total.second(down_back)
    sides = [half(16, 24, 4 * D + 128)] * 2
    input_grad, mix_kept, mix_gone = on_core(
        local_mix_back,
        [shape_of(256, D)] + sides,
        (
            sum_rows,
            back_rows,
            flat_tokens,
            first_group,
            out_grad,
            sums_one,
            sums_two,
            bias_grad,
        ),
        4 * 256 * D * 3 * D,
        scratch=[pltpu.VMEM((128, D), jnp.float32)],
    )
    mix_total = Sum(mix_kept.reshape(4, 4, 24, 3200))
    up_back, down_onward, mix_gone, packs[2] = stage(
        up_back, down_onward, mix_gone.reshape(4, 4, 24, 3200), packs[2]
    )

    mix_got, down_last = swap_core(mix_gone), swap_two(down_onward)
    up_onward = up_total.second(up_back)
    my_rows = join_dp(packs)

    up_last = swap_two(up_onward)
    mix_sent = mix_total.first(mix_got)
    down_others = down_total.third(down_last)
    up_last, mix_sent, my_rows, *down_others = stage(up_last, mix_sent, my_rows, *down_others)
    other_rows = swap_core(my_rows)

    mix_back, down_others = swap_one(mix_sent), send_dp(down_others)
    up_others = up_total.third(up_last)
    mix_back, other_rows, *others = stage(mix_back, other_rows, *down_others, *up_others)
    down_others, up_others = others[:3], others[3:]

    mix_last = swap_two(mix_total.second(mix_back))
    up_others = send_dp(up_others)
    down_sum = down_total.total(down_others)
    mix_last, down_sum, other_rows = stage(mix_last, down_sum, other_rows)

    mix_others = send_dp(mix_total.third(mix_last))
    up_sum = up_total.total(up_others)
    cross_grads = on_core(
        cross_owner,
        [
            shape_of(24, 3 * D),
            shape_of(24, D),
            shape_of(24, 4 * D),
            shape_of(96, D),
            shape_of(8, 24),
            shape_of(1, 96),
            shape_of(64, 24),
        ],
        (my_rows, other_rows, cross_mix),
        0,
        scratch=[
            pltpu.VMEM((4, 64, D), jnp.float32),
            pltpu.VMEM((4, 64, D), jnp.float32),
            pltpu.VMEM((5, 64, D), jnp.float32),
            pltpu.VMEM((64, D), jnp.float32),
            pltpu.VMEM((8, D), jnp.float32),
            pltpu.VMEM((64, 128), jnp.float32),
        ],
    )
    mix_sum, out_sum, vectors_sum, bias_sum = on_core(
        finish_mix,
        [shape_of(24, 3 * D), shape_of(24, D), shape_of(8, 24), shape_of(1, 96)],
        (mix_total.own, *mix_others),
        0,
        grid=(1,),
        in_specs=plain(*[(24, 4 * D + 128)] * 4),
        out_specs=plain((24, 3 * D), (24, D), (8, 24), (1, 96)),
        scratch=[pltpu.VMEM((128, 128), jnp.float32)],
    )
    return (
        layer_output.reshape(2, SEG, D),
        input_grad.reshape(2, SEG, D),
        mix_sum,
        out_sum,
        up_sum,
        down_sum,
        vectors_sum,
        bias_sum.reshape(96),
        *cross_grads[:5],
        cross_grads[5].reshape(96),
        cross_grads[6],
    )


def solution(mesh):
    flat = dict(mesh.shape) == {"dp": 4, "seq": 8}
    return jax.shard_map(
        plane_shards if flat else shards,
        mesh=mesh,
        in_specs=(
            P("dp", "seq", None),
            P("dp", "seq", None),
            P("dp", "seq"),
            P("dp", None),
            P("dp", "seq"),
            P(("dp", "seq"), None),
            P(("dp", "seq"), None),
            P(("dp", "seq"), None),
            P(("dp", "seq"), None),
            P(None, ("dp", "seq")),
            P(("dp", "seq")),
            P(("dp", "seq"), None),
            P(("dp", "seq"), None),
            P(("dp", "seq"), None),
            P(("dp", "seq"), None),
            P(None, ("dp", "seq")),
            P(("dp", "seq")),
            P(None, ("dp", "seq")),
        ),
        out_specs=(
            P("dp", "seq", None),
            P("dp", "seq", None),
            P(("dp", "seq"), None),
            P(("dp", "seq"), None),
            P(("dp", "seq"), None),
            P(("dp", "seq"), None),
            P(None, ("dp", "seq")),
            P(("dp", "seq")),
            P(("dp", "seq"), None),
            P(("dp", "seq"), None),
            P(("dp", "seq"), None),
            P(("dp", "seq"), None),
            P(None, ("dp", "seq")),
            P(("dp", "seq")),
            P(None, ("dp", "seq")),
        ),
        check_vma=False,
    )
```
